128 devices in a mesh: dp: 32 (over x, y, core), ctx: 4 (over z).
Axes of the slice: x: 4, y: 4, z: 4, core: 2. Of those that a mesh axis runs over, the one named last changes fastest.
Arguments:
- tokens: bfloat16 [65536, 576], P(('dp', 'ctx')), may hold values from -6 to 6
- cotangent: bfloat16 [65536, 576], P(('dp', 'ctx')), may hold values from -6 to 6
- w_qkv: float32 [576, 960], P('ctx'), may hold values from -0.375 to 0.375
- w_out: float32 [576, 576], P('ctx'), may hold values from -0.75 to 0.75
- w_gate_up: float32 [576, 3072], P('ctx'), may hold values from -0.25 to 0.25
- w_down: float32 [1536, 576], P('ctx'), may hold values from -0.15625 to 0.15625
- vectors: float32 [2112], P('ctx'), may hold values from -1 to 1.4, as said below
- first_qkv: float32 [576, 960], P('ctx'), may hold values from -128 to 128
- first_out: float32 [576, 576], P('ctx'), may hold values from -64 to 64
- first_gate_up: float32 [576, 3072], P('ctx'), may hold values from -48 to 48
- first_down: float32 [1536, 576], P('ctx'), may hold values from -96 to 96
- first_vectors: float32 [2112], P('ctx'), may hold values from -160 to 160
- second_qkv: float32 [576, 960], P('ctx'), may hold values from 41.94304 to 167.77216
- second_out: float32 [576, 576], P('ctx'), may hold values from 8.51968 to 34.07872
- second_gate_up: float32 [576, 3072], P('ctx'), may hold values from 5.89824 to 23.59296
- second_down: float32 [1536, 576], P('ctx'), may hold values from 23.59296 to 94.37184
- second_vectors: float32 [2112], P('ctx'), may hold values from 65.536 to 262.144
Outputs:
- block_out: float32 [65536, 576], P(('dp', 'ctx'))
- input_grad: float32 [65536, 576], P(('dp', 'ctx'))
- new_qkv: float32 [576, 960], P('ctx')
- new_out: float32 [576, 576], P('ctx')
- new_gate_up: float32 [576, 3072], P('ctx')
- new_down: float32 [1536, 576], P('ctx')
- new_vectors: float32 [2112], P('ctx')
- moment_qkv: float32 [576, 960], P('ctx')
- moment_out: float32 [576, 576], P('ctx')
- moment_gate_up: float32 [576, 3072], P('ctx')
- moment_down: float32 [1536, 576], P('ctx')
- moment_vectors: float32 [2112], P('ctx')
- square_qkv: float32 [576, 960], P('ctx')
- square_out: float32 [576, 576], P('ctx')
- square_gate_up: float32 [576, 3072], P('ctx')
- square_down: float32 [1536, 576], P('ctx')
- square_vectors: float32 [2112], P('ctx')
The draws below stay inside these ranges and needn't reach their ends.
Inputs may be any that keep to these rules, and one draw needn't show every extreme that they name: `vectors`: the first 1152 entries are the two norms' gains, the others the query, key and value biases.
All inputs are finite; a program needn't handle non-finite values.
Results may differ from the reference program's by a relative error of at most 0.013.
The reference program's roundings to bfloat16 on the way count: a program that leaves them out, or rounds other values in their place, can miss the bound.
Values may be sent and summed in bfloat16 or wider, within the bound.
A program may use at most 256 MiB of HBM per device.

```python
import math
import jax
import jax.numpy as jnp
from jax import lax

D = 576
HEADS = 9
KV_HEADS = 3
HEAD_DIM = 64
FF = 1536
STEP = 10
LEN = 2048
TOKENS = 65536
QKV = 960
VEC = 2112
N_DP = 32


def draw_vectors(key, part):
    key = jax.random.fold_in(key, 5)
    gain_key, bias_key = jax.random.split(key)
    bias_count = D + 2 * KV_HEADS * HEAD_DIM
    gain_part = jax.random.uniform(gain_key, (2 * D,), jnp.float32, 0.6, 1.4)
    bias_part = jnp.clip(0.4 * jax.random.normal(bias_key, (bias_count,), jnp.float32), -1.0, 1.0)
    return jnp.concatenate([gain_part, bias_part])


def shard_levels(stream_key, shape, cuts, low, largest):
    gain, own = 1.0, jax.random.fold_in(stream_key, 6)
    for dim, shards_of in cuts:
        steps = jnp.exp(jax.random.uniform(jax.random.fold_in(own, dim), (shards_of,), jnp.float32, low / len(cuts), largest / len(cuts)))
        gain = gain * jnp.repeat(steps, shape[dim] // shards_of).reshape([-1 if axis == dim else 1 for axis in range(len(shape))])
    return gain


def bell_draw(own_key, shape, width, limit, pieces=(), kind=jnp.bfloat16):
    level = shard_levels(own_key, shape, pieces, -0.22, 0.18) if pieces else 1.0
    array = jax.random.normal(own_key, shape, jnp.float32) * width * level
    return jnp.minimum(jnp.maximum(array, -limit), limit).astype(kind)


def setup_inputs(seed: int = 0) -> dict:
    arg_keys = jax.random.split(jax.random.key(seed), 18)
    tokens = bell_draw(arg_keys[0], (TOKENS, D), 1.0, 6.0, ((0, 128),))
    cotangent = bell_draw(arg_keys[1], (TOKENS, D), 1.0, 6.0, ((0, 128),))
    w_qkv = bell_draw(arg_keys[2], (D, QKV), (D // 2) ** -0.5, 0.375, ((0, 4),), jnp.float32)
    w_out = bell_draw(arg_keys[3], (D, D), (D // 8) ** -0.5, 0.75, ((0, 4),), jnp.float32)
    w_gate_up = bell_draw(arg_keys[4], (D, 2 * FF), D ** -0.5, 0.25, ((0, 4),), jnp.float32)
    w_down = bell_draw(arg_keys[5], (FF, D), FF ** -0.5, 0.15625, ((0, 4),), jnp.float32)
    vectors = draw_vectors(jax.random.fold_in(arg_keys[17], 71), 0)
    first_qkv = bell_draw(arg_keys[7], (D, QKV), (0.088 * TOKENS ** 0.5), 128.0, ((0, 4),), jnp.float32)
    first_out = bell_draw(arg_keys[8], (D, D), (0.04 * TOKENS ** 0.5), 64.0, ((0, 4),), jnp.float32)
    first_gate_up = bell_draw(arg_keys[9], (D, 2 * FF), (0.033 * TOKENS ** 0.5), 48.0, ((0, 4),), jnp.float32)
    first_down = bell_draw(arg_keys[10], (FF, D), (0.066 * TOKENS ** 0.5), 96.0, ((0, 4),), jnp.float32)
    first_vectors = bell_draw(arg_keys[11], (VEC,), (0.11 * TOKENS ** 0.5), 160.0, ((0, 4),), jnp.float32)
    second_qkv = jnp.clip(jnp.exp(math.log(167.77216) - 1.3862944 * jax.random.uniform(arg_keys[12], (D, QKV), jnp.float32) ** shard_levels(arg_keys[12], (D, QKV), ((0, 4),), -0.2, 0.2)), 41.94304, 167.77216)
    second_out = jnp.clip(jnp.exp(math.log(34.07872) - 1.3862944 * jax.random.uniform(arg_keys[13], (D, D), jnp.float32) ** shard_levels(arg_keys[13], (D, D), ((0, 4),), -0.2, 0.2)), 8.51968, 34.07872)
    second_gate_up = jnp.clip(jnp.exp(math.log(23.59296) - 1.3862944 * jax.random.uniform(arg_keys[14], (D, 2 * FF), jnp.float32) ** shard_levels(arg_keys[14], (D, 2 * FF), ((0, 4),), -0.2, 0.2)), 5.89824, 23.59296)
    second_down = jnp.clip(jnp.exp(math.log(94.37184) - 1.3862944 * jax.random.uniform(arg_keys[15], (FF, D), jnp.float32) ** shard_levels(arg_keys[15], (FF, D), ((0, 4),), -0.2, 0.2)), 23.59296, 94.37184)
    second_vectors = jnp.clip(jnp.exp(math.log(262.144) - 1.3862944 * jax.random.uniform(arg_keys[16], (VEC,), jnp.float32) ** shard_levels(arg_keys[16], (VEC,), ((0, 4),), -0.2, 0.2)), 65.536, 262.144)
    return {"tokens": tokens, "cotangent": cotangent, "w_qkv": w_qkv, "w_out": w_out, "w_gate_up": w_gate_up, "w_down": w_down, "vectors": vectors, "first_qkv": first_qkv, "first_out": first_out, "first_gate_up": first_gate_up, "first_down": first_down, "first_vectors": first_vectors, "second_qkv": second_qkv, "second_out": second_out, "second_gate_up": second_gate_up, "second_down": second_down, "second_vectors": second_vectors}


@jax.custom_vjp
def low(v):
    return lax.optimization_barrier(v.astype(jnp.bfloat16)).astype(jnp.float32)

@jax.custom_vjp
def low_back(v):
    return v

def low_keep(v):
    return (low(v), None)

def low_pass(kept, grad):
    return (grad,)

def back_keep(v):
    return (v, None)

def back_low(kept, grad):
    return (low(grad),)
low.defvjp(low_keep, low_pass)
low_back.defvjp(back_keep, back_low)
EPS = 1e-05
ROPE_BASE = 100000.0
MASK_FILL = -1e+30
BETA_ONE = 0.9
BETA_TWO = 0.999
ADAM_EPS = 1e-08
RATE_MATRIX = 0.05
RATE_VECTOR = 0.5
DECAY_MATRIX = 0.1

def matmul_high(left, right):
    return jnp.dot(left, right, precision=lax.Precision.HIGHEST, preferred_element_type=jnp.float32)

def rotary_tables(positions):
    half_dim = HEAD_DIM // 2
    exponent = jnp.arange(half_dim, dtype=jnp.float32) * (2.0 / HEAD_DIM)
    inverse = ROPE_BASE ** (-exponent)
    angles = positions[:, None] * inverse[None, :]
    return (jnp.cos(angles), jnp.sin(angles))

def rotate(head_rows, cosine, sine_table):
    half_dim = head_rows.shape[-1] // 2
    first_half = head_rows[..., :half_dim]
    second_half = head_rows[..., half_dim:]
    cosine = cosine[:, None, :]
    sine_table = sine_table[:, None, :]
    return jnp.concatenate([first_half * cosine - second_half * sine_table, second_half * cosine + first_half * sine_table], axis=-1)

def rms_norm(row_values, gain_vector):
    inverse = lax.rsqrt(lax.optimization_barrier(jnp.mean(row_values * row_values, axis=-1, keepdims=True)) + EPS)
    return row_values * inverse * gain_vector

def attend_block(query_block, key_rows, value_rows, block_start):
    block_rows = query_block.shape[0]
    scores = jnp.einsum('qkgd,skd->kgqs', query_block, key_rows, precision=lax.Precision.HIGHEST)
    scores = low_back(scores * HEAD_DIM ** (-0.5))
    query_pos = block_start + jnp.arange(block_rows, dtype=jnp.int32)
    key_pos = jnp.arange(key_rows.shape[0], dtype=jnp.int32)
    allowed = key_pos[None, :] <= query_pos[:, None]
    scores = jnp.where(allowed, scores, MASK_FILL)
    row_peak = lax.optimization_barrier(jnp.max(scores, axis=-1, keepdims=True))
    expo = jnp.exp(scores - row_peak)
    attention_probs = low(expo / lax.optimization_barrier(jnp.sum(expo, axis=-1, keepdims=True)))
    return jnp.einsum('kgqs,skd->qkgd', attention_probs, value_rows, precision=lax.Precision.HIGHEST)

def block_layer(masters, inputs):
    w_qkv, w_out, w_gate_up, w_down, vectors = [low(master_piece) for master_piece in masters]
    kv_width = KV_HEADS * HEAD_DIM
    group_size = HEADS // KV_HEADS
    gain_attn = vectors[:D]
    gain_mlp = vectors[D:2 * D]
    bias_all = vectors[2 * D:]
    length = inputs.shape[0]
    normed_one = low(rms_norm(inputs, gain_attn))
    projected = low_back(matmul_high(normed_one, w_qkv) + bias_all)
    queries = projected[:, :D].reshape(length, HEADS, HEAD_DIM)
    key_rows = projected[:, D:D + kv_width].reshape(length, KV_HEADS, HEAD_DIM)
    value_rows = low(projected[:, D + kv_width:]).reshape(length, KV_HEADS, HEAD_DIM)
    cosine, sine_table = rotary_tables(jnp.arange(length, dtype=jnp.float32))
    queries = low(rotate(queries, cosine, sine_table))
    key_rows = low(rotate(key_rows, cosine, sine_table))
    block_rows = min(512, length)
    block_count = length // block_rows
    query_blocks = queries.reshape(block_count, block_rows, KV_HEADS, group_size, HEAD_DIM)
    block_starts = jnp.arange(block_count, dtype=jnp.int32) * block_rows

    def one_block(block_pair):
        return attend_block(block_pair[0], key_rows, value_rows, block_pair[1])
    mixed_heads = lax.map(jax.checkpoint(one_block), (query_blocks, block_starts))
    mixed_heads = low(low_back(mixed_heads.reshape(length, D)))
    hidden = inputs + low_back(matmul_high(mixed_heads, w_out))
    normed_two = low(rms_norm(hidden, gain_mlp))
    gate_up = low_back(matmul_high(normed_two, w_gate_up))
    activated = low(jax.nn.silu(gate_up[:, :FF]) * gate_up[:, FF:])
    return hidden + low_back(matmul_high(activated, w_down))

def adam_step(weight, first_state, second_state, gradient, learn_rate, decay_rate):
    first_new = BETA_ONE * first_state + (1.0 - BETA_ONE) * gradient
    second_new = BETA_TWO * second_state + (1.0 - BETA_TWO) * gradient * gradient
    corr_one = 1.0 - BETA_ONE ** STEP
    corr_two = 1.0 - BETA_TWO ** STEP
    update = first_new / corr_one / (jnp.sqrt(second_new / corr_two) + ADAM_EPS)
    weight_new = weight - learn_rate * (update + decay_rate * weight)
    return (weight_new, first_new, second_new)

def reference(tokens, cotangent, w_qkv, w_out, w_gate_up, w_down, vectors, first_qkv, first_out, first_gate_up, first_down, first_vectors, second_qkv, second_out, second_gate_up, second_down, second_vectors):
    masters = (w_qkv, w_out, w_gate_up, w_down, vectors)
    inputs_all = tokens.astype(jnp.float32).reshape(N_DP, LEN, D)
    cot_all = cotangent.astype(jnp.float32).reshape(N_DP, LEN, D)

    def one_sequence(running, sequence_pair):
        sequence_in, sequence_cot = sequence_pair
        output, pullback = jax.vjp(block_layer, masters, sequence_in)
        grad_masters, grad_in = pullback(sequence_cot)
        running = jax.tree.map(lambda left, right: left + right, running, grad_masters)
        return (running, (output, grad_in))
    zeros_init = jax.tree.map(lambda master_piece: jnp.zeros(master_piece.shape, jnp.float32), masters)
    grads, (outputs, grad_inputs) = lax.scan(one_sequence, zeros_init, (inputs_all, cot_all))
    firsts = (first_qkv, first_out, first_gate_up, first_down, first_vectors)
    seconds = (second_qkv, second_out, second_gate_up, second_down, second_vectors)
    new_weights = []
    new_firsts = []
    new_seconds = []
    for index_piece in range(5):
        learn_rate = RATE_VECTOR if index_piece == 4 else RATE_MATRIX
        decay_rate = 0.0 if index_piece == 4 else DECAY_MATRIX
        weight_new, first_new, second_new = adam_step(masters[index_piece], firsts[index_piece], seconds[index_piece], grads[index_piece], learn_rate, decay_rate)
        new_weights.append(weight_new)
        new_firsts.append(first_new)
        new_seconds.append(second_new)
    return (outputs.reshape(TOKENS, D), grad_inputs.reshape(TOKENS, D), new_weights[0], new_weights[1], new_weights[2], new_weights[3], new_weights[4], new_firsts[0], new_firsts[1], new_firsts[2], new_firsts[3], new_firsts[4], new_seconds[0], new_seconds[1], new_seconds[2], new_seconds[3], new_seconds[4])
```

```python
import functools

import jax
import jax.numpy as jnp
import numpy as np
from jax import lax
from jax.experimental import pallas as pl
from jax.experimental.pallas import tpu as pltpu
from jax.sharding import PartitionSpec as P

D = 576
HEADS = 9
KV_HEADS = 3
GROUP = 3
HEAD_DIM = 64
FF = 1536
STEP = 10
LEN = 2048
ROWS = 512
QW = 1024
OW = 768
VW = 2304
NX = 4
NY = 4
NZ = 4

EPS = 1e-05
ROPE_BASE = 100000.0
MASK_FILL = -1e30
BETA_ONE = 0.9
BETA_TWO = 0.999
ADAM_EPS = 1e-08
RATE_MATRIX = 0.05
RATE_VECTOR = 0.5
DECAY_MATRIX = 0.1

F32 = jnp.float32
BF16 = jnp.bfloat16
MESH = pl.DeviceIdType.MESH
VM = pltpu.VMEM
ANY = pl.ANY


def rope_tables():
    half = HEAD_DIM // 2
    exponent = np.arange(half, dtype=np.float32) * np.float32(2.0 / HEAD_DIM)
    inverse = (np.float64(ROPE_BASE) ** (-exponent.astype(np.float64))).astype(np.float32)
    angles = np.arange(LEN, dtype=np.float32)[:, None] * inverse[None, :]
    cosine = np.cos(angles.astype(np.float64)).astype(np.float32)
    sine = np.sin(angles.astype(np.float64)).astype(np.float32)
    cos_all = np.concatenate([cosine] * 4, axis=1)
    sin_all = np.concatenate([-sine, sine, -sine, sine], axis=1)
    return cos_all, sin_all


def dot(a, b, ca=1, cb=0):
    return lax.dot_general(a, b, (((ca,), (cb,)), ((), ())), preferred_element_type=F32)


def place():
    dp = lax.axis_index("dp")
    z = lax.axis_index("ctx")
    x = lax.div(dp, NY * 2)
    y = lax.rem(lax.div(dp, 2), NY)
    c = lax.rem(dp, 2)
    return x, y, c, z


def device(x, y, c, z):
    return (x * (NY * 2) + y * 2 + c, z)


def wrap(i, n):
    return lax.rem(i, n)


def remote(src, dst, ssem, rsem, dev):
    return pltpu.make_async_remote_copy(
        src_ref=src, dst_ref=dst, send_sem=ssem, recv_sem=rsem, device_id=dev, device_id_type=MESH
    )


def greet(peers):
    barrier = pltpu.get_barrier_semaphore()
    for peer in peers:
        pl.semaphore_signal(barrier, inc=1, device_id=peer, device_id_type=MESH)
    pl.semaphore_wait(barrier, len(peers))


def swap_halves(v):
    width = v.shape[1]
    lane = lax.broadcasted_iota(jnp.int32, v.shape, 1)
    down = pltpu.roll(v, width - 32, 1)
    up = pltpu.roll(v, 32, 1)
    return jnp.where(lax.rem(lane, 64) < 32, down, up)


def low_lanes(v):
    lane = lax.broadcasted_iota(jnp.int32, v.shape, 1)
    return lane < 64


def forward_kernel(
    tok, wq_in, vec_in, cos_hbm, sin_hbm, wo_in, wgu_in, wdn_in,
    q_out, qt_out, kv_out, att_out, lse_out, n1_out, wq_out, vec_out, wo_all, wgu_all, wdn_all,
    bq, wq_v, vec_v, cos_v, sin_v, f_out, f_gu, f_dn, b_out, b_gu, b_dn,
    kvs, kvt, m_s, l_s, ot_s,
    loc_sem, zq_s, zq_r, cq_s, cq_r, zv_s, zv_r, zw_s, zw_r, aw_s, aw_r, cw_s, cw_r, kv_s, kv_r,
):
    x, y, c, z = place()
    sib = device(x, y, 1 - c, z)
    zdev = [device(x, y, c, wrap(z + d, NZ)) for d in range(1, NZ)]
    xdev = [device(wrap(x + d, NX), y, c, z) for d in range(1, NX)]
    ydev = [device(x, wrap(y + d, NY), c, z) for d in range(1, NY)]
    row0 = pl.multiple_of(z * ROWS, ROWS)
    loads = [
        pltpu.make_async_copy(cos_hbm.at[pl.ds(row0, ROWS)], cos_v, loc_sem.at[0]),
        pltpu.make_async_copy(sin_hbm.at[pl.ds(row0, ROWS)], sin_v, loc_sem.at[1]),
        pltpu.make_async_copy(wo_in, f_out, loc_sem.at[2]),
        pltpu.make_async_copy(wgu_in, f_gu, loc_sem.at[3]),
        pltpu.make_async_copy(wdn_in, f_dn, loc_sem.at[4]),
    ]
    for load in loads:
        load.start()
    bq[:, 0:896] = wq_in[:, 0:896].astype(BF16)
    bq[:, 896:1024] = jnp.concatenate(
        [wq_in[:, 896:960].astype(BF16), jnp.zeros((144, 64), BF16)], axis=1
    )
    greet(zdev + xdev + ydev + [sib])

    qrows = pl.multiple_of(z * 144, 144)
    qcol = pl.multiple_of(c * 512, 512)
    sends_q = []
    for d in range(1, NZ):
        sends_q.append(
            remote(bq.at[:, pl.ds(qcol, 512)], wq_v.at[pl.ds(qrows, 144), pl.ds(qcol, 512)],
                   zq_s.at[d - 1], zq_r.at[d - 1], zdev[d - 1]))
        sends_q.append(
            remote(vec_in, vec_v.at[d], zv_s.at[d - 1], zv_r.at[d - 1], zdev[d - 1]))
    for s in sends_q:
        s.start()
    wq_v[pl.ds(qrows, 144), :] = bq[...]
    vec_v[0] = vec_in[...]
    inputs = tok[...].astype(F32)
    unit = inputs * lax.rsqrt(jnp.mean(inputs * inputs, axis=-1, keepdims=True) + EPS)

    loads[2].wait()
    b_out[:, 0:576] = f_out[...].astype(BF16)
    b_out[:, 576:768] = jnp.zeros((144, 192), BF16)
    loads[3].wait()
    for i in range(8):
        b_gu[:, 384 * i : 384 * i + 384] = f_gu[:, 384 * i : 384 * i + 384].astype(BF16)
    loads[4].wait()
    b_dn[...] = f_dn[...].astype(BF16)
    own = [
        pltpu.make_async_copy(b_out, wo_all.at[pl.ds(qrows, 144), :], loc_sem.at[5]),
        pltpu.make_async_copy(b_gu, wgu_all.at[pl.ds(qrows, 144), :], loc_sem.at[6]),
        pltpu.make_async_copy(b_dn, wdn_all.at[pl.ds(pl.multiple_of(z * 384, 384), 384), :], loc_sem.at[7]),
    ]
    for copy in own:
        copy.start()

    for s in sends_q:
        s.wait_recv()
    swaps = []
    for d in range(1, NZ):
        rows = pl.ds(pl.multiple_of(wrap(z + NZ - d, NZ) * 144, 144), 144)
        ref = wq_v.at[rows, pl.ds(qcol, 512)]
        swaps.append(remote(ref, ref, cq_s.at[d - 1], cq_r.at[d - 1], sib))
    for s in swaps:
        s.start()
    for s in swaps:
        s.wait_recv()

    vec = vec_v[0] + vec_v[1] + vec_v[2] + vec_v[3]
    vec = vec.astype(BF16).astype(F32)
    vec_out[...] = vec
    n1 = (unit * vec[:, 0:576]).astype(BF16)
    n1_out[...] = n1
    loads[0].wait()
    loads[1].wait()
    proj = dot(n1, wq_v[...]) + vec[:, 1280:2304]
    cos6 = jnp.concatenate([cos_v[...]] * 6, axis=1)
    sin6 = jnp.concatenate([sin_v[...]] * 6, axis=1)
    qk = proj[:, 0:768]
    rot = qk * cos6 + swap_halves(qk) * sin6
    low = low_lanes(rot[:, 0:128])

    def tile_of(v, t):
        return v[:, 128 * t : 128 * t + 128]

    def head_low(v, h):
        part = tile_of(v, h // 2)
        return part if h % 2 == 0 else pltpu.roll(part, 64, 1)

    for g in range(KV_HEADS):
        key = head_low(rot, HEADS + g)
        val = tile_of(proj, 6 + g // 2)
        val = val if g % 2 == 1 else pltpu.roll(val, 64, 1)
        kvs[z, g] = jnp.where(low, key, val).astype(BF16)
    kv_sends = []
    for d in range(1, NZ):
        kv_sends.append(
            remote(kvs.at[z], kvs.at[z], kv_s.at[d - 1], kv_r.at[d - 1], device(x, y, c, wrap(z + d, NZ))))

        @pl.when(z + d < NZ)
        def _(d=d):
            kv_sends[d - 1].start()

    pgu = pl.multiple_of((c * 4 + x) * 384, 128)
    pdn = (c * 4 + y) * 48
    oc = pl.multiple_of(c * 384, 128)
    wsend = []
    for d in range(1, NZ):
        wsend.append(
            remote(b_out.at[:, pl.ds(oc, 384)], wo_all.at[pl.ds(qrows, 144), pl.ds(oc, 384)],
                   zw_s.at[0, d - 1], zw_r.at[0, d - 1], zdev[d - 1]))
        wsend.append(
            remote(b_gu.at[:, pl.ds(pgu, 384)], wgu_all.at[pl.ds(qrows, 144), pl.ds(pgu, 384)],
                   zw_s.at[1, d - 1], zw_r.at[1, d - 1], zdev[d - 1]))
        wsend.append(
            remote(b_dn.at[pl.ds(pl.multiple_of(pdn, 48), 48), :],
                   wdn_all.at[pl.ds(pl.multiple_of(z * 384 + pdn, 48), 48), :],
                   zw_s.at[2, d - 1], zw_r.at[2, d - 1], zdev[d - 1]))
    for s in wsend:
        s.start()

    for h in range(HEADS):
        qh = jnp.where(low, head_low(rot, h), 0.0) * (HEAD_DIM ** -0.5)
        q_out[h] = qh.astype(BF16)
        qt_out[h] = jnp.transpose(qh).astype(BF16)

    def step(j, diagonal):
        for g in range(KV_HEADS):
            kvt[g] = jnp.transpose(kvs[j, g].astype(F32)).astype(BF16)

        def head(h, carry):
            g = lax.div(h, GROUP)
            st = dot(kvs[j, g], qt_out[h])
            if diagonal:
                kpos = lax.broadcasted_iota(jnp.int32, st.shape, 0)
                qpos = lax.broadcasted_iota(jnp.int32, st.shape, 1)
                st = jnp.where(kpos <= qpos, st, MASK_FILL)
            peak = jnp.max(st, axis=0, keepdims=True)
            if not diagonal:
                peak_old = m_s[h]
                peak = jnp.maximum(peak, peak_old)
                alpha = jnp.exp(peak_old - peak)
            p = jnp.exp(st - peak)
            total = jnp.sum(p, axis=0, keepdims=True)
            out = dot(kvt[g], p.astype(BF16))
            if not diagonal:
                total = total + l_s[h] * alpha
                out = out + ot_s[h] * alpha
            m_s[h] = peak
            l_s[h] = total
            ot_s[h] = out
            return carry

        lax.fori_loop(0, HEADS, head, 0)

    step(z, True)

    for s in wsend:
        s.wait_recv()
    leg = []
    for e in range(1, NZ):
        src_z = wrap(z + NZ - e, NZ)
        rows = pl.ds(pl.multiple_of(src_z * 144, 144), 144)
        ref_gu = wgu_all.at[rows, pl.ds(pgu, 384)]
        ref_dn = wdn_all.at[pl.ds(pl.multiple_of(src_z * 384 + pdn, 48), 48), :]
        for d in range(1, NX):
            leg.append(remote(ref_gu, ref_gu, aw_s.at[0, e - 1, d - 1], aw_r.at[0, e - 1, d - 1], xdev[d - 1]))
            leg.append(remote(ref_dn, ref_dn, aw_s.at[1, e - 1, d - 1], aw_r.at[1, e - 1, d - 1], ydev[d - 1]))
    for s in leg:
        s.start()
    last = []
    for e in range(1, NZ):
        src_z = wrap(z + NZ - e, NZ)
        rows = pl.ds(pl.multiple_of(src_z * 144, 144), 144)
        ref_o = wo_all.at[rows, pl.ds(oc, 384)]
        last.append(remote(ref_o, ref_o, cw_s.at[0, e - 1], cw_r.at[0, e - 1], sib))
    for s in last:
        s.start()

    for d in range(1, NZ):
        if d == 2:
            for s in leg:
                s.wait_recv()
            for e in range(1, NZ):
                src_z = wrap(z + NZ - e, NZ)
                rows = pl.ds(pl.multiple_of(src_z * 144, 144), 144)
                ref_g = wgu_all.at[rows, pl.ds(pl.multiple_of(c * 1536, 128), 1536)]
                ref_d = wdn_all.at[pl.ds(pl.multiple_of(src_z * 384 + c * 192, 192), 192), :]
                more = [
                    remote(ref_g, ref_g, cw_s.at[1, e - 1], cw_r.at[1, e - 1], sib),
                    remote(ref_d, ref_d, cw_s.at[2, e - 1], cw_r.at[2, e - 1], sib),
                ]
                for s in more:
                    s.start()
                last.extend(more)

        @pl.when(z >= d)
        def _(d=d):
            kv_sends[d - 1].wait_recv()
            step(z - d, False)

    kv_out[...] = kvs[...]
    wq_out[...] = wq_v[...]
    for h in range(HEADS):
        inv = 1.0 / l_s[h]
        ot_s[h] = ot_s[h] * inv
        lse_out[h] = m_s[h] + jnp.log(l_s[h])
    for t in range(5):
        top = ot_s[2 * t, 64:128, :]
        bottom = ot_s[2 * t + 1, 64:128, :] if 2 * t + 1 < HEADS else jnp.zeros((64, ROWS), F32)
        att_out[:, 128 * t : 128 * t + 128] = jnp.transpose(jnp.concatenate([top, bottom], axis=0))

    for s in last:
        s.wait_recv()
    for s in sends_q + swaps + wsend + leg + last:
        s.wait_send()
    for d in range(1, NZ):

        @pl.when(z + d < NZ)
        def _(d=d):
            kv_sends[d - 1].wait_send()

    for copy in own:
        copy.wait()


def forward(tok, wq, vec, cos_t, sin_t, wo, wgu, wdn):
    sd = jax.ShapeDtypeStruct
    v = pl.BlockSpec(memory_space=VM)
    a = pl.BlockSpec(memory_space=ANY)
    dma = pltpu.SemaphoreType.DMA
    return pl.pallas_call(
        forward_kernel,
        out_shape=(
            sd((HEADS, ROWS, 128), BF16),
            sd((HEADS, 128, ROWS), BF16),
            sd((NZ, KV_HEADS, ROWS, 128), BF16),
            sd((ROWS, 640), F32),
            sd((HEADS, 1, ROWS), F32),
            sd((ROWS, D), BF16),
            sd((D, QW), BF16),
            sd((1, VW), F32),
            sd((D, OW), BF16),
            sd((D, 2 * FF), BF16),
            sd((FF, D), BF16),
        ),
        in_specs=[v, v, v, a, a, a, a, a],
        out_specs=(v,) * 8 + (a,) * 3,
        scratch_shapes=[
            VM((144, QW), BF16), VM((D, QW), BF16), VM((NZ, 1, VW), F32),
            VM((ROWS, 128), F32), VM((ROWS, 128), F32),
            VM((144, D), F32), VM((144, 2 * FF), F32), VM((384, D), F32),
            VM((144, OW), BF16), VM((144, 2 * FF), BF16), VM((384, D), BF16),
            VM((NZ, KV_HEADS, ROWS, 128), BF16), VM((KV_HEADS, 128, ROWS), BF16),
            VM((HEADS, 1, ROWS), F32), VM((HEADS, 1, ROWS), F32), VM((HEADS, 128, ROWS), F32),
            dma((8,)), dma((3,)), dma((3,)), dma((3,)), dma((3,)), dma((3,)), dma((3,)),
            dma((3, 3)), dma((3, 3)), dma((2, 3, 3)), dma((2, 3, 3)), dma((3, 3)), dma((3, 3)),
            dma((3,)), dma((3,)),
        ],
        compiler_params=pltpu.CompilerParams(
            collective_id=0, has_side_effects=True, vmem_limit_bytes=56 << 20),
        name="gather_attend",
    )(tok, wq, vec, cos_t, sin_t, wo, wgu, wdn)


def middle_kernel(
    att, wo, tok, cot, vec, wg, wu, wd,
    block_out, gh_out, do_out, dot_out, delta_out, ggu_out, gdn_out, go_out, gain_out,
    hid, n2, n2t, gn2, inv,
):
    i = pl.program_id(0)
    gain = vec[:, 640:1216]

    @pl.when(i == 0)
    def _():
        low = att[:, 0:576].astype(BF16)
        h = tok[...].astype(F32) + dot(low, wo[:, 0:576])
        hid[...] = h
        block_out[...] = h
        r = lax.rsqrt(jnp.mean(h * h, axis=-1, keepdims=True) + EPS)
        inv[...] = jnp.broadcast_to(r, (ROWS, 128))
        normed = h * r * gain
        n2[...] = normed.astype(BF16)
        n2t[...] = jnp.transpose(normed).astype(BF16)
        gn2[...] = jnp.zeros_like(gn2)

    gate = dot(n2[...], wg[...])
    up = dot(n2[...], wu[...])
    sg = jax.nn.sigmoid(gate)
    silu = gate * sg
    act = (silu * up).astype(BF16)
    block_out[...] += dot(act, wd[...])
    ga = dot(cot[...], wd[...], 1, 1)
    gg = (ga * up * sg * (1.0 + gate * (1.0 - sg))).astype(BF16)
    gu = (ga * silu).astype(BF16)
    gdn = dot(act, cot[...], 0, 0).astype(BF16)
    for p in range(8):
        gdn_out[p // 4, p % 4, 0] = gdn[48 * p : 48 * p + 48, :]
    ggu_out[0, 0] = dot(n2t[...], gg).astype(BF16)
    ggu_out[1, 0] = dot(n2t[...], gu).astype(BF16)
    gn2[...] += dot(gg, wg[...], 1, 1) + dot(gu, wu[...], 1, 1)

    @pl.when(i == pl.num_programs(0) - 1)
    def _():
        r = inv[:, 0:1]
        u = hid[...] * r
        e = gn2[...]
        f = e * gain
        gain_out[:, 0:576] = jnp.sum(e * u, axis=0, keepdims=True)
        gain_out[:, 576:640] = jnp.zeros((1, 64), F32)
        gh = cot[...].astype(F32) + r * (f - u * jnp.mean(f * u, axis=-1, keepdims=True))
        gh_out[...] = gh
        ghl = gh.astype(BF16)
        go = dot(att[:, 0:576].astype(BF16), ghl, 0, 0).astype(BF16)
        for p in range(8):
            if p < 4:
                part = go[:, 128 * p : 128 * p + 128]
            elif p == 4:
                part = jnp.concatenate([go[:, 512:576], jnp.zeros((D, 64), BF16)], axis=1)
            else:
                part = jnp.zeros((D, 128), BF16)
            go_out[p // 4, p % 4] = part
        gm = dot(ghl, wo[:, 0:576], 1, 1).astype(BF16).astype(F32)
        prod = gm * att[:, 0:576]
        high = prod.astype(BF16)
        rest = (prod - high.astype(F32)).astype(BF16)
        head_of = lax.broadcasted_iota(jnp.int32, (16, D), 1) // HEAD_DIM
        pick = (head_of == lax.broadcasted_iota(jnp.int32, (16, D), 0)).astype(F32).astype(BF16)
        delta = dot(pick, high, 1, 1) + dot(pick, rest, 1, 1)
        for h in range(HEADS):
            delta_out[h] = delta[h : h + 1, :]
        gm = jnp.concatenate([gm, jnp.zeros((ROWS, 64), F32)], axis=1)
        low = low_lanes(gm[:, 0:128])
        for h in range(HEADS):
            part = gm[:, 128 * (h // 2) : 128 * (h // 2) + 128]
            part = part if h % 2 == 1 else pltpu.roll(part, 64, 1)
            part = jnp.where(low, 0.0, part)
            do_out[h] = part.astype(BF16)
            dot_out[h] = jnp.transpose(part).astype(BF16)


def middle(att, wo, tok, cot, vec, wgu, wdn):
    sd = jax.ShapeDtypeStruct

    def whole(shape):
        return pl.BlockSpec(shape, lambda i: (0,) * len(shape))

    return pl.pallas_call(
        middle_kernel,
        grid=(4,),
        out_shape=(
            sd((ROWS, D), F32),
            sd((ROWS, D), F32),
            sd((HEADS, ROWS, 128), BF16),
            sd((HEADS, 128, ROWS), BF16),
            sd((HEADS, 1, ROWS), F32),
            sd((2, 4, D, 384), BF16),
            sd((2, 4, NZ, 48, D), BF16),
            sd((2, 4, D, 128), BF16),
            sd((1, 640), F32),
        ),
        in_specs=[
            whole((ROWS, 640)), whole((D, OW)), whole((ROWS, D)), whole((ROWS, D)), whole((1, VW)),
            pl.BlockSpec((D, 384), lambda i: (0, i)),
            pl.BlockSpec((D, 384), lambda i: (0, i + 4)),
            pl.BlockSpec((384, D), lambda i: (i, 0)),
        ],
        out_specs=(
            whole((ROWS, D)), whole((ROWS, D)), whole((HEADS, ROWS, 128)), whole((HEADS, 128, ROWS)),
            whole((HEADS, 1, ROWS)),
            pl.BlockSpec((2, 1, D, 384), lambda i: (0, i, 0, 0)),
            pl.BlockSpec((2, 4, 1, 48, D), lambda i: (0, 0, i, 0, 0)),
            whole((2, 4, D, 128)), whole((1, 640)),
        ),
        scratch_shapes=[
            VM((ROWS, D), F32), VM((ROWS, D), BF16), VM((D, ROWS), BF16), VM((ROWS, D), F32),
            VM((ROWS, 128), F32),
        ],
        compiler_params=pltpu.CompilerParams(
            vmem_limit_bytes=56 << 20, dimension_semantics=("arbitrary",)),
        name="feed_forward",
    )(att, wo, tok, cot, vec, wgu, wgu, wdn)


class Reduction:
    SCRATCH = 8

    @staticmethod
    def scratch(r, w):
        dma = pltpu.SemaphoreType.DMA
        return [
            VM((4, 4, r, w), BF16), VM((4, 4, r, w), BF16), VM((3, 4, r, w), BF16), VM((4, r, w), BF16),
            VM((3, r, w), BF16), VM((4, r, w), BF16), dma((18,)), dma((18,)),
        ]

    def __init__(self, own, fin, fin_at, bufs, along_x):
        self.own, self.fin, self.fin_at = own, fin, fin_at
        self.mine, self.rc, self.r1, self.s1, self.r2, self.r3, self.ss, self.rs = bufs
        x, y, c, z = place()
        self.c, self.z = c, z
        if along_x:
            self.a, self.b = x, y
            self.at = lambda a, b, cc, zz: device(a, b, cc, zz)
        else:
            self.a, self.b = y, x
            self.at = lambda a, b, cc, zz: device(b, a, cc, zz)
        self.sends = []

    def go(self, src, dst, k, dev):
        copy = remote(src, dst, self.ss.at[k], self.rs.at[k], dev)
        copy.start()
        self.sends.append(copy)
        return copy

    def start(self, load_sem=None):
        a, b, c, z = self.a, self.b, self.c, self.z
        self.core = self.go(self.own.at[1 - c], self.rc, 0, self.at(a, b, 1 - c, z))
        self.load = None
        if load_sem is not None:
            self.load = pltpu.make_async_copy(self.own.at[c], self.mine, load_sem)
            self.load.start()

    def stage1(self):
        a, b, c, z = self.a, self.b, self.c, self.z
        self.core.wait_recv()
        if self.load is not None:
            self.load.wait()
        mine = self.mine

        def add(k, carry):
            i = lax.div(k, 4)
            j = lax.rem(k, 4)
            left = mine[i, j] if self.load is not None else self.own[c, i, j]
            mine[i, j] = (left.astype(F32) + self.rc[i, j].astype(F32)).astype(BF16)
            return carry

        lax.fori_loop(0, 16, add, 0)
        self.first = []
        for d in range(1, 4):
            to = wrap(a + d, 4)
            self.first.append(self.go(mine.at[to], self.r1.at[d - 1], d, self.at(to, b, c, z)))

    def stage2(self):
        a, b, c, z = self.a, self.b, self.c, self.z
        for copy in self.first:
            copy.wait_recv()

        def add(j, carry):
            total = self.mine[a, j].astype(F32) + self.r1[0, j].astype(F32)
            total = total + self.r1[1, j].astype(F32) + self.r1[2, j].astype(F32)
            self.s1[j] = total.astype(BF16)
            return carry

        lax.fori_loop(0, 4, add, 0)
        self.second = []
        for d in range(1, 4):
            to = wrap(z + d, 4)
            self.second.append(self.go(self.s1.at[to], self.r2.at[d - 1], 3 + d, self.at(a, b, c, to)))

    def stage3(self):
        a, b, c, z = self.a, self.b, self.c, self.z
        for copy in self.second:
            copy.wait_recv()
        total = self.s1[z].astype(F32) + self.r2[0].astype(F32)
        total = total + self.r2[1].astype(F32) + self.r2[2].astype(F32)
        self.r3[b] = total.astype(BF16)
        self.third = []
        for d in range(1, 4):
            to = wrap(b + d, 4)
            self.third.append(self.go(self.r3.at[b], self.r3.at[b], 6 + d, self.at(a, to, c, z)))

    def stage4(self):
        a, b, c, z = self.a, self.b, self.c, self.z
        for copy in self.third:
            copy.wait_recv()
        total = self.r3[0].astype(F32) + self.r3[1].astype(F32)
        total = total + self.r3[2].astype(F32) + self.r3[3].astype(F32)
        where = self.fin_at(c, a)
        ref = self.fin.at[where]
        self.fin[where] = total.astype(BF16)
        self.fourth = []
        k = 9
        for e in range(2):
            for d in range(4):
                if e == 0 and d == 0:
                    continue
                k += 1
                to = self.at(wrap(a + d, 4), b, wrap(c + e, 2), z)
                self.fourth.append(self.go(ref, ref, k, to))

    def finish(self):
        for copy in self.fourth:
            copy.wait_recv()
        for copy in self.sends:
            copy.wait_send()


class VectorSum:
    @staticmethod
    def scratch():
        dma = pltpu.SemaphoreType.DMA
        return [VM((2, 24, 128), F32), VM((3, 4, 24, 128), F32), dma((10,)), dma((10,))]

    def __init__(self, bufs):
        self.rc, self.r, self.ss, self.rs = bufs
        self.sends = []

    def start(self):
        x, y, c, z = place()
        self.pending = [remote(self.rc.at[0], self.rc.at[1], self.ss.at[0], self.rs.at[0], device(x, y, 1 - c, z))]
        self.pending[0].start()
        self.sends += self.pending

    def next(self, k):
        x, y, c, z = place()
        for copy in self.pending:
            copy.wait_recv()
        if k == 0:
            total = self.rc[0] + self.rc[1]
        else:
            total = self.r[k - 1, 0] + self.r[k - 1, 1] + self.r[k - 1, 2] + self.r[k - 1, 3]
        if k == 3:
            return total
        me = (y, z, x)[k]
        self.r[k, me] = total
        self.pending = []
        for d in range(1, 4):
            to = wrap(me + d, 4)
            dev = (device(x, to, c, z), device(x, y, c, to), device(to, y, c, z))[k]
            copy = remote(self.r.at[k, me], self.r.at[k, me], self.ss.at[3 * k + d], self.rs.at[3 * k + d], dev)
            copy.start()
            self.pending.append(copy)
        self.sends += self.pending
        return None

    def finish(self):
        for copy in self.sends:
            copy.wait_send()


def backward_kernel(
    q_in, qt_in, do_in, dot_in, kv_in, lse_in, delta_in, n1_in, tok, gh_in, wq, vec, gain_in, cos_hbm, sin_hbm,
    ggu, gdn, go,
    grad_in, fgu, fdn, fo, fq, vsum,
    kt, dqt, acc, own_kv, skv, rkv, gq, cos_v, sin_v, n1t,
    *rest,
):
    n = Reduction.SCRATCH
    red_gu = Reduction(
        ggu, fgu, lambda c, a: (slice(None), pl.ds(pl.multiple_of((c * 4 + a) * 384, 128), 384)), rest[0:n], True)
    red_dn = Reduction(
        gdn, fdn, lambda c, a: (pl.ds(pl.multiple_of((c * 4 + a) * 48, 48), 48), slice(None)), rest[n : 2 * n], False)
    lanes = lambda c, a: (slice(None), pl.ds(pl.multiple_of((c * 4 + a) * 128, 128), 128))
    red_o = Reduction(go, fo, lanes, rest[2 * n : 3 * n], False)
    red_q = Reduction(gq, fq, lanes, rest[3 * n : 4 * n], False)
    vecs = VectorSum(rest[4 * n : 4 * n + 4])
    loc_sem, kv_s, kv_r = rest[4 * n + 4 :]
    x, y, c, z = place()
    zdev = [device(x, y, c, wrap(z + d, NZ)) for d in range(1, NZ)]
    peers = list(zdev)
    for e in range(2):
        for d in range(4):
            if e or d:
                peers.append(device(wrap(x + d, NX), y, wrap(c + e, 2), z))
            if d:
                peers.append(device(x, wrap(y + d, NY), wrap(c + e, 2), z))
    row0 = pl.multiple_of(z * ROWS, ROWS)
    loads = [
        pltpu.make_async_copy(cos_hbm.at[pl.ds(row0, ROWS)], cos_v, loc_sem.at[0]),
        pltpu.make_async_copy(sin_hbm.at[pl.ds(row0, ROWS)], sin_v, loc_sem.at[1]),
    ]
    for load in loads:
        load.start()
    greet(peers)
    red_gu.start(loc_sem.at[2])
    red_dn.start(loc_sem.at[3])
    red_o.start(loc_sem.at[4])
    n1t[...] = jnp.transpose(n1_in[...].astype(F32)).astype(BF16)

    def attend(g, j, diagonal):
        kt[...] = jnp.transpose(kv_in[j, g].astype(F32)).astype(BF16)

        def head(k, carry):
            h = g * GROUP + k
            st = dot(kv_in[j, g], qt_in[h])
            pt = jnp.exp(st - lse_in[h])
            if diagonal:
                kpos = lax.broadcasted_iota(jnp.int32, st.shape, 0)
                qpos = lax.broadcasted_iota(jnp.int32, st.shape, 1)
                pt = jnp.where(kpos <= qpos, pt, 0.0)
            dpt = dot(kv_in[j, g], dot_in[h])
            dst = (pt * (dpt - delta_in[h])).astype(BF16)
            both = dot(dst, q_in[h]) + dot(pt.astype(BF16), do_in[h])
            dq = dot(kt[...], dst)

            @pl.when(k == 0)
            def _():
                acc[...] = both

            @pl.when(k > 0)
            def _():
                acc[...] += both

            if diagonal:

                @pl.when(z == 0)
                def _():
                    dqt[h] = dq

                @pl.when(z > 0)
                def _():
                    dqt[h] += dq
            else:

                @pl.when(j == 0)
                def _():
                    dqt[h] = dq

                @pl.when(j > 0)
                def _():
                    dqt[h] += dq

            return carry

        lax.fori_loop(0, GROUP, head, 0)

    def kv_copy(g, s, dev):
        return remote(skv.at[g, s - 1], rkv.at[g, s - 1], kv_s.at[g, s - 1], kv_r.at[g, s - 1], dev)

    for g in range(KV_HEADS):

        def far(j, carry):
            attend(g, j, False)
            s = z - j
            skv[g, s - 1] = acc[...].astype(BF16)
            kv_copy(g, s, device(x, y, c, j)).start()
            return carry

        lax.fori_loop(0, z, far, 0)
        if g == 0:
            red_gu.stage1()
            red_dn.stage1()
            red_o.stage1()
        attend(g, z, True)
        own_kv[g] = acc[...]
        if g == 1:
            red_dn.stage2()
            red_o.stage2()
            red_gu.stage2()

    loads[0].wait()
    loads[1].wait()
    red_dn.stage3()
    red_o.stage3()
    red_gu.stage3()

    kvg = []
    for g in range(KV_HEADS):
        for s in range(1, NZ):

            @pl.when(z + s < NZ)
            def _(g=g, s=s):
                kv_copy(g, s, zdev[0]).wait_recv()
                own_kv[g] += rkv[g, s - 1].astype(F32)

        kvg.append(own_kv[g])
    low = low_lanes(kvg[0])

    def pair(left, right):
        return jnp.where(low, left, pltpu.roll(right, 64, 1))

    tiles = []
    for t in range(5):
        top = dqt[2 * t, 0:64, :]
        bottom = dqt[2 * t + 1, 0:64, :] if 2 * t + 1 < HEADS else jnp.zeros((64, ROWS), F32)
        tiles.append(jnp.transpose(jnp.concatenate([top, bottom], axis=0)) * (HEAD_DIM ** -0.5))
    tiles[4] = pair(tiles[4], kvg[0])
    tiles.append(pair(kvg[1], kvg[2]))
    cosine, sine = cos_v[...], sin_v[...]
    tiles = [t * cosine - swap_halves(t) * sine for t in tiles]
    tiles.append(jnp.where(low, pltpu.roll(kvg[0], 64, 1), kvg[1]))
    tiles.append(jnp.where(low, pltpu.roll(kvg[2], 64, 1), 0.0))
    gp = [t.astype(BF16) for t in tiles]
    gn1 = None
    for t in range(8):
        full = dot(n1t[...], gp[t]).astype(BF16)
        for k in range(NZ):
            gq[t // 4, t % 4, k] = full[144 * k : 144 * k + 144, :]
    red_q.start()
    vecs.rc[0, 10:18, :] = jnp.concatenate(
        [jnp.sum(t.astype(F32), axis=0, keepdims=True) for t in gp], axis=0)
    gn1 = dot(jnp.concatenate(gp, axis=1), wq[...], 1, 1)
    inputs = tok[...].astype(F32)
    r = lax.rsqrt(jnp.mean(inputs * inputs, axis=-1, keepdims=True) + EPS)
    u = inputs * r
    f = gn1 * vec[:, 0:576]
    gain = jnp.sum(gn1 * u, axis=0, keepdims=True)
    gain = jnp.concatenate([gain, jnp.zeros((1, 64), F32)], axis=1)
    for t in range(5):
        vecs.rc[0, t : t + 1, :] = gain[:, 128 * t : 128 * t + 128]
        vecs.rc[0, 5 + t : 6 + t, :] = gain_in[:, 128 * t : 128 * t + 128]
    vecs.rc[0, 18:24, :] = jnp.zeros((6, 128), F32)
    vecs.start()
    red_q.stage1()
    red_dn.stage4()
    red_o.stage4()
    red_gu.stage4()
    grad_in[...] = gh_in[...] + r * (f - u * jnp.mean(f * u, axis=-1, keepdims=True))
    vecs.next(0)
    red_q.stage2()
    vecs.next(1)
    red_q.stage3()
    vecs.next(2)
    red_q.stage4()
    vsum[...] = vecs.next(3)
    for red in (red_dn, red_o, red_gu, red_q):
        red.finish()
    vecs.finish()
    for g in range(KV_HEADS):
        for s in range(1, NZ):

            @pl.when(z >= s)
            def _(g=g, s=s):
                kv_copy(g, s, device(x, y, c, wrap(z + NZ - s, NZ))).wait_send()


def backward(q, qt, do, dt, kv, lse, delta, n1, tok, gh, wq, vec, gain, cos_t, sin_t, ggu, gdn, go):
    sd = jax.ShapeDtypeStruct
    v = pl.BlockSpec(memory_space=VM)
    a = pl.BlockSpec(memory_space=ANY)
    dma = pltpu.SemaphoreType.DMA
    return pl.pallas_call(
        backward_kernel,
        out_shape=(
            sd((ROWS, D), F32),
            sd((144, 2 * FF), BF16),
            sd((384, D), BF16),
            sd((144, QW), BF16),
            sd((144, QW), BF16),
            sd((24, 128), F32),
        ),
        in_specs=[v] * 13 + [a] * 5,
        out_specs=(v,) * 6,
        scratch_shapes=[
            VM((128, ROWS), BF16), VM((HEADS, 128, ROWS), F32), VM((ROWS, 128), F32),
            VM((KV_HEADS, ROWS, 128), F32), VM((KV_HEADS, 3, ROWS, 128), BF16), VM((KV_HEADS, 3, ROWS, 128), BF16),
            VM((2, 4, NZ, 144, 128), BF16), VM((ROWS, 128), F32), VM((ROWS, 128), F32), VM((D, ROWS), BF16),
            *Reduction.scratch(144, 384), *Reduction.scratch(48, 576), *Reduction.scratch(144, 128),
            *Reduction.scratch(144, 128), *VectorSum.scratch(),
            dma((5,)), dma((3, 3)), dma((3, 3)),
        ],
        compiler_params=pltpu.CompilerParams(
            collective_id=1, has_side_effects=True, vmem_limit_bytes=60 << 20),
        name="attend_back_reduce",
    )(q, qt, do, dt, kv, lse, delta, n1, tok, gh, wq, vec, gain, cos_t, sin_t, ggu, gdn, go)


def adam_step(weight, first_state, second_state, gradient, learn_rate, decay_rate):
    first_new = BETA_ONE * first_state + (1.0 - BETA_ONE) * gradient
    second_new = BETA_TWO * second_state + (1.0 - BETA_TWO) * gradient * gradient
    corr_one = 1.0 - BETA_ONE**STEP
    corr_two = 1.0 - BETA_TWO**STEP
    update = first_new / corr_one / (jnp.sqrt(second_new / corr_two) + ADAM_EPS)
    weight_new = weight - learn_rate * (update + decay_rate * weight)
    return (weight_new, first_new, second_new)


def per_device(
    tokens, cotangent, w_qkv, w_out, w_gate_up, w_down, vectors,
    first_qkv, first_out, first_gate_up, first_down, first_vectors,
    second_qkv, second_out, second_gate_up, second_down, second_vectors,
):
    z = lax.axis_index("ctx")
    cos_np, sin_np = rope_tables()
    cos_t, sin_t = jnp.asarray(cos_np), jnp.asarray(sin_np)
    shard = vectors.shape[0]
    placed = lax.dynamic_update_slice(jnp.zeros((NZ * shard,), F32), vectors, (z * shard,))
    pad64 = jnp.zeros((64,), F32)
    placed = jnp.concatenate([placed[:D], pad64, placed[D : 2 * D], pad64, placed[2 * D :], pad64])[None, :]

    q, qt, kv, att, lse, n1, wq, vec, wo, wgu, wdn = forward(
        tokens, w_qkv, placed, cos_t, sin_t, w_out, w_gate_up, w_down)
    block_out, gh, do, dt, delta, ggu, gdn, go, gain = middle(att, wo, tokens, cotangent, vec, wgu, wdn)
    ggu = ggu.reshape(2, 4, NZ, 144, 384)
    go = go.reshape(2, 4, NZ, 144, 128)
    grad_in, fgu, fdn, fo, fq, vsum = backward(
        q, qt, do, dt, kv, lse, delta, n1, tokens, gh, wq, vec, gain, cos_t, sin_t, ggu, gdn, go)

    flat = vsum.reshape(-1)
    flat = jnp.concatenate([flat[:D], flat[640 : 640 + D], flat[1280 : 1280 + 960]])
    gvec = lax.dynamic_slice(flat, (z * shard,), (shard,))
    grads = (fq[:, :960], fo[:, :D], fgu, fdn, gvec)
    masters = (w_qkv, w_out, w_gate_up, w_down, vectors)
    firsts = (first_qkv, first_out, first_gate_up, first_down, first_vectors)
    seconds = (second_qkv, second_out, second_gate_up, second_down, second_vectors)
    results = []
    for k in range(5):
        results.append(
            adam_step(
                masters[k], firsts[k], seconds[k], grads[k].astype(F32),
                RATE_VECTOR if k == 4 else RATE_MATRIX, 0.0 if k == 4 else DECAY_MATRIX))
    return (block_out, grad_in) + tuple(results[k][i] for i in range(3) for k in range(5))


def solution(mesh):
    tokens = P(("dp", "ctx"), None)
    state = (P("ctx", None),) * 4 + (P("ctx"),)
    return jax.shard_map(
        per_device, mesh=mesh, in_specs=(tokens, tokens) + state * 3, out_specs=(tokens, tokens) + state * 3,
        check_vma=False,
    )
```

```python
import functools

import jax
import jax.numpy as jnp
import numpy as np
from jax import lax
from jax.experimental import pallas as pl
from jax.experimental.pallas import tpu as pltpu
from jax.sharding import PartitionSpec as P

D = 576
HEADS = 9
KV_HEADS = 3
GROUP = 3
HEAD_DIM = 64
FF = 1536
STEP = 10
LEN = 2048
ROWS = 512
QW = 1024
OW = 640
VW = 2304
NX = 4
NY = 4
NZ = 4

EPS = 1e-05
ROPE_BASE = 100000.0
MASK_FILL = -1e30
BETA_ONE = 0.9
BETA_TWO = 0.999
ADAM_EPS = 1e-08
RATE_MATRIX = 0.05
RATE_VECTOR = 0.5
DECAY_MATRIX = 0.1

F32 = jnp.float32
BF16 = jnp.bfloat16
MESH = pl.DeviceIdType.MESH
VM = pltpu.VMEM
ANY = pl.ANY


def rope_tables():
    half = HEAD_DIM // 2
    exponent = np.arange(half, dtype=np.float32) * np.float32(2.0 / HEAD_DIM)
    inverse = (np.float64(ROPE_BASE) ** (-exponent.astype(np.float64))).astype(np.float32)
    angles = np.arange(LEN, dtype=np.float32)[:, None] * inverse[None, :]
    cosine = np.cos(angles.astype(np.float64)).astype(np.float32)
    sine = np.sin(angles.astype(np.float64)).astype(np.float32)
    cos_all = np.concatenate([cosine] * 4, axis=1)
    sin_all = np.concatenate([-sine, sine, -sine, sine], axis=1)
    return cos_all, sin_all


def dot(a, b, ca=1, cb=0):
    return lax.dot_general(a, b, (((ca,), (cb,)), ((), ())), preferred_element_type=F32)


def place():
    dp = lax.axis_index("dp")
    z = lax.axis_index("ctx")
    x = lax.div(dp, NY * 2)
    y = lax.rem(lax.div(dp, 2), NY)
    c = lax.rem(dp, 2)
    return x, y, c, z


def device(x, y, c, z):
    return (x * (NY * 2) + y * 2 + c, z)


def wrap(i, n):
    return lax.rem(i, n)


def remote(src, dst, ssem, rsem, dev):
    return pltpu.make_async_remote_copy(
        src_ref=src, dst_ref=dst, send_sem=ssem, recv_sem=rsem, device_id=dev, device_id_type=MESH
    )


def greet(peers):
    barrier = pltpu.get_barrier_semaphore()
    for peer in peers:
        pl.semaphore_signal(barrier, inc=1, device_id=peer, device_id_type=MESH)
    pl.semaphore_wait(barrier, len(peers))


def swap_halves(v):
    width = v.shape[1]
    lane = lax.broadcasted_iota(jnp.int32, v.shape, 1)
    down = pltpu.roll(v, width - 32, 1)
    up = pltpu.roll(v, 32, 1)
    return jnp.where(lax.rem(lane, 64) < 32, down, up)


def low_lanes(v):
    lane = lax.broadcasted_iota(jnp.int32, v.shape, 1)
    return lane < 64


def forward_kernel(
    tok_t, wq_in, vec_in, cos_hbm, sin_hbm, wo_in, wgu_in, wdn_in,
    att_out, lse_out, vec_out, q_out, qt_out, kv_out, n1t_out, wq_out, wo_all, wgu_all, wdn_all,
    wq_v, vec_v, cos_v, sin_v, f_out, f_gu, f_dn, b_out, b_gu, b_dn,
    q_s, qt_s, n1t_s, kvs, m_s, l_s, ot_s,
    loc_sem, out_sem, zq_s, zq_r, cq_s, cq_r, zv_s, zv_r, zw_s, zw_r, aw_s, aw_r, cw_s, cw_r, kv_s, kv_r,
):
    x, y, c, z = place()
    sib = device(x, y, 1 - c, z)
    zdev = [device(x, y, c, wrap(z + d, NZ)) for d in range(1, NZ)]
    xdev = [device(wrap(x + d, NX), y, c, z) for d in range(1, NX)]
    ydev = [device(x, wrap(y + d, NY), c, z) for d in range(1, NY)]
    row0 = pl.multiple_of(z * ROWS, ROWS)
    loads = [
        pltpu.make_async_copy(cos_hbm.at[pl.ds(row0, ROWS)], cos_v, loc_sem.at[0]),
        pltpu.make_async_copy(sin_hbm.at[pl.ds(row0, ROWS)], sin_v, loc_sem.at[1]),
        pltpu.make_async_copy(wo_in, f_out, loc_sem.at[2]),
        pltpu.make_async_copy(wgu_in, f_gu, loc_sem.at[3]),
        pltpu.make_async_copy(wdn_in, f_dn, loc_sem.at[4]),
    ]
    for load in loads:
        load.start()
    qrows = pl.ds(pl.multiple_of(z * 144, 144), 144)
    wq_v[qrows, 0:896] = wq_in[:, 0:896].astype(BF16)
    wq_v[qrows, 896:1024] = jnp.concatenate(
        [wq_in[:, 896:960].astype(BF16), jnp.zeros((144, 64), BF16)], axis=1
    )
    vec_v[0] = jnp.zeros((1, VW), F32)
    vec_v[0, :, 0:528] = vec_in[...]
    rolled = pltpu.roll(jnp.broadcast_to(vec_v[0], (8, VW)), z * 528, 1)
    vec_v[0] = rolled[0:1, :]
    greet(zdev + xdev + ydev + [sib])

    sends = []
    waits_q = [[], []]

    def send_part(part):
        cols = pl.ds(pl.multiple_of((1 - part) * 512 + c * 256, 256), 256)
        for d in range(1, NZ):
            ref = wq_v.at[qrows, cols]
            waits_q[part].append(remote(ref, ref, zq_s.at[part, d - 1], zq_r.at[part, d - 1], zdev[d - 1]))
            if part == 0:
                waits_q[part].append(
                    remote(vec_v.at[0], vec_v.at[d], zv_s.at[d - 1], zv_r.at[d - 1], zdev[d - 1]))
        for s in waits_q[part]:
            s.start()
        sends.extend(waits_q[part])

    def swap_part(part):
        cols = pl.ds(pl.multiple_of((1 - part) * 512 + c * 256, 256), 256)
        swaps = []
        for d in range(1, NZ):
            rows = pl.ds(pl.multiple_of(wrap(z + NZ - d, NZ) * 144, 144), 144)
            ref = wq_v.at[rows, cols]
            swaps.append(remote(ref, ref, cq_s.at[part, d - 1], cq_r.at[part, d - 1], sib))
        for s in swaps:
            s.start()
        sends.extend(swaps)
        return swaps

    send_part(0)
    inputs = jnp.transpose(tok_t[...].astype(F32))
    unit = inputs * lax.rsqrt(jnp.mean(inputs * inputs, axis=-1, keepdims=True) + EPS)

    loads[2].wait()
    b_out[:, 0:512] = f_out[:, 0:512].astype(BF16)
    b_out[:, 512:640] = jnp.concatenate([f_out[:, 512:576].astype(BF16), jnp.zeros((144, 64), BF16)], axis=1)
    loads[3].wait()
    for i in range(8):
        b_gu[:, 384 * i : 384 * i + 384] = f_gu[:, 384 * i : 384 * i + 384].astype(BF16)
    loads[4].wait()
    b_dn[...] = jnp.transpose(f_dn[...]).astype(BF16)
    own = [
        pltpu.make_async_copy(b_out, wo_all.at[qrows, :], loc_sem.at[5]),
        pltpu.make_async_copy(b_gu, wgu_all.at[qrows, :], loc_sem.at[6]),
        pltpu.make_async_copy(b_dn, wdn_all.at[pl.ds(pl.multiple_of(z * 384, 384), 384), :], loc_sem.at[7]),
    ]
    for copy in own:
        copy.start()

    for s in waits_q[0]:
        s.wait_recv()
    swaps = swap_part(0)
    send_part(1)

    pgu = pl.multiple_of((c * 4 + x) * 384, 128)
    pdn = (c * 4 + y) * 48
    po = jnp.minimum(c * 4 + y, 4)
    has_o = c * 4 + y < 5
    oc = pl.multiple_of(po * 128, 128)
    wsend = []
    osend = []
    for d in range(1, NZ):
        osend.append(
            remote(b_out.at[:, pl.ds(oc, 128)], wo_all.at[qrows, pl.ds(oc, 128)],
                   zw_s.at[0, d - 1], zw_r.at[0, d - 1], zdev[d - 1]))
        wsend.append(
            remote(b_gu.at[:, pl.ds(pgu, 384)], wgu_all.at[qrows, pl.ds(pgu, 384)],
                   zw_s.at[1, d - 1], zw_r.at[1, d - 1], zdev[d - 1]))
        wsend.append(
            remote(b_dn.at[pl.ds(pl.multiple_of(pdn, 48), 48), :],
                   wdn_all.at[pl.ds(pl.multiple_of(z * 384 + pdn, 48), 48), :],
                   zw_s.at[2, d - 1], zw_r.at[2, d - 1], zdev[d - 1]))

    @pl.when(has_o)
    def _():
        for s in osend:
            s.start()

    for s in wsend:
        s.start()
    sends.extend(wsend)

    vec = vec_v[0] + vec_v[1] + vec_v[2] + vec_v[3]
    vec = vec.astype(BF16).astype(F32)
    wide = jnp.broadcast_to(vec, (8, VW))
    lane640 = lax.broadcasted_iota(jnp.int32, (1, 640), 1)
    vec_out[:, 0:640] = jnp.where(lane640 < 576, vec[:, 0:640], 0.0)
    vec_out[:, 640:1280] = jnp.where(lane640 < 576, pltpu.roll(wide, VW - 576, 1)[0:1, 0:640], 0.0)
    vec_out[:, 1280:2304] = vec[:, 1152:2176]
    normed = unit * vec[:, 0:576]
    n1 = normed.astype(BF16)
    n1t_s[...] = jnp.transpose(normed).astype(BF16)
    loads[0].wait()
    loads[1].wait()
    cosine, sine = cos_v[...], sin_v[...]
    for s in swaps:
        s.wait_recv()

    def tile_of(v, t):
        return v[:, 128 * t : 128 * t + 128]

    def rotated(v):
        return v * cosine + swap_halves(v) * sine

    proj = dot(n1, wq_v[:, 512:1024]) + vec[:, 1664:2176]
    rot4, rot5 = rotated(tile_of(proj, 0)), rotated(tile_of(proj, 1))
    val6, val7 = tile_of(proj, 2), tile_of(proj, 3)
    low = low_lanes(rot4)

    def turn(v):
        return pltpu.roll(v, 64, 1)

    kvs[z, 0] = jnp.where(low, turn(rot4), turn(val6)).astype(BF16)
    kvs[z, 1] = jnp.where(low, rot5, val6).astype(BF16)
    kvs[z, 2] = jnp.where(low, turn(rot5), turn(val7)).astype(BF16)
    kv_sends = []
    for d in range(1, NZ):
        kv_sends.append(
            remote(kvs.at[z], kvs.at[z], kv_s.at[d - 1], kv_r.at[d - 1], device(x, y, c, wrap(z + d, NZ))))

        @pl.when(z + d < NZ)
        def _(d=d):
            kv_sends[d - 1].start()

    for s in waits_q[1]:
        s.wait_recv()
    swaps = swap_part(1)

    def put_query(h, part):
        qh = jnp.where(low, part, 0.0) * (HEAD_DIM ** -0.5)
        q_s[h] = qh.astype(BF16)
        qt_s[h] = jnp.transpose(qh).astype(BF16)

    put_query(8, rot4)
    for s in swaps:
        s.wait_recv()
    proj = dot(n1, wq_v[:, 0:512]) + vec[:, 1152:1664]
    for t in range(4):
        rot = rotated(tile_of(proj, t))
        put_query(2 * t, rot)
        put_query(2 * t + 1, turn(rot))

    outs = [
        pltpu.make_async_copy(q_s, q_out, out_sem.at[0]),
        pltpu.make_async_copy(qt_s, qt_out, out_sem.at[1]),
        pltpu.make_async_copy(n1t_s, n1t_out, out_sem.at[2]),
        pltpu.make_async_copy(wq_v, wq_out, out_sem.at[3]),
    ]
    for copy in outs:
        copy.start()

    def step(j):
        kvt = [jnp.transpose(kvs[j, g].astype(F32)).astype(BF16)[64:128, :] for g in range(KV_HEADS)]
        heads = range(HEADS)
        sts = [dot(kvs[j, h // GROUP], qt_s[h]) for h in heads]
        olds = [m_s[h] for h in heads]
        peaks = [jnp.maximum(jnp.max(s, axis=0, keepdims=True), o) for s, o in zip(sts, olds)]
        alphas = [jnp.exp(o - p) for o, p in zip(olds, peaks)]
        ps = [jnp.exp(s - p) for s, p in zip(sts, peaks)]
        totals = [jnp.sum(p, axis=0, keepdims=True) + l_s[h] * a for h, p, a in zip(heads, ps, alphas)]
        outs = [dot(kvt[h // GROUP], p.astype(BF16)) + ot_s[h] * a for h, p, a in zip(heads, ps, alphas)]
        for h in heads:
            m_s[h] = peaks[h]
            l_s[h] = totals[h]
            ot_s[h] = outs[h]

    def first_step():
        kvt = [jnp.transpose(kvs[z, g].astype(F32)).astype(BF16)[64:128, :] for g in range(KV_HEADS)]
        heads = range(HEADS)
        keep_a = lax.broadcasted_iota(jnp.int32, (256, 512), 0) <= lax.broadcasted_iota(jnp.int32, (256, 512), 1)
        keep_b = keep_a[:, 0:256]
        st_a = [jnp.where(keep_a, dot(kvs[z, h // GROUP, 0:256], qt_s[h]), MASK_FILL) for h in heads]
        st_b = [jnp.where(keep_b, dot(kvs[z, h // GROUP, 256:512], qt_s[h, :, 256:512]), MASK_FILL) for h in heads]
        none = jnp.full((1, 256), MASK_FILL, F32)
        zero = jnp.zeros((1, 256), F32)
        zeros = jnp.zeros((64, 256), F32)
        peaks = [
            jnp.maximum(
                jnp.max(a, axis=0, keepdims=True),
                jnp.concatenate([none, jnp.max(b, axis=0, keepdims=True)], axis=1))
            for a, b in zip(st_a, st_b)]
        p_a = [jnp.exp(a - p) for a, p in zip(st_a, peaks)]
        p_b = [jnp.exp(b - p[:, 256:512]) for b, p in zip(st_b, peaks)]
        totals = [
            jnp.sum(a, axis=0, keepdims=True) + jnp.concatenate([zero, jnp.sum(b, axis=0, keepdims=True)], axis=1)
            for a, b in zip(p_a, p_b)]
        outs = [
            dot(kvt[h // GROUP][:, 0:256], p_a[h].astype(BF16))
            + jnp.concatenate([zeros, dot(kvt[h // GROUP][:, 256:512], p_b[h].astype(BF16))], axis=1)
            for h in heads]
        for h in heads:
            m_s[h] = peaks[h]
            l_s[h] = totals[h]
            ot_s[h] = outs[h]

    first_step()

    for s in wsend:
        s.wait_recv()

    @pl.when(has_o)
    def _():
        for s in osend:
            s.wait_recv()

    leg = []
    oleg = []
    for e in range(1, NZ):
        src_z = wrap(z + NZ - e, NZ)
        rows = pl.ds(pl.multiple_of(src_z * 144, 144), 144)
        ref_gu = wgu_all.at[rows, pl.ds(pgu, 384)]
        ref_dn = wdn_all.at[pl.ds(pl.multiple_of(src_z * 384 + pdn, 48), 48), :]
        ref_o = wo_all.at[rows, pl.ds(oc, 128)]
        for d in range(1, NX):
            leg.append(remote(ref_gu, ref_gu, aw_s.at[0, e - 1, d - 1], aw_r.at[0, e - 1, d - 1], xdev[d - 1]))
            leg.append(remote(ref_dn, ref_dn, aw_s.at[1, e - 1, d - 1], aw_r.at[1, e - 1, d - 1], ydev[d - 1]))
            oleg.append(remote(ref_o, ref_o, aw_s.at[2, e - 1, d - 1], aw_r.at[2, e - 1, d - 1], ydev[d - 1]))
    for s in leg:
        s.start()
    sends.extend(leg)

    @pl.when(has_o)
    def _():
        for s in oleg:
            s.start()

    last = []
    last_o = [[], []]
    for d in range(1, NZ):
        if d == NZ - 1:
            for s in leg:
                s.wait_recv()
            for dd in range(1, NY):
                from_y = wrap(y + NY - dd, NY)

                @pl.when(c * 4 + from_y < 5)
                def _(dd=dd):
                    for e in range(1, NZ):
                        oleg[(e - 1) * 3 + dd - 1].wait_recv()

            for e in range(1, NZ):
                src_z = wrap(z + NZ - e, NZ)
                rows = pl.ds(pl.multiple_of(src_z * 144, 144), 144)
                ref_g = wgu_all.at[rows, pl.ds(pl.multiple_of(c * 1536, 128), 1536)]
                ref_d = wdn_all.at[pl.ds(pl.multiple_of(src_z * 384 + c * 192, 192), 192), :]
                last.append(remote(ref_g, ref_g, cw_s.at[1, e - 1], cw_r.at[1, e - 1], sib))
                last.append(remote(ref_d, ref_d, cw_s.at[2, e - 1], cw_r.at[2, e - 1], sib))
                for core, cols in enumerate((slice(0, 512), slice(512, 640))):
                    ref_o = wo_all.at[rows, cols]
                    last_o[core].append(remote(ref_o, ref_o, cw_s.at[0, e - 1], cw_r.at[0, e - 1], sib))
            for s in last:
                s.start()
            sends.extend(last)
            for core in range(2):

                @pl.when(c == core)
                def _(core=core):
                    for s in last_o[core]:
                        s.start()

        @pl.when(z >= d)
        def _(d=d):
            kv_sends[d - 1].wait_recv()
            step(z - d)

    kv_copy = pltpu.make_async_copy(kvs, kv_out, out_sem.at[4])
    kv_copy.start()
    for h in range(HEADS):
        ot_s[h] = ot_s[h] * (1.0 / l_s[h])
        lse_out[h] = m_s[h] + jnp.log(l_s[h])
    for t in range(5):
        top = ot_s[2 * t]
        bottom = ot_s[2 * t + 1] if 2 * t + 1 < HEADS else jnp.zeros((64, ROWS), F32)
        att_out[:, 128 * t : 128 * t + 128] = jnp.transpose(jnp.concatenate([top, bottom], axis=0))

    for s in last:
        s.wait_recv()
    for core in range(2):

        @pl.when(c == core)
        def _(core=core):
            for s in last_o[1 - core]:
                s.wait_recv()
            for s in last_o[core]:
                s.wait_send()

    for s in sends:
        s.wait_send()

    @pl.when(has_o)
    def _():
        for s in osend + oleg:
            s.wait_send()

    for d in range(1, NZ):

        @pl.when(z + d < NZ)
        def _(d=d):
            kv_sends[d - 1].wait_send()

    for copy in own + outs + [kv_copy]:
        copy.wait()


def forward(tok_t, wq, vec, cos_t, sin_t, wo, wgu, wdn_t):
    sd = jax.ShapeDtypeStruct
    v = pl.BlockSpec(memory_space=VM)
    a = pl.BlockSpec(memory_space=ANY)
    dma = pltpu.SemaphoreType.DMA
    return pl.pallas_call(
        forward_kernel,
        out_shape=(
            sd((ROWS, 640), F32),
            sd((HEADS, 1, ROWS), F32),
            sd((1, VW), F32),
            sd((HEADS, ROWS, 128), BF16),
            sd((HEADS, 128, ROWS), BF16),
            sd((NZ, KV_HEADS, ROWS, 128), BF16),
            sd((D, ROWS), BF16),
            sd((D, QW), BF16),
            sd((D, OW), BF16),
            sd((D, 2 * FF), BF16),
            sd((FF, D), BF16),
        ),
        in_specs=[v, v, v, a, a, a, a, a],
        out_specs=(v,) * 3 + (a,) * 8,
        scratch_shapes=[
            VM((D, QW), BF16), VM((NZ, 1, VW), F32),
            VM((ROWS, 128), F32), VM((ROWS, 128), F32),
            VM((144, D), F32), VM((144, 2 * FF), F32), VM((D, 384), F32),
            VM((144, OW), BF16), VM((144, 2 * FF), BF16), VM((384, D), BF16),
            VM((HEADS, ROWS, 128), BF16), VM((HEADS, 128, ROWS), BF16), VM((D, ROWS), BF16),
            VM((NZ, KV_HEADS, ROWS, 128), BF16),
            VM((HEADS, 1, ROWS), F32), VM((HEADS, 1, ROWS), F32), VM((HEADS, 64, ROWS), F32),
            dma((8,)), dma((5,)), dma((2, 3)), dma((2, 3)), dma((2, 3)), dma((2, 3)), dma((3,)), dma((3,)),
            dma((3, 3)), dma((3, 3)), dma((3, 3, 3)), dma((3, 3, 3)), dma((3, 3)), dma((3, 3)),
            dma((3,)), dma((3,)),
        ],
        compiler_params=pltpu.CompilerParams(
            collective_id=0, has_side_effects=True, vmem_limit_bytes=58 << 20),
        name="gather_attend",
    )(tok_t, wq, vec, cos_t, sin_t, wo, wgu, wdn_t)


class Reduction:
    SCRATCH = 7

    @staticmethod
    def scratch(lead, r, w, both=False):
        dma = pltpu.SemaphoreType.DMA
        first = VM((15, r, w), BF16) if both else VM((3, 4, r, w), BF16)
        return [
            VM(lead + (r, w), BF16), first, VM((4, r, w), BF16),
            VM((3, r, w), BF16), VM((4, r, w), BF16), dma((32,)), dma((32,)),
        ]

    def __init__(self, own, fin, fin_at, bufs, along_x, z_first):
        self.own, self.fin, self.fin_at, self.z_first = own, fin, fin_at, z_first
        self.rc, self.r1, self.s1, self.r2, self.r3, self.ss, self.rs = bufs
        x, y, c, z = place()
        self.c, self.z = c, z
        if along_x:
            self.a, self.b = x, y
            self.at = lambda a, b, cc, zz: device(a, b, cc, zz)
        else:
            self.a, self.b = y, x
            self.at = lambda a, b, cc, zz: device(b, a, cc, zz)
        self.sends = []

    def copy(self, src, dst, k, dev):
        return remote(src, dst, self.ss.at[k], self.rs.at[k], dev)

    def go(self, src, dst, k, dev):
        copy = self.copy(src, dst, k, dev)
        copy.start()
        self.sends.append(copy)
        return copy

    def mine(self, a, z):
        return (self.c, z, a) if self.z_first else (self.c, a, z)

    def all_z(self, a):
        return self.own.at[self.c, :, a] if self.z_first else self.own.at[self.c, a]

    def core_copy(self, k):
        return self.copy(
            self.own.at[1 - self.c, k], self.rc.at[k], k, self.at(self.a, self.b, 1 - self.c, self.z))

    def core_add(self, k):
        self.core_copy(k).wait_recv()

        def add(j, carry):
            total = self.own[self.c, k, j].astype(F32) + self.rc[k, j].astype(F32)
            self.own[self.c, k, j] = total.astype(BF16)
            return carry

        lax.fori_loop(0, 4, add, 0)

    def core_all(self, act):
        def one(k, carry):
            act(k)
            return carry

        lax.fori_loop(0, 4, one, 0)

    def first_copy(self, d):
        to = wrap(self.a + d, 4)
        return self.copy(self.all_z(to), self.r1.at[d - 1], 3 + d, self.at(to, self.b, self.c, self.z))

    def first_start(self):
        for d in range(1, 4):
            self.first_copy(d).start()

    def first_sum(self):
        for d in range(1, 4):
            self.first_copy(d).wait_recv()

        def add(j, carry):
            total = self.own[self.mine(self.a, j)].astype(F32) + self.r1[0, j].astype(F32)
            total = total + self.r1[1, j].astype(F32) + self.r1[2, j].astype(F32)
            self.s1[j] = total.astype(BF16)
            return carry

        lax.fori_loop(0, 4, add, 0)

    def z_start(self):
        self.second = []
        for d in range(1, 4):
            to = wrap(self.z + d, 4)
            self.second.append(
                self.go(self.s1.at[to], self.r2.at[d - 1], 6 + d, self.at(self.a, self.b, self.c, to)))

    def z_sum(self):
        for copy in self.second:
            copy.wait_recv()
        total = self.s1[self.z].astype(F32) + self.r2[0].astype(F32)
        total = total + self.r2[1].astype(F32) + self.r2[2].astype(F32)
        self.r3[self.b] = total.astype(BF16)

    def both_start(self):
        self.second = []
        k = 16
        for da in range(4):
            for dz in range(4):
                if da or dz:
                    to_a, to_z = wrap(self.a + da, 4), wrap(self.z + dz, 4)
                    k += 1
                    self.second.append(
                        self.go(self.own.at[self.mine(to_a, to_z)], self.r1.at[k - 17], k,
                                self.at(to_a, self.b, self.c, to_z)))

    def both_sum(self):
        for copy in self.second:
            copy.wait_recv()

        def add(j, total):
            return total + self.r1[j].astype(F32)

        total = lax.fori_loop(0, 15, add, self.own[self.mine(self.a, self.z)].astype(F32))
        self.r3[self.b] = total.astype(BF16)

    def exchange_start(self):
        self.third = []
        for d in range(1, 4):
            to = wrap(self.b + d, 4)
            ref = self.r3.at[self.b]
            self.third.append(self.go(ref, ref, 9 + d, self.at(self.a, to, self.c, self.z)))

    def gather_start(self, sems):
        for copy in self.third:
            copy.wait_recv()
        total = self.r3[0].astype(F32) + self.r3[1].astype(F32)
        total = total + self.r3[2].astype(F32) + self.r3[3].astype(F32)
        where = self.fin_at(self.c, self.a)
        ref = self.fin.at[where]
        self.fin[where] = total.astype(BF16)
        self.fourth = []
        k = -1
        for e in range(2):
            for d in range(4):
                if e or d:
                    k += 1
                    to = self.at(wrap(self.a + d, 4), self.b, wrap(self.c + e, 2), self.z)
                    self.fourth.append(remote(ref, ref, sems[0].at[k], sems[1].at[k], to))
        for copy in self.fourth:
            copy.start()

    def gather_wait(self):
        for copy in self.fourth:
            copy.wait_recv()

    def finish(self, along_first):
        for copy in self.sends + self.fourth:
            copy.wait_send()
        self.core_all(lambda k: self.core_copy(k).wait_send())
        if along_first:
            for d in range(1, 4):
                self.first_copy(d).wait_send()


class VectorSum:
    SCRATCH = 4

    @staticmethod
    def scratch():
        dma = pltpu.SemaphoreType.DMA
        return [VM((2, 24, 128), F32), VM((3, 4, 24, 128), F32), dma((10,)), dma((10,))]

    def __init__(self, bufs):
        self.rc, self.r, self.ss, self.rs = bufs
        self.sends = []

    def start(self):
        x, y, c, z = place()
        self.pending = [remote(self.rc.at[0], self.rc.at[1], self.ss.at[0], self.rs.at[0], device(x, y, 1 - c, z))]
        self.pending[0].start()
        self.sends += self.pending

    def next(self, k):
        x, y, c, z = place()
        for copy in self.pending:
            copy.wait_recv()
        if k == 0:
            total = self.rc[0] + self.rc[1]
        else:
            total = self.r[k - 1, 0] + self.r[k - 1, 1] + self.r[k - 1, 2] + self.r[k - 1, 3]
        if k == 3:
            return total
        me = (y, z, x)[k]
        self.r[k, me] = total
        self.pending = []
        for d in range(1, 4):
            to = wrap(me + d, 4)
            dev = (device(x, to, c, z), device(x, y, c, to), device(to, y, c, z))[k]
            copy = remote(self.r.at[k, me], self.r.at[k, me], self.ss.at[3 * k + d], self.rs.at[3 * k + d], dev)
            copy.start()
            self.pending.append(copy)
        self.sends += self.pending
        return None

    def finish(self):
        for copy in self.sends:
            copy.wait_send()


def layer_kernel(
    att, wo, tok_t, cot_t, vec, lse_in, wgu, wdn, q_hbm, qt_hbm, kv_hbm, n1t_hbm, wq_hbm, cos_hbm, sin_hbm,
    block_out, grad_in, fgu, fdn_t, fo, fq, vsum,
    cot, gh, n2, n2t, gn2, wgs, wus, wds,
    q_in, qt_in, do_in, dot_in, kv_in, n1t, wq, cos_v, sin_v, delta_in, gain_row,
    ggu, gdn, go, gq, fdn, dqt, own_kv, skv, rkv,
    *rest,
):
    n = Reduction.SCRATCH
    lanes = lambda c, a: (slice(None), pl.ds(pl.multiple_of((c * 4 + a) * 128, 128), 128))
    red_gu = Reduction(
        ggu, fgu, lambda c, a: (slice(None), pl.ds(pl.multiple_of((c * 4 + a) * 384, 128), 384)),
        rest[0:n], True, False)
    red_dn = Reduction(
        gdn, fdn, lambda c, a: (pl.ds(pl.multiple_of((c * 4 + a) * 48, 48), 48), slice(None)),
        rest[n : 2 * n], False, True)
    red_o = Reduction(go, fo, lanes, rest[2 * n : 3 * n], False, False)
    red_q = Reduction(gq, fq, lanes, rest[3 * n : 4 * n], False, False)
    vecs = VectorSum(rest[4 * n : 4 * n + 4])
    loc_sem, w_sem, kv_s, kv_r, ag_s, ag_r = rest[4 * n + 4 :]
    x, y, c, z = place()
    zdev = [device(x, y, c, wrap(z + d, NZ)) for d in range(1, NZ)]
    peers = []
    for dy in range(4):
        for dz in range(4):
            if dy or dz:
                peers.append(device(x, wrap(y + dy, NY), c, wrap(z + dz, NZ)))
    for d in range(1, 4):
        peers.append(device(wrap(x + d, NX), y, c, z))
        peers.append(device(wrap(x + d, NX), y, 1 - c, z))
        peers.append(device(x, wrap(y + d, NY), 1 - c, z))
    peers.append(device(x, y, 1 - c, z))
    row0 = pl.multiple_of(z * ROWS, ROWS)

    def weights(i, slot):
        col = pl.multiple_of(wrap(x + 1 + i, 4) * 384, 384)
        return [
            pltpu.make_async_copy(wgu.at[:, pl.ds(col, 384)], wgs.at[slot], w_sem.at[0, slot]),
            pltpu.make_async_copy(
                wgu.at[:, pl.ds(pl.multiple_of(col + FF, 384), 384)], wus.at[slot], w_sem.at[1, slot]),
            pltpu.make_async_copy(wdn.at[pl.ds(col, 384), :], wds.at[slot], w_sem.at[2, slot]),
        ]

    for load in weights(0, 0):
        load.start()
    loads = [
        pltpu.make_async_copy(q_hbm, q_in, loc_sem.at[0]),
        pltpu.make_async_copy(qt_hbm, qt_in, loc_sem.at[1]),
        pltpu.make_async_copy(kv_hbm, kv_in, loc_sem.at[2]),
        pltpu.make_async_copy(n1t_hbm, n1t, loc_sem.at[3]),
        pltpu.make_async_copy(wq_hbm, wq, loc_sem.at[4]),
        pltpu.make_async_copy(cos_hbm.at[pl.ds(row0, ROWS)], cos_v, loc_sem.at[5]),
        pltpu.make_async_copy(sin_hbm.at[pl.ds(row0, ROWS)], sin_v, loc_sem.at[6]),
    ]
    for load in loads:
        load.start()

    gain = vec[:, 640:1216]
    inputs = jnp.transpose(tok_t[...].astype(F32))
    hid = inputs + dot(att[:, 0:576].astype(BF16), wo[:, 0:576])
    inv_two = lax.rsqrt(jnp.mean(hid * hid, axis=-1, keepdims=True) + EPS)
    normed = hid * inv_two * gain
    n2[...] = normed.astype(BF16)
    n2t[...] = jnp.transpose(normed).astype(BF16)
    gh[...] = hid
    block_out[...] = jnp.transpose(hid)
    cot[...] = jnp.transpose(cot_t[...].astype(F32)).astype(BF16)
    gn2[...] = jnp.zeros_like(gn2)
    greet(peers)

    def chunk(i, carry):
        slot = lax.rem(i, 2)
        here = wrap(x + 1 + i, 4)
        for load in weights(i, slot):
            load.wait()

        @pl.when(i < 3)
        def _():
            for load in weights(i + 1, 1 - slot):
                load.start()

        gate = dot(n2[...], wgs[slot])
        up = dot(n2[...], wus[slot])
        sg = jax.nn.sigmoid(gate)
        silu = gate * sg
        act = (silu * up).astype(BF16)
        ga = dot(cot[...], wds[slot], 1, 1)
        gg = (ga * up * sg * (1.0 + gate * (1.0 - sg))).astype(BF16)
        gu = (ga * silu).astype(BF16)
        ggu[0, here] = dot(n2t[...], gg).astype(BF16).reshape(NZ, 144, 384)
        ggu[1, here] = dot(n2t[...], gu).astype(BF16).reshape(NZ, 144, 384)
        red_gu.core_copy(here).start()
        down = dot(act, cot[...], 0, 0).astype(BF16)
        for p in range(8):
            gdn[p // 4, here, p % 4] = down[48 * p : 48 * p + 48, :]
        red_dn.core_copy(here).start()
        block_out[...] += lax.dot_general(wds[slot], act, (((0,), (1,)), ((), ())), preferred_element_type=F32)
        gn2[...] += dot(gg, wgs[slot], 1, 1) + dot(gu, wus[slot], 1, 1)

        @pl.when(i > 0)
        def _():
            red_gu.core_add(wrap(x + i, 4))
            red_gu.first_copy(i).start()

        return carry

    lax.fori_loop(0, 4, chunk, 0)
    red_dn.core_all(red_dn.core_add)
    red_dn.first_start()
    red_gu.core_add(x)

    hid = gh[...]
    inv_two = lax.rsqrt(jnp.mean(hid * hid, axis=-1, keepdims=True) + EPS)
    u = hid * inv_two
    e = gn2[...]
    f = e * gain
    gain_row[:, 0:576] = jnp.sum(e * u, axis=0, keepdims=True)
    gain_row[:, 576:640] = jnp.zeros((1, 64), F32)
    grad_hidden = cot[...].astype(F32) + inv_two * (f - u * jnp.mean(f * u, axis=-1, keepdims=True))
    gh[...] = grad_hidden
    ghl = grad_hidden.astype(BF16)
    grad_out = dot(att[:, 0:576].astype(BF16), ghl, 0, 0).astype(BF16)
    for p in range(8):
        if p < 4:
            part = grad_out[:, 128 * p : 128 * p + 128]
        elif p == 4:
            part = jnp.concatenate([grad_out[:, 512:576], jnp.zeros((D, 64), BF16)], axis=1)
        else:
            part = jnp.zeros((D, 128), BF16)
        go[p // 4, p % 4] = part.reshape(NZ, 144, 128)
    red_o.core_all(lambda k: red_o.core_copy(k).start())
    gm = dot(ghl, wo[:, 0:576], 1, 1).astype(BF16).astype(F32)
    prod = gm * att[:, 0:576]
    high = prod.astype(BF16)
    low_part = (prod - high.astype(F32)).astype(BF16)
    head_of = lax.broadcasted_iota(jnp.int32, (16, D), 1) // HEAD_DIM
    pick = (head_of == lax.broadcasted_iota(jnp.int32, (16, D), 0)).astype(F32).astype(BF16)
    delta = dot(pick, high, 1, 1) + dot(pick, low_part, 1, 1)
    for h in range(HEADS):
        delta_in[h] = delta[h : h + 1, :]
    gm = jnp.concatenate([gm, jnp.zeros((ROWS, 64), F32)], axis=1)
    low = low_lanes(gm[:, 0:128])
    for h in range(HEADS):
        part = gm[:, 128 * (h // 2) : 128 * (h // 2) + 128]
        part = part if h % 2 == 1 else pltpu.roll(part, 64, 1)
        part = jnp.where(low, 0.0, part)
        do_in[h] = part.astype(BF16)
        dot_in[h] = jnp.transpose(part).astype(BF16)
    for load in loads:
        load.wait()

    def attend(g, j):
        kv = kv_in[j, g]
        kt = jnp.transpose(kv.astype(F32)).astype(BF16)[0:64, :]
        hs = [g * GROUP + k for k in range(GROUP)]
        sts = [dot(kv, qt_in[h]) for h in hs]
        dpts = [dot(kv, dot_in[h]) for h in hs]
        pts = [jnp.exp(s - lse_in[h]) for s, h in zip(sts, hs)]
        dsts = [(p * (d - delta_in[h])).astype(BF16) for p, d, h in zip(pts, dpts, hs)]
        both = [dot(d, q_in[h]) + dot(p.astype(BF16), do_in[h]) for p, d, h in zip(pts, dsts, hs)]
        dqs = [dot(kt, d) for d in dsts]
        for h, dq in zip(hs, dqs):
            dqt[h] += dq
        return both[0] + both[1] + both[2]

    def attend_own(g):
        keep_a = lax.broadcasted_iota(jnp.int32, (256, 512), 0) <= lax.broadcasted_iota(jnp.int32, (256, 512), 1)
        keep_b = keep_a[:, 0:256]
        kv_a, kv_b = kv_in[z, g, 0:256], kv_in[z, g, 256:512]
        kt = jnp.transpose(kv_in[z, g].astype(F32)).astype(BF16)[0:64, :]
        right = slice(256, 512)
        zeros = jnp.zeros((64, 256), F32)
        hs = [g * GROUP + k for k in range(GROUP)]
        pt_a = [jnp.where(keep_a, jnp.exp(dot(kv_a, qt_in[h]) - lse_in[h]), 0.0) for h in hs]
        pt_b = [jnp.where(keep_b, jnp.exp(dot(kv_b, qt_in[h, :, right]) - lse_in[h, :, right]), 0.0) for h in hs]
        ds_a = [(p * (dot(kv_a, dot_in[h]) - delta_in[h])).astype(BF16) for p, h in zip(pt_a, hs)]
        ds_b = [
            (p * (dot(kv_b, dot_in[h, :, right]) - delta_in[h, :, right])).astype(BF16) for p, h in zip(pt_b, hs)]
        all_a = [dot(d, q_in[h]) + dot(p.astype(BF16), do_in[h]) for p, d, h in zip(pt_a, ds_a, hs)]
        all_b = [dot(d, q_in[h, right]) + dot(p.astype(BF16), do_in[h, right]) for p, d, h in zip(pt_b, ds_b, hs)]
        dqs = [
            dot(kt[:, 0:256], a) + jnp.concatenate([zeros, dot(kt[:, 256:512], b)], axis=1)
            for a, b in zip(ds_a, ds_b)]
        for h, dq in zip(hs, dqs):
            dqt[h] = dq
        own_kv[g, 0:256] = all_a[0] + all_a[1] + all_a[2]
        own_kv[g, 256:512] = all_b[0] + all_b[1] + all_b[2]

    def kv_copy(g, s, dev):
        return remote(skv.at[g, s - 1], rkv.at[g, s - 1], kv_s.at[g, s - 1], kv_r.at[g, s - 1], dev)

    def far(g):
        def one(j, carry):
            s = z - j
            skv[g, s - 1] = attend(g, j).astype(BF16)
            kv_copy(g, s, device(x, y, c, j)).start()
            return carry

        lax.fori_loop(0, z, one, 0)

    attend_own(0)
    attend_own(1)
    red_o.core_all(red_o.core_add)
    red_o.first_start()
    attend_own(2)
    far(0)
    red_gu.first_sum()
    red_gu.z_start()
    far(1)
    red_gu.z_sum()
    red_gu.exchange_start()
    far(2)
    red_dn.first_sum()
    red_dn.z_start()
    red_o.first_sum()
    red_o.z_start()
    red_gu.gather_start((ag_s.at[0], ag_r.at[0]))

    kvg = []
    for g in range(KV_HEADS):
        for s in range(1, NZ):

            @pl.when(z + s < NZ)
            def _(g=g, s=s):
                kv_copy(g, s, zdev[0]).wait_recv()
                own_kv[g] += rkv[g, s - 1].astype(F32)

        kvg.append(own_kv[g])

    def pair(left, right):
        return jnp.where(low, left, pltpu.roll(right, 64, 1))

    tiles = []
    for t in range(5):
        top = dqt[2 * t]
        bottom = dqt[2 * t + 1] if 2 * t + 1 < HEADS else jnp.zeros((64, ROWS), F32)
        tiles.append(jnp.transpose(jnp.concatenate([top, bottom], axis=0)) * (HEAD_DIM ** -0.5))
    tiles[4] = pair(tiles[4], kvg[0])
    tiles.append(pair(kvg[1], kvg[2]))
    cosine, sine = cos_v[...], sin_v[...]
    tiles = [t * cosine - swap_halves(t) * sine for t in tiles]
    tiles.append(jnp.where(low, pltpu.roll(kvg[0], 64, 1), kvg[1]))
    tiles.append(jnp.where(low, pltpu.roll(kvg[2], 64, 1), 0.0))
    gp = [t.astype(BF16) for t in tiles]
    for t in range(8):
        gq[t // 4, t % 4] = dot(n1t[...], gp[t]).astype(BF16).reshape(NZ, 144, 128)
    red_q.core_all(lambda k: red_q.core_copy(k).start())
    vecs.rc[0, 10:18, :] = jnp.concatenate(
        [jnp.sum(t.astype(F32), axis=0, keepdims=True) for t in gp], axis=0)
    gn1 = dot(jnp.concatenate(gp, axis=1), wq[...], 1, 1)
    inputs = jnp.transpose(tok_t[...].astype(F32))
    r = lax.rsqrt(jnp.mean(inputs * inputs, axis=-1, keepdims=True) + EPS)
    u = inputs * r
    f = gn1 * vec[:, 0:576]
    row = jnp.sum(gn1 * u, axis=0, keepdims=True)
    row = jnp.concatenate([row, jnp.zeros((1, 64), F32)], axis=1)
    for t in range(5):
        vecs.rc[0, t : t + 1, :] = row[:, 128 * t : 128 * t + 128]
        vecs.rc[0, 5 + t : 6 + t, :] = gain_row[:, 128 * t : 128 * t + 128]
    vecs.rc[0, 18:24, :] = jnp.zeros((6, 128), F32)
    vecs.start()
    red_q.core_all(red_q.core_add)
    red_q.both_start()
    red_dn.z_sum()
    red_dn.exchange_start()
    red_o.z_sum()
    red_o.exchange_start()
    vecs.next(0)
    grad_in[...] = jnp.transpose(gh[...] + r * (f - u * jnp.mean(f * u, axis=-1, keepdims=True)))
    vecs.next(1)
    red_q.both_sum()
    red_q.exchange_start()
    vecs.next(2)
    red_dn.gather_start((ag_s.at[1], ag_r.at[1]))
    red_o.gather_start((ag_s.at[2], ag_r.at[2]))
    red_q.gather_start((ag_s.at[3], ag_r.at[3]))
    vsum[...] = vecs.next(3)
    for red in (red_gu, red_dn, red_o, red_q):
        red.gather_wait()
    fdn_t[...] = jnp.transpose(fdn[...].astype(F32))
    for red, first in ((red_gu, True), (red_dn, True), (red_o, True), (red_q, False)):
        red.finish(first)
    vecs.finish()
    for g in range(KV_HEADS):
        for s in range(1, NZ):

            @pl.when(z >= s)
            def _(g=g, s=s):
                kv_copy(g, s, device(x, y, c, wrap(z + NZ - s, NZ))).wait_send()


def layer(att, wo, tok_t, cot_t, vec, lse, wgu, wdn, q, qt, kv, n1t, wq, cos_t, sin_t):
    sd = jax.ShapeDtypeStruct
    v = pl.BlockSpec(memory_space=VM)
    a = pl.BlockSpec(memory_space=ANY)
    dma = pltpu.SemaphoreType.DMA
    return pl.pallas_call(
        layer_kernel,
        out_shape=(
            sd((D, ROWS), F32),
            sd((D, ROWS), F32),
            sd((144, 2 * FF), BF16),
            sd((D, 384), F32),
            sd((144, QW), BF16),
            sd((144, QW), BF16),
            sd((24, 128), F32),
        ),
        in_specs=[v] * 6 + [a] * 9,
        out_specs=(v,) * 7,
        scratch_shapes=[
            VM((ROWS, D), BF16), VM((ROWS, D), F32), VM((ROWS, D), BF16), VM((D, ROWS), BF16), VM((ROWS, D), F32),
            VM((2, D, 384), BF16), VM((2, D, 384), BF16), VM((2, 384, D), BF16),
            VM((HEADS, ROWS, 128), BF16), VM((HEADS, 128, ROWS), BF16),
            VM((HEADS, ROWS, 128), BF16), VM((HEADS, 128, ROWS), BF16),
            VM((NZ, KV_HEADS, ROWS, 128), BF16), VM((D, ROWS), BF16), VM((D, QW), BF16),
            VM((ROWS, 128), F32), VM((ROWS, 128), F32), VM((HEADS, 1, ROWS), F32), VM((1, 640), F32),
            VM((2, 4, NZ, 144, 384), BF16), VM((2, NZ, 4, 48, D), BF16), VM((2, 4, NZ, 144, 128), BF16),
            VM((2, 4, NZ, 144, 128), BF16), VM((384, D), BF16),
            VM((HEADS, 64, ROWS), F32), VM((KV_HEADS, ROWS, 128), F32),
            VM((KV_HEADS, 3, ROWS, 128), BF16), VM((KV_HEADS, 3, ROWS, 128), BF16),
            *Reduction.scratch((4, 4), 144, 384), *Reduction.scratch((4, 4), 48, D),
            *Reduction.scratch((4, 4), 144, 128), *Reduction.scratch((4, 4), 144, 128, True),
            *VectorSum.scratch(),
            dma((7,)), dma((3, 2)), dma((3, 3)), dma((3, 3)), dma((4, 7)), dma((4, 7)),
        ],
        compiler_params=pltpu.CompilerParams(
            collective_id=1, has_side_effects=True, vmem_limit_bytes=62 << 20),
        name="layer_reduce",
    )(att, wo, tok_t, cot_t, vec, lse, wgu, wdn, q, qt, kv, n1t, wq, cos_t, sin_t)


def adam_step(weight, first_state, second_state, gradient, learn_rate, decay_rate):
    first_new = BETA_ONE * first_state + (1.0 - BETA_ONE) * gradient
    second_new = BETA_TWO * second_state + (1.0 - BETA_TWO) * gradient * gradient
    corr_one = 1.0 - BETA_ONE**STEP
    corr_two = 1.0 - BETA_TWO**STEP
    update = first_new / corr_one / (jnp.sqrt(second_new / corr_two) + ADAM_EPS)
    weight_new = weight - learn_rate * (update + decay_rate * weight)
    return (weight_new, first_new, second_new)


def adam_kernel(*refs):
    grads, states = refs[0:5], refs[5:20]
    passed, outs = refs[20:22], refs[22:]
    outs[0][...] = passed[0][...]
    outs[1][...] = passed[1][...]
    for k in range(4):
        grad = grads[k][...].astype(F32)
        if k == 0:
            grad = grad[:, 0:960]
        if k == 1:
            grad = grad[:, 0:576]
        new = adam_step(
            states[k][...], states[5 + k][...], states[10 + k][...], grad, RATE_MATRIX, DECAY_MATRIX)
        for i in range(3):
            outs[2 + 5 * i + k][...] = new[i]

    @pl.when(pl.program_id(0) == 0)
    def _():
        z = lax.axis_index("ctx")
        total = jnp.concatenate([grads[4][t : t + 1, :] for t in range(18)], axis=1)
        pad = jnp.zeros((1, VW - 640), F32)
        flat = jnp.concatenate([total[:, 0:640], pad], axis=1)
        mid = jnp.concatenate([total[:, 640:1280], pad], axis=1)
        flat = flat + pltpu.roll(jnp.broadcast_to(mid, (8, VW)), 576, 1)[0:1, :]
        flat = flat + jnp.concatenate(
            [jnp.zeros((1, 1152), F32), total[:, 1280:2304], jnp.zeros((1, 128), F32)], axis=1)
        shift = lax.rem(VW - z * 528, VW)
        grad = pltpu.roll(jnp.broadcast_to(flat, (8, VW)), shift, 1)[0:1, 0:528]
        new = adam_step(states[4][...], states[9][...], states[14][...], grad, RATE_VECTOR, 0.0)
        for i in range(3):
            outs[2 + 5 * i + 4][...] = new[i]


def adam(grads, states, passed):
    sd = jax.ShapeDtypeStruct
    steps = 9

    def rows(array):
        return pl.BlockSpec((array.shape[0] // steps, array.shape[1]), lambda i: (i, 0))

    def whole(array):
        return pl.BlockSpec(array.shape, lambda i: (0, 0))

    specs_g = [rows(g) for g in grads[0:4]] + [whole(grads[4])]
    specs_s = [whole(s) if k % 5 == 4 else rows(s) for k, s in enumerate(states)]
    specs_p = [rows(p) for p in passed]
    return pl.pallas_call(
        adam_kernel,
        grid=(steps,),
        out_shape=tuple(sd(p.shape, F32) for p in passed) + tuple(sd(s.shape, F32) for s in states),
        in_specs=specs_g + specs_s + specs_p,
        out_specs=tuple(specs_p) + tuple(specs_s),
        compiler_params=pltpu.CompilerParams(
            vmem_limit_bytes=40 << 20, dimension_semantics=("arbitrary",)),
        name="adam",
    )(*grads, *states, *passed)


def per_device(
    tokens, cotangent, w_qkv, w_out, w_gate_up, w_down, vectors,
    first_qkv, first_out, first_gate_up, first_down, first_vectors,
    second_qkv, second_out, second_gate_up, second_down, second_vectors,
):
    cos_np, sin_np = rope_tables()
    cos_t, sin_t = jnp.asarray(cos_np), jnp.asarray(sin_np)
    tok_t, cot_t = tokens.T, cotangent.T
    att, lse, vec, q, qt, kv, n1t, wq, wo, wgu, wdn = forward(
        tok_t, w_qkv, vectors[None, :], cos_t, sin_t, w_out, w_gate_up, w_down.T)
    block_t, grad_t, fgu, fdn_t, fo, fq, vsum = layer(
        att, wo, tok_t, cot_t, vec, lse, wgu, wdn, q, qt, kv, n1t, wq, cos_t, sin_t)
    states = (
        w_qkv, w_out, w_gate_up, w_down.T, vectors[None, :],
        first_qkv, first_out, first_gate_up, first_down.T, first_vectors[None, :],
        second_qkv, second_out, second_gate_up, second_down.T, second_vectors[None, :],
    )
    out = adam((fq, fo, fgu, fdn_t, vsum), states, (block_t, grad_t))
    out = list(out)
    for i in (0, 1, 5, 10, 15):
        out[i] = out[i].T
    for i in (6, 11, 16):
        out[i] = out[i][0]
    return tuple(out)


def solution(mesh):
    tokens = P(("dp", "ctx"), None)
    state = (P("ctx", None),) * 4 + (P("ctx"),)
    return jax.shard_map(
        per_device, mesh=mesh, in_specs=(tokens, tokens) + state * 3, out_specs=(tokens, tokens) + state * 3,
        check_vma=False,
    )
```

```python
import functools

import jax
import jax.numpy as jnp
import numpy as np
from jax import lax
from jax.experimental import pallas as pl
from jax.experimental.pallas import tpu as pltpu
from jax.sharding import PartitionSpec as P

D = 576
HEADS = 9
KV_HEADS = 3
GROUP = 3
HEAD_DIM = 64
FF = 1536
STEP = 10
LEN = 2048
ROWS = 512
QW = 1024
OW = 640
VW = 2304
NX = 4
NY = 4
NZ = 4

EPS = 1e-05
ROPE_BASE = 100000.0
MASK_FILL = -1e30
BETA_ONE = 0.9
BETA_TWO = 0.999
ADAM_EPS = 1e-08
RATE_MATRIX = 0.05
RATE_VECTOR = 0.5
DECAY_MATRIX = 0.1

F32 = jnp.float32
BF16 = jnp.bfloat16
MESH = pl.DeviceIdType.MESH
VM = pltpu.VMEM
ANY = pl.ANY


def rope_tables():
    half = HEAD_DIM // 2
    exponent = np.arange(half, dtype=np.float32) * np.float32(2.0 / HEAD_DIM)
    inverse = (np.float64(ROPE_BASE) ** (-exponent.astype(np.float64))).astype(np.float32)
    angles = np.arange(LEN, dtype=np.float32)[:, None] * inverse[None, :]
    cosine = np.cos(angles.astype(np.float64)).astype(np.float32)
    sine = np.sin(angles.astype(np.float64)).astype(np.float32)
    cos_all = np.concatenate([cosine] * 4, axis=1)
    sin_all = np.concatenate([-sine, sine, -sine, sine], axis=1)
    return cos_all, sin_all


def dot(a, b, ca=1, cb=0):
    return lax.dot_general(a, b, (((ca,), (cb,)), ((), ())), preferred_element_type=F32)


def place():
    dp = lax.axis_index("dp")
    z = lax.axis_index("ctx")
    x = lax.div(dp, NY * 2)
    y = lax.rem(lax.div(dp, 2), NY)
    c = lax.rem(dp, 2)
    return x, y, c, z


def device(x, y, c, z):
    return (x * (NY * 2) + y * 2 + c, z)


def wrap(i, n):
    return lax.rem(i, n)


def remote(src, dst, ssem, rsem, dev):
    return pltpu.make_async_remote_copy(
        src_ref=src, dst_ref=dst, send_sem=ssem, recv_sem=rsem, device_id=dev, device_id_type=MESH
    )


def greet(peers):
    barrier = pltpu.get_barrier_semaphore()
    for peer in peers:
        pl.semaphore_signal(barrier, inc=1, device_id=peer, device_id_type=MESH)
    pl.semaphore_wait(barrier, len(peers))


def swap_halves(v):
    width = v.shape[1]
    lane = lax.broadcasted_iota(jnp.int32, v.shape, 1)
    down = pltpu.roll(v, width - 32, 1)
    up = pltpu.roll(v, 32, 1)
    return jnp.where(lax.rem(lane, 64) < 32, down, up)


def low_lanes(v):
    lane = lax.broadcasted_iota(jnp.int32, v.shape, 1)
    return lane < 64


class Reduction:
    SCRATCH = 7

    @staticmethod
    def scratch(lead, r, w, both=False):
        dma = pltpu.SemaphoreType.DMA
        first = VM((15, r, w), BF16) if both else VM((3, 4, r, w), BF16)
        return [
            VM(lead + (r, w), BF16), first, VM((4, r, w), BF16),
            VM((3, r, w), BF16), VM((4, r, w), BF16), dma((32,)), dma((32,)),
        ]

    def __init__(self, own, fin, fin_at, bufs, along_x, z_first):
        self.own, self.fin, self.fin_at, self.z_first = own, fin, fin_at, z_first
        self.rc, self.r1, self.s1, self.r2, self.r3, self.ss, self.rs = bufs
        x, y, c, z = place()
        self.c, self.z = c, z
        if along_x:
            self.a, self.b = x, y
            self.at = lambda a, b, cc, zz: device(a, b, cc, zz)
        else:
            self.a, self.b = y, x
            self.at = lambda a, b, cc, zz: device(b, a, cc, zz)
        self.sends = []

    def copy(self, src, dst, k, dev):
        return remote(src, dst, self.ss.at[k], self.rs.at[k], dev)

    def go(self, src, dst, k, dev):
        copy = self.copy(src, dst, k, dev)
        copy.start()
        self.sends.append(copy)
        return copy

    def mine(self, a, z):
        return (self.c, z, a) if self.z_first else (self.c, a, z)

    def all_z(self, a):
        return self.own.at[self.c, :, a] if self.z_first else self.own.at[self.c, a]

    def core_copy(self, k):
        return self.copy(
            self.own.at[1 - self.c, k], self.rc.at[k], k, self.at(self.a, self.b, 1 - self.c, self.z))

    def core_add(self, k):
        self.core_copy(k).wait_recv()

        def add(j, carry):
            total = self.own[self.c, k, j].astype(F32) + self.rc[k, j].astype(F32)
            self.own[self.c, k, j] = total.astype(BF16)
            return carry

        lax.fori_loop(0, 4, add, 0)

    def core_all(self, act):
        def one(k, carry):
            act(k)
            return carry

        lax.fori_loop(0, 4, one, 0)

    def first_copy(self, d):
        to = wrap(self.a + d, 4)
        return self.copy(self.all_z(to), self.r1.at[d - 1], 3 + d, self.at(to, self.b, self.c, self.z))

    def first_start(self):
        for d in range(1, 4):
            self.first_copy(d).start()

    def first_sum(self):
        for d in range(1, 4):
            self.first_copy(d).wait_recv()

        def add(j, carry):
            total = self.own[self.mine(self.a, j)].astype(F32) + self.r1[0, j].astype(F32)
            total = total + self.r1[1, j].astype(F32) + self.r1[2, j].astype(F32)
            self.s1[j] = total.astype(BF16)
            return carry

        lax.fori_loop(0, 4, add, 0)

    def z_start(self):
        self.second = []
        for d in range(1, 4):
            to = wrap(self.z + d, 4)
            self.second.append(
                self.go(self.s1.at[to], self.r2.at[d - 1], 6 + d, self.at(self.a, self.b, self.c, to)))

    def z_sum(self):
        for copy in self.second:
            copy.wait_recv()
        total = self.s1[self.z].astype(F32) + self.r2[0].astype(F32)
        total = total + self.r2[1].astype(F32) + self.r2[2].astype(F32)
        self.r3[self.b] = total.astype(BF16)

    def both_start(self):
        self.second = []
        k = 16
        for da in range(4):
            for dz in range(4):
                if da or dz:
                    to_a, to_z = wrap(self.a + da, 4), wrap(self.z + dz, 4)
                    k += 1
                    self.second.append(
                        self.go(self.own.at[self.mine(to_a, to_z)], self.r1.at[k - 17], k,
                                self.at(to_a, self.b, self.c, to_z)))

    def both_sum(self):
        for copy in self.second:
            copy.wait_recv()

        def add(j, total):
            return total + self.r1[j].astype(F32)

        total = lax.fori_loop(0, 15, add, self.own[self.mine(self.a, self.z)].astype(F32))
        self.r3[self.b] = total.astype(BF16)

    def exchange_start(self):
        self.third = []
        for d in range(1, 4):
            to = wrap(self.b + d, 4)
            ref = self.r3.at[self.b]
            self.third.append(self.go(ref, ref, 9 + d, self.at(self.a, to, self.c, self.z)))

    def gather_start(self, sems):
        for copy in self.third:
            copy.wait_recv()
        total = self.r3[0].astype(F32) + self.r3[1].astype(F32)
        total = total + self.r3[2].astype(F32) + self.r3[3].astype(F32)
        where = self.fin_at(self.c, self.a)
        ref = self.fin.at[where]
        self.fin[where] = total.astype(BF16)
        self.fourth = []
        k = -1
        for e in range(2):
            for d in range(4):
                if e or d:
                    k += 1
                    to = self.at(wrap(self.a + d, 4), self.b, wrap(self.c + e, 2), self.z)
                    self.fourth.append(remote(ref, ref, sems[0].at[k], sems[1].at[k], to))
        for copy in self.fourth:
            copy.start()

    def gather_wait(self):
        for copy in self.fourth:
            copy.wait_recv()

    def finish(self, along_first):
        for copy in self.sends + self.fourth:
            copy.wait_send()
        self.core_all(lambda k: self.core_copy(k).wait_send())
        if along_first:
            for d in range(1, 4):
                self.first_copy(d).wait_send()


class VectorSum:
    SCRATCH = 4

    @staticmethod
    def scratch():
        dma = pltpu.SemaphoreType.DMA
        return [VM((2, 24, 128), F32), VM((3, 4, 24, 128), F32), dma((10,)), dma((10,))]

    def __init__(self, bufs):
        self.rc, self.r, self.ss, self.rs = bufs
        self.sends = []

    def start(self):
        x, y, c, z = place()
        self.pending = [remote(self.rc.at[0], self.rc.at[1], self.ss.at[0], self.rs.at[0], device(x, y, 1 - c, z))]
        self.pending[0].start()
        self.sends += self.pending

    def next(self, k):
        x, y, c, z = place()
        for copy in self.pending:
            copy.wait_recv()
        if k == 0:
            total = self.rc[0] + self.rc[1]
        else:
            total = self.r[k - 1, 0] + self.r[k - 1, 1] + self.r[k - 1, 2] + self.r[k - 1, 3]
        if k == 3:
            return total
        me = (y, z, x)[k]
        self.r[k, me] = total
        self.pending = []
        for d in range(1, 4):
            to = wrap(me + d, 4)
            dev = (device(x, to, c, z), device(x, y, c, to), device(to, y, c, z))[k]
            copy = remote(self.r.at[k, me], self.r.at[k, me], self.ss.at[3 * k + d], self.rs.at[3 * k + d], dev)
            copy.start()
            self.pending.append(copy)
        self.sends += self.pending
        return None

    def finish(self):
        for copy in self.sends:
            copy.wait_send()


def step_kernel(
    tok_t, cot_t, cos_hbm, sin_hbm, vstates, states,
    block_out, grad_in, new_states, new_vectors, wo_all, wgu_all, wdn_all, s,
):
    x, y, c, z = place()
    sib = device(x, y, 1 - c, z)
    zdev = [device(x, y, c, wrap(z + d, NZ)) for d in range(1, NZ)]
    xdev = [device(wrap(x + d, NX), y, c, z) for d in range(1, NX)]
    ydev = [device(x, wrap(y + d, NY), c, z) for d in range(1, NY)]
    peers = [sib] + xdev
    for dy in range(4):
        for dz in range(4):
            if dy or dz:
                peers.append(device(x, wrap(y + dy, NY), c, wrap(z + dz, NZ)))
    for d in range(1, 4):
        peers.append(device(wrap(x + d, NX), y, 1 - c, z))
        peers.append(device(x, wrap(y + d, NY), 1 - c, z))
    wq_v, vec_v, q_s, qt_s, kvs = s["wq"], s["vec"], s["q"], s["qt"], s["kv"]
    b_out, b_gu, b_dn, n1t = s["b_out"], s["ggu"].at[0, 0:2], s["gdn"].at[0, 0:2], s["n1t"]
    m_s, l_s, ot_s, lse, att = s["m"], s["l"], s["ot"], s["lse"], s["att"]
    loc_sem = s["loc"]
    row0 = pl.multiple_of(z * ROWS, ROWS)
    loads = [
        pltpu.make_async_copy(cos_hbm.at[pl.ds(row0, ROWS)], s["cos"], loc_sem.at[0]),
        pltpu.make_async_copy(sin_hbm.at[pl.ds(row0, ROWS)], s["sin"], loc_sem.at[1]),
        pltpu.make_async_copy(cot_t, s["n2t"], loc_sem.at[2]),
    ]
    masters = new_states[0]
    master_loads = [
        pltpu.make_async_copy(states[0][k], masters[k], s["st_sem"].at[0, k]) for k in range(4)]
    for load in master_loads + loads:
        load.start()
    vec_v[0] = jnp.zeros((1, VW), F32)
    vec_v[0, :, 0:528] = vstates[0][...].reshape(1, 528)
    rolled = pltpu.roll(jnp.broadcast_to(vec_v[0], (8, VW)), z * 528, 1)
    vec_v[0] = rolled[0:1, :]
    qrows = pl.ds(pl.multiple_of(z * 144, 144), 144)
    master_loads[0].wait()
    wq_v[qrows, 0:896] = masters[0][:, 0:896].astype(BF16)
    wq_v[qrows, 896:1024] = jnp.concatenate(
        [masters[0][:, 896:960].astype(BF16), jnp.zeros((144, 64), BF16)], axis=1
    )
    greet(peers)

    sends = []
    kcols = pl.ds(pl.multiple_of(512 + c * 256, 256), 256)
    xcols = pl.ds(pl.multiple_of(x * 128, 128), 128)
    kwaits = []
    qwaits = []
    for d in range(1, NZ):
        ref = wq_v.at[qrows, kcols]
        kwaits.append(remote(ref, ref, s["zk_s"].at[d - 1], s["zk_r"].at[d - 1], zdev[d - 1]))
        kwaits.append(
            remote(vec_v.at[0], vec_v.at[d], s["zv_s"].at[d - 1], s["zv_r"].at[d - 1], zdev[d - 1]))
        ref = wq_v.at[qrows, xcols]
        qwaits.append(remote(ref, ref, s["zq_s"].at[d - 1], s["zq_r"].at[d - 1], zdev[d - 1]))
    for copy in kwaits:
        copy.start()

    @pl.when(c == 0)
    def _():
        for copy in qwaits:
            copy.start()

    sends.extend(kwaits)

    def block_rows(e, n):
        return pl.ds(pl.multiple_of(wrap(z + NZ - e, NZ) * n, n), n)

    inputs = jnp.transpose(tok_t[...].astype(F32))
    unit = inputs * lax.rsqrt(jnp.mean(inputs * inputs, axis=-1, keepdims=True) + EPS)

    master_loads[1].wait()
    b_out[:, 0:512] = masters[1][:, 0:512].astype(BF16)
    b_out[:, 512:640] = jnp.concatenate(
        [masters[1][:, 512:576].astype(BF16), jnp.zeros((144, 64), BF16)], axis=1)
    own = [pltpu.make_async_copy(b_out, wo_all.at[qrows, :], loc_sem.at[3])]
    master_loads[2].wait()
    master_loads[3].wait()
    down = jnp.transpose(masters[3][...]).astype(BF16)
    for p in range(8):
        b_gu[p // 4, p % 4] = masters[2][:, 384 * p : 384 * p + 384].astype(BF16)
        b_dn[p // 4, p % 4] = down[48 * p : 48 * p + 48, :]
        own.append(
            pltpu.make_async_copy(
                b_gu.at[p // 4, p % 4], wgu_all.at[qrows, 384 * p : 384 * p + 384], s["own"].at[0, p]))
        own.append(
            pltpu.make_async_copy(
                b_dn.at[p // 4, p % 4], wdn_all.at[pl.ds(pl.multiple_of(z * 384 + 48 * p, 48), 48), :],
                s["own"].at[1, p]))
    for copy in own:
        copy.start()

    for copy in kwaits:
        copy.wait_recv()
    kswaps = []
    for e in range(1, NZ):
        ref = wq_v.at[block_rows(e, 144), kcols]
        kswaps.append(remote(ref, ref, s["ck_s"].at[e - 1], s["ck_r"].at[e - 1], sib))
    for copy in kswaps:
        copy.start()
    sends.extend(kswaps)

    pgu = pl.multiple_of((c * 4 + x) * 384, 128)
    pdn = (c * 4 + y) * 48
    po = jnp.minimum(c * 4 + y, 4)
    has_o = c * 4 + y < 5
    oc = pl.multiple_of(po * 128, 128)
    wsend = []
    osend = []
    for d in range(1, NZ):
        osend.append(
            remote(b_out.at[:, pl.ds(oc, 128)], wo_all.at[qrows, pl.ds(oc, 128)],
                   s["zw_s"].at[0, d - 1], s["zw_r"].at[0, d - 1], zdev[d - 1]))
        wsend.append(
            remote(b_gu.at[c, x], wgu_all.at[qrows, pl.ds(pgu, 384)],
                   s["zw_s"].at[1, d - 1], s["zw_r"].at[1, d - 1], zdev[d - 1]))
        wsend.append(
            remote(b_dn.at[c, y],
                   wdn_all.at[pl.ds(pl.multiple_of(z * 384 + pdn, 48), 48), :],
                   s["zw_s"].at[2, d - 1], s["zw_r"].at[2, d - 1], zdev[d - 1]))

    @pl.when(has_o)
    def _():
        for copy in osend:
            copy.start()

    for copy in wsend:
        copy.start()

    qleg = []
    qswaps = []
    for e in range(1, NZ):
        ref = wq_v.at[block_rows(e, 144), xcols]
        for d in range(1, NX):
            qleg.append(remote(ref, ref, s["xq_s"].at[e - 1, d - 1], s["xq_r"].at[e - 1, d - 1], xdev[d - 1]))
        ref = wq_v.at[block_rows(e, 144), 0:512]
        qswaps.append(remote(ref, ref, s["cq_s"].at[e - 1], s["cq_r"].at[e - 1], sib))

    @pl.when(c == 0)
    def _():
        for copy in qwaits:
            copy.wait_recv()
        for copy in qleg:
            copy.start()

    raw = vec_v[0] + vec_v[1] + vec_v[2] + vec_v[3]
    raw = raw.astype(BF16).astype(F32)
    wide = jnp.broadcast_to(raw, (8, VW))
    gain_one = raw[:, 0:576]
    gain_two = pltpu.roll(wide, VW - 576, 1)[0:1, 0:576]
    bias = raw[:, 1152:2176]
    normed = unit * gain_one
    n1 = normed.astype(BF16)
    n1t[...] = jnp.transpose(normed).astype(BF16)
    for load in loads:
        load.wait()
    cosine, sine = s["cos"][...], s["sin"][...]

    for copy in kswaps:
        copy.wait_recv()

    def tile_of(v, t):
        return v[:, 128 * t : 128 * t + 128]

    def rotated(v):
        return v * cosine + swap_halves(v) * sine

    def turn(v):
        return pltpu.roll(v, 64, 1)

    proj = dot(n1, wq_v[:, 512:1024]) + bias[:, 512:1024]
    rot4, rot5 = rotated(tile_of(proj, 0)), rotated(tile_of(proj, 1))
    val6, val7 = tile_of(proj, 2), tile_of(proj, 3)
    low = low_lanes(rot4)
    kvs[z, 0] = jnp.where(low, turn(rot4), turn(val6)).astype(BF16)
    kvs[z, 1] = jnp.where(low, rot5, val6).astype(BF16)
    kvs[z, 2] = jnp.where(low, turn(rot5), turn(val7)).astype(BF16)
    kv_sends = []
    for d in range(1, NZ):
        kv_sends.append(
            remote(kvs.at[z], kvs.at[z], s["kv_s"].at[d - 1], s["kv_r"].at[d - 1],
                   device(x, y, c, wrap(z + d, NZ))))

        @pl.when(z + d < NZ)
        def _(d=d):
            kv_sends[d - 1].start()

    def put_query(h, part):
        qh = jnp.where(low, part, 0.0) * (HEAD_DIM ** -0.5)
        q_s[h] = qh.astype(BF16)
        qt_s[h] = jnp.transpose(qh).astype(BF16)

    put_query(8, rot4)

    @pl.when(c == 0)
    def _():
        for copy in qleg:
            copy.wait_recv()
        for copy in qswaps:
            copy.start()

    @pl.when(c == 1)
    def _():
        for copy in qswaps:
            copy.wait_recv()

    proj = dot(n1, wq_v[:, 0:512]) + bias[:, 0:512]
    for t in range(4):
        rot = rotated(tile_of(proj, t))
        put_query(2 * t, rot)
        put_query(2 * t + 1, turn(rot))

    def step(j):
        kvt = [jnp.transpose(kvs[j, g].astype(F32)).astype(BF16)[64:128, :] for g in range(KV_HEADS)]
        heads = range(HEADS)
        sts = [dot(kvs[j, h // GROUP], qt_s[h]) for h in heads]
        olds = [m_s[h] for h in heads]
        peaks = [jnp.maximum(jnp.max(v, axis=0, keepdims=True), o) for v, o in zip(sts, olds)]
        alphas = [jnp.exp(o - p) for o, p in zip(olds, peaks)]
        ps = [jnp.exp(v - p) for v, p in zip(sts, peaks)]
        totals = [jnp.sum(p, axis=0, keepdims=True) + l_s[h] * a for h, p, a in zip(heads, ps, alphas)]
        outs = [dot(kvt[h // GROUP], p.astype(BF16)) + ot_s[h] * a for h, p, a in zip(heads, ps, alphas)]
        for h in heads:
            m_s[h] = peaks[h]
            l_s[h] = totals[h]
            ot_s[h] = outs[h]

    def visible(width):
        shape = (256, width)
        return lax.broadcasted_iota(jnp.int32, shape, 0) <= lax.broadcasted_iota(jnp.int32, shape, 1)

    right = slice(256, 512)
    always = z >= 0

    @pl.when(always)
    def _():
        keep_a, keep_b = visible(512), visible(256)
        kvt = [jnp.transpose(kvs[z, g].astype(F32)).astype(BF16)[64:128, :] for g in range(KV_HEADS)]
        heads = range(HEADS)
        st_a = [jnp.where(keep_a, dot(kvs[z, h // GROUP, 0:256], qt_s[h]), MASK_FILL) for h in heads]
        st_b = [jnp.where(keep_b, dot(kvs[z, h // GROUP, right], qt_s[h, :, right]), MASK_FILL) for h in heads]
        none = jnp.full((1, 256), MASK_FILL, F32)
        zero = jnp.zeros((1, 256), F32)
        zeros = jnp.zeros((64, 256), F32)
        peaks = [
            jnp.maximum(
                jnp.max(a, axis=0, keepdims=True),
                jnp.concatenate([none, jnp.max(b, axis=0, keepdims=True)], axis=1))
            for a, b in zip(st_a, st_b)]
        p_a = [jnp.exp(a - p) for a, p in zip(st_a, peaks)]
        p_b = [jnp.exp(b - p[:, right]) for b, p in zip(st_b, peaks)]
        totals = [
            jnp.sum(a, axis=0, keepdims=True) + jnp.concatenate([zero, jnp.sum(b, axis=0, keepdims=True)], axis=1)
            for a, b in zip(p_a, p_b)]
        outs = [
            dot(kvt[h // GROUP][:, 0:256], p_a[h].astype(BF16))
            + jnp.concatenate([zeros, dot(kvt[h // GROUP][:, right], p_b[h].astype(BF16))], axis=1)
            for h in heads]
        for h in heads:
            m_s[h] = peaks[h]
            l_s[h] = totals[h]
            ot_s[h] = outs[h]

    for copy in wsend:
        copy.wait_recv()

    @pl.when(has_o)
    def _():
        for copy in osend:
            copy.wait_recv()

    leg = []
    oleg = []
    aw_s, aw_r = s["aw_s"], s["aw_r"]
    for e in range(1, NZ):
        src_z = wrap(z + NZ - e, NZ)
        ref_gu = wgu_all.at[block_rows(e, 144), pl.ds(pgu, 384)]
        ref_dn = wdn_all.at[pl.ds(pl.multiple_of(src_z * 384 + pdn, 48), 48), :]
        ref_o = wo_all.at[block_rows(e, 144), pl.ds(oc, 128)]
        for d in range(1, NX):
            leg.append(remote(ref_gu, ref_gu, aw_s.at[0, e - 1, d - 1], aw_r.at[0, e - 1, d - 1], xdev[d - 1]))
            leg.append(remote(ref_dn, ref_dn, aw_s.at[1, e - 1, d - 1], aw_r.at[1, e - 1, d - 1], ydev[d - 1]))
            oleg.append(remote(ref_o, ref_o, aw_s.at[2, e - 1, d - 1], aw_r.at[2, e - 1, d - 1], ydev[d - 1]))

    @pl.when(has_o)
    def _():
        for copy in oleg:
            copy.start()

    for copy in leg:
        copy.start()
    sends.extend(leg)

    last = []
    last_o = [[], []]
    for d in range(1, NZ):
        if d == NZ - 1:
            for copy in leg:
                copy.wait_recv()
            for dd in range(1, NY):
                from_y = wrap(y + NY - dd, NY)

                @pl.when(c * 4 + from_y < 5)
                def _(dd=dd):
                    for e in range(1, NZ):
                        oleg[(e - 1) * 3 + dd - 1].wait_recv()

            for e in range(1, NZ):
                src_z = wrap(z + NZ - e, NZ)
                rows = block_rows(e, 144)
                ref_g = wgu_all.at[rows, pl.ds(pl.multiple_of(c * 1536, 128), 1536)]
                ref_d = wdn_all.at[pl.ds(pl.multiple_of(src_z * 384 + c * 192, 192), 192), :]
                cw_s, cw_r = s["cw_s"], s["cw_r"]
                for core, cols in enumerate((slice(0, 512), slice(512, 640))):
                    ref_o = wo_all.at[rows, cols]
                    last_o[core].append(remote(ref_o, ref_o, cw_s.at[0, e - 1], cw_r.at[0, e - 1], sib))
                last.append(remote(ref_g, ref_g, cw_s.at[1, e - 1], cw_r.at[1, e - 1], sib))
                last.append(remote(ref_d, ref_d, cw_s.at[2, e - 1], cw_r.at[2, e - 1], sib))
            for core in range(2):

                @pl.when(c == core)
                def _(core=core):
                    for copy in last_o[core]:
                        copy.start()

            for copy in last:
                copy.start()
            sends.extend(last)

        @pl.when(z >= d)
        def _(d=d):
            kv_sends[d - 1].wait_recv()
            step(z - d)

    for h in range(HEADS):
        ot_s[h] = ot_s[h] * (1.0 / l_s[h])
        lse[h] = m_s[h] + jnp.log(l_s[h])
    for t in range(5):
        top = ot_s[2 * t]
        bottom = ot_s[2 * t + 1] if 2 * t + 1 < HEADS else jnp.zeros((64, ROWS), F32)
        att[:, 128 * t : 128 * t + 128] = jnp.transpose(jnp.concatenate([top, bottom], axis=0)).astype(BF16)

    for core in range(2):

        @pl.when(c == core)
        def _(core=core):
            for copy in last_o[1 - core]:
                copy.wait_recv()

    for copy in own:
        copy.wait()
    wo = s["wo"]
    load_o = pltpu.make_async_copy(wo_all, wo, loc_sem.at[4])
    load_o.start()
    for copy in last:
        copy.wait_recv()
    for copy in wsend:
        copy.wait_send()
    wgs, wus, wds, w_sem = s["wgs"], s["wus"], s["wds"], s["w_sem"]

    def weights(i, slot):
        col = pl.multiple_of(wrap(x + 1 + i, 4) * 384, 384)
        return [
            pltpu.make_async_copy(wgu_all.at[:, pl.ds(col, 384)], wgs.at[slot], w_sem.at[0, slot]),
            pltpu.make_async_copy(
                wgu_all.at[:, pl.ds(pl.multiple_of(col + FF, 384), 384)], wus.at[slot], w_sem.at[1, slot]),
            pltpu.make_async_copy(wdn_all.at[pl.ds(col, 384), :], wds.at[slot], w_sem.at[2, slot]),
        ]

    for load in weights(0, 0):
        load.start()

    ggu, gdn, go, gq, fin = s["ggu"], s["gdn"], s["go"], s["gq"], s["fin"]
    lanes = lambda cc, a: (slice(None), pl.ds(pl.multiple_of((cc * 4 + a) * 128, 128), 128))
    red_gu = Reduction(
        ggu, fin["gu"], lambda cc, a: (slice(None), pl.ds(pl.multiple_of((cc * 4 + a) * 384, 128), 384)),
        s["red_gu"], True, False)
    red_dn = Reduction(
        gdn, fin["dn"], lambda cc, a: (pl.ds(pl.multiple_of((cc * 4 + a) * 48, 48), 48), slice(None)),
        s["red_dn"], False, True)
    red_o = Reduction(go, fin["o"], lanes, s["red_o"], False, False)
    red_q = Reduction(gq, fin["q"], lanes, s["red_q"], False, False)
    vecs = VectorSum(s["vecs"])
    ag_s, ag_r = s["ag_s"], s["ag_r"]
    cot, gh, n2, n2t, gn2t = s["cot"], s["gh"], s["n2"], s["n2t"], grad_in
    do_in, dot_in, delta_in, gain_row = s["do"], s["dot"], s["delta"], s["gain_row"]
    dqt, own_kv, skv, rkv = ot_s, s["own_kv"], s["skv"], s["rkv"]

    s["cot"][...] = jnp.transpose(s["n2t"][...].astype(F32)).astype(BF16)
    gn2t[...] = jnp.zeros_like(gn2t)
    inputs = jnp.transpose(tok_t[...].astype(F32))
    load_o.wait()
    hid = inputs + dot(att[:, 0:576], wo[:, 0:576])
    inv_two = lax.rsqrt(jnp.mean(hid * hid, axis=-1, keepdims=True) + EPS)
    normed = hid * inv_two * gain_two
    n2[...] = normed.astype(BF16)
    n2t[...] = jnp.transpose(normed).astype(BF16)
    gh[...] = hid
    block_out[...] = jnp.transpose(hid)

    def chunk(i, carry):
        slot = lax.rem(i, 2)
        here = wrap(x + 1 + i, 4)
        for load in weights(i, slot):
            load.wait()

        @pl.when(i < 3)
        def _():
            for load in weights(i + 1, 1 - slot):
                load.start()

        gate = dot(n2[...], wgs[slot])
        up = dot(n2[...], wus[slot])
        sg = jax.nn.sigmoid(gate)
        silu = gate * sg
        act = (silu * up).astype(BF16)
        ga = dot(cot[...], wds[slot], 1, 1)
        gg = (ga * up * sg * (1.0 + gate * (1.0 - sg))).astype(BF16)
        gu = (ga * silu).astype(BF16)
        ggu[0, here] = dot(n2t[...], gg).astype(BF16).reshape(NZ, 144, 384)
        ggu[1, here] = dot(n2t[...], gu).astype(BF16).reshape(NZ, 144, 384)
        red_gu.core_copy(here).start()
        down = dot(act, cot[...], 0, 0).astype(BF16)
        for p in range(8):
            gdn[p // 4, here, p % 4] = down[48 * p : 48 * p + 48, :]
        red_dn.core_copy(here).start()
        block_out[...] += lax.dot_general(wds[slot], act, (((0,), (1,)), ((), ())), preferred_element_type=F32)
        gn2t[...] += dot(wgs[slot], gg, 1, 1) + dot(wus[slot], gu, 1, 1)

        @pl.when(i > 0)
        def _():
            red_gu.core_add(wrap(x + i, 4))
            red_gu.first_copy(i).start()

        return carry

    lax.fori_loop(0, 4, chunk, 0)

    red_dn.core_all(red_dn.core_add)
    red_dn.first_start()
    red_gu.core_add(x)
    state_loads = []
    for i in range(1, 3):
        for k in range(4):
            copy = pltpu.make_async_copy(states[i][k], new_states[i][k], s["st_sem"].at[i, k])
            copy.start()
            state_loads.append(copy)

    @pl.when(always)
    def _():
        hid = gh[...]
        inv_two = lax.rsqrt(jnp.mean(hid * hid, axis=-1, keepdims=True) + EPS)
        u = hid * inv_two
        e = jnp.transpose(gn2t[...])
        f = e * gain_two
        gain_row[:, 0:576] = jnp.sum(e * u, axis=0, keepdims=True)
        gain_row[:, 576:640] = jnp.zeros((1, 64), F32)
        grad_hidden = cot[...].astype(F32) + inv_two * (f - u * jnp.mean(f * u, axis=-1, keepdims=True))
        gh[...] = grad_hidden
        ghl = grad_hidden.astype(BF16)
        grad_out = dot(att[:, 0:576], ghl, 0, 0).astype(BF16)
        for p in range(8):
            if p < 4:
                part = grad_out[:, 128 * p : 128 * p + 128]
            elif p == 4:
                part = jnp.concatenate([grad_out[:, 512:576], jnp.zeros((D, 64), BF16)], axis=1)
            else:
                part = jnp.zeros((D, 128), BF16)
            go[p // 4, p % 4] = part.reshape(NZ, 144, 128)
        red_o.core_all(lambda k: red_o.core_copy(k).start())
        gm = dot(ghl, wo[:, 0:576], 1, 1).astype(BF16).astype(F32)
        gm = jnp.concatenate([gm, jnp.zeros((ROWS, 64), F32)], axis=1)
        for h in range(HEADS):
            part = gm[:, 128 * (h // 2) : 128 * (h // 2) + 128]
            part = part if h % 2 == 1 else turn(part)
            part = jnp.where(low_lanes(part), 0.0, part)
            do_in[h] = part.astype(BF16)
            part = jnp.transpose(part)
            dot_in[h] = part.astype(BF16)
            delta_in[h] = jnp.sum(part[64:128, :] * ot_s[h], axis=0, keepdims=True)

    def attend(g, j):
        kv = kvs[j, g]
        kt = jnp.transpose(kv.astype(F32)).astype(BF16)[0:64, :]
        hs = [g * GROUP + k for k in range(GROUP)]
        sts = [dot(kv, qt_s[h]) for h in hs]
        dpts = [dot(kv, dot_in[h]) for h in hs]
        pts = [jnp.exp(v - lse[h]) for v, h in zip(sts, hs)]
        dsts = [(p * (d - delta_in[h])).astype(BF16) for p, d, h in zip(pts, dpts, hs)]
        both = [dot(d, q_s[h]) + dot(p.astype(BF16), do_in[h]) for p, d, h in zip(pts, dsts, hs)]
        dqs = [dot(kt, d) for d in dsts]
        for h, dq in zip(hs, dqs):
            dqt[h] += dq
        return both[0] + both[1] + both[2]

    def attend_own(g):
        keep_a, keep_b = visible(512), visible(256)
        kv_a, kv_b = kvs[z, g, 0:256], kvs[z, g, 256:512]
        kt = jnp.transpose(kvs[z, g].astype(F32)).astype(BF16)[0:64, :]
        zeros = jnp.zeros((64, 256), F32)
        hs = [g * GROUP + k for k in range(GROUP)]
        pt_a = [jnp.where(keep_a, jnp.exp(dot(kv_a, qt_s[h]) - lse[h]), 0.0) for h in hs]
        pt_b = [jnp.where(keep_b, jnp.exp(dot(kv_b, qt_s[h, :, right]) - lse[h, :, right]), 0.0) for h in hs]
        ds_a = [(p * (dot(kv_a, dot_in[h]) - delta_in[h])).astype(BF16) for p, h in zip(pt_a, hs)]
        ds_b = [
            (p * (dot(kv_b, dot_in[h, :, right]) - delta_in[h, :, right])).astype(BF16) for p, h in zip(pt_b, hs)]
        all_a = [dot(d, q_s[h]) + dot(p.astype(BF16), do_in[h]) for p, d, h in zip(pt_a, ds_a, hs)]
        all_b = [dot(d, q_s[h, right]) + dot(p.astype(BF16), do_in[h, right]) for p, d, h in zip(pt_b, ds_b, hs)]
        dqs = [
            dot(kt[:, 0:256], a) + jnp.concatenate([zeros, dot(kt[:, right], b)], axis=1)
            for a, b in zip(ds_a, ds_b)]
        for h, dq in zip(hs, dqs):
            dqt[h] = dq
        own_kv[g, 0:256] = all_a[0] + all_a[1] + all_a[2]
        own_kv[g, 256:512] = all_b[0] + all_b[1] + all_b[2]

    def kv_copy(g, k, dev):
        return remote(
            skv.at[g, k - 1], rkv.at[g, k - 1], s["dkv_s"].at[g, k - 1], s["dkv_r"].at[g, k - 1], dev)

    def far(g):
        def one(j, carry):
            k = z - j
            skv[g, k - 1] = attend(g, j).astype(BF16)
            kv_copy(g, k, device(x, y, c, j)).start()
            return carry

        lax.fori_loop(0, z, one, 0)

    for g in range(2):
        pl.when(always)(functools.partial(attend_own, g))
    red_o.core_all(red_o.core_add)
    red_o.first_start()
    pl.when(always)(functools.partial(attend_own, 2))
    far(0)
    red_gu.first_sum()
    red_gu.z_start()
    far(1)
    red_dn.first_sum()
    red_dn.z_start()
    red_o.first_sum()
    red_o.z_start()
    red_gu.z_sum()
    red_gu.exchange_start()
    far(2)
    red_dn.z_sum()
    red_dn.exchange_start()
    red_o.z_sum()
    red_o.exchange_start()
    red_gu.gather_start((ag_s.at[0], ag_r.at[0]))

    for g in range(KV_HEADS):
        for k in range(1, NZ):

            @pl.when(z + k < NZ)
            def _(g=g, k=k):
                kv_copy(g, k, zdev[0]).wait_recv()
                own_kv[g] += rkv[g, k - 1].astype(F32)

    kvg = [own_kv[g] for g in range(KV_HEADS)]
    low = low_lanes(kvg[0])
    cosine, sine = s["cos"][...], s["sin"][...]

    def pair(left, other):
        return jnp.where(low, left, turn(other))

    tiles = []
    for t in range(5):
        top = dqt[2 * t]
        bottom = dqt[2 * t + 1] if 2 * t + 1 < HEADS else jnp.zeros((64, ROWS), F32)
        tiles.append(jnp.transpose(jnp.concatenate([top, bottom], axis=0)) * (HEAD_DIM ** -0.5))
    tiles[4] = pair(tiles[4], kvg[0])
    tiles.append(pair(kvg[1], kvg[2]))
    tiles = [t * cosine - swap_halves(t) * sine for t in tiles]
    tiles.append(jnp.where(low, turn(kvg[0]), kvg[1]))
    tiles.append(jnp.where(low, turn(kvg[2]), 0.0))
    gp = [t.astype(BF16) for t in tiles]
    for t in range(8):
        q_s[t] = gp[t]
        gq[t // 4, t % 4] = dot(n1t[...], gp[t]).astype(BF16).reshape(NZ, 144, 128)
    red_q.core_all(lambda k: red_q.core_copy(k).start())
    vecs.rc[0, 10:18, :] = jnp.concatenate(
        [jnp.sum(q_s[t].astype(F32), axis=0, keepdims=True) for t in range(8)], axis=0)
    gn1 = dot(jnp.concatenate([q_s[t] for t in range(8)], axis=1), wq_v[...], 1, 1)
    inputs = jnp.transpose(tok_t[...].astype(F32))
    r = lax.rsqrt(jnp.mean(inputs * inputs, axis=-1, keepdims=True) + EPS)
    u = inputs * r
    f = gn1 * gain_one
    row = jnp.sum(gn1 * u, axis=0, keepdims=True)
    row = jnp.concatenate([row, jnp.zeros((1, 64), F32)], axis=1)
    for t in range(5):
        vecs.rc[0, t : t + 1, :] = row[:, 128 * t : 128 * t + 128]
        vecs.rc[0, 5 + t : 6 + t, :] = gain_row[:, 128 * t : 128 * t + 128]
    vecs.rc[0, 18:24, :] = jnp.zeros((6, 128), F32)
    vecs.start()
    red_q.core_all(red_q.core_add)
    vecs.next(0)
    red_q.both_start()
    grad_in[...] = jnp.transpose(gh[...] + r * (f - u * jnp.mean(f * u, axis=-1, keepdims=True)))
    red_dn.gather_start((ag_s.at[1], ag_r.at[1]))
    red_o.gather_start((ag_s.at[2], ag_r.at[2]))
    vecs.next(1)

    def update(k, grad):
        new = adam_step(
            new_states[0][k][...], new_states[1][k][...], new_states[2][k][...], grad, RATE_MATRIX, DECAY_MATRIX)
        for i in range(3):
            new_states[i][k][...] = new[i]

    for load in state_loads:
        load.wait()
    red_gu.gather_wait()
    update(2, fin["gu"][...].astype(F32))
    red_q.both_sum()
    red_q.exchange_start()
    vecs.next(2)
    red_dn.gather_wait()
    update(3, jnp.transpose(fin["dn"][...].astype(F32)))
    red_o.gather_wait()
    update(1, fin["o"][:, 0:576].astype(F32))
    red_q.gather_start((ag_s.at[3], ag_r.at[3]))
    total = vecs.next(3)
    total = jnp.concatenate([total[t : t + 1, :] for t in range(18)], axis=1)
    pad = jnp.zeros((1, VW - 640), F32)
    flat = jnp.concatenate([total[:, 0:640], pad], axis=1)
    mid = jnp.concatenate([total[:, 640:1280], pad], axis=1)
    flat = flat + pltpu.roll(jnp.broadcast_to(mid, (8, VW)), 576, 1)[0:1, :]
    flat = flat + jnp.concatenate(
        [jnp.zeros((1, 1152), F32), total[:, 1280:2304], jnp.zeros((1, 128), F32)], axis=1)
    shift = lax.rem(VW - z * 528, VW)
    grad = pltpu.roll(jnp.broadcast_to(flat, (8, VW)), shift, 1)[0:1, 0:528]
    new = adam_step(*[v[...].reshape(1, 528) for v in vstates], grad, RATE_VECTOR, 0.0)
    for i in range(3):
        new_vectors[i][...] = new[i].reshape(528)
    red_q.gather_wait()
    update(0, fin["q"][:, 0:960].astype(F32))
    for red, first in ((red_gu, True), (red_dn, True), (red_o, True), (red_q, False)):
        red.finish(first)
    vecs.finish()
    for copy in sends:
        copy.wait_send()
    for g in range(KV_HEADS):
        for k in range(1, NZ):

            @pl.when(z >= k)
            def _(g=g, k=k):
                kv_copy(g, k, device(x, y, c, wrap(z + NZ - k, NZ))).wait_send()

    for d in range(1, NZ):

        @pl.when(z + d < NZ)
        def _(d=d):
            kv_sends[d - 1].wait_send()

    @pl.when(has_o)
    def _():
        for copy in osend + oleg:
            copy.wait_send()

    for core in range(2):

        @pl.when(c == core)
        def _(core=core):
            for copy in last_o[core]:
                copy.wait_send()

    @pl.when(c == 0)
    def _():
        for copy in qwaits + qleg + qswaps:
            copy.wait_send()


MATRICES = ((144, 960), (144, D), (144, 2 * FF), (D, 384))


def train(tok_t, cot_t, cos_t, sin_t, vstates, states):
    sd = jax.ShapeDtypeStruct
    v = pl.BlockSpec(memory_space=VM)
    a = pl.BlockSpec(memory_space=ANY)
    dma = pltpu.SemaphoreType.DMA
    scratch = dict(
        wq=VM((D, QW), BF16), vec=VM((NZ, 1, VW), F32), cos=VM((ROWS, 128), F32), sin=VM((ROWS, 128), F32),
        b_out=VM((144, OW), BF16), own=dma((2, 8)),
        q=VM((HEADS, ROWS, 128), BF16), qt=VM((HEADS, 128, ROWS), BF16), n1t=VM((D, ROWS), BF16),
        kv=VM((NZ, KV_HEADS, ROWS, 128), BF16),
        m=VM((HEADS, 1, ROWS), F32), l=VM((HEADS, 1, ROWS), F32), ot=VM((HEADS, 64, ROWS), F32),
        lse=VM((HEADS, 1, ROWS), F32), att=VM((ROWS, 640), BF16), wo=VM((D, OW), BF16),
        loc=dma((5,)), zk_s=dma((3,)), zk_r=dma((3,)), zv_s=dma((3,)), zv_r=dma((3,)),
        zq_s=dma((3,)), zq_r=dma((3,)), ck_s=dma((3,)), ck_r=dma((3,)), xq_s=dma((3, 3)), xq_r=dma((3, 3)),
        cq_s=dma((3,)), cq_r=dma((3,)), zw_s=dma((3, 3)), zw_r=dma((3, 3)),
        aw_s=dma((3, 3, 3)), aw_r=dma((3, 3, 3)), cw_s=dma((3, 3)), cw_r=dma((3, 3)),
        kv_s=dma((3,)), kv_r=dma((3,)),
        cot=VM((ROWS, D), BF16), gh=VM((ROWS, D), F32), n2=VM((ROWS, D), BF16), n2t=VM((D, ROWS), BF16),
        wgs=VM((2, D, 384), BF16), wus=VM((2, D, 384), BF16), wds=VM((2, 384, D), BF16), w_sem=dma((3, 2)),
        do=VM((HEADS, ROWS, 128), BF16), dot=VM((HEADS, 128, ROWS), BF16), delta=VM((HEADS, 1, ROWS), F32),
        gain_row=VM((1, 640), F32),
        ggu=VM((2, 4, NZ, 144, 384), BF16), gdn=VM((2, NZ, 4, 48, D), BF16), go=VM((2, 4, NZ, 144, 128), BF16),
        gq=VM((2, 4, NZ, 144, 128), BF16),
        fin=dict(gu=VM((144, 2 * FF), BF16), dn=VM((384, D), BF16), o=VM((144, QW), BF16), q=VM((144, QW), BF16)),
        own_kv=VM((KV_HEADS, ROWS, 128), F32),
        skv=VM((KV_HEADS, 3, ROWS, 128), BF16), rkv=VM((KV_HEADS, 3, ROWS, 128), BF16),
        dkv_s=dma((3, 3)), dkv_r=dma((3, 3)), ag_s=dma((4, 7)), ag_r=dma((4, 7)), st_sem=dma((3, 4)),
        red_gu=Reduction.scratch((4, 4), 144, 384), red_dn=Reduction.scratch((4, 4), 48, D),
        red_o=Reduction.scratch((4, 4), 144, 128), red_q=Reduction.scratch((4, 4), 144, 128, True),
        vecs=VectorSum.scratch(),
    )
    fast = lambda shape: VM(shape, F32)
    return pl.pallas_call(
        step_kernel,
        out_shape=(
            fast((D, ROWS)),
            fast((D, ROWS)),
            [[fast(shape) for shape in MATRICES] for _ in range(3)],
            [fast((528,)) for _ in range(3)],
            pltpu.HBM((D, OW), BF16),
            pltpu.HBM((D, 2 * FF), BF16),
            pltpu.HBM((FF, D), BF16),
        ),
        in_specs=[v, a, a, a, [v] * 3, [[a] * 4] * 3],
        out_specs=(v, v, [[v] * 4] * 3, [v] * 3, a, a, a),
        scratch_shapes=[scratch],
        compiler_params=pltpu.CompilerParams(
            collective_id=0, has_side_effects=True, vmem_limit_bytes=51 << 20),
        name="train_step",
    )(tok_t, cot_t, cos_t, sin_t, vstates, states)


def adam_step(weight, first_state, second_state, gradient, learn_rate, decay_rate):
    first_new = BETA_ONE * first_state + (1.0 - BETA_ONE) * gradient
    second_new = BETA_TWO * second_state + (1.0 - BETA_TWO) * gradient * gradient
    corr_one = 1.0 - BETA_ONE**STEP
    corr_two = 1.0 - BETA_TWO**STEP
    update = first_new / corr_one / (jnp.sqrt(second_new / corr_two) + ADAM_EPS)
    weight_new = weight - learn_rate * (update + decay_rate * weight)
    return (weight_new, first_new, second_new)


def store_kernel(sources, *rest):
    targets, sems = rest[:-1], rest[-1]
    copies = [
        pltpu.make_async_copy(a, b, sems.at[k])
        for k, (a, b) in enumerate(zip(jax.tree.leaves(sources), jax.tree.leaves(targets)))]
    for copy in copies:
        copy.start()
    for copy in copies:
        copy.wait()


def store(arrays):
    shapes = jax.tree.map(lambda t: jax.ShapeDtypeStruct(t.shape, t.dtype), arrays)
    count = len(jax.tree.leaves(arrays))
    v = pl.BlockSpec(memory_space=VM)
    a = pl.BlockSpec(memory_space=ANY)
    return pl.pallas_call(
        store_kernel,
        out_shape=shapes,
        in_specs=[jax.tree.map(lambda t: v, arrays)],
        out_specs=jax.tree.map(lambda t: a, arrays),
        scratch_shapes=[pltpu.SemaphoreType.DMA((count,))],
        compiler_params=pltpu.CompilerParams(vmem_limit_bytes=8 << 20),
        name="store",
    )(arrays)


def per_device(
    tokens, cotangent, w_qkv, w_out, w_gate_up, w_down, vectors,
    first_qkv, first_out, first_gate_up, first_down, first_vectors,
    second_qkv, second_out, second_gate_up, second_down, second_vectors,
):
    cos_np, sin_np = rope_tables()
    cos_t, sin_t = jnp.asarray(cos_np), jnp.asarray(sin_np)
    states = [
        [w_qkv, w_out, w_gate_up, w_down.T],
        [first_qkv, first_out, first_gate_up, first_down.T],
        [second_qkv, second_out, second_gate_up, second_down.T],
    ]
    vstates = [vectors, first_vectors, second_vectors]
    outs = train(
        tokens.T, cotangent.T, cos_t, sin_t, vstates, states)
    block_t, grad_t, matrices, vecs = store(tuple(outs[0:4]))
    out = [block_t.T, grad_t.T]
    for i in range(3):
        out += list(matrices[i][0:3]) + [matrices[i][3].T, vecs[i]]
    return tuple(out)


def solution(mesh):
    tokens = P(("dp", "ctx"), None)
    state = (P("ctx", None),) * 4 + (P("ctx"),)
    return jax.shard_map(
        per_device, mesh=mesh, in_specs=(tokens, tokens) + state * 3, out_specs=(tokens, tokens) + state * 3,
        check_vma=False,
    )
```

```python
import functools

import jax
import jax.numpy as jnp
import numpy as np
from jax import lax
from jax.experimental import pallas as pl
from jax.experimental.pallas import tpu as pltpu
from jax.sharding import PartitionSpec as P

D = 576
HEADS = 9
KV_HEADS = 3
GROUP = 3
HEAD_DIM = 64
FF = 1536
STEP = 10
LEN = 2048
ROWS = 512
QW = 1024
OW = 640
VW = 2304
NX = 4
NY = 4
NZ = 4

EPS = 1e-05
ROPE_BASE = 100000.0
MASK_FILL = -1e30
BETA_ONE = 0.9
BETA_TWO = 0.999
ADAM_EPS = 1e-08
RATE_MATRIX = 0.05
RATE_VECTOR = 0.5
DECAY_MATRIX = 0.1

F32 = jnp.float32
BF16 = jnp.bfloat16
MESH = pl.DeviceIdType.MESH
VM = pltpu.VMEM
ANY = pl.ANY


def rope_tables():
    half = HEAD_DIM // 2
    exponent = np.arange(half, dtype=np.float32) * np.float32(2.0 / HEAD_DIM)
    inverse = (np.float64(ROPE_BASE) ** (-exponent.astype(np.float64))).astype(np.float32)
    angles = np.arange(LEN, dtype=np.float32)[:, None] * inverse[None, :]
    cosine = np.cos(angles.astype(np.float64)).astype(np.float32)
    sine = np.sin(angles.astype(np.float64)).astype(np.float32)
    cos_all = np.concatenate([cosine] * 4, axis=1)
    sin_all = np.concatenate([-sine, sine, -sine, sine], axis=1)
    return cos_all, sin_all


def dot(a, b, ca=1, cb=0):
    return lax.dot_general(a, b, (((ca,), (cb,)), ((), ())), preferred_element_type=F32)


def place():
    dp = lax.axis_index("dp")
    z = lax.axis_index("ctx")
    x = lax.div(dp, NY * 2)
    y = lax.rem(lax.div(dp, 2), NY)
    c = lax.rem(dp, 2)
    return x, y, c, z


def device(x, y, c, z):
    return (x * (NY * 2) + y * 2 + c, z)


def wrap(i, n):
    return lax.rem(i, n)


def remote(src, dst, ssem, rsem, dev):
    return pltpu.make_async_remote_copy(
        src_ref=src, dst_ref=dst, send_sem=ssem, recv_sem=rsem, device_id=dev, device_id_type=MESH
    )


def greet(peers):
    barrier = pltpu.get_barrier_semaphore()
    for peer in peers:
        pl.semaphore_signal(barrier, inc=1, device_id=peer, device_id_type=MESH)
    pl.semaphore_wait(barrier, len(peers))


def swap_halves(v):
    width = v.shape[1]
    lane = lax.broadcasted_iota(jnp.int32, v.shape, 1)
    down = pltpu.roll(v, width - 32, 1)
    up = pltpu.roll(v, 32, 1)
    return jnp.where(lax.rem(lane, 64) < 32, down, up)


def low_lanes(v):
    lane = lax.broadcasted_iota(jnp.int32, v.shape, 1)
    return lane < 64


class Reduction:
    @staticmethod
    def scratch(lead, r, w):
        dma = pltpu.SemaphoreType.DMA
        return [
            VM(lead + (r, w), BF16), VM((3, 4, r, w), BF16), VM((4, r, w), BF16),
            VM((3, r, w), BF16), VM((4, r, w), BF16), dma((6,)), dma((10,)),
        ]

    def __init__(self, own, fin, fin_at, bufs, along_x, z_first):
        self.own, self.fin, self.fin_at, self.z_first = own, fin, fin_at, z_first
        self.rc, self.r1, self.s1, self.r2, self.r3, self.ss, self.rs = bufs
        x, y, c, z = place()
        self.c, self.z = c, z
        if along_x:
            self.a, self.b = x, y
            self.at = lambda a, b, cc, zz: device(a, b, cc, zz)
        else:
            self.a, self.b = y, x
            self.at = lambda a, b, cc, zz: device(b, a, cc, zz)
        self.other = self.at(self.a, self.b, 1 - c, z)

    def copy(self, src, dst, k, dev, into=None):
        return remote(src, dst, self.ss.at[k], self.rs.at[k if into is None else into], dev)

    def whole(self, ref, k):
        return self.copy(ref, ref, k, self.other)

    def mine(self, a, z):
        return (self.c, z, a) if self.z_first else (self.c, a, z)

    def all_z(self, a):
        return self.own.at[self.c, :, a] if self.z_first else self.own.at[self.c, a]

    def core_copy(self, k):
        return self.copy(self.own.at[1 - self.c, k], self.rc.at[k], 0, self.other, 6 + k)

    def core_add(self, k):
        self.core_copy(k).wait_recv()

        def add(j, carry):
            total = self.own[self.c, k, j].astype(F32) + self.rc[k, j].astype(F32)
            self.own[self.c, k, j] = total.astype(BF16)
            return carry

        lax.fori_loop(0, 4, add, 0)

    def core_all(self, act):
        def one(k, carry):
            act(k)
            return carry

        lax.fori_loop(0, 4, one, 0)

    def first_copy(self, d):
        to = wrap(self.a + d, 4)
        return self.copy(self.all_z(to), self.r1.at[d - 1], 1, self.at(to, self.b, self.c, self.z))

    def first_start(self):
        for d in range(1, 4):
            self.first_copy(d).start()

    def first_sum(self):
        self.whole(self.r1, 1).wait_recv()

        def add(j, carry):
            total = self.own[self.mine(self.a, j)].astype(F32) + self.r1[0, j].astype(F32)
            total = total + self.r1[1, j].astype(F32) + self.r1[2, j].astype(F32)
            self.s1[j] = total.astype(BF16)
            return carry

        lax.fori_loop(0, 4, add, 0)

    def z_start(self):
        for d in range(1, 4):
            to = wrap(self.z + d, 4)
            self.copy(self.s1.at[to], self.r2.at[d - 1], 2, self.at(self.a, self.b, self.c, to)).start()

    def z_sum(self):
        self.whole(self.r2, 2).wait_recv()
        total = self.s1[self.z].astype(F32) + self.r2[0].astype(F32)
        total = total + self.r2[1].astype(F32) + self.r2[2].astype(F32)
        self.r3[self.b] = total.astype(BF16)

    def exchange_start(self):
        for d in range(1, 4):
            to = wrap(self.b + d, 4)
            ref = self.r3.at[self.b]
            self.copy(ref, ref, 3, self.at(self.a, to, self.c, self.z)).start()

    def gather_start(self):
        self.whole(self.r3.at[0:3], 3).wait_recv()
        total = self.r3[0].astype(F32) + self.r3[1].astype(F32)
        total = total + self.r3[2].astype(F32) + self.r3[3].astype(F32)
        where = self.fin_at(self.c, self.a, 1)
        self.fin[where] = total.astype(BF16)
        ref = self.fin.at[where]
        for d in range(1, 4):
            self.copy(ref, ref, 4, self.at(wrap(self.a + d, 4), self.b, self.c, self.z)).start()

    def gather_forward(self):
        self.whole(self.fin.at[self.fin_at(0, 0, 3)], 4).wait_recv()
        ref = self.fin.at[self.fin_at(self.c, 0, 4)]
        self.copy(ref, ref, 5, self.other).start()

    def gather_wait(self):
        self.whole(self.fin.at[self.fin_at(0, 0, 4)], 5).wait_recv()

    def finish(self):
        for ref, k in (
            (self.rc, 0), (self.r1, 1), (self.r2, 2), (self.r3.at[0:3], 3),
            (self.fin.at[self.fin_at(0, 0, 3)], 4), (self.fin.at[self.fin_at(0, 0, 4)], 5),
        ):
            self.whole(ref, k).wait_send()


class VectorSum:
    SCRATCH = 4

    @staticmethod
    def scratch():
        dma = pltpu.SemaphoreType.DMA
        return [VM((2, 24, 128), F32), VM((3, 4, 24, 128), F32), dma((4,)), dma((4,))]

    def __init__(self, bufs):
        self.rc, self.r, self.ss, self.rs = bufs
        x, y, c, z = place()
        self.sibling = device(x, y, 1 - c, z)

    def copy(self, src, dst, k, dev):
        return remote(src, dst, self.ss.at[k], self.rs.at[k], dev)

    def stage(self, k):
        ref = self.rc.at[1] if k == 0 else self.r.at[k - 1, 0:3]
        return self.copy(ref, ref, k, self.sibling)

    def start(self):
        self.copy(self.rc.at[0], self.rc.at[1], 0, self.sibling).start()

    def next(self, k):
        x, y, c, z = place()
        self.stage(k).wait_recv()
        if k == 0:
            total = self.rc[0] + self.rc[1]
        else:
            total = self.r[k - 1, 0] + self.r[k - 1, 1] + self.r[k - 1, 2] + self.r[k - 1, 3]
        if k == 3:
            return total
        me = (y, z, x)[k]
        self.r[k, me] = total
        for d in range(1, 4):
            to = wrap(me + d, 4)
            dev = (device(x, to, c, z), device(x, y, c, to), device(to, y, c, z))[k]
            self.copy(self.r.at[k, me], self.r.at[k, me], k + 1, dev).start()
        return None

    def finish(self):
        for k in range(4):
            self.stage(k).wait_send()


READY = ((0, 1), (2, 3, 4), (5, 6, 7))


class TileReduction:
    @staticmethod
    def scratch():
        dma = pltpu.SemaphoreType.DMA
        return [
            VM((4, NZ, 144, 128), BF16), VM((15, 144, 128), BF16), VM((4, 144, 128), BF16),
            dma((4,)), dma((7,)),
        ]

    def __init__(self, own, fin, bufs):
        self.own, self.fin = own, fin
        self.rc, self.r1, self.r3, self.ss, self.rs = bufs
        self.x, self.y, self.c, self.z = place()

    def core_copy(self, t):
        return remote(
            self.own.at[t], self.rc.at[t // 2], self.ss.at[0], self.rs.at[t // 2],
            device(self.x, self.y, 1 - self.c, self.z))

    def whole(self, ref, k):
        return remote(
            ref, ref, self.ss.at[k], self.rs.at[3 + k], device(self.x, self.y, 1 - self.c, self.z))

    def core_start(self, tiles):
        for t in tiles:

            @pl.when(self.c != t % 2)
            def _(t=t):
                self.core_copy(t).start()

    def core_add(self, tiles):
        for t in tiles:

            @pl.when(self.c == t % 2)
            def _(t=t):
                self.core_copy(t).wait_recv()
                for j in range(NZ):
                    total = self.own[t, j].astype(F32) + self.rc[t // 2, j].astype(F32)
                    self.own[t, j] = total.astype(BF16)

    def both_copy(self, t, dz):
        to_y = t // 2
        dy = wrap(to_y + NY - self.y, NY)
        to_z = wrap(self.z + dz, NZ)
        k = jnp.maximum(dy * NZ + dz - 1, 0)
        return remote(
            self.own.at[t, to_z], self.r1.at[k], self.ss.at[1], self.rs.at[4],
            device(self.x, to_y, self.c, to_z))

    def both_each(self, tiles, act):
        for t in tiles:

            @pl.when(self.c == t % 2)
            def _(t=t):
                for dz in range(NZ):
                    if dz:
                        act(self.both_copy(t, dz))
                    else:

                        @pl.when(self.y != t // 2)
                        def _():
                            act(self.both_copy(t, 0))

    def both_start(self, tiles):
        self.both_each(tiles, lambda copy: copy.start())

    def both_sum(self):
        self.whole(self.r1, 1).wait_recv()

        def add(j, total):
            return total + self.r1[j].astype(F32)

        total = lax.fori_loop(0, 15, add, self.own[2 * self.y + self.c, self.z].astype(F32))
        self.r3[self.x] = total.astype(BF16)

    def exchange(self):
        ref = self.r3.at[self.x]
        return [
            remote(ref, ref, self.ss.at[2], self.rs.at[5],
                   device(wrap(self.x + d, NX), self.y, self.c, self.z))
            for d in range(1, NX)]

    def exchange_start(self):
        for copy in self.exchange():
            copy.start()

    def gather(self):
        cols = pl.ds(pl.multiple_of((2 * self.y + self.c) * 128, 128), 128)
        ref = self.fin.at[:, cols]
        copies = []
        for e in range(2):
            for d in range(NY):
                if e or d:
                    copies.append(
                        remote(ref, ref, self.ss.at[3], self.rs.at[6],
                               device(self.x, wrap(self.y + d, NY), wrap(self.c + e, 2), self.z)))
        return copies

    def gather_start(self):
        self.whole(self.r3.at[0:3], 2).wait_recv()
        total = self.r3[0].astype(F32) + self.r3[1].astype(F32)
        total = total + self.r3[2].astype(F32) + self.r3[3].astype(F32)
        self.fin[:, pl.ds(pl.multiple_of((2 * self.y + self.c) * 128, 128), 128)] = total.astype(BF16)
        for copy in self.gather():
            copy.start()

    def gather_wait(self):
        self.whole(self.fin.at[:, 0:896], 3).wait_recv()

    def finish(self):
        for ref, k in ((self.rc, 0), (self.r1, 1), (self.r3.at[0:3], 2), (self.fin.at[:, 0:896], 3)):
            self.whole(ref, k).wait_send()


def step_kernel(
    tok_t, cot_t, cos_hbm, sin_hbm, vstates, states,
    block_out, grad_in, new_states, new_vectors, wo_all, wgu_all, wdn_all, s,
):
    x, y, c, z = place()
    sib = device(x, y, 1 - c, z)
    zdev = [device(x, y, c, wrap(z + d, NZ)) for d in range(1, NZ)]
    xdev = [device(wrap(x + d, NX), y, c, z) for d in range(1, NX)]
    ydev = [device(x, wrap(y + d, NY), c, z) for d in range(1, NY)]
    peers = [sib] + xdev
    for dy in range(4):
        for dz in range(4):
            if dy or dz:
                peers.append(device(x, wrap(y + dy, NY), c, wrap(z + dz, NZ)))
    for d in range(1, 4):
        peers.append(device(wrap(x + d, NX), y, 1 - c, z))
        peers.append(device(x, wrap(y + d, NY), 1 - c, z))
    barrier = pltpu.get_barrier_semaphore()
    for peer in peers:
        pl.semaphore_signal(barrier, inc=1, device_id=peer, device_id_type=MESH)
    wq_v, vec_v, q_s, qt_s, kvs = s["wq"], s["vec"], s["q"], s["qt"], s["kv"]
    b_out, b_gu, b_dn, n1t = s["b_out"], s["ggu"].at[0, 0:2], s["gdn"].at[0, 0:2], s["n1t"]
    m_s, l_s, ot_s, lse, att = s["m"], s["l"], s["ot"], s["lse"], s["att"]
    loc_sem = s["loc"]
    row0 = pl.multiple_of(z * ROWS, ROWS)
    loads = [
        pltpu.make_async_copy(cos_hbm.at[pl.ds(row0, ROWS)], s["cos"], loc_sem.at[0]),
        pltpu.make_async_copy(sin_hbm.at[pl.ds(row0, ROWS)], s["sin"], loc_sem.at[1]),
        pltpu.make_async_copy(cot_t, s["n2t"], loc_sem.at[2]),
    ]
    masters = new_states[0]
    master_loads = [
        pltpu.make_async_copy(states[0][k], masters[k], s["st_sem"].at[0, k]) for k in range(4)]
    for load in master_loads + loads:
        load.start()
    vec_v[0] = jnp.zeros((1, VW), F32)
    vec_v[0, :, 0:528] = vstates[0][...].reshape(1, 528)
    rolled = pltpu.roll(jnp.broadcast_to(vec_v[0], (8, VW)), z * 528, 1)
    vec_v[0] = rolled[0:1, :]
    qrows = pl.ds(pl.multiple_of(z * 144, 144), 144)
    master_loads[0].wait()
    wq_v[qrows, 0:896] = masters[0][:, 0:896].astype(BF16)
    wq_v[qrows, 896:1024] = jnp.concatenate(
        [masters[0][:, 896:960].astype(BF16), jnp.zeros((144, 64), BF16)], axis=1
    )
    pl.semaphore_wait(barrier, len(peers))

    sent = []

    def group(copies, name, shape):
        whole = remote(shape, shape, s["ss"].at[name], s["rs"].at[name], sib)
        return copies, whole

    def pair_of(name):
        return s["ss"].at[name], s["rs"].at[name]

    def begin(batch):
        for copy in batch[0]:
            copy.start()
        sent.append(batch[1])

    kcols = pl.ds(pl.multiple_of(512 + c * 256, 256), 256)
    xcols = pl.ds(pl.multiple_of(x * 128, 128), 128)
    ref_k, ref_q = wq_v.at[qrows, kcols], wq_v.at[qrows, xcols]
    k_over_z = group([remote(ref_k, ref_k, *pair_of(0), dev) for dev in zdev], 0, wq_v.at[0:432, 0:256])
    v_over_z = group(
        [remote(vec_v.at[0], vec_v.at[d], *pair_of(1), zdev[d - 1]) for d in range(1, NZ)], 1, vec_v.at[1:4])
    q_over_z = group([remote(ref_q, ref_q, *pair_of(2), dev) for dev in zdev], 2, wq_v.at[0:432, 0:128])
    begin(k_over_z)
    begin(v_over_z)

    @pl.when(c == 0)
    def _():
        for copy in q_over_z[0]:
            copy.start()

    def block_rows(e, n):
        return pl.ds(pl.multiple_of(wrap(z + NZ - e, NZ) * n, n), n)

    inputs = jnp.transpose(tok_t[...].astype(F32))
    unit = inputs * lax.rsqrt(jnp.mean(inputs * inputs, axis=-1, keepdims=True) + EPS)

    master_loads[1].wait()
    b_out[:, 0:512] = masters[1][:, 0:512].astype(BF16)
    b_out[:, 512:640] = jnp.concatenate(
        [masters[1][:, 512:576].astype(BF16), jnp.zeros((144, 64), BF16)], axis=1)
    own = [pltpu.make_async_copy(b_out, wo_all.at[qrows, :], loc_sem.at[3])]
    master_loads[2].wait()
    master_loads[3].wait()
    down = jnp.transpose(masters[3][...]).astype(BF16)
    zrows = pl.ds(pl.multiple_of(z * 384, 384), 384)
    for p in range(8):
        b_gu[p // 4, p % 4] = masters[2][:, 384 * p : 384 * p + 384].astype(BF16)
        b_dn[p // 4, p % 4] = down[48 * p : 48 * p + 48, :]
        own.append(
            pltpu.make_async_copy(
                b_gu.at[p // 4, p % 4], wgu_all.at[qrows, 384 * p : 384 * p + 384], loc_sem.at[5]))
        own.append(
            pltpu.make_async_copy(
                b_dn.at[p // 4, p % 4], wdn_all.at[pl.ds(pl.multiple_of(z * 384 + 48 * p, 48), 48), :],
                loc_sem.at[6]))
    own_done = [
        own[0],
        pltpu.make_async_copy(wgu_all.at[qrows, :], wgu_all.at[qrows, :], loc_sem.at[5]),
        pltpu.make_async_copy(wdn_all.at[zrows, :], wdn_all.at[zrows, :], loc_sem.at[6]),
    ]
    for copy in own:
        copy.start()

    pgu = pl.multiple_of((c * 4 + x) * 384, 128)
    pdn = (c * 4 + y) * 48
    po = jnp.minimum(c * 4 + y, 4)
    has_o = c * 4 + y < 5
    oc = pl.multiple_of(po * 128, 128)

    def down_rows(zz):
        return wdn_all.at[pl.ds(pl.multiple_of(zz * 384 + pdn, 48), 48), :]

    o_over_z = group(
        [remote(b_out.at[:, pl.ds(oc, 128)], wo_all.at[qrows, pl.ds(oc, 128)], *pair_of(3), dev) for dev in zdev],
        3, wo_all.at[0:432, 0:128])
    gu_over_z = group(
        [remote(b_gu.at[c, x], wgu_all.at[qrows, pl.ds(pgu, 384)], *pair_of(4), dev) for dev in zdev],
        4, wgu_all.at[0:432, 0:384])
    dn_over_z = group(
        [remote(b_dn.at[c, y], down_rows(z), *pair_of(5), dev) for dev in zdev], 5, wdn_all.at[0:144, :])

    def weights_over_z():
        @pl.when(has_o)
        def _():
            for copy in o_over_z[0]:
                copy.start()

        for copy in dn_over_z[0] + gu_over_z[0]:
            copy.start()

    weights_over_z()
    k_over_z[1].wait_recv()
    v_over_z[1].wait_recv()
    others = range(1, NZ)
    k_over_c = group(
        [remote(wq_v.at[block_rows(e, 144), kcols], wq_v.at[block_rows(e, 144), kcols], *pair_of(6), sib)
         for e in others], 6, wq_v.at[0:432, 0:256])
    begin(k_over_c)

    q_over_x = group(
        [remote(wq_v.at[block_rows(e, 144), xcols], wq_v.at[block_rows(e, 144), xcols], *pair_of(7), dev)
         for e in others for dev in xdev], 7, wq_v.at[0:432, 0:384])
    q_over_c = group(
        [remote(wq_v.at[block_rows(e, 144), 0:512], wq_v.at[block_rows(e, 144), 0:512], *pair_of(8), sib)
         for e in others], 8, wq_v.at[0:432, 0:512])

    @pl.when(c == 0)
    def _():
        q_over_z[1].wait_recv()
        for copy in q_over_x[0]:
            copy.start()

    raw = vec_v[0] + vec_v[1] + vec_v[2] + vec_v[3]
    raw = raw.astype(BF16).astype(F32)
    wide = jnp.broadcast_to(raw, (8, VW))
    gain_one = raw[:, 0:576]
    gain_two = pltpu.roll(wide, VW - 576, 1)[0:1, 0:576]
    bias = raw[:, 1152:2176]
    normed = unit * gain_one
    n1 = normed.astype(BF16)
    n1t[...] = jnp.transpose(normed).astype(BF16)
    for load in loads:
        load.wait()
    cosine, sine = s["cos"][...], s["sin"][...]

    k_over_c[1].wait_recv()

    def tile_of(v, t):
        return v[:, 128 * t : 128 * t + 128]

    def rotated(v):
        return v * cosine + swap_halves(v) * sine

    def turn(v):
        return pltpu.roll(v, 64, 1)

    proj = dot(n1, wq_v[:, 512:1024]) + bias[:, 512:1024]
    rot4, rot5 = rotated(tile_of(proj, 0)), rotated(tile_of(proj, 1))
    val6, val7 = tile_of(proj, 2), tile_of(proj, 3)
    low = low_lanes(rot4)
    kvs[z, 0] = jnp.where(low, turn(rot4), turn(val6)).astype(BF16)
    kvs[z, 1] = jnp.where(low, rot5, val6).astype(BF16)
    kvs[z, 2] = jnp.where(low, turn(rot5), turn(val7)).astype(BF16)
    kv_sends = []
    for d in range(1, NZ):
        kv_sends.append(
            remote(kvs.at[z], kvs.at[z], s["kv_s"].at[d - 1], s["kv_r"].at[d - 1],
                   device(x, y, c, wrap(z + d, NZ))))

        @pl.when(z + d < NZ)
        def _(d=d):
            kv_sends[d - 1].start()

    def put_query(h, part):
        qh = jnp.where(low, part, 0.0) * (HEAD_DIM ** -0.5)
        q_s[h] = qh.astype(BF16)
        qt_s[h] = jnp.transpose(qh).astype(BF16)

    put_query(8, rot4)

    @pl.when(c == 0)
    def _():
        q_over_x[1].wait_recv()
        for copy in q_over_c[0]:
            copy.start()

    @pl.when(c == 1)
    def _():
        q_over_c[1].wait_recv()

    proj = dot(n1, wq_v[:, 0:512]) + bias[:, 0:512]
    for t in range(4):
        rot = rotated(tile_of(proj, t))
        put_query(2 * t, rot)
        put_query(2 * t + 1, turn(rot))

    def step(j):
        kvt = [jnp.transpose(kvs[j, g].astype(F32)).astype(BF16)[64:128, :] for g in range(KV_HEADS)]
        heads = range(HEADS)
        sts = [dot(kvs[j, h // GROUP], qt_s[h]) for h in heads]
        olds = [m_s[h] for h in heads]
        peaks = [jnp.maximum(jnp.max(v, axis=0, keepdims=True), o) for v, o in zip(sts, olds)]
        alphas = [jnp.exp(o - p) for o, p in zip(olds, peaks)]
        ps = [jnp.exp(v - p) for v, p in zip(sts, peaks)]
        totals = [jnp.sum(p, axis=0, keepdims=True) + l_s[h] * a for h, p, a in zip(heads, ps, alphas)]
        outs = [dot(kvt[h // GROUP], p.astype(BF16)) + ot_s[h] * a for h, p, a in zip(heads, ps, alphas)]
        for h in heads:
            m_s[h] = peaks[h]
            l_s[h] = totals[h]
            ot_s[h] = outs[h]

    def visible(width):
        shape = (256, width)
        return lax.broadcasted_iota(jnp.int32, shape, 0) <= lax.broadcasted_iota(jnp.int32, shape, 1)

    right = slice(256, 512)
    always = z >= 0

    @pl.when(always)
    def _():
        keep_a, keep_b = visible(512), visible(256)
        kvt = [jnp.transpose(kvs[z, g].astype(F32)).astype(BF16)[64:128, :] for g in range(KV_HEADS)]
        heads = range(HEADS)
        st_a = [jnp.where(keep_a, dot(kvs[z, h // GROUP, 0:256], qt_s[h]), MASK_FILL) for h in heads]
        st_b = [jnp.where(keep_b, dot(kvs[z, h // GROUP, right], qt_s[h, :, right]), MASK_FILL) for h in heads]
        none = jnp.full((1, 256), MASK_FILL, F32)
        zero = jnp.zeros((1, 256), F32)
        zeros = jnp.zeros((64, 256), F32)
        peaks = [
            jnp.maximum(
                jnp.max(a, axis=0, keepdims=True),
                jnp.concatenate([none, jnp.max(b, axis=0, keepdims=True)], axis=1))
            for a, b in zip(st_a, st_b)]
        p_a = [jnp.exp(a - p) for a, p in zip(st_a, peaks)]
        p_b = [jnp.exp(b - p[:, right]) for b, p in zip(st_b, peaks)]
        totals = [
            jnp.sum(a, axis=0, keepdims=True) + jnp.concatenate([zero, jnp.sum(b, axis=0, keepdims=True)], axis=1)
            for a, b in zip(p_a, p_b)]
        outs = [
            dot(kvt[h // GROUP][:, 0:256], p_a[h].astype(BF16))
            + jnp.concatenate([zeros, dot(kvt[h // GROUP][:, right], p_b[h].astype(BF16))], axis=1)
            for h in heads]
        for h in heads:
            m_s[h] = peaks[h]
            l_s[h] = totals[h]
            ot_s[h] = outs[h]

    gu_over_z[1].wait_recv()
    dn_over_z[1].wait_recv()

    @pl.when(has_o)
    def _():
        o_over_z[1].wait_recv()

    def gu_piece(e, xx):
        return wgu_all.at[block_rows(e, 144), pl.ds(pl.multiple_of((c * 4 + xx) * 384, 128), 384)]

    def o_piece(e):
        return wo_all.at[block_rows(e, 144), pl.ds(oc, 128)]

    def dn_half(e):
        return wdn_all.at[
            pl.ds(pl.multiple_of(wrap(z + NZ - e, NZ) * 384 + c * 192, 192), 192), :]

    def dn_piece(e):
        return down_rows(wrap(z + NZ - e, NZ))

    gu_over_x = group(
        [remote(gu_piece(e, x), gu_piece(e, x), *pair_of(9), dev) for e in others for dev in xdev],
        9, wgu_all.at[0:432, 0:1152])
    dn_over_y = group(
        [remote(dn_piece(e), dn_piece(e), *pair_of(10), dev) for e in others for dev in ydev],
        10, wdn_all.at[0:432, :])
    o_over_y = [
        [remote(o_piece(e), o_piece(e), s["ss"].at[11], s["os"].at[d - 1], ydev[d - 1]) for e in others]
        for d in range(1, NY)]
    o_sent = remote(wo_all.at[0:432, 0:384], wo_all.at[0:432, 0:384], s["ss"].at[11], s["os"].at[0], sib)
    own_over_c = group(
        [remote(gu_piece(e, x), gu_piece(e, x), *pair_of(12), sib) for e in others], 12, wgu_all.at[0:432, 0:384])
    gu_over_c = group(
        [remote(gu_piece(e, wrap(x + d, NX)), gu_piece(e, wrap(x + d, NX)), *pair_of(13), sib)
         for e in others for d in range(1, NX)], 13, wgu_all.at[0:432, 0:1152])
    dn_over_c = group(
        [remote(dn_half(e), dn_half(e), *pair_of(14), sib) for e in others], 14, wdn_all.at[0:576, :])
    o_over_c = []
    for core, cols in enumerate((slice(0, 512), slice(512, 640))):
        o_over_c.append(
            group(
                [remote(wo_all.at[block_rows(e, 144), cols], wo_all.at[block_rows(e, 144), cols], *pair_of(15), sib)
                 for e in others], 15, wo_all.at[0:432, cols]))

    @pl.when(has_o)
    def _():
        for copies in o_over_y:
            for copy in copies:
                copy.start()

    begin(dn_over_y)
    begin(gu_over_x)
    begin(own_over_c)

    for d in range(1, NZ):
        if d == NZ - 1:
            for dd in range(1, NY):
                from_y = wrap(y + NY - dd, NY)

                @pl.when(c * 4 + from_y < 5)
                def _(dd=dd):
                    remote(wo_all.at[0:432, 0:128], wo_all.at[0:432, 0:128], s["ss"].at[11], s["os"].at[dd - 1],
                           sib).wait_recv()

            for core in range(2):

                @pl.when(c == core)
                def _(core=core):
                    for copy in o_over_c[core][0]:
                        copy.start()

            dn_over_y[1].wait_recv()
            begin(dn_over_c)

        @pl.when(z >= d)
        def _(d=d):
            kv_sends[d - 1].wait_recv()
            step(z - d)

    for h in range(HEADS):
        ot_s[h] = ot_s[h] * (1.0 / l_s[h])
        lse[h] = m_s[h] + jnp.log(l_s[h])
    for t in range(5):
        top = ot_s[2 * t]
        bottom = ot_s[2 * t + 1] if 2 * t + 1 < HEADS else jnp.zeros((64, ROWS), F32)
        att[:, 128 * t : 128 * t + 128] = jnp.transpose(jnp.concatenate([top, bottom], axis=0)).astype(BF16)

    for core in range(2):

        @pl.when(c == core)
        def _(core=core):
            o_over_c[1 - core][1].wait_recv()

    for copy in own_done:
        copy.wait()
    wo = s["wo"]
    load_o = pltpu.make_async_copy(wo_all, wo, loc_sem.at[4])
    load_o.start()
    wgu, wds, w_sem = s["wgu"], s["wds"], s["w_sem"]

    def weights(i, slot):
        col = pl.multiple_of(wrap(x + i, 4) * 384, 384)
        return [
            pltpu.make_async_copy(
                wgu_all.at[:, pl.ds(col, 384)], wgu.at[slot, :, 0:384], w_sem.at[0, slot]),
            pltpu.make_async_copy(
                wgu_all.at[:, pl.ds(pl.multiple_of(col + FF, 384), 384)], wgu.at[slot, :, 384:768],
                w_sem.at[0, slot]),
            pltpu.make_async_copy(wdn_all.at[pl.ds(col, 384), :], wds.at[slot], w_sem.at[1, slot]),
        ]

    def weights_wait(slot):
        pltpu.make_async_copy(wgu_all.at[:, 0:768], wgu.at[slot], w_sem.at[0, slot]).wait()
        pltpu.make_async_copy(wdn_all.at[0:384, :], wds.at[slot], w_sem.at[1, slot]).wait()

    ggu, gdn, go, gq, fin = s["ggu"], s["gdn"], s["go"], s["gq"], s["fin"]
    def columns(width):
        def at(cc, a, count):
            return (slice(None), pl.ds(pl.multiple_of((cc * 4 + a) * width, 128), count * width))

        return at

    def down_at(cc, a, count):
        return (pl.ds(pl.multiple_of((cc * 4 + a) * 48, 48), count * 48), slice(None))

    red_gu = Reduction(ggu, fin["gu"], columns(384), s["red_gu"], True, False)
    red_dn = Reduction(gdn, fin["dn"], down_at, s["red_dn"], False, True)
    red_o = Reduction(go, fin["o"], columns(128), s["red_o"], False, False)
    red_q = TileReduction(gq, fin["q"], s["red_q"])
    vecs = VectorSum(s["vecs"])
    cot, gh, n2, n2t, gn2t = s["cot"], s["gh"], s["n2"], s["n2t"], grad_in
    do_in, dot_in, delta_in, gain_row = s["do"], s["dot"], s["delta"], s["gain_row"]
    dqt, own_kv, skv, rkv = ot_s, s["own_kv"], s["skv"], s["rkv"]

    s["cot"][...] = jnp.transpose(s["n2t"][...].astype(F32)).astype(BF16)
    gn2t[...] = jnp.zeros_like(gn2t)
    inputs = jnp.transpose(tok_t[...].astype(F32))
    load_o.wait()
    hid = inputs + dot(att[:, 0:576], wo[:, 0:576])
    inv_two = lax.rsqrt(jnp.mean(hid * hid, axis=-1, keepdims=True) + EPS)
    normed = hid * inv_two * gain_two
    n2[...] = normed.astype(BF16)
    n2t[...] = jnp.transpose(normed).astype(BF16)
    gh[...] = hid
    block_out[...] = jnp.transpose(hid)

    gu_over_z[1].wait_send()
    dn_over_z[1].wait_send()
    dn_over_c[1].wait_recv()
    own_over_c[1].wait_recv()
    for load in weights(0, 0):
        load.start()
    gu_over_x[1].wait_recv()
    begin(gu_over_c)

    def chunk(i, carry):
        slot = lax.rem(i, 2)
        here = wrap(x + i, 4)
        weights_wait(slot)

        @pl.when(jnp.logical_and(i > 0, i < 3))
        def _():
            for load in weights(i + 1, 1 - slot):
                load.start()

        both = dot(n2[...], wgu[slot])
        gate, up = both[:, 0:384], both[:, 384:768]
        sg = jax.nn.sigmoid(gate)
        silu = gate * sg
        act = (silu * up).astype(BF16)
        ga = dot(cot[...], wds[slot], 1, 1)
        gg = (ga * up * sg * (1.0 + gate * (1.0 - sg))).astype(BF16)
        gu = (ga * silu).astype(BF16)
        grads = jnp.concatenate([gg, gu], axis=1)
        both = dot(n2t[...], grads).astype(BF16)
        ggu[0, here] = both[:, 0:384].reshape(NZ, 144, 384)
        ggu[1, here] = both[:, 384:768].reshape(NZ, 144, 384)
        red_gu.core_copy(here).start()
        down = dot(act, cot[...], 0, 0).astype(BF16)
        for p in range(8):
            gdn[p // 4, here, p % 4] = down[48 * p : 48 * p + 48, :]
        red_dn.core_copy(here).start()

        @pl.when(i == 0)
        def _():
            gu_over_c[1].wait_recv()
            for load in weights(1, 1):
                load.start()

        @pl.when(i > 0)
        def _():
            red_gu.core_add(wrap(x + i + 3, 4))

        @pl.when(i > 1)
        def _():
            red_gu.first_copy(i - 1).start()

        block_out[...] += lax.dot_general(wds[slot], act, (((0,), (1,)), ((), ())), preferred_element_type=F32)
        gn2t[...] += dot(wgu[slot], grads, 1, 1)

        return carry

    lax.fori_loop(0, 4, chunk, 0)

    red_dn.core_all(red_dn.core_add)
    red_dn.first_start()
    red_gu.core_add(wrap(x + 3, 4))
    red_gu.first_copy(3).start()
    state_loads = []
    for i in range(1, 3):
        for k in range(4):
            copy = pltpu.make_async_copy(states[i][k], new_states[i][k], s["st_sem"].at[i, k])
            copy.start()
            state_loads.append(copy)

    @pl.when(always)
    def _():
        hid = gh[...]
        inv_two = lax.rsqrt(jnp.mean(hid * hid, axis=-1, keepdims=True) + EPS)
        u = hid * inv_two
        e = jnp.transpose(gn2t[...])
        f = e * gain_two
        gain_row[:, 0:576] = jnp.sum(e * u, axis=0, keepdims=True)
        gain_row[:, 576:640] = jnp.zeros((1, 64), F32)
        grad_hidden = cot[...].astype(F32) + inv_two * (f - u * jnp.mean(f * u, axis=-1, keepdims=True))
        gh[...] = grad_hidden
        ghl = grad_hidden.astype(BF16)
        grad_out = dot(att[:, 0:576], ghl, 0, 0).astype(BF16)
        for p in range(8):
            if p < 4:
                part = grad_out[:, 128 * p : 128 * p + 128]
            elif p == 4:
                part = jnp.concatenate([grad_out[:, 512:576], jnp.zeros((D, 64), BF16)], axis=1)
            else:
                part = jnp.zeros((D, 128), BF16)
            go[p // 4, p % 4] = part.reshape(NZ, 144, 128)
        red_o.core_all(lambda k: red_o.core_copy(k).start())
        gm = dot(ghl, wo[:, 0:576], 1, 1).astype(BF16).astype(F32)
        gm = jnp.concatenate([gm, jnp.zeros((ROWS, 64), F32)], axis=1)
        for h in range(HEADS):
            part = gm[:, 128 * (h // 2) : 128 * (h // 2) + 128]
            part = part if h % 2 == 1 else turn(part)
            part = jnp.where(low_lanes(part), 0.0, part)
            do_in[h] = part.astype(BF16)
            part = jnp.transpose(part)
            dot_in[h] = part.astype(BF16)
            delta_in[h] = jnp.sum(part[64:128, :] * ot_s[h], axis=0, keepdims=True)

    def attend(g, j):
        kv = kvs[j, g]
        kt = jnp.transpose(kv.astype(F32)).astype(BF16)[0:64, :]
        hs = [g * GROUP + k for k in range(GROUP)]
        sts = [dot(kv, qt_s[h]) for h in hs]
        dpts = [dot(kv, dot_in[h]) for h in hs]
        pts = [jnp.exp(v - lse[h]) for v, h in zip(sts, hs)]
        dsts = [(p * (d - delta_in[h])).astype(BF16) for p, d, h in zip(pts, dpts, hs)]
        both = [dot(d, q_s[h]) + dot(p.astype(BF16), do_in[h]) for p, d, h in zip(pts, dsts, hs)]
        dqs = [dot(kt, d) for d in dsts]
        for h, dq in zip(hs, dqs):
            dqt[h] += dq
        return both[0] + both[1] + both[2]

    def attend_own(g):
        keep_a, keep_b = visible(512), visible(256)
        kv_a, kv_b = kvs[z, g, 0:256], kvs[z, g, 256:512]
        kt = jnp.transpose(kvs[z, g].astype(F32)).astype(BF16)[0:64, :]
        zeros = jnp.zeros((64, 256), F32)
        hs = [g * GROUP + k for k in range(GROUP)]
        pt_a = [jnp.where(keep_a, jnp.exp(dot(kv_a, qt_s[h]) - lse[h]), 0.0) for h in hs]
        pt_b = [jnp.where(keep_b, jnp.exp(dot(kv_b, qt_s[h, :, right]) - lse[h, :, right]), 0.0) for h in hs]
        ds_a = [(p * (dot(kv_a, dot_in[h]) - delta_in[h])).astype(BF16) for p, h in zip(pt_a, hs)]
        ds_b = [
            (p * (dot(kv_b, dot_in[h, :, right]) - delta_in[h, :, right])).astype(BF16) for p, h in zip(pt_b, hs)]
        all_a = [dot(d, q_s[h]) + dot(p.astype(BF16), do_in[h]) for p, d, h in zip(pt_a, ds_a, hs)]
        all_b = [dot(d, q_s[h, right]) + dot(p.astype(BF16), do_in[h, right]) for p, d, h in zip(pt_b, ds_b, hs)]
        dqs = [
            dot(kt[:, 0:256], a) + jnp.concatenate([zeros, dot(kt[:, right], b)], axis=1)
            for a, b in zip(ds_a, ds_b)]
        for h, dq in zip(hs, dqs):
            dqt[h] += dq
        own_kv[g, 0:256] = all_a[0] + all_a[1] + all_a[2]
        own_kv[g, 256:512] = all_b[0] + all_b[1] + all_b[2]

    def kv_copy(g, k, dev):
        return remote(
            skv.at[g, k - 1], rkv.at[g, k - 1], s["ss"].at[16], s["dkv_r"].at[g], dev)

    def far(g, k):
        @pl.when(z >= k)
        def _():
            skv[g, k - 1] = attend(g, z - k).astype(BF16)
            kv_copy(g, k, device(x, y, c, z - k)).start()

    def own_block(g):
        pl.when(always)(functools.partial(attend_own, g))

    gps = q_s

    def kv_wait(g):
        for count in range(1, NZ):

            @pl.when(z + count == NZ - 1)
            def _(count=count):
                part = rkv.at[g, 0:count]
                remote(part, part, s["ss"].at[16], s["dkv_r"].at[g], sib).wait_recv()
                total = own_kv[g]
                for k in range(count):
                    total = total + rkv[g, k].astype(F32)
                own_kv[g] = total

    def group_tiles(g):
        cos_t, sin_t = s["cos"][...], s["sin"][...]
        low = low_lanes(cos_t)
        kv = own_kv[g]

        def query(top, bottom):
            both = [dqt[h] if h is not None else jnp.zeros((64, ROWS), F32) for h in (top, bottom)]
            return jnp.transpose(jnp.concatenate(both, axis=0)) * (HEAD_DIM ** -0.5)

        def back(t):
            return t * cos_t - swap_halves(t) * sin_t

        if g == 0:
            return {
                0: back(query(0, 1)),
                1: back(jnp.where(low, query(2, None), turn(kv))),
                2: jnp.where(low, turn(kv), 0.0),
            }
        if g == 1:
            return {
                2: jnp.where(low, 0.0, back(query(None, 3))),
                3: back(query(4, 5)),
                4: jnp.where(low, back(kv), kv),
            }
        return {
            5: back(query(6, 7)),
            6: back(jnp.where(low, query(8, None), turn(kv))),
            7: jnp.where(low, turn(kv), 0.0),
        }

    def tiles_of(g):
        @pl.when(always)
        def _():
            for t, tile in group_tiles(g).items():
                if t == 2 and g == 0:
                    gps[2] = tile.astype(BF16)
                    continue
                if t == 2:
                    tile = tile + gps[2].astype(F32)
                low_tile = tile.astype(BF16)
                gps[t] = low_tile
                gq[t] = dot(n1t[...], low_tile).astype(BF16).reshape(NZ, 144, 128)

        red_q.core_start((READY[g]))

    dqt[...] = jnp.zeros_like(dqt)
    far(0, 3)
    red_o.core_all(red_o.core_add)
    far(0, 2)
    far(0, 1)
    own_block(0)
    far(1, 3)
    red_dn.first_sum()
    red_dn.z_start()
    red_o.first_start()
    far(1, 2)
    kv_wait(0)
    tiles_of(0)
    far(1, 1)
    red_q.core_add(READY[0])
    red_q.both_start(READY[0])
    red_gu.first_sum()
    red_gu.z_start()
    own_block(1)
    red_dn.z_sum()
    red_dn.exchange_start()
    far(2, 3)
    red_o.first_sum()
    red_o.z_start()
    far(2, 2)
    kv_wait(1)
    tiles_of(1)
    red_dn.gather_start()
    far(2, 1)
    red_q.core_add(READY[1])
    red_q.both_start(READY[1])
    red_gu.z_sum()
    red_gu.exchange_start()
    own_block(2)
    red_o.z_sum()
    red_o.exchange_start()
    red_dn.gather_forward()
    kv_wait(2)
    tiles_of(2)
    low = low_lanes(s["cos"][...])

    def halves(t):
        tile = gps[t].astype(F32)
        return tile, turn(tile)

    (t0, _), (t1, u1), (t2, u2), (t3, u3) = [halves(t) for t in range(4)]
    (t4, u4), (t5, _), (t6, u6), (t7, _) = [halves(t) for t in range(4, 8)]
    ordered = [
        t0,
        jnp.where(low, t1, t2),
        t3,
        t5,
        jnp.where(low, t6, t1),
        jnp.where(low, t4, t6),
        jnp.where(low, t2, t4),
        t7,
    ]
    vecs.rc[0, 10:18, :] = jnp.concatenate(
        [jnp.sum(t, axis=0, keepdims=True) for t in ordered], axis=0)
    gn1 = dot(jnp.concatenate([t.astype(BF16) for t in ordered], axis=1), wq_v[...], 1, 1)
    inputs = jnp.transpose(tok_t[...].astype(F32))
    r = lax.rsqrt(jnp.mean(inputs * inputs, axis=-1, keepdims=True) + EPS)
    u = inputs * r
    f = gn1 * gain_one
    row = jnp.sum(gn1 * u, axis=0, keepdims=True)
    row = jnp.concatenate([row, jnp.zeros((1, 64), F32)], axis=1)
    for t in range(5):
        vecs.rc[0, t : t + 1, :] = row[:, 128 * t : 128 * t + 128]
        vecs.rc[0, 5 + t : 6 + t, :] = gain_row[:, 128 * t : 128 * t + 128]
    vecs.rc[0, 18:24, :] = jnp.zeros((6, 128), F32)
    vecs.start()
    red_q.core_add(READY[2])
    red_q.both_start(READY[2])
    vecs.next(0)
    early = 2 * y + c <= 4
    late = 2 * y + c > 4

    @pl.when(early)
    def _():
        red_q.both_sum()
        red_q.exchange_start()

    red_gu.gather_start()
    grad_in[...] = jnp.transpose(gh[...] + r * (f - u * jnp.mean(f * u, axis=-1, keepdims=True)))

    def update(k, grad):
        new = adam_step(
            new_states[0][k][...], new_states[1][k][...], new_states[2][k][...], grad, RATE_MATRIX, DECAY_MATRIX)
        for i in range(3):
            new_states[i][k][...] = new[i]

    for load in state_loads:
        load.wait()
    red_dn.gather_wait()
    update(3, jnp.transpose(fin["dn"][...].astype(F32)))
    red_o.gather_start()

    @pl.when(late)
    def _():
        red_q.both_sum()
        red_q.exchange_start()

    vecs.next(1)

    @pl.when(early)
    def _():
        red_q.gather_start()

    red_o.gather_forward()
    red_gu.gather_forward()
    @pl.when(late)
    def _():
        red_q.gather_start()

    vecs.next(2)
    red_o.gather_wait()
    update(1, fin["o"][:, 0:576].astype(F32))
    red_gu.gather_wait()
    update(2, fin["gu"][...].astype(F32))
    total = vecs.next(3)
    total = jnp.concatenate([total[t : t + 1, :] for t in range(18)], axis=1)
    pad = jnp.zeros((1, VW - 640), F32)
    flat = jnp.concatenate([total[:, 0:640], pad], axis=1)
    mid = jnp.concatenate([total[:, 640:1280], pad], axis=1)
    flat = flat + pltpu.roll(jnp.broadcast_to(mid, (8, VW)), 576, 1)[0:1, :]
    flat = flat + jnp.concatenate(
        [jnp.zeros((1, 1152), F32), total[:, 1280:2304], jnp.zeros((1, 128), F32)], axis=1)
    shift = lax.rem(VW - z * 528, VW)
    grad = pltpu.roll(jnp.broadcast_to(flat, (8, VW)), shift, 1)[0:1, 0:528]
    new = adam_step(*[v[...].reshape(1, 528) for v in vstates], grad, RATE_VECTOR, 0.0)
    for i in range(3):
        new_vectors[i][...] = new[i].reshape(528)
    red_q.gather_wait()
    tq = [fin["q"][:, 128 * t : 128 * t + 128].astype(F32) for t in range(8)]
    lowq = low_lanes(tq[0])
    ordered = [
        tq[0],
        jnp.where(lowq, tq[1], tq[2]),
        tq[3],
        tq[5],
        jnp.where(lowq, tq[6], tq[1]),
        jnp.where(lowq, tq[4], tq[6]),
        jnp.where(lowq, tq[2], tq[4]),
        tq[7],
    ]
    update(0, jnp.concatenate(ordered, axis=1)[:, 0:960])
    for red in (red_gu, red_dn, red_o):
        red.finish()
    red_q.finish()
    vecs.finish()
    for whole in sent:
        whole.wait_send()
    for count in range(1, NZ):

        @pl.when(z == count)
        def _(count=count):
            part = (skv.at[0], skv.at[0:2], skv)[count - 1]
            remote(part, part, s["ss"].at[16], s["dkv_r"].at[0], sib).wait_send()

    for d in range(1, NZ):

        @pl.when(z + d < NZ)
        def _(d=d):
            kv_sends[d - 1].wait_send()

    @pl.when(has_o)
    def _():
        o_over_z[1].wait_send()
        o_sent.wait_send()

    for core in range(2):

        @pl.when(c == core)
        def _(core=core):
            o_over_c[core][1].wait_send()

    @pl.when(c == 0)
    def _():
        for batch in (q_over_z, q_over_x, q_over_c):
            batch[1].wait_send()


MATRICES = ((144, 960), (144, D), (144, 2 * FF), (D, 384))


def train(tok_t, cot_t, cos_t, sin_t, vstates, states):
    sd = jax.ShapeDtypeStruct
    v = pl.BlockSpec(memory_space=VM)
    a = pl.BlockSpec(memory_space=ANY)
    dma = pltpu.SemaphoreType.DMA
    scratch = dict(
        wq=VM((D, QW), BF16), vec=VM((NZ, 1, VW), F32), cos=VM((ROWS, 128), F32), sin=VM((ROWS, 128), F32),
        b_out=VM((144, OW), BF16),
        q=VM((HEADS, ROWS, 128), BF16), qt=VM((HEADS, 128, ROWS), BF16), n1t=VM((D, ROWS), BF16),
        kv=VM((NZ, KV_HEADS, ROWS, 128), BF16),
        m=VM((HEADS, 1, ROWS), F32), l=VM((HEADS, 1, ROWS), F32), ot=VM((HEADS, 64, ROWS), F32),
        lse=VM((HEADS, 1, ROWS), F32), att=VM((ROWS, 640), BF16), wo=VM((D, OW), BF16),
        loc=dma((7,)), ss=dma((17,)), rs=dma((16,)), os=dma((3,)), kv_s=dma((3,)), kv_r=dma((3,)),
        cot=VM((ROWS, D), BF16), gh=VM((ROWS, D), F32), n2=VM((ROWS, D), BF16), n2t=VM((D, ROWS), BF16),
        wgu=VM((2, D, 768), BF16), wds=VM((2, 384, D), BF16), w_sem=dma((2, 2)),
        do=VM((HEADS, ROWS, 128), BF16), dot=VM((HEADS, 128, ROWS), BF16), delta=VM((HEADS, 1, ROWS), F32),
        gain_row=VM((1, 640), F32),
        ggu=VM((2, 4, NZ, 144, 384), BF16), gdn=VM((2, NZ, 4, 48, D), BF16), go=VM((2, 4, NZ, 144, 128), BF16),
        gq=VM((8, NZ, 144, 128), BF16),
        fin=dict(gu=VM((144, 2 * FF), BF16), dn=VM((384, D), BF16), o=VM((144, QW), BF16), q=VM((144, QW), BF16)),
        own_kv=VM((KV_HEADS, ROWS, 128), F32),
        skv=VM((KV_HEADS, 3, ROWS, 128), BF16), rkv=VM((KV_HEADS, 3, ROWS, 128), BF16),
        dkv_r=dma((3,)), st_sem=dma((3, 4)),
        red_gu=Reduction.scratch((4, 4), 144, 384), red_dn=Reduction.scratch((4, 4), 48, D),
        red_o=Reduction.scratch((4, 4), 144, 128), red_q=TileReduction.scratch(),
        vecs=VectorSum.scratch(),
    )
    fast = lambda shape: VM(shape, F32)
    return pl.pallas_call(
        step_kernel,
        out_shape=(
            fast((D, ROWS)),
            fast((D, ROWS)),
            [[fast(shape) for shape in MATRICES] for _ in range(3)],
            [fast((528,)) for _ in range(3)],
            pltpu.HBM((D, OW), BF16),
            pltpu.HBM((D, 2 * FF), BF16),
            pltpu.HBM((FF, D), BF16),
        ),
        in_specs=[v, a, a, a, [v] * 3, [[a] * 4] * 3],
        out_specs=(v, v, [[v] * 4] * 3, [v] * 3, a, a, a),
        scratch_shapes=[scratch],
        compiler_params=pltpu.CompilerParams(
            collective_id=0, has_side_effects=True, vmem_limit_bytes=51 << 20),
        name="train_step",
    )(tok_t, cot_t, cos_t, sin_t, vstates, states)


def adam_step(weight, first_state, second_state, gradient, learn_rate, decay_rate):
    first_new = BETA_ONE * first_state + (1.0 - BETA_ONE) * gradient
    second_new = BETA_TWO * second_state + (1.0 - BETA_TWO) * gradient * gradient
    corr_one = 1.0 - BETA_ONE**STEP
    corr_two = 1.0 - BETA_TWO**STEP
    update = first_new / corr_one / (jnp.sqrt(second_new / corr_two) + ADAM_EPS)
    weight_new = weight - learn_rate * (update + decay_rate * weight)
    return (weight_new, first_new, second_new)


def store_kernel(sources, *rest):
    targets, sems = rest[:-1], rest[-1]
    copies = [
        pltpu.make_async_copy(a, b, sems.at[k])
        for k, (a, b) in enumerate(zip(jax.tree.leaves(sources), jax.tree.leaves(targets)))]
    for copy in copies:
        copy.start()
    for copy in copies:
        copy.wait()


def store(arrays):
    shapes = jax.tree.map(lambda t: jax.ShapeDtypeStruct(t.shape, t.dtype), arrays)
    count = len(jax.tree.leaves(arrays))
    v = pl.BlockSpec(memory_space=VM)
    a = pl.BlockSpec(memory_space=ANY)
    return pl.pallas_call(
        store_kernel,
        out_shape=shapes,
        in_specs=[jax.tree.map(lambda t: v, arrays)],
        out_specs=jax.tree.map(lambda t: a, arrays),
        scratch_shapes=[pltpu.SemaphoreType.DMA((count,))],
        compiler_params=pltpu.CompilerParams(vmem_limit_bytes=8 << 20),
        name="store",
    )(arrays)


def per_device(
    tokens, cotangent, w_qkv, w_out, w_gate_up, w_down, vectors,
    first_qkv, first_out, first_gate_up, first_down, first_vectors,
    second_qkv, second_out, second_gate_up, second_down, second_vectors,
):
    cos_np, sin_np = rope_tables()
    cos_t, sin_t = jnp.asarray(cos_np), jnp.asarray(sin_np)
    states = [
        [w_qkv, w_out, w_gate_up, w_down.T],
        [first_qkv, first_out, first_gate_up, first_down.T],
        [second_qkv, second_out, second_gate_up, second_down.T],
    ]
    vstates = [vectors, first_vectors, second_vectors]
    outs = train(
        tokens.T, cotangent.T, cos_t, sin_t, vstates, states)
    block_t, grad_t, matrices, vecs = store(tuple(outs[0:4]))
    out = [block_t.T, grad_t.T]
    for i in range(3):
        out += list(matrices[i][0:3]) + [matrices[i][3].T, vecs[i]]
    return tuple(out)


def solution(mesh):
    tokens = P(("dp", "ctx"), None)
    state = (P("ctx", None),) * 4 + (P("ctx"),)
    return jax.shard_map(
        per_device, mesh=mesh, in_specs=(tokens, tokens) + state * 3, out_specs=(tokens, tokens) + state * 3,
        check_vma=False,
    )
```

```python
import functools

import jax
import jax.numpy as jnp
import numpy as np
from jax import lax
from jax.experimental import pallas as pl
from jax.experimental.pallas import tpu as pltpu
from jax.sharding import PartitionSpec as P

D = 576
HEADS = 9
KV_HEADS = 3
GROUP = 3
HEAD_DIM = 64
FF = 1536
STEP = 10
LEN = 2048
ROWS = 512
QW = 1024
OW = 640
VW = 2304
NX = 4
NY = 4
NZ = 4

EPS = 1e-05
ROPE_BASE = 100000.0
MASK_FILL = -1e30
BETA_ONE = 0.9
BETA_TWO = 0.999
ADAM_EPS = 1e-08
RATE_MATRIX = 0.05
RATE_VECTOR = 0.5
DECAY_MATRIX = 0.1

F32 = jnp.float32
BF16 = jnp.bfloat16
MESH = pl.DeviceIdType.MESH
VM = pltpu.VMEM
ANY = pl.ANY


def rope_tables():
    half = HEAD_DIM // 2
    exponent = np.arange(half, dtype=np.float32) * np.float32(2.0 / HEAD_DIM)
    inverse = (np.float64(ROPE_BASE) ** (-exponent.astype(np.float64))).astype(np.float32)
    angles = np.arange(LEN, dtype=np.float32)[:, None] * inverse[None, :]
    cosine = np.cos(angles.astype(np.float64)).astype(np.float32)
    sine = np.sin(angles.astype(np.float64)).astype(np.float32)
    cos_all = np.concatenate([cosine] * 4, axis=1)
    sin_all = np.concatenate([-sine, sine, -sine, sine], axis=1)
    return cos_all, sin_all


def dot(a, b, ca=1, cb=0):
    return lax.dot_general(a, b, (((ca,), (cb,)), ((), ())), preferred_element_type=F32)


def place():
    dp = lax.axis_index("dp")
    z = lax.axis_index("ctx")
    x = lax.div(dp, NY * 2)
    y = lax.rem(lax.div(dp, 2), NY)
    c = lax.rem(dp, 2)
    return x, y, c, z


def device(x, y, c, z):
    return (x * (NY * 2) + y * 2 + c, z)


def wrap(i, n):
    return lax.rem(i, n)


def remote(src, dst, ssem, rsem, dev):
    return pltpu.make_async_remote_copy(
        src_ref=src, dst_ref=dst, send_sem=ssem, recv_sem=rsem, device_id=dev, device_id_type=MESH
    )


def greet(peers):
    barrier = pltpu.get_barrier_semaphore()
    for peer in peers:
        pl.semaphore_signal(barrier, inc=1, device_id=peer, device_id_type=MESH)
    pl.semaphore_wait(barrier, len(peers))


def swap_halves(v):
    width = v.shape[1]
    lane = lax.broadcasted_iota(jnp.int32, v.shape, 1)
    down = pltpu.roll(v, width - 32, 1)
    up = pltpu.roll(v, 32, 1)
    return jnp.where(lax.rem(lane, 64) < 32, down, up)


def low_lanes(v):
    lane = lax.broadcasted_iota(jnp.int32, v.shape, 1)
    return lane < 64


class Reduction:
    @staticmethod
    def scratch(lead, r, w):
        dma = pltpu.SemaphoreType.DMA
        return [
            VM(lead + (r, w), BF16), VM((3, 4, r, w), BF16), VM((4, r, w), BF16),
            VM((3, r, w), BF16), VM((4, r, w), BF16), dma((6,)), dma((10,)),
        ]

    def __init__(self, own, fin, fin_at, bufs, along_x, z_first):
        self.own, self.fin, self.fin_at, self.z_first = own, fin, fin_at, z_first
        self.rc, self.r1, self.s1, self.r2, self.r3, self.ss, self.rs = bufs
        x, y, c, z = place()
        self.c, self.z = c, z
        if along_x:
            self.a, self.b = x, y
            self.at = lambda a, b, cc, zz: device(a, b, cc, zz)
        else:
            self.a, self.b = y, x
            self.at = lambda a, b, cc, zz: device(b, a, cc, zz)
        self.other = self.at(self.a, self.b, 1 - c, z)

    def copy(self, src, dst, k, dev, into=None):
        return remote(src, dst, self.ss.at[k], self.rs.at[k if into is None else into], dev)

    def whole(self, ref, k):
        return self.copy(ref, ref, k, self.other)

    def mine(self, a, z):
        return (self.c, z, a) if self.z_first else (self.c, a, z)

    def all_z(self, a):
        return self.own.at[self.c, :, a] if self.z_first else self.own.at[self.c, a]

    def core_copy(self, k):
        return self.copy(self.own.at[1 - self.c, k], self.rc.at[k], 0, self.other, 6 + k)

    def core_add(self, k):
        self.core_copy(k).wait_recv()

        def add(j, carry):
            self.own[self.c, k, j] = self.own[self.c, k, j] + self.rc[k, j]
            return carry

        lax.fori_loop(0, 4, add, 0)

    def core_all(self, act):
        def one(k, carry):
            act(k)
            return carry

        lax.fori_loop(0, 4, one, 0)

    def first_copy(self, d):
        to = wrap(self.a + d, 4)
        return self.copy(self.all_z(to), self.r1.at[d - 1], 1, self.at(to, self.b, self.c, self.z))

    def first_start(self):
        for d in range(1, 4):
            self.first_copy(d).start()

    def first_sum(self):
        self.whole(self.r1, 1).wait_recv()

        def add(j, carry):
            total = self.own[self.mine(self.a, j)].astype(F32) + self.r1[0, j].astype(F32)
            total = total + self.r1[1, j].astype(F32) + self.r1[2, j].astype(F32)
            self.s1[j] = total.astype(BF16)
            return carry

        lax.fori_loop(0, 4, add, 0)

    def z_start(self):
        for d in range(1, 4):
            to = wrap(self.z + d, 4)
            self.copy(self.s1.at[to], self.r2.at[d - 1], 2, self.at(self.a, self.b, self.c, to)).start()

    def z_sum(self):
        self.whole(self.r2, 2).wait_recv()
        total = self.s1[self.z].astype(F32) + self.r2[0].astype(F32)
        total = total + self.r2[1].astype(F32) + self.r2[2].astype(F32)
        self.r3[self.b] = total.astype(BF16)

    def exchange_start(self):
        for d in range(1, 4):
            to = wrap(self.b + d, 4)
            ref = self.r3.at[self.b]
            self.copy(ref, ref, 3, self.at(self.a, to, self.c, self.z)).start()

    def gather_start(self):
        self.whole(self.r3.at[0:3], 3).wait_recv()
        total = self.r3[0].astype(F32) + self.r3[1].astype(F32)
        total = total + self.r3[2].astype(F32) + self.r3[3].astype(F32)
        where = self.fin_at(self.c, self.a, 1)
        self.fin[where] = total.astype(BF16)
        ref = self.fin.at[where]
        for d in range(1, 4):
            self.copy(ref, ref, 4, self.at(wrap(self.a + d, 4), self.b, self.c, self.z)).start()

    def gather_forward(self):
        self.whole(self.fin.at[self.fin_at(0, 0, 3)], 4).wait_recv()
        ref = self.fin.at[self.fin_at(self.c, 0, 4)]
        self.copy(ref, ref, 5, self.other).start()

    def gather_wait(self):
        self.whole(self.fin.at[self.fin_at(0, 0, 4)], 5).wait_recv()

    def finish(self):
        for ref, k in (
            (self.rc, 0), (self.r1, 1), (self.r2, 2), (self.r3.at[0:3], 3),
            (self.fin.at[self.fin_at(0, 0, 3)], 4), (self.fin.at[self.fin_at(0, 0, 4)], 5),
        ):
            self.whole(ref, k).wait_send()


class VectorSum:
    SCRATCH = 4

    @staticmethod
    def scratch():
        dma = pltpu.SemaphoreType.DMA
        return [VM((2, 24, 128), F32), VM((3, 4, 24, 128), F32), dma((4,)), dma((4,))]

    def __init__(self, bufs):
        self.rc, self.r, self.ss, self.rs = bufs
        x, y, c, z = place()
        self.sibling = device(x, y, 1 - c, z)

    def copy(self, src, dst, k, dev):
        return remote(src, dst, self.ss.at[k], self.rs.at[k], dev)

    def stage(self, k):
        ref = self.rc.at[1] if k == 0 else self.r.at[k - 1, 0:3]
        return self.copy(ref, ref, k, self.sibling)

    def start(self):
        self.copy(self.rc.at[0], self.rc.at[1], 0, self.sibling).start()

    def next(self, k):
        x, y, c, z = place()
        self.stage(k).wait_recv()
        if k == 0:
            total = self.rc[0] + self.rc[1]
        else:
            total = self.r[k - 1, 0] + self.r[k - 1, 1] + self.r[k - 1, 2] + self.r[k - 1, 3]
        if k == 3:
            return total
        me = (y, z, x)[k]
        self.r[k, me] = total
        for d in range(1, 4):
            to = wrap(me + d, 4)
            dev = (device(x, to, c, z), device(x, y, c, to), device(to, y, c, z))[k]
            self.copy(self.r.at[k, me], self.r.at[k, me], k + 1, dev).start()
        return None

    def finish(self):
        for k in range(4):
            self.stage(k).wait_send()


READY = ((0, 1), (2, 3, 4), (5, 6, 7))
TILE_X = (0, 1, 2, 3, 3, 0, 1, 2)


class TileReduction:
    @staticmethod
    def scratch():
        dma = pltpu.SemaphoreType.DMA
        return [
            VM((4, NZ, 144, 128), BF16), VM((3, NZ, 144, 128), BF16), VM((NZ, 144, 128), BF16),
            VM((3, 144, 128), BF16), VM((4, 144, 128), BF16), dma((5,)), dma((8,)),
        ]

    def __init__(self, own, fin, bufs):
        self.own, self.fin = own, fin
        self.rc, self.r1, self.s1, self.r2, self.r3, self.ss, self.rs = bufs
        self.x, self.y, self.c, self.z = place()
        last = jnp.where(self.x == 3, 4, 5 + self.x)
        self.tile = jnp.where(self.c == lax.rem(self.x + 1, 2), self.x, last)

    def whole(self, ref, k):
        return remote(
            ref, ref, self.ss.at[k], self.rs.at[3 + k], device(self.x, self.y, 1 - self.c, self.z))

    def core_copy(self, t):
        return remote(
            self.own.at[t], self.rc.at[t // 2], self.ss.at[0], self.rs.at[t // 2],
            device(self.x, self.y, 1 - self.c, self.z))

    def core_start(self, tiles):
        for t in tiles:

            @pl.when(self.c == t % 2)
            def _(t=t):
                self.core_copy(t).start()

    def core_add(self, tiles):
        for t in tiles:

            @pl.when(self.c != t % 2)
            def _(t=t):
                self.core_copy(t).wait_recv()
                for j in range(NZ):
                    self.own[t, j] = self.own[t, j] + self.rc[t // 2, j]

    def first_start(self, tiles):
        for t in tiles:
            to = TILE_X[t]

            @pl.when(jnp.logical_and(self.c != t % 2, self.x != to))
            def _(t=t, to=to):
                k = jnp.maximum(wrap(to + NX - self.x, NX) - 1, 0)
                remote(
                    self.own.at[t], self.r1.at[k], self.ss.at[1], self.rs.at[4],
                    device(to, self.y, self.c, self.z)).start()

    def first_sum(self):
        self.whole(self.r1, 1).wait_recv()
        for j in range(NZ):
            total = self.own[self.tile, j].astype(F32) + self.r1[0, j].astype(F32)
            total = total + self.r1[1, j].astype(F32) + self.r1[2, j].astype(F32)
            self.s1[j] = total.astype(BF16)

    def z_start(self):
        for d in range(1, NZ):
            to = wrap(self.z + d, NZ)
            remote(
                self.s1.at[to], self.r2.at[d - 1], self.ss.at[2], self.rs.at[5],
                device(self.x, self.y, self.c, to)).start()

    def z_sum(self):
        self.whole(self.r2, 2).wait_recv()
        total = self.s1[self.z].astype(F32) + self.r2[0].astype(F32)
        total = total + self.r2[1].astype(F32) + self.r2[2].astype(F32)
        self.r3[self.y] = total.astype(BF16)

    def exchange_start(self):
        ref = self.r3.at[self.y]
        for d in range(1, NY):
            remote(ref, ref, self.ss.at[3], self.rs.at[6],
                   device(self.x, wrap(self.y + d, NY), self.c, self.z)).start()

    def gather_start(self):
        self.whole(self.r3.at[0:3], 3).wait_recv()
        total = self.r3[0].astype(F32) + self.r3[1].astype(F32)
        total = total + self.r3[2].astype(F32) + self.r3[3].astype(F32)
        where = (slice(None), pl.ds(pl.multiple_of(self.tile * 128, 128), 128))
        self.fin[where] = total.astype(BF16)
        ref = self.fin.at[where]
        for e in range(2):
            for d in range(NX):
                if e or d:
                    remote(ref, ref, self.ss.at[4], self.rs.at[7],
                           device(wrap(self.x + d, NX), self.y, wrap(self.c + e, 2), self.z)).start()

    def gather_wait(self):
        self.whole(self.fin.at[:, 0:896], 4).wait_recv()

    def finish(self):
        for ref, k in (
            (self.rc, 0), (self.r1, 1), (self.r2, 2), (self.r3.at[0:3], 3), (self.fin.at[:, 0:896], 4),
        ):
            self.whole(ref, k).wait_send()


def step_kernel(
    tok_hbm, cot_hbm, cos_hbm, sin_hbm, vstates, states,
    block_out, grad_in, new_states, new_vectors, wo_all, wgu_all, wdn_all, s,
):
    x, y, c, z = place()
    sib = device(x, y, 1 - c, z)
    zdev = [device(x, y, c, wrap(z + d, NZ)) for d in range(1, NZ)]
    xdev = [device(wrap(x + d, NX), y, c, z) for d in range(1, NX)]
    ydev = [device(x, wrap(y + d, NY), c, z) for d in range(1, NY)]
    peers = [sib] + xdev
    for dy in range(4):
        for dz in range(4):
            if dy or dz:
                peers.append(device(x, wrap(y + dy, NY), c, wrap(z + dz, NZ)))
    for d in range(1, 4):
        peers.append(device(wrap(x + d, NX), y, 1 - c, z))
        peers.append(device(x, wrap(y + d, NY), 1 - c, z))
    barrier = pltpu.get_barrier_semaphore()
    for peer in peers:
        pl.semaphore_signal(barrier, inc=1, device_id=peer, device_id_type=MESH)
    wq_v, vec_v, q_s, qt_s, kvs = s["wq"], s["vec"], s["q"], s["qt"], s["kv"]
    b_out, b_gu, b_dn, n1t = s["b_out"], s["ggu"].at[0, 0:2], s["gdn"].at[0, 0:2], s["n1t"]
    m_s, l_s, ot_s, lse, att = s["m"], s["l"], s["ot"], s["lse"], s["att"]
    loc_sem = s["loc"]
    row0 = pl.multiple_of(z * ROWS, ROWS)
    loads = [
        pltpu.make_async_copy(cos_hbm.at[pl.ds(row0, ROWS)], s["cos"], loc_sem.at[0]),
        pltpu.make_async_copy(sin_hbm.at[pl.ds(row0, ROWS)], s["sin"], loc_sem.at[1]),
        pltpu.make_async_copy(cot_hbm, s["n2t"], loc_sem.at[2]),
    ]
    masters = new_states[0]
    master_loads = [
        pltpu.make_async_copy(states[0][k], masters[k], s["st_sem"].at[0, k]) for k in range(4)]
    tok_t = s["tok"]
    tok_load = pltpu.make_async_copy(tok_hbm, tok_t, loc_sem.at[7])
    vector_loads = [
        pltpu.make_async_copy(vstates[i], new_vectors[i], s["v_sem"].at[i]) for i in range(3)]
    for load in vector_loads[0:1] + master_loads[0:1] + [tok_load] + master_loads[1:] + vector_loads[1:] + loads:
        load.start()
    vec_v[0] = jnp.zeros((1, VW), F32)
    vector_loads[0].wait()
    vec_v[0, :, 0:528] = new_vectors[0][...].reshape(1, 528)
    rolled = pltpu.roll(jnp.broadcast_to(vec_v[0], (8, VW)), z * 528, 1)
    vec_v[0] = rolled[0:1, :]
    qrows = pl.ds(pl.multiple_of(z * 144, 144), 144)
    master_loads[0].wait()
    wq_v[qrows, 0:896] = masters[0][:, 0:896].astype(BF16)
    wq_v[qrows, 896:1024] = jnp.concatenate(
        [masters[0][:, 896:960].astype(BF16), jnp.zeros((144, 64), BF16)], axis=1
    )
    pl.semaphore_wait(barrier, len(peers))

    sent = []

    def group(copies, name, shape):
        whole = remote(shape, shape, s["ss"].at[name], s["rs"].at[name], sib)
        return copies, whole

    def pair_of(name):
        return s["ss"].at[name], s["rs"].at[name]

    def begin(batch):
        for copy in batch[0]:
            copy.start()
        sent.append(batch[1])

    kcols = pl.ds(pl.multiple_of(512 + c * 256, 256), 256)
    xcols = pl.ds(pl.multiple_of(x * 128, 128), 128)
    ref_k, ref_q = wq_v.at[qrows, kcols], wq_v.at[qrows, xcols]
    k_over_z = group([remote(ref_k, ref_k, *pair_of(0), dev) for dev in zdev], 0, wq_v.at[0:432, 0:256])
    v_over_z = group(
        [remote(vec_v.at[0], vec_v.at[d], *pair_of(1), zdev[d - 1]) for d in range(1, NZ)], 1, vec_v.at[1:4])
    q_over_z = group([remote(ref_q, ref_q, *pair_of(2), dev) for dev in zdev], 2, wq_v.at[0:432, 0:128])
    begin(k_over_z)
    begin(v_over_z)

    @pl.when(c == 0)
    def _():
        for copy in q_over_z[0]:
            copy.start()

    def block_rows(e, n):
        return pl.ds(pl.multiple_of(wrap(z + NZ - e, NZ) * n, n), n)

    tok_load.wait()
    inputs = jnp.transpose(tok_t[...].astype(F32))
    s["gh"][...] = inputs
    unit = inputs * lax.rsqrt(jnp.mean(inputs * inputs, axis=-1, keepdims=True) + EPS)

    master_loads[1].wait()
    b_out[:, 0:512] = masters[1][:, 0:512].astype(BF16)
    b_out[:, 512:640] = jnp.concatenate(
        [masters[1][:, 512:576].astype(BF16), jnp.zeros((144, 64), BF16)], axis=1)
    own = [pltpu.make_async_copy(b_out, wo_all.at[qrows, :], loc_sem.at[3])]
    master_loads[2].wait()
    master_loads[3].wait()
    down = jnp.transpose(masters[3][...]).astype(BF16)
    zrows = pl.ds(pl.multiple_of(z * 384, 384), 384)
    for p in range(8):
        b_gu[p // 4, p % 4] = masters[2][:, 384 * p : 384 * p + 384].astype(BF16)
        b_dn[p // 4, p % 4] = down[48 * p : 48 * p + 48, :]
        own.append(
            pltpu.make_async_copy(
                b_gu.at[p // 4, p % 4], wgu_all.at[qrows, 384 * p : 384 * p + 384], loc_sem.at[5]))
        own.append(
            pltpu.make_async_copy(
                b_dn.at[p // 4, p % 4], wdn_all.at[pl.ds(pl.multiple_of(z * 384 + 48 * p, 48), 48), :],
                loc_sem.at[6]))
    own_done = [
        own[0],
        pltpu.make_async_copy(wgu_all.at[qrows, :], wgu_all.at[qrows, :], loc_sem.at[5]),
        pltpu.make_async_copy(wdn_all.at[zrows, :], wdn_all.at[zrows, :], loc_sem.at[6]),
    ]
    for copy in own:
        copy.start()

    pgu = pl.multiple_of((c * 4 + x) * 384, 128)
    pdn = (c * 4 + y) * 48
    po = jnp.minimum(c * 4 + y, 4)
    has_o = c * 4 + y < 5
    oc = pl.multiple_of(po * 128, 128)

    def down_rows(zz):
        return wdn_all.at[pl.ds(pl.multiple_of(zz * 384 + pdn, 48), 48), :]

    o_over_z = group(
        [remote(b_out.at[:, pl.ds(oc, 128)], wo_all.at[qrows, pl.ds(oc, 128)], *pair_of(3), dev) for dev in zdev],
        3, wo_all.at[0:432, 0:128])
    gu_over_z = group(
        [remote(b_gu.at[c, x], wgu_all.at[qrows, pl.ds(pgu, 384)], *pair_of(4), dev) for dev in zdev],
        4, wgu_all.at[0:432, 0:384])
    dn_over_z = group(
        [remote(b_dn.at[c, y], down_rows(z), *pair_of(5), dev) for dev in zdev], 5, wdn_all.at[0:144, :])

    def weights_over_z():
        @pl.when(has_o)
        def _():
            for copy in o_over_z[0]:
                copy.start()

        for copy in dn_over_z[0] + gu_over_z[0]:
            copy.start()

    weights_over_z()
    k_over_z[1].wait_recv()
    v_over_z[1].wait_recv()
    others = range(1, NZ)
    k_over_c = group(
        [remote(wq_v.at[block_rows(e, 144), kcols], wq_v.at[block_rows(e, 144), kcols], *pair_of(6), sib)
         for e in others], 6, wq_v.at[0:432, 0:256])
    begin(k_over_c)

    q_over_x = group(
        [remote(wq_v.at[block_rows(e, 144), xcols], wq_v.at[block_rows(e, 144), xcols], *pair_of(7), dev)
         for e in others for dev in xdev], 7, wq_v.at[0:432, 0:384])
    q_over_c = group(
        [remote(wq_v.at[block_rows(e, 144), 0:512], wq_v.at[block_rows(e, 144), 0:512], *pair_of(8), sib)
         for e in others], 8, wq_v.at[0:432, 0:512])

    @pl.when(c == 0)
    def _():
        q_over_z[1].wait_recv()
        for copy in q_over_x[0]:
            copy.start()

    raw = vec_v[0] + vec_v[1] + vec_v[2] + vec_v[3]
    raw = raw.astype(BF16).astype(F32)
    wide = jnp.broadcast_to(raw, (8, VW))
    gain_one = raw[:, 0:576]
    gain_two = pltpu.roll(wide, VW - 576, 1)[0:1, 0:576]
    bias = raw[:, 1152:2176]
    normed = unit * gain_one
    n1 = normed.astype(BF16)
    n1t[...] = jnp.transpose(normed).astype(BF16)
    for load in loads:
        load.wait()
    cosine, sine = s["cos"][...], s["sin"][...]

    k_over_c[1].wait_recv()

    def tile_of(v, t):
        return v[:, 128 * t : 128 * t + 128]

    def rotated(v):
        return v * cosine + swap_halves(v) * sine

    def turn(v):
        return pltpu.roll(v, 64, 1)

    proj = dot(n1, wq_v[:, 512:1024]) + bias[:, 512:1024]
    rot4, rot5 = rotated(tile_of(proj, 0)), rotated(tile_of(proj, 1))
    val6, val7 = tile_of(proj, 2), tile_of(proj, 3)
    low = low_lanes(rot4)
    kvs[z, 0] = jnp.where(low, turn(rot4), turn(val6)).astype(BF16)
    kvs[z, 1] = jnp.where(low, rot5, val6).astype(BF16)
    kvs[z, 2] = jnp.where(low, turn(rot5), turn(val7)).astype(BF16)
    kv_sends = []
    for d in range(1, NZ):
        kv_sends.append(
            remote(kvs.at[z], kvs.at[z], s["kv_s"].at[d - 1], s["kv_r"].at[d - 1],
                   device(x, y, c, wrap(z + d, NZ))))

        @pl.when(z + d < NZ)
        def _(d=d):
            kv_sends[d - 1].start()

    def put_query(h, part):
        qh = jnp.where(low, part, 0.0) * (HEAD_DIM ** -0.5)
        q_s[h] = qh.astype(BF16)
        qt_s[h] = jnp.transpose(qh).astype(BF16)

    put_query(8, rot4)
    s["cot"][...] = jnp.transpose(s["n2t"][...].astype(F32)).astype(BF16)

    @pl.when(c == 0)
    def _():
        q_over_x[1].wait_recv()
        for copy in q_over_c[0]:
            copy.start()

    @pl.when(c == 1)
    def _():
        q_over_c[1].wait_recv()

    proj = dot(n1, wq_v[:, 0:512]) + bias[:, 0:512]
    for t in range(4):
        rot = rotated(tile_of(proj, t))
        put_query(2 * t, rot)
        put_query(2 * t + 1, turn(rot))

    def step(j):
        kvt = [jnp.transpose(kvs[j, g].astype(F32)).astype(BF16)[64:128, :] for g in range(KV_HEADS)]
        heads = range(HEADS)
        sts = [dot(kvs[j, h // GROUP], qt_s[h]) for h in heads]
        olds = [m_s[h] for h in heads]
        peaks = [jnp.maximum(jnp.max(v, axis=0, keepdims=True), o) for v, o in zip(sts, olds)]
        alphas = [jnp.exp(o - p) for o, p in zip(olds, peaks)]
        ps = [jnp.exp(v - p) for v, p in zip(sts, peaks)]
        totals = [jnp.sum(p, axis=0, keepdims=True) + l_s[h] * a for h, p, a in zip(heads, ps, alphas)]
        outs = [dot(kvt[h // GROUP], p.astype(BF16)) + ot_s[h] * a for h, p, a in zip(heads, ps, alphas)]
        for h in heads:
            m_s[h] = peaks[h]
            l_s[h] = totals[h]
            ot_s[h] = outs[h]

    def visible(width):
        shape = (256, width)
        return lax.broadcasted_iota(jnp.int32, shape, 0) <= lax.broadcasted_iota(jnp.int32, shape, 1)

    right = slice(256, 512)
    always = z >= 0

    @pl.when(always)
    def _():
        keep_a, keep_b = visible(512), visible(256)
        kvt = [jnp.transpose(kvs[z, g].astype(F32)).astype(BF16)[64:128, :] for g in range(KV_HEADS)]
        heads = range(HEADS)
        st_a = [jnp.where(keep_a, dot(kvs[z, h // GROUP, 0:256], qt_s[h]), MASK_FILL) for h in heads]
        st_b = [jnp.where(keep_b, dot(kvs[z, h // GROUP, right], qt_s[h, :, right]), MASK_FILL) for h in heads]
        none = jnp.full((1, 256), MASK_FILL, F32)
        zero = jnp.zeros((1, 256), F32)
        zeros = jnp.zeros((64, 256), F32)
        peaks = [
            jnp.maximum(
                jnp.max(a, axis=0, keepdims=True),
                jnp.concatenate([none, jnp.max(b, axis=0, keepdims=True)], axis=1))
            for a, b in zip(st_a, st_b)]
        p_a = [jnp.exp(a - p) for a, p in zip(st_a, peaks)]
        p_b = [jnp.exp(b - p[:, right]) for b, p in zip(st_b, peaks)]
        totals = [
            jnp.sum(a, axis=0, keepdims=True) + jnp.concatenate([zero, jnp.sum(b, axis=0, keepdims=True)], axis=1)
            for a, b in zip(p_a, p_b)]
        outs = [
            dot(kvt[h // GROUP][:, 0:256], p_a[h].astype(BF16))
            + jnp.concatenate([zeros, dot(kvt[h // GROUP][:, right], p_b[h].astype(BF16))], axis=1)
            for h in heads]
        for h in heads:
            m_s[h] = peaks[h]
            l_s[h] = totals[h]
            ot_s[h] = outs[h]

    gu_over_z[1].wait_recv()
    dn_over_z[1].wait_recv()

    @pl.when(has_o)
    def _():
        o_over_z[1].wait_recv()

    def gu_piece(e, xx):
        return wgu_all.at[block_rows(e, 144), pl.ds(pl.multiple_of((c * 4 + xx) * 384, 128), 384)]

    def o_piece(e):
        return wo_all.at[block_rows(e, 144), pl.ds(oc, 128)]

    def dn_half(e):
        return wdn_all.at[
            pl.ds(pl.multiple_of(wrap(z + NZ - e, NZ) * 384 + c * 192, 192), 192), :]

    def dn_piece(e):
        return down_rows(wrap(z + NZ - e, NZ))

    gu_over_x = group(
        [remote(gu_piece(e, x), gu_piece(e, x), *pair_of(9), dev) for e in others for dev in xdev],
        9, wgu_all.at[0:432, 0:1152])
    dn_over_y = group(
        [remote(dn_piece(e), dn_piece(e), *pair_of(10), dev) for e in others for dev in ydev],
        10, wdn_all.at[0:432, :])
    o_over_y = [
        [remote(o_piece(e), o_piece(e), s["ss"].at[11], s["os"].at[d - 1], ydev[d - 1]) for e in others]
        for d in range(1, NY)]
    o_sent = remote(wo_all.at[0:432, 0:384], wo_all.at[0:432, 0:384], s["ss"].at[11], s["os"].at[0], sib)
    own_over_c = group(
        [remote(gu_piece(e, x), gu_piece(e, x), *pair_of(12), sib) for e in others], 12, wgu_all.at[0:432, 0:384])
    gu_over_c = group(
        [remote(gu_piece(e, wrap(x + d, NX)), gu_piece(e, wrap(x + d, NX)), *pair_of(13), sib)
         for e in others for d in range(1, NX)], 13, wgu_all.at[0:432, 0:1152])
    dn_over_c = group(
        [remote(dn_half(e), dn_half(e), *pair_of(14), sib) for e in others], 14, wdn_all.at[0:576, :])
    o_over_c = []
    for core, cols in enumerate((slice(0, 512), slice(512, 640))):
        o_over_c.append(
            group(
                [remote(wo_all.at[block_rows(e, 144), cols], wo_all.at[block_rows(e, 144), cols], *pair_of(15), sib)
                 for e in others], 15, wo_all.at[0:432, cols]))

    @pl.when(has_o)
    def _():
        for copies in o_over_y:
            for copy in copies:
                copy.start()

    begin(dn_over_y)
    begin(gu_over_x)
    begin(own_over_c)

    for d in range(1, NZ):
        if d == NZ - 1:
            for dd in range(1, NY):
                from_y = wrap(y + NY - dd, NY)

                @pl.when(c * 4 + from_y < 5)
                def _(dd=dd):
                    remote(wo_all.at[0:432, 0:128], wo_all.at[0:432, 0:128], s["ss"].at[11], s["os"].at[dd - 1],
                           sib).wait_recv()

            for core in range(2):

                @pl.when(c == core)
                def _(core=core):
                    for copy in o_over_c[core][0]:
                        copy.start()

            dn_over_y[1].wait_recv()
            begin(dn_over_c)

        @pl.when(z >= d)
        def _(d=d):
            kv_sends[d - 1].wait_recv()
            step(z - d)

    for h in range(HEADS):
        ot_s[h] = ot_s[h] * (1.0 / l_s[h])
        lse[h] = m_s[h] + jnp.log(l_s[h])
    for t in range(5):
        top = ot_s[2 * t]
        bottom = ot_s[2 * t + 1] if 2 * t + 1 < HEADS else jnp.zeros((64, ROWS), F32)
        att[:, 128 * t : 128 * t + 128] = jnp.transpose(jnp.concatenate([top, bottom], axis=0)).astype(BF16)

    for core in range(2):

        @pl.when(c == core)
        def _(core=core):
            o_over_c[1 - core][1].wait_recv()

    for copy in own_done:
        copy.wait()
    wo = s["wo"]
    load_o = pltpu.make_async_copy(wo_all, wo, loc_sem.at[4])
    load_o.start()
    wgu, wds, w_sem = s["wgu"], s["wds"], s["w_sem"]

    def weights(i, slot):
        col = pl.multiple_of(wrap(x + i, 4) * 384, 384)
        return [
            pltpu.make_async_copy(
                wgu_all.at[:, pl.ds(col, 384)], wgu.at[slot, :, 0:384], w_sem.at[0, slot]),
            pltpu.make_async_copy(
                wgu_all.at[:, pl.ds(pl.multiple_of(col + FF, 384), 384)], wgu.at[slot, :, 384:768],
                w_sem.at[0, slot]),
            pltpu.make_async_copy(wdn_all.at[pl.ds(col, 384), :], wds.at[slot], w_sem.at[1, slot]),
        ]

    def weights_wait(slot):
        pltpu.make_async_copy(wgu_all.at[:, 0:768], wgu.at[slot], w_sem.at[0, slot]).wait()
        pltpu.make_async_copy(wdn_all.at[0:384, :], wds.at[slot], w_sem.at[1, slot]).wait()

    gu_over_z[1].wait_send()
    dn_over_z[1].wait_send()
    dn_over_c[1].wait_recv()
    own_over_c[1].wait_recv()
    for load in weights(0, 0):
        load.start()
    gu_over_x[1].wait_recv()
    begin(gu_over_c)

    ggu, gdn, go, gq, fin = s["ggu"], s["gdn"], s["go"], s["gq"], s["fin"]
    def columns(width):
        def at(cc, a, count):
            return (slice(None), pl.ds(pl.multiple_of((cc * 4 + a) * width, 128), count * width))

        return at

    def down_at(cc, a, count):
        return (pl.ds(pl.multiple_of((cc * 4 + a) * 48, 48), count * 48), slice(None))

    red_gu = Reduction(ggu, fin["gu"], columns(384), s["red_gu"], True, False)
    red_dn = Reduction(gdn, fin["dn"], down_at, s["red_dn"], False, True)
    red_o = Reduction(go, fin["o"], columns(128), s["red_o"], False, False)
    red_q = TileReduction(gq, fin["q"], s["red_q"])
    vecs = VectorSum(s["vecs"])
    cot, gh, n2, n2t, gn2t = s["cot"], s["gh"], s["n2"], s["n2t"], grad_in
    do_in, dot_in, delta_in, gain_row = s["do"], s["dot"], s["delta"], s["gain_row"]
    dqt, own_kv, skv, rkv = ot_s, s["own_kv"], s["skv"], s["rkv"]

    gn2t[...] = jnp.zeros_like(gn2t)
    load_o.wait()
    hid = gh[...] + dot(att[:, 0:576], wo[:, 0:576])
    inv_two = lax.rsqrt(jnp.mean(hid * hid, axis=-1, keepdims=True) + EPS)
    normed = hid * inv_two * gain_two
    n2[...] = normed.astype(BF16)
    n2t[...] = jnp.transpose(normed).astype(BF16)
    gh[...] = hid
    block_out[...] = jnp.transpose(hid)

    def chunk(i, carry):
        slot = lax.rem(i, 2)
        here = wrap(x + i, 4)
        weights_wait(slot)

        @pl.when(jnp.logical_and(i > 0, i < 3))
        def _():
            for load in weights(i + 1, 1 - slot):
                load.start()

        both = dot(n2[...], wgu[slot])
        gate, up = both[:, 0:384], both[:, 384:768]
        sg = jax.nn.sigmoid(gate)
        silu = gate * sg
        act = (silu * up).astype(BF16)
        ga = dot(cot[...], wds[slot], 1, 1)
        gg = (ga * up * sg * (1.0 + gate * (1.0 - sg))).astype(BF16)
        gu = (ga * silu).astype(BF16)
        grads = jnp.concatenate([gg, gu], axis=1)
        both = dot(n2t[...], grads).astype(BF16)
        ggu[0, here] = both[:, 0:384].reshape(NZ, 144, 384)
        ggu[1, here] = both[:, 384:768].reshape(NZ, 144, 384)
        red_gu.core_copy(here).start()
        down = dot(act, cot[...], 0, 0).astype(BF16)
        for p in range(8):
            gdn[p // 4, here, p % 4] = down[48 * p : 48 * p + 48, :]
        red_dn.core_copy(here).start()

        @pl.when(i == 0)
        def _():
            gu_over_c[1].wait_recv()
            for load in weights(1, 1):
                load.start()

        @pl.when(i > 0)
        def _():
            red_gu.core_add(wrap(x + i + 3, 4))

        @pl.when(i > 1)
        def _():
            red_gu.first_copy(i - 1).start()

        block_out[...] += lax.dot_general(wds[slot], act, (((0,), (1,)), ((), ())), preferred_element_type=F32)
        gn2t[...] += dot(wgu[slot], grads, 1, 1)

        return carry

    lax.fori_loop(0, 4, chunk, 0)

    red_dn.core_all(red_dn.core_add)
    red_dn.first_start()
    red_gu.core_add(wrap(x + 3, 4))
    red_gu.first_copy(3).start()
    state_loads = []
    for i in range(1, 3):
        for k in range(4):
            copy = pltpu.make_async_copy(states[i][k], new_states[i][k], s["st_sem"].at[i, k])
            copy.start()
            state_loads.append(copy)

    @pl.when(always)
    def _():
        hid = gh[...]
        inv_two = lax.rsqrt(jnp.mean(hid * hid, axis=-1, keepdims=True) + EPS)
        u = hid * inv_two
        e = jnp.transpose(gn2t[...])
        f = e * gain_two
        gain_row[:, 0:576] = jnp.sum(e * u, axis=0, keepdims=True)
        gain_row[:, 576:640] = jnp.zeros((1, 64), F32)
        grad_hidden = cot[...].astype(F32) + inv_two * (f - u * jnp.mean(f * u, axis=-1, keepdims=True))
        gh[...] = grad_hidden
        ghl = grad_hidden.astype(BF16)
        grad_out = dot(att[:, 0:576], ghl, 0, 0).astype(BF16)
        for p in range(8):
            if p < 4:
                part = grad_out[:, 128 * p : 128 * p + 128]
            elif p == 4:
                part = jnp.concatenate([grad_out[:, 512:576], jnp.zeros((D, 64), BF16)], axis=1)
            else:
                part = jnp.zeros((D, 128), BF16)
            go[p // 4, p % 4] = part.reshape(NZ, 144, 128)
        red_o.core_all(lambda k: red_o.core_copy(k).start())
        gm = dot(ghl, wo[:, 0:576], 1, 1).astype(BF16).astype(F32)
        gm = jnp.concatenate([gm, jnp.zeros((ROWS, 64), F32)], axis=1)
        for h in range(HEADS):
            part = gm[:, 128 * (h // 2) : 128 * (h // 2) + 128]
            part = part if h % 2 == 1 else turn(part)
            part = jnp.where(low_lanes(part), 0.0, part)
            do_in[h] = part.astype(BF16)
            part = jnp.transpose(part)
            dot_in[h] = part.astype(BF16)
            delta_in[h] = jnp.sum(part[64:128, :] * ot_s[h], axis=0, keepdims=True)

    def attend(g, j):
        kv = kvs[j, g]
        kt = jnp.transpose(kv.astype(F32)).astype(BF16)[0:64, :]
        hs = [g * GROUP + k for k in range(GROUP)]
        sts = [dot(kv, qt_s[h]) for h in hs]
        dpts = [dot(kv, dot_in[h]) for h in hs]
        pts = [jnp.exp(v - lse[h]) for v, h in zip(sts, hs)]
        dsts = [(p * (d - delta_in[h])).astype(BF16) for p, d, h in zip(pts, dpts, hs)]
        both = [dot(d, q_s[h]) + dot(p.astype(BF16), do_in[h]) for p, d, h in zip(pts, dsts, hs)]
        dqs = [dot(kt, d) for d in dsts]
        for h, dq in zip(hs, dqs):
            dqt[h] += dq
        return both[0] + both[1] + both[2]

    def attend_own(g):
        keep_a, keep_b = visible(512), visible(256)
        kv_a, kv_b = kvs[z, g, 0:256], kvs[z, g, 256:512]
        kt = jnp.transpose(kvs[z, g].astype(F32)).astype(BF16)[0:64, :]
        zeros = jnp.zeros((64, 256), F32)
        hs = [g * GROUP + k for k in range(GROUP)]
        pt_a = [jnp.where(keep_a, jnp.exp(dot(kv_a, qt_s[h]) - lse[h]), 0.0) for h in hs]
        pt_b = [jnp.where(keep_b, jnp.exp(dot(kv_b, qt_s[h, :, right]) - lse[h, :, right]), 0.0) for h in hs]
        ds_a = [(p * (dot(kv_a, dot_in[h]) - delta_in[h])).astype(BF16) for p, h in zip(pt_a, hs)]
        ds_b = [
            (p * (dot(kv_b, dot_in[h, :, right]) - delta_in[h, :, right])).astype(BF16) for p, h in zip(pt_b, hs)]
        all_a = [dot(d, q_s[h]) + dot(p.astype(BF16), do_in[h]) for p, d, h in zip(pt_a, ds_a, hs)]
        all_b = [dot(d, q_s[h, right]) + dot(p.astype(BF16), do_in[h, right]) for p, d, h in zip(pt_b, ds_b, hs)]
        dqs = [
            dot(kt[:, 0:256], a) + jnp.concatenate([zeros, dot(kt[:, right], b)], axis=1)
            for a, b in zip(ds_a, ds_b)]
        for h, dq in zip(hs, dqs):
            dqt[h] += dq
        own_kv[g, 0:256] = all_a[0] + all_a[1] + all_a[2]
        own_kv[g, 256:512] = all_b[0] + all_b[1] + all_b[2]

    def kv_copy(g, k, dev):
        return remote(
            skv.at[g, k - 1], rkv.at[g, k - 1], s["ss"].at[16], s["dkv_r"].at[g], dev)

    def far(g, k):
        @pl.when(z >= k)
        def _():
            skv[g, k - 1] = attend(g, z - k).astype(BF16)
            kv_copy(g, k, device(x, y, c, z - k)).start()

    def own_block(g):
        pl.when(always)(functools.partial(attend_own, g))

    gps = q_s

    def kv_wait(g):
        for count in range(1, NZ):

            @pl.when(z + count == NZ - 1)
            def _(count=count):
                part = rkv.at[g, 0:count]
                remote(part, part, s["ss"].at[16], s["dkv_r"].at[g], sib).wait_recv()
                total = own_kv[g]
                for k in range(count):
                    total = total + rkv[g, k].astype(F32)
                own_kv[g] = total

    def group_tiles(g):
        cos_t, sin_t = s["cos"][...], s["sin"][...]
        low = low_lanes(cos_t)
        kv = own_kv[g]

        def query(top, bottom):
            both = [dqt[h] if h is not None else jnp.zeros((64, ROWS), F32) for h in (top, bottom)]
            return jnp.transpose(jnp.concatenate(both, axis=0)) * (HEAD_DIM ** -0.5)

        def back(t):
            return t * cos_t - swap_halves(t) * sin_t

        if g == 0:
            return {
                0: back(query(0, 1)),
                1: back(jnp.where(low, query(2, None), turn(kv))),
                2: jnp.where(low, turn(kv), 0.0),
            }
        if g == 1:
            return {
                2: jnp.where(low, 0.0, back(query(None, 3))),
                3: back(query(4, 5)),
                4: jnp.where(low, back(kv), kv),
            }
        return {
            5: back(query(6, 7)),
            6: back(jnp.where(low, query(8, None), turn(kv))),
            7: jnp.where(low, turn(kv), 0.0),
        }

    def tiles_of(g):
        @pl.when(always)
        def _():
            for t, tile in group_tiles(g).items():
                if t == 2 and g == 0:
                    gps[2] = tile.astype(BF16)
                    continue
                if t == 2:
                    tile = tile + gps[2].astype(F32)
                low_tile = tile.astype(BF16)
                gps[t] = low_tile
                gq[t] = dot(n1t[...], low_tile).astype(BF16).reshape(NZ, 144, 128)

        red_q.core_start((READY[g]))

    dqt[...] = jnp.zeros_like(dqt)
    early = red_q.tile <= 4
    late = red_q.tile > 4
    far(0, 3)
    red_o.core_all(red_o.core_add)
    far(0, 2)
    far(0, 1)
    own_block(0)
    far(1, 3)
    red_o.first_start()
    far(1, 2)
    kv_wait(0)
    tiles_of(0)
    far(1, 1)
    red_q.core_add(READY[0])
    red_q.first_start(READY[0])
    red_gu.first_sum()
    red_gu.z_start()
    far(2, 3)
    far(2, 2)
    far(2, 1)
    own_block(1)
    kv_wait(1)
    tiles_of(1)
    red_q.core_add(READY[1])
    red_q.first_start(READY[1])
    red_gu.z_sum()
    red_gu.exchange_start()
    own_block(2)
    red_dn.first_sum()
    red_dn.z_start()
    red_o.first_sum()
    red_o.z_start()
    kv_wait(2)
    tiles_of(2)
    low = low_lanes(s["cos"][...])

    def halves(t):
        tile = gps[t].astype(F32)
        return tile, turn(tile)

    (t0, _), (t1, u1), (t2, u2), (t3, u3) = [halves(t) for t in range(4)]
    (t4, u4), (t5, _), (t6, u6), (t7, _) = [halves(t) for t in range(4, 8)]
    ordered = [
        t0,
        jnp.where(low, t1, t2),
        t3,
        t5,
        jnp.where(low, t6, t1),
        jnp.where(low, t4, t6),
        jnp.where(low, t2, t4),
        t7,
    ]
    vecs.rc[0, 10:18, :] = jnp.concatenate(
        [jnp.sum(t, axis=0, keepdims=True) for t in ordered], axis=0)
    gn1 = dot(jnp.concatenate([t.astype(BF16) for t in ordered], axis=1), wq_v[...], 1, 1)
    inputs = jnp.transpose(tok_t[...].astype(F32))
    r = lax.rsqrt(jnp.mean(inputs * inputs, axis=-1, keepdims=True) + EPS)
    u = inputs * r
    f = gn1 * gain_one
    row = jnp.sum(gn1 * u, axis=0, keepdims=True)
    row = jnp.concatenate([row, jnp.zeros((1, 64), F32)], axis=1)
    for t in range(5):
        vecs.rc[0, t : t + 1, :] = row[:, 128 * t : 128 * t + 128]
        vecs.rc[0, 5 + t : 6 + t, :] = gain_row[:, 128 * t : 128 * t + 128]
    vecs.rc[0, 18:24, :] = jnp.zeros((6, 128), F32)
    vecs.start()
    red_q.core_add(READY[2])
    red_q.first_start(READY[2])
    vecs.next(0)

    @pl.when(early)
    def _():
        red_q.first_sum()
        red_q.z_start()

    grad_in[...] = jnp.transpose(gh[...] + r * (f - u * jnp.mean(f * u, axis=-1, keepdims=True)))

    red_dn.z_sum()
    red_dn.exchange_start()
    red_o.z_sum()
    red_o.exchange_start()

    @pl.when(late)
    def _():
        red_q.first_sum()
        red_q.z_start()

    vecs.next(1)
    red_gu.gather_start()

    def update(k, grad):
        new = adam_step(
            new_states[0][k][...], new_states[1][k][...], new_states[2][k][...], grad, RATE_MATRIX, DECAY_MATRIX)
        for i in range(3):
            new_states[i][k][...] = new[i]

    @pl.when(early)
    def _():
        red_q.z_sum()
        red_q.exchange_start()

    @pl.when(late)
    def _():
        red_q.z_sum()
        red_q.exchange_start()

    red_dn.gather_start()
    red_o.gather_start()

    @pl.when(early)
    def _():
        red_q.gather_start()

    vecs.next(2)

    @pl.when(late)
    def _():
        red_q.gather_start()

    red_gu.gather_forward()
    red_dn.gather_forward()
    red_o.gather_forward()
    for load in state_loads:
        load.wait()
    red_gu.gather_wait()
    update(2, fin["gu"][...].astype(F32))
    red_dn.gather_wait()
    update(3, jnp.transpose(fin["dn"][...].astype(F32)))
    red_o.gather_wait()
    update(1, fin["o"][:, 0:576].astype(F32))
    total = vecs.next(3)
    total = jnp.concatenate([total[t : t + 1, :] for t in range(18)], axis=1)
    pad = jnp.zeros((1, VW - 640), F32)
    flat = jnp.concatenate([total[:, 0:640], pad], axis=1)
    mid = jnp.concatenate([total[:, 640:1280], pad], axis=1)
    flat = flat + pltpu.roll(jnp.broadcast_to(mid, (8, VW)), 576, 1)[0:1, :]
    flat = flat + jnp.concatenate(
        [jnp.zeros((1, 1152), F32), total[:, 1280:2304], jnp.zeros((1, 128), F32)], axis=1)
    shift = lax.rem(VW - z * 528, VW)
    grad = pltpu.roll(jnp.broadcast_to(flat, (8, VW)), shift, 1)[0:1, 0:528]
    for load in vector_loads[1:]:
        load.wait()
    new = adam_step(*[v[...].reshape(1, 528) for v in new_vectors], grad, RATE_VECTOR, 0.0)
    for i in range(3):
        new_vectors[i][...] = new[i].reshape(528)
    red_q.gather_wait()
    tq = [fin["q"][:, 128 * t : 128 * t + 128].astype(F32) for t in range(8)]
    lowq = low_lanes(tq[0])
    ordered = [
        tq[0],
        jnp.where(lowq, tq[1], tq[2]),
        tq[3],
        tq[5],
        jnp.where(lowq, tq[6], tq[1]),
        jnp.where(lowq, tq[4], tq[6]),
        jnp.where(lowq, tq[2], tq[4]),
        tq[7],
    ]
    update(0, jnp.concatenate(ordered, axis=1)[:, 0:960])
    for red in (red_gu, red_dn, red_o):
        red.finish()
    red_q.finish()
    vecs.finish()
    for whole in sent:
        whole.wait_send()
    for count in range(1, NZ):

        @pl.when(z == count)
        def _(count=count):
            part = (skv.at[0], skv.at[0:2], skv)[count - 1]
            remote(part, part, s["ss"].at[16], s["dkv_r"].at[0], sib).wait_send()

    for d in range(1, NZ):

        @pl.when(z + d < NZ)
        def _(d=d):
            kv_sends[d - 1].wait_send()

    @pl.when(has_o)
    def _():
        o_over_z[1].wait_send()
        o_sent.wait_send()

    for core in range(2):

        @pl.when(c == core)
        def _(core=core):
            o_over_c[core][1].wait_send()

    @pl.when(c == 0)
    def _():
        for batch in (q_over_z, q_over_x, q_over_c):
            batch[1].wait_send()


MATRICES = ((144, 960), (144, D), (144, 2 * FF), (D, 384))


def train(tok_t, cot_t, cos_t, sin_t, vstates, states):
    sd = jax.ShapeDtypeStruct
    v = pl.BlockSpec(memory_space=VM)
    a = pl.BlockSpec(memory_space=ANY)
    dma = pltpu.SemaphoreType.DMA
    scratch = dict(
        wq=VM((D, QW), BF16), vec=VM((NZ, 1, VW), F32), cos=VM((ROWS, 128), F32), sin=VM((ROWS, 128), F32),
        b_out=VM((144, OW), BF16),
        q=VM((HEADS, ROWS, 128), BF16), qt=VM((HEADS, 128, ROWS), BF16), n1t=VM((D, ROWS), BF16),
        kv=VM((NZ, KV_HEADS, ROWS, 128), BF16),
        m=VM((HEADS, 1, ROWS), F32), l=VM((HEADS, 1, ROWS), F32), ot=VM((HEADS, 64, ROWS), F32),
        lse=VM((HEADS, 1, ROWS), F32), att=VM((ROWS, 640), BF16), wo=VM((D, OW), BF16),
        loc=dma((8,)), v_sem=dma((3,)), tok=VM((D, ROWS), BF16), ss=dma((17,)), rs=dma((16,)), os=dma((3,)), kv_s=dma((3,)), kv_r=dma((3,)),
        cot=VM((ROWS, D), BF16), gh=VM((ROWS, D), F32), n2=VM((ROWS, D), BF16), n2t=VM((D, ROWS), BF16),
        wgu=VM((2, D, 768), BF16), wds=VM((2, 384, D), BF16), w_sem=dma((2, 2)),
        do=VM((HEADS, ROWS, 128), BF16), dot=VM((HEADS, 128, ROWS), BF16), delta=VM((HEADS, 1, ROWS), F32),
        gain_row=VM((1, 640), F32),
        ggu=VM((2, 4, NZ, 144, 384), BF16), gdn=VM((2, NZ, 4, 48, D), BF16), go=VM((2, 4, NZ, 144, 128), BF16),
        gq=VM((8, NZ, 144, 128), BF16),
        fin=dict(gu=VM((144, 2 * FF), BF16), dn=VM((384, D), BF16), o=VM((144, QW), BF16), q=VM((144, QW), BF16)),
        own_kv=VM((KV_HEADS, ROWS, 128), F32),
        skv=VM((KV_HEADS, 3, ROWS, 128), BF16), rkv=VM((KV_HEADS, 3, ROWS, 128), BF16),
        dkv_r=dma((3,)), st_sem=dma((3, 4)),
        red_gu=Reduction.scratch((4, 4), 144, 384), red_dn=Reduction.scratch((4, 4), 48, D),
        red_o=Reduction.scratch((4, 4), 144, 128), red_q=TileReduction.scratch(),
        vecs=VectorSum.scratch(),
    )
    fast = lambda shape: VM(shape, F32)
    return pl.pallas_call(
        step_kernel,
        out_shape=(
            fast((D, ROWS)),
            fast((D, ROWS)),
            [[fast(shape) for shape in MATRICES] for _ in range(3)],
            [fast((528,)) for _ in range(3)],
            pltpu.HBM((D, OW), BF16),
            pltpu.HBM((D, 2 * FF), BF16),
            pltpu.HBM((FF, D), BF16),
        ),
        in_specs=[a, a, a, a, [a] * 3, [[a] * 4] * 3],
        out_specs=(v, v, [[v] * 4] * 3, [v] * 3, a, a, a),
        scratch_shapes=[scratch],
        compiler_params=pltpu.CompilerParams(
            collective_id=0, has_side_effects=True, vmem_limit_bytes=51 << 20),
        name="train_step",
    )(tok_t, cot_t, cos_t, sin_t, vstates, states)


def adam_step(weight, first_state, second_state, gradient, learn_rate, decay_rate):
    first_new = BETA_ONE * first_state + (1.0 - BETA_ONE) * gradient
    second_new = BETA_TWO * second_state + (1.0 - BETA_TWO) * gradient * gradient
    corr_one = 1.0 - BETA_ONE**STEP
    corr_two = 1.0 - BETA_TWO**STEP
    update = first_new / corr_one / (jnp.sqrt(second_new / corr_two) + ADAM_EPS)
    weight_new = weight - learn_rate * (update + decay_rate * weight)
    return (weight_new, first_new, second_new)


def store_kernel(sources, *rest):
    targets, sems = rest[:-1], rest[-1]
    copies = [
        pltpu.make_async_copy(a, b, sems.at[k])
        for k, (a, b) in enumerate(zip(jax.tree.leaves(sources), jax.tree.leaves(targets)))]
    for copy in copies:
        copy.start()
    for copy in copies:
        copy.wait()


def store(arrays):
    shapes = jax.tree.map(lambda t: jax.ShapeDtypeStruct(t.shape, t.dtype), arrays)
    count = len(jax.tree.leaves(arrays))
    v = pl.BlockSpec(memory_space=VM)
    a = pl.BlockSpec(memory_space=ANY)
    return pl.pallas_call(
        store_kernel,
        out_shape=shapes,
        in_specs=[jax.tree.map(lambda t: v, arrays)],
        out_specs=jax.tree.map(lambda t: a, arrays),
        scratch_shapes=[pltpu.SemaphoreType.DMA((count,))],
        compiler_params=pltpu.CompilerParams(vmem_limit_bytes=8 << 20),
        name="store",
    )(arrays)


def per_device(
    tokens, cotangent, w_qkv, w_out, w_gate_up, w_down, vectors,
    first_qkv, first_out, first_gate_up, first_down, first_vectors,
    second_qkv, second_out, second_gate_up, second_down, second_vectors,
):
    cos_np, sin_np = rope_tables()
    cos_t, sin_t = jnp.asarray(cos_np), jnp.asarray(sin_np)
    states = [
        [w_qkv, w_out, w_gate_up, w_down.T],
        [first_qkv, first_out, first_gate_up, first_down.T],
        [second_qkv, second_out, second_gate_up, second_down.T],
    ]
    vstates = [vectors, first_vectors, second_vectors]
    outs = train(
        tokens.T, cotangent.T, cos_t, sin_t, vstates, states)
    block_t, grad_t, matrices, vecs = store(tuple(outs[0:4]))
    out = [block_t.T, grad_t.T]
    for i in range(3):
        out += list(matrices[i][0:3]) + [matrices[i][3].T, vecs[i]]
    return tuple(out)


def solution(mesh):
    tokens = P(("dp", "ctx"), None)
    state = (P("ctx", None),) * 4 + (P("ctx"),)
    return jax.shard_map(
        per_device, mesh=mesh, in_specs=(tokens, tokens) + state * 3, out_specs=(tokens, tokens) + state * 3,
        check_vma=False,
    )
```

```python
import functools

import jax
import jax.numpy as jnp
import numpy as np
from jax import lax
from jax.experimental import pallas as pl
from jax.experimental.pallas import tpu as pltpu
from jax.sharding import PartitionSpec as P

D = 576
HEADS = 9
KV_HEADS = 3
GROUP = 3
HEAD_DIM = 64
FF = 1536
STEP = 10
LEN = 2048
ROWS = 512
QW = 1024
OW = 640
VW = 2304
NX = 4
NY = 4
NZ = 4

EPS = 1e-05
ROPE_BASE = 100000.0
MASK_FILL = -1e30
BETA_ONE = 0.9
BETA_TWO = 0.999
ADAM_EPS = 1e-08
RATE_MATRIX = 0.05
RATE_VECTOR = 0.5
DECAY_MATRIX = 0.1

F32 = jnp.float32
BF16 = jnp.bfloat16
MESH = pl.DeviceIdType.MESH
VM = pltpu.VMEM
ANY = pl.ANY


def rope_tables():
    half = HEAD_DIM // 2
    exponent = np.arange(half, dtype=np.float32) * np.float32(2.0 / HEAD_DIM)
    inverse = (np.float64(ROPE_BASE) ** (-exponent.astype(np.float64))).astype(np.float32)
    angles = np.arange(LEN, dtype=np.float32)[:, None] * inverse[None, :]
    cosine = np.cos(angles.astype(np.float64)).astype(np.float32)
    sine = np.sin(angles.astype(np.float64)).astype(np.float32)
    cos_all = np.concatenate([cosine] * 4, axis=1)
    sin_all = np.concatenate([-sine, sine, -sine, sine], axis=1)
    return cos_all, sin_all


def dot(a, b, ca=1, cb=0):
    return lax.dot_general(a, b, (((ca,), (cb,)), ((), ())), preferred_element_type=F32)


def place():
    dp = lax.axis_index("dp")
    z = lax.axis_index("ctx")
    x = lax.div(dp, NY * 2)
    y = lax.rem(lax.div(dp, 2), NY)
    c = lax.rem(dp, 2)
    return x, y, c, z


def device(x, y, c, z):
    return (x * (NY * 2) + y * 2 + c, z)


def wrap(i, n):
    return lax.rem(i, n)


def remote(src, dst, ssem, rsem, dev):
    return pltpu.make_async_remote_copy(
        src_ref=src, dst_ref=dst, send_sem=ssem, recv_sem=rsem, device_id=dev, device_id_type=MESH
    )


def greet(peers):
    barrier = pltpu.get_barrier_semaphore()
    for peer in peers:
        pl.semaphore_signal(barrier, inc=1, device_id=peer, device_id_type=MESH)
    pl.semaphore_wait(barrier, len(peers))


def swap_halves(v):
    width = v.shape[1]
    lane = lax.broadcasted_iota(jnp.int32, v.shape, 1)
    down = pltpu.roll(v, width - 32, 1)
    up = pltpu.roll(v, 32, 1)
    return jnp.where(lax.rem(lane, 64) < 32, down, up)


def low_lanes(v):
    lane = lax.broadcasted_iota(jnp.int32, v.shape, 1)
    return lane < 64


class Reduction:
    @staticmethod
    def scratch(lead, r, w):
        dma = pltpu.SemaphoreType.DMA
        return [
            VM(lead + (r, w), BF16), VM((3, 4, r, w), BF16), VM((4, r, w), BF16),
            VM((3, r, w), BF16), VM((4, r, w), BF16), dma((6,)), dma((10,)),
        ]

    def __init__(self, own, fin, fin_at, bufs, swap, z_first):
        self.own, self.fin, self.fin_at, self.z_first = own, fin, fin_at, z_first
        self.rc, self.r1, self.s1, self.r2, self.r3, self.ss, self.rs = bufs
        x, y, c, z = place()
        self.c, self.z = c, z
        flip = c != swap
        self.a, self.b = jnp.where(flip, y, x), jnp.where(flip, x, y)
        self.at = lambda a, b, cc, zz: device(jnp.where(flip, b, a), jnp.where(flip, a, b), cc, zz)
        self.other = self.at(self.a, self.b, 1 - c, z)

    def copy(self, src, dst, k, dev, into=None):
        return remote(src, dst, self.ss.at[k], self.rs.at[k if into is None else into], dev)

    def whole(self, ref, k):
        return self.copy(ref, ref, k, self.other)

    def mine(self, a, z):
        return (self.c, z, a) if self.z_first else (self.c, a, z)

    def all_z(self, a):
        return self.own.at[self.c, :, a] if self.z_first else self.own.at[self.c, a]

    def core_copy(self, k):
        return self.copy(self.own.at[1 - self.c, k], self.rc.at[k], 0, self.other, 6 + k)

    def core_add(self, k):
        self.core_copy(k).wait_recv()

        def add(j, carry):
            self.own[self.c, k, j] = self.own[self.c, k, j] + self.rc[k, j]
            return carry

        lax.fori_loop(0, 4, add, 0)

    def core_all(self, act):
        def one(k, carry):
            act(k)
            return carry

        lax.fori_loop(0, 4, one, 0)

    def first_copy(self, d):
        to = wrap(self.a + d, 4)
        return self.copy(self.all_z(to), self.r1.at[d - 1], 1, self.at(to, self.b, self.c, self.z))

    def first_start(self):
        for d in range(1, 4):
            self.first_copy(d).start()

    def first_piece(self, piece):
        d = wrap(piece + 4 - self.a, 4)

        @pl.when(d > 0)
        def _():
            self.first_copy(jnp.maximum(d, 1)).start()

    def first_sum(self):
        self.whole(self.r1, 1).wait_recv()

        def add(j, carry):
            total = self.own[self.mine(self.a, j)].astype(F32) + self.r1[0, j].astype(F32)
            total = total + self.r1[1, j].astype(F32) + self.r1[2, j].astype(F32)
            self.s1[j] = total.astype(BF16)
            return carry

        lax.fori_loop(0, 4, add, 0)

    def z_start(self):
        for d in range(1, 4):
            to = wrap(self.z + d, 4)
            self.copy(self.s1.at[to], self.r2.at[d - 1], 2, self.at(self.a, self.b, self.c, to)).start()

    def z_sum(self):
        self.whole(self.r2, 2).wait_recv()
        total = self.s1[self.z].astype(F32) + self.r2[0].astype(F32)
        total = total + self.r2[1].astype(F32) + self.r2[2].astype(F32)
        self.r3[self.b] = total.astype(BF16)

    def exchange_start(self):
        for d in range(1, 4):
            to = wrap(self.b + d, 4)
            ref = self.r3.at[self.b]
            self.copy(ref, ref, 3, self.at(self.a, to, self.c, self.z)).start()

    def gather_start(self):
        self.whole(self.r3.at[0:3], 3).wait_recv()
        total = self.r3[0].astype(F32) + self.r3[1].astype(F32)
        total = total + self.r3[2].astype(F32) + self.r3[3].astype(F32)
        where = self.fin_at(self.c, self.a, 1)
        self.fin[where] = total.astype(BF16)
        ref = self.fin.at[where]
        for d in range(1, 4):
            self.copy(ref, ref, 4, self.at(wrap(self.a + d, 4), self.b, self.c, self.z)).start()

    def gather_forward(self):
        self.whole(self.fin.at[self.fin_at(0, 0, 3)], 4).wait_recv()
        ref = self.fin.at[self.fin_at(self.c, 0, 4)]
        self.copy(ref, ref, 5, self.other).start()

    def gather_wait(self):
        self.whole(self.fin.at[self.fin_at(0, 0, 4)], 5).wait_recv()

    def finish(self):
        for ref, k in (
            (self.rc, 0), (self.r1, 1), (self.r2, 2), (self.r3.at[0:3], 3),
            (self.fin.at[self.fin_at(0, 0, 3)], 4), (self.fin.at[self.fin_at(0, 0, 4)], 5),
        ):
            self.whole(ref, k).wait_send()


class VectorSum:
    SCRATCH = 4

    @staticmethod
    def scratch():
        dma = pltpu.SemaphoreType.DMA
        return [VM((2, 24, 128), F32), VM((3, 4, 24, 128), F32), dma((4,)), dma((4,))]

    def __init__(self, bufs):
        self.rc, self.r, self.ss, self.rs = bufs
        x, y, c, z = place()
        self.sibling = device(x, y, 1 - c, z)

    def copy(self, src, dst, k, dev):
        return remote(src, dst, self.ss.at[k], self.rs.at[k], dev)

    def stage(self, k):
        ref = self.rc.at[1] if k == 0 else self.r.at[k - 1, 0:3]
        return self.copy(ref, ref, k, self.sibling)

    def start(self):
        self.copy(self.rc.at[0], self.rc.at[1], 0, self.sibling).start()

    def next(self, k):
        x, y, c, z = place()
        self.stage(k).wait_recv()
        if k == 0:
            total = self.rc[0] + self.rc[1]
        else:
            total = self.r[k - 1, 0] + self.r[k - 1, 1] + self.r[k - 1, 2] + self.r[k - 1, 3]
        if k == 3:
            return total
        me = (y, z, x)[k]
        self.r[k, me] = total
        for d in range(1, 4):
            to = wrap(me + d, 4)
            dev = (device(x, to, c, z), device(x, y, c, to), device(to, y, c, z))[k]
            self.copy(self.r.at[k, me], self.r.at[k, me], k + 1, dev).start()
        return None

    def finish(self):
        for k in range(4):
            self.stage(k).wait_send()


READY = ((0, 1), (2, 3, 4), (5, 6, 7))
TILE_A = (0, 1, 2, 3, 3, 0, 1, 2)


class TileReduction:
    @staticmethod
    def scratch():
        dma = pltpu.SemaphoreType.DMA
        return [
            VM((4, NZ, 144, 128), BF16), VM((3, NZ, 144, 128), BF16), VM((NZ, 144, 128), BF16),
            VM((3, 144, 128), BF16), VM((4, 144, 128), BF16), dma((5,)), dma((8,)),
        ]

    def __init__(self, own, fin, bufs):
        self.own, self.fin = own, fin
        self.rc, self.r1, self.s1, self.r2, self.r3, self.ss, self.rs = bufs
        self.x, self.y, self.c, self.z = place()
        self.flip = self.c == 1
        self.a, self.b = jnp.where(self.flip, self.y, self.x), jnp.where(self.flip, self.x, self.y)
        last = jnp.where(self.a == 3, 4, 5 + self.a)
        self.tile = jnp.where(self.c == lax.rem(self.a + 1, 2), self.a, last)

    def at(self, a, b, z, core=None):
        core = self.c if core is None else core
        return device(jnp.where(self.flip, b, a), jnp.where(self.flip, a, b), core, z)

    def whole(self, ref, k):
        return remote(
            ref, ref, self.ss.at[k], self.rs.at[3 + k], device(self.x, self.y, 1 - self.c, self.z))

    def core_copy(self, t):
        return remote(
            self.own.at[t], self.rc.at[t // 2], self.ss.at[0], self.rs.at[t // 2],
            device(self.x, self.y, 1 - self.c, self.z))

    def core_start(self, tiles):
        for t in tiles:

            @pl.when(self.c == t % 2)
            def _(t=t):
                self.core_copy(t).start()

    def core_add(self, tiles):
        for t in tiles:

            @pl.when(self.c != t % 2)
            def _(t=t):
                self.core_copy(t).wait_recv()
                for j in range(NZ):
                    self.own[t, j] = self.own[t, j] + self.rc[t // 2, j]

    def first_start(self, tiles):
        for t in tiles:
            to = TILE_A[t]

            @pl.when(jnp.logical_and(self.c != t % 2, self.a != to))
            def _(t=t, to=to):
                k = jnp.maximum(wrap(to + NX - self.a, NX) - 1, 0)
                remote(
                    self.own.at[t], self.r1.at[k], self.ss.at[1], self.rs.at[4],
                    self.at(to, self.b, self.z)).start()

    def first_sum(self):
        self.whole(self.r1, 1).wait_recv()
        for j in range(NZ):
            total = self.own[self.tile, j].astype(F32) + self.r1[0, j].astype(F32)
            total = total + self.r1[1, j].astype(F32) + self.r1[2, j].astype(F32)
            self.s1[j] = total.astype(BF16)

    def z_start(self):
        for d in range(1, NZ):
            to = wrap(self.z + d, NZ)
            remote(
                self.s1.at[to], self.r2.at[d - 1], self.ss.at[2], self.rs.at[5],
                device(self.x, self.y, self.c, to)).start()

    def z_sum(self):
        self.whole(self.r2, 2).wait_recv()
        total = self.s1[self.z].astype(F32) + self.r2[0].astype(F32)
        total = total + self.r2[1].astype(F32) + self.r2[2].astype(F32)
        self.r3[self.b] = total.astype(BF16)

    def exchange_start(self):
        ref = self.r3.at[self.b]
        for d in range(1, NY):
            remote(ref, ref, self.ss.at[3], self.rs.at[6],
                   self.at(self.a, wrap(self.b + d, NY), self.z)).start()

    def gather_start(self):
        self.whole(self.r3.at[0:3], 3).wait_recv()
        total = self.r3[0].astype(F32) + self.r3[1].astype(F32)
        total = total + self.r3[2].astype(F32) + self.r3[3].astype(F32)
        where = (slice(None), pl.ds(pl.multiple_of(self.tile * 128, 128), 128))
        self.fin[where] = total.astype(BF16)
        ref = self.fin.at[where]
        for e in range(2):
            for d in range(NX):
                if e or d:
                    remote(ref, ref, self.ss.at[4], self.rs.at[7],
                           self.at(wrap(self.a + d, 4), self.b, self.z, wrap(self.c + e, 2))).start()

    def gather_wait(self):
        self.whole(self.fin.at[:, 0:896], 4).wait_recv()

    def finish(self):
        for ref, k in (
            (self.rc, 0), (self.r1, 1), (self.r2, 2), (self.r3.at[0:3], 3), (self.fin.at[:, 0:896], 4),
        ):
            self.whole(ref, k).wait_send()


def step_kernel(
    tok_hbm, cot_hbm, cos_hbm, sin_hbm, vstates, states,
    block_out, grad_in, new_states, new_vectors, wo_all, wgu_all, wdn_all, s,
):
    x, y, c, z = place()
    sib = device(x, y, 1 - c, z)
    zdev = [device(x, y, c, wrap(z + d, NZ)) for d in range(1, NZ)]
    xdev = [device(wrap(x + d, NX), y, c, z) for d in range(1, NX)]
    ydev = [device(x, wrap(y + d, NY), c, z) for d in range(1, NY)]
    peers = [sib] + xdev + ydev + zdev
    for d in range(1, 4):
        peers.append(device(wrap(x + d, NX), y, 1 - c, z))
        peers.append(device(x, wrap(y + d, NY), 1 - c, z))
    barrier = pltpu.get_barrier_semaphore()
    for peer in peers:
        pl.semaphore_signal(barrier, inc=1, device_id=peer, device_id_type=MESH)
    wq_v, vec_v, q_s, qt_s, kvs = s["wq"], s["vec"], s["q"], s["qt"], s["kv"]
    b_out, b_gu, b_dn, n1t = s["b_out"], s["ggu"].at[0, 0:2], s["gdn"].at[0, 0:2], s["n1t"]
    m_s, l_s, ot_s, lse, att = s["m"], s["l"], s["ot"], s["lse"], s["att"]
    loc_sem = s["loc"]
    row0 = pl.multiple_of(z * ROWS, ROWS)
    loads = [
        pltpu.make_async_copy(cos_hbm.at[pl.ds(row0, ROWS)], s["cos"], loc_sem.at[0]),
        pltpu.make_async_copy(sin_hbm.at[pl.ds(row0, ROWS)], s["sin"], loc_sem.at[1]),
        pltpu.make_async_copy(cot_hbm, s["n2t"], loc_sem.at[2]),
    ]
    masters = new_states[0]
    master_loads = [
        pltpu.make_async_copy(states[0][k], masters[k], s["st_sem"].at[0, k]) for k in range(4)]
    tok_t = s["tok"]
    tok_load = pltpu.make_async_copy(tok_hbm, tok_t, loc_sem.at[7])
    vector_loads = [
        pltpu.make_async_copy(vstates[i], new_vectors[i], s["v_sem"].at[i]) for i in range(3)]
    for load in vector_loads[0:1] + master_loads[0:1] + [tok_load] + master_loads[1:] + vector_loads[1:] + loads:
        load.start()
    vec_v[0] = jnp.zeros((1, VW), F32)
    vector_loads[0].wait()
    vec_v[0, :, 0:528] = new_vectors[0][...].reshape(1, 528)
    rolled = pltpu.roll(jnp.broadcast_to(vec_v[0], (8, VW)), z * 528, 1)
    vec_v[0] = rolled[0:1, :]
    qrows = pl.ds(pl.multiple_of(z * 144, 144), 144)
    master_loads[0].wait()
    wq_v[qrows, 0:896] = masters[0][:, 0:896].astype(BF16)
    wq_v[qrows, 896:1024] = jnp.concatenate(
        [masters[0][:, 896:960].astype(BF16), jnp.zeros((144, 64), BF16)], axis=1
    )
    pl.semaphore_wait(barrier, len(peers))

    sent = []

    def group(copies, name, shape):
        whole = remote(shape, shape, s["ss"].at[name], s["rs"].at[name], sib)
        return copies, whole

    def pair_of(name):
        return s["ss"].at[name], s["rs"].at[name]

    def begin(batch):
        for copy in batch[0]:
            copy.start()
        sent.append(batch[1])

    kcols = pl.ds(pl.multiple_of(512 + c * 256, 256), 256)
    xcols = pl.ds(pl.multiple_of(x * 128, 128), 128)
    ref_k, ref_q = wq_v.at[qrows, kcols], wq_v.at[qrows, xcols]
    k_over_z = group([remote(ref_k, ref_k, *pair_of(0), dev) for dev in zdev], 0, wq_v.at[0:432, 0:256])
    v_over_z = group(
        [remote(vec_v.at[0], vec_v.at[d], *pair_of(1), zdev[d - 1]) for d in range(1, NZ)], 1, vec_v.at[1:4])
    q_over_z = group([remote(ref_q, ref_q, *pair_of(2), dev) for dev in zdev], 2, wq_v.at[0:432, 0:128])
    begin(k_over_z)
    begin(v_over_z)

    @pl.when(c == 0)
    def _():
        for copy in q_over_z[0]:
            copy.start()

    def block_rows(e, n):
        return pl.ds(pl.multiple_of(wrap(z + NZ - e, NZ) * n, n), n)

    tok_load.wait()
    inputs = jnp.transpose(tok_t[...].astype(F32))
    s["gh"][...] = inputs
    unit = inputs * lax.rsqrt(jnp.mean(inputs * inputs, axis=-1, keepdims=True) + EPS)

    master_loads[1].wait()
    b_out[:, 0:512] = masters[1][:, 0:512].astype(BF16)
    b_out[:, 512:640] = jnp.concatenate(
        [masters[1][:, 512:576].astype(BF16), jnp.zeros((144, 64), BF16)], axis=1)
    own = [pltpu.make_async_copy(b_out, wo_all.at[qrows, :], loc_sem.at[3])]
    master_loads[2].wait()
    master_loads[3].wait()
    down = jnp.transpose(masters[3][...]).astype(BF16)
    zrows = pl.ds(pl.multiple_of(z * 384, 384), 384)
    for p in range(8):
        b_gu[p // 4, p % 4] = masters[2][:, 384 * p : 384 * p + 384].astype(BF16)
        b_dn[p // 4, p % 4] = down[48 * p : 48 * p + 48, :]
        own.append(
            pltpu.make_async_copy(
                b_gu.at[p // 4, p % 4], wgu_all.at[qrows, 384 * p : 384 * p + 384], loc_sem.at[5]))
        own.append(
            pltpu.make_async_copy(
                b_dn.at[p // 4, p % 4], wdn_all.at[pl.ds(pl.multiple_of(z * 384 + 48 * p, 48), 48), :],
                loc_sem.at[6]))
    own_done = [
        own[0],
        pltpu.make_async_copy(wgu_all.at[qrows, :], wgu_all.at[qrows, :], loc_sem.at[5]),
        pltpu.make_async_copy(wdn_all.at[zrows, :], wdn_all.at[zrows, :], loc_sem.at[6]),
    ]
    for copy in own:
        copy.start()

    w = wrap(x + y, 4)
    pgu = pl.multiple_of((c * 4 + w) * 384, 128)
    pdn = (c * 4 + y) * 48
    po = jnp.minimum(c * 4 + y, 4)
    has_o = c * 4 + y < 5
    oc = pl.multiple_of(po * 128, 128)

    def down_rows(zz):
        return wdn_all.at[pl.ds(pl.multiple_of(zz * 384 + pdn, 48), 48), :]

    o_over_z = group(
        [remote(b_out.at[:, pl.ds(oc, 128)], wo_all.at[qrows, pl.ds(oc, 128)], *pair_of(3), dev) for dev in zdev],
        3, wo_all.at[0:432, 0:128])
    gu_over_z = group(
        [remote(b_gu.at[c, w], wgu_all.at[qrows, pl.ds(pgu, 384)], *pair_of(4), dev) for dev in zdev],
        4, wgu_all.at[0:432, 0:384])
    dn_over_z = group(
        [remote(b_dn.at[c, y], down_rows(z), *pair_of(5), dev) for dev in zdev], 5, wdn_all.at[0:144, :])

    def weights_over_z():
        @pl.when(has_o)
        def _():
            for copy in o_over_z[0]:
                copy.start()

        for copy in dn_over_z[0] + gu_over_z[0]:
            copy.start()

    weights_over_z()
    k_over_z[1].wait_recv()
    v_over_z[1].wait_recv()
    others = range(1, NZ)
    k_over_c = group(
        [remote(wq_v.at[block_rows(e, 144), kcols], wq_v.at[block_rows(e, 144), kcols], *pair_of(6), sib)
         for e in others], 6, wq_v.at[0:432, 0:256])
    begin(k_over_c)

    q_over_x = group(
        [remote(wq_v.at[block_rows(e, 144), xcols], wq_v.at[block_rows(e, 144), xcols], *pair_of(7), dev)
         for e in others for dev in xdev], 7, wq_v.at[0:432, 0:384])
    q_over_c = group(
        [remote(wq_v.at[block_rows(e, 144), 0:512], wq_v.at[block_rows(e, 144), 0:512], *pair_of(8), sib)
         for e in others], 8, wq_v.at[0:432, 0:512])

    @pl.when(c == 0)
    def _():
        q_over_z[1].wait_recv()
        for copy in q_over_x[0]:
            copy.start()

    raw = vec_v[0] + vec_v[1] + vec_v[2] + vec_v[3]
    raw = raw.astype(BF16).astype(F32)
    wide = jnp.broadcast_to(raw, (8, VW))
    gain_one = raw[:, 0:576]
    gain_two = pltpu.roll(wide, VW - 576, 1)[0:1, 0:576]
    bias = raw[:, 1152:2176]
    normed = unit * gain_one
    n1 = normed.astype(BF16)
    n1t[...] = jnp.transpose(normed).astype(BF16)
    for load in loads:
        load.wait()
    cosine, sine = s["cos"][...], s["sin"][...]

    k_over_c[1].wait_recv()

    def tile_of(v, t):
        return v[:, 128 * t : 128 * t + 128]

    def rotated(v):
        return v * cosine + swap_halves(v) * sine

    def turn(v):
        return pltpu.roll(v, 64, 1)

    proj = dot(n1, wq_v[:, 512:1024]) + bias[:, 512:1024]
    rot4, rot5 = rotated(tile_of(proj, 0)), rotated(tile_of(proj, 1))
    val6, val7 = tile_of(proj, 2), tile_of(proj, 3)
    low = low_lanes(rot4)
    kvs[z, 0] = jnp.where(low, turn(rot4), turn(val6)).astype(BF16)
    kvs[z, 1] = jnp.where(low, rot5, val6).astype(BF16)
    kvs[z, 2] = jnp.where(low, turn(rot5), turn(val7)).astype(BF16)
    kv_sends = []
    for d in range(1, NZ):
        kv_sends.append(
            remote(kvs.at[z], kvs.at[z], s["kv_s"].at[d - 1], s["kv_r"].at[d - 1],
                   device(x, y, c, wrap(z + d, NZ))))

        @pl.when(z + d < NZ)
        def _(d=d):
            kv_sends[d - 1].start()

    def put_query(h, part):
        qh = jnp.where(low, part, 0.0) * (HEAD_DIM ** -0.5)
        q_s[h] = qh.astype(BF16)
        qt_s[h] = jnp.transpose(qh).astype(BF16)

    put_query(8, rot4)
    s["cot"][...] = jnp.transpose(s["n2t"][...].astype(F32)).astype(BF16)

    @pl.when(c == 0)
    def _():
        q_over_x[1].wait_recv()
        for copy in q_over_c[0]:
            copy.start()

    @pl.when(c == 1)
    def _():
        q_over_c[1].wait_recv()

    proj = dot(n1, wq_v[:, 0:512]) + bias[:, 0:512]
    for t in range(4):
        rot = rotated(tile_of(proj, t))
        put_query(2 * t, rot)
        put_query(2 * t + 1, turn(rot))

    def step(j):
        kvt = [jnp.transpose(kvs[j, g].astype(F32)).astype(BF16)[64:128, :] for g in range(KV_HEADS)]
        heads = range(HEADS)
        sts = [dot(kvs[j, h // GROUP], qt_s[h]) for h in heads]
        olds = [m_s[h] for h in heads]
        peaks = [jnp.maximum(jnp.max(v, axis=0, keepdims=True), o) for v, o in zip(sts, olds)]
        alphas = [jnp.exp(o - p) for o, p in zip(olds, peaks)]
        ps = [jnp.exp(v - p) for v, p in zip(sts, peaks)]
        totals = [jnp.sum(p, axis=0, keepdims=True) + l_s[h] * a for h, p, a in zip(heads, ps, alphas)]
        outs = [dot(kvt[h // GROUP], p.astype(BF16)) + ot_s[h] * a for h, p, a in zip(heads, ps, alphas)]
        for h in heads:
            m_s[h] = peaks[h]
            l_s[h] = totals[h]
            ot_s[h] = outs[h]

    def visible(width):
        shape = (256, width)
        return lax.broadcasted_iota(jnp.int32, shape, 0) <= lax.broadcasted_iota(jnp.int32, shape, 1)

    right = slice(256, 512)
    always = z >= 0

    @pl.when(always)
    def _():
        keep_a, keep_b = visible(512), visible(256)
        kvt = [jnp.transpose(kvs[z, g].astype(F32)).astype(BF16)[64:128, :] for g in range(KV_HEADS)]
        heads = range(HEADS)
        st_a = [jnp.where(keep_a, dot(kvs[z, h // GROUP, 0:256], qt_s[h]), MASK_FILL) for h in heads]
        st_b = [jnp.where(keep_b, dot(kvs[z, h // GROUP, right], qt_s[h, :, right]), MASK_FILL) for h in heads]
        none = jnp.full((1, 256), MASK_FILL, F32)
        zero = jnp.zeros((1, 256), F32)
        zeros = jnp.zeros((64, 256), F32)
        peaks = [
            jnp.maximum(
                jnp.max(a, axis=0, keepdims=True),
                jnp.concatenate([none, jnp.max(b, axis=0, keepdims=True)], axis=1))
            for a, b in zip(st_a, st_b)]
        p_a = [jnp.exp(a - p) for a, p in zip(st_a, peaks)]
        p_b = [jnp.exp(b - p[:, right]) for b, p in zip(st_b, peaks)]
        totals = [
            jnp.sum(a, axis=0, keepdims=True) + jnp.concatenate([zero, jnp.sum(b, axis=0, keepdims=True)], axis=1)
            for a, b in zip(p_a, p_b)]
        outs = [
            dot(kvt[h // GROUP][:, 0:256], p_a[h].astype(BF16))
            + jnp.concatenate([zeros, dot(kvt[h // GROUP][:, right], p_b[h].astype(BF16))], axis=1)
            for h in heads]
        for h in heads:
            m_s[h] = peaks[h]
            l_s[h] = totals[h]
            ot_s[h] = outs[h]

    gu_over_z[1].wait_recv()
    dn_over_z[1].wait_recv()

    @pl.when(has_o)
    def _():
        o_over_z[1].wait_recv()

    def gu_piece(e, ww):
        return wgu_all.at[block_rows(e, 144), pl.ds(pl.multiple_of((c * 4 + ww) * 384, 128), 384)]

    def o_piece(e):
        return wo_all.at[block_rows(e, 144), pl.ds(oc, 128)]

    def dn_half(e):
        return wdn_all.at[
            pl.ds(pl.multiple_of(wrap(z + NZ - e, NZ) * 384 + c * 192, 192), 192), :]

    def dn_piece(e):
        return down_rows(wrap(z + NZ - e, NZ))

    gu_over_x = group(
        [remote(gu_piece(e, w), gu_piece(e, w), *pair_of(9), dev) for e in others for dev in xdev],
        9, wgu_all.at[0:432, 0:1152])
    dn_over_y = group(
        [remote(dn_piece(e), dn_piece(e), *pair_of(10), dev) for e in others for dev in ydev],
        10, wdn_all.at[0:432, :])
    o_over_y = [
        [remote(o_piece(e), o_piece(e), s["ss"].at[11], s["os"].at[d - 1], ydev[d - 1]) for e in others]
        for d in range(1, NY)]
    o_sent = remote(wo_all.at[0:432, 0:384], wo_all.at[0:432, 0:384], s["ss"].at[11], s["os"].at[0], sib)
    own_over_c = group(
        [remote(gu_piece(e, w), gu_piece(e, w), *pair_of(12), sib) for e in others], 12, wgu_all.at[0:432, 0:384])
    gu_over_c = group(
        [remote(gu_piece(e, wrap(w + d, NX)), gu_piece(e, wrap(w + d, NX)), *pair_of(13), sib)
         for e in others for d in range(1, NX)], 13, wgu_all.at[0:432, 0:1152])
    dn_over_c = group(
        [remote(dn_half(e), dn_half(e), *pair_of(14), sib) for e in others], 14, wdn_all.at[0:576, :])
    o_over_c = []
    for core, cols in enumerate((slice(0, 512), slice(512, 640))):
        o_over_c.append(
            group(
                [remote(wo_all.at[block_rows(e, 144), cols], wo_all.at[block_rows(e, 144), cols], *pair_of(15), sib)
                 for e in others], 15, wo_all.at[0:432, cols]))

    @pl.when(has_o)
    def _():
        for copies in o_over_y:
            for copy in copies:
                copy.start()

    begin(dn_over_y)
    begin(gu_over_x)
    begin(own_over_c)

    def earlier(d, carry):
        @pl.when(d == NZ - 1)
        def _():
            for dd in range(1, NY):
                from_y = wrap(y + NY - dd, NY)

                @pl.when(c * 4 + from_y < 5)
                def _(dd=dd):
                    remote(wo_all.at[0:432, 0:128], wo_all.at[0:432, 0:128], s["ss"].at[11], s["os"].at[dd - 1],
                           sib).wait_recv()

            for core in range(2):

                @pl.when(c == core)
                def _(core=core):
                    for copy in o_over_c[core][0]:
                        copy.start()

            dn_over_y[1].wait_recv()
            begin(dn_over_c)

        @pl.when(z >= d)
        def _():
            remote(kvs.at[z], kvs.at[z], s["kv_s"].at[d - 1], s["kv_r"].at[d - 1], sib).wait_recv()
            step(z - d)

        return carry

    lax.fori_loop(1, NZ, earlier, 0)

    for h in range(HEADS):
        ot_s[h] = ot_s[h] * (1.0 / l_s[h])
        lse[h] = m_s[h] + jnp.log(l_s[h])
    for t in range(5):
        top = ot_s[2 * t]
        bottom = ot_s[2 * t + 1] if 2 * t + 1 < HEADS else jnp.zeros((64, ROWS), F32)
        att[:, 128 * t : 128 * t + 128] = jnp.transpose(jnp.concatenate([top, bottom], axis=0)).astype(BF16)

    for core in range(2):

        @pl.when(c == core)
        def _(core=core):
            o_over_c[1 - core][1].wait_recv()

    for copy in own_done:
        copy.wait()
    wo = s["wo"]
    load_o = pltpu.make_async_copy(wo_all, wo, loc_sem.at[4])
    load_o.start()
    wgu, wds, w_sem = s["wgu"], s["wds"], s["w_sem"]

    def weights(i, slot):
        col = pl.multiple_of(wrap(w + i, 4) * 384, 384)
        return [
            pltpu.make_async_copy(
                wgu_all.at[:, pl.ds(col, 384)], wgu.at[slot, :, 0:384], w_sem.at[0, slot]),
            pltpu.make_async_copy(
                wgu_all.at[:, pl.ds(pl.multiple_of(col + FF, 384), 384)], wgu.at[slot, :, 384:768],
                w_sem.at[0, slot]),
            pltpu.make_async_copy(wdn_all.at[pl.ds(col, 384), :], wds.at[slot], w_sem.at[1, slot]),
        ]

    def weights_wait(slot):
        pltpu.make_async_copy(wgu_all.at[:, 0:768], wgu.at[slot], w_sem.at[0, slot]).wait()
        pltpu.make_async_copy(wdn_all.at[0:384, :], wds.at[slot], w_sem.at[1, slot]).wait()

    gu_over_z[1].wait_send()
    dn_over_z[1].wait_send()
    dn_over_c[1].wait_recv()
    own_over_c[1].wait_recv()
    for load in weights(0, 0):
        load.start()
    gu_over_x[1].wait_recv()
    begin(gu_over_c)

    ggu, gdn, go, gq, fin = s["ggu"], s["gdn"], s["go"], s["gq"], s["fin"]
    def columns(width):
        def at(cc, a, count):
            return (slice(None), pl.ds(pl.multiple_of((cc * 4 + a) * width, 128), count * width))

        return at

    def down_at(cc, a, count):
        return (pl.ds(pl.multiple_of((cc * 4 + a) * 48, 48), count * 48), slice(None))

    red_gu = Reduction(ggu, fin["gu"], columns(384), s["red_gu"], 0, False)
    red_dn = Reduction(gdn, fin["dn"], down_at, s["red_dn"], 1, True)
    red_o = Reduction(go, fin["o"], columns(128), s["red_o"], 0, False)
    red_q = TileReduction(gq, fin["q"], s["red_q"])
    vecs = VectorSum(s["vecs"])
    cot, gh, n2, n2t, gn2t = s["cot"], s["gh"], s["n2"], s["n2t"], grad_in
    do_in, dot_in, delta_in, gain_row = s["do"], s["dot"], s["delta"], s["gain_row"]
    dqt, own_kv, skv, rkv = ot_s, s["own_kv"], s["skv"], s["rkv"]

    gn2t[...] = jnp.zeros_like(gn2t)
    load_o.wait()
    hid = gh[...] + dot(att[:, 0:576], wo[:, 0:576])
    inv_two = lax.rsqrt(jnp.mean(hid * hid, axis=-1, keepdims=True) + EPS)
    normed = hid * inv_two * gain_two
    n2[...] = normed.astype(BF16)
    n2t[...] = jnp.transpose(normed).astype(BF16)
    gh[...] = hid
    block_out[...] = jnp.transpose(hid)

    def chunk(i, carry):
        slot = lax.rem(i, 2)
        here = wrap(w + i, 4)
        weights_wait(slot)

        @pl.when(jnp.logical_and(i > 0, i < 3))
        def _():
            for load in weights(i + 1, 1 - slot):
                load.start()

        both = dot(n2[...], wgu[slot])
        gate, up = both[:, 0:384], both[:, 384:768]
        sg = jax.nn.sigmoid(gate)
        silu = gate * sg
        act = (silu * up).astype(BF16)
        ga = dot(cot[...], wds[slot], 1, 1)
        gg = (ga * up * sg * (1.0 + gate * (1.0 - sg))).astype(BF16)
        gu = (ga * silu).astype(BF16)
        grads = jnp.concatenate([gg, gu], axis=1)
        both = dot(n2t[...], grads).astype(BF16)
        ggu[0, here] = both[:, 0:384].reshape(NZ, 144, 384)
        ggu[1, here] = both[:, 384:768].reshape(NZ, 144, 384)
        red_gu.core_copy(here).start()
        down = dot(act, cot[...], 0, 0).astype(BF16)
        for p in range(8):
            gdn[p // 4, here, p % 4] = down[48 * p : 48 * p + 48, :]
        red_dn.core_copy(here).start()

        @pl.when(i == 0)
        def _():
            gu_over_c[1].wait_recv()
            for load in weights(1, 1):
                load.start()

        @pl.when(i > 0)
        def _():
            red_gu.core_add(wrap(w + i + 3, 4))
            red_gu.first_piece(wrap(w + i + 3, 4))

        block_out[...] += lax.dot_general(wds[slot], act, (((0,), (1,)), ((), ())), preferred_element_type=F32)
        gn2t[...] += dot(wgu[slot], grads, 1, 1)

        return carry

    lax.fori_loop(0, 4, chunk, 0)

    red_dn.core_all(red_dn.core_add)
    red_dn.first_start()
    red_gu.core_add(wrap(w + 3, 4))
    red_gu.first_piece(wrap(w + 3, 4))
    state_loads = []
    for i in range(1, 3):
        for k in range(4):
            copy = pltpu.make_async_copy(states[i][k], new_states[i][k], s["st_sem"].at[i, k])
            copy.start()
            state_loads.append(copy)

    @pl.when(always)
    def _():
        hid = gh[...]
        inv_two = lax.rsqrt(jnp.mean(hid * hid, axis=-1, keepdims=True) + EPS)
        u = hid * inv_two
        e = jnp.transpose(gn2t[...])
        f = e * gain_two
        gain_row[:, 0:576] = jnp.sum(e * u, axis=0, keepdims=True)
        gain_row[:, 576:640] = jnp.zeros((1, 64), F32)
        grad_hidden = cot[...].astype(F32) + inv_two * (f - u * jnp.mean(f * u, axis=-1, keepdims=True))
        gh[...] = grad_hidden
        ghl = grad_hidden.astype(BF16)
        grad_out = dot(att[:, 0:576], ghl, 0, 0).astype(BF16)
        for p in range(8):
            if p < 4:
                part = grad_out[:, 128 * p : 128 * p + 128]
            elif p == 4:
                part = jnp.concatenate([grad_out[:, 512:576], jnp.zeros((D, 64), BF16)], axis=1)
            else:
                part = jnp.zeros((D, 128), BF16)
            go[p // 4, p % 4] = part.reshape(NZ, 144, 128)
        red_o.core_all(lambda k: red_o.core_copy(k).start())
        gm = dot(ghl, wo[:, 0:576], 1, 1).astype(BF16).astype(F32)
        gm = jnp.concatenate([gm, jnp.zeros((ROWS, 64), F32)], axis=1)
        for h in range(HEADS):
            part = gm[:, 128 * (h // 2) : 128 * (h // 2) + 128]
            part = part if h % 2 == 1 else turn(part)
            part = jnp.where(low_lanes(part), 0.0, part)
            do_in[h] = part.astype(BF16)
            part = jnp.transpose(part)
            dot_in[h] = part.astype(BF16)
            delta_in[h] = jnp.sum(part[64:128, :] * ot_s[h], axis=0, keepdims=True)

    def attend(g, j):
        kv = kvs[j, g]
        kt = jnp.transpose(kv.astype(F32)).astype(BF16)[0:64, :]
        totals = [None, None]
        for i in range(GROUP):
            h = g * GROUP + i
            dq = None
            for half in range(2):
                rows = slice(256 * half, 256 * half + 256)
                pt = jnp.exp(dot(kv[rows], qt_s[h]) - lse[h])
                dst = (pt * (dot(kv[rows], dot_in[h]) - delta_in[h])).astype(BF16)
                both = dot(dst, q_s[h]) + dot(pt.astype(BF16), do_in[h])
                totals[half] = both if i == 0 else totals[half] + both
                part = dot(kt[:, rows], dst)
                dq = part if half == 0 else dq + part
            dqt[h] += dq
        return totals

    def attend_own(g):
        keep_a, keep_b = visible(512), visible(256)
        kv = kvs[z, g]
        kt = jnp.transpose(kv.astype(F32)).astype(BF16)[0:64, :]
        left = slice(0, 256)
        totals = [None, None]
        for i in range(GROUP):
            h = g * GROUP + i
            pt = jnp.where(keep_a, jnp.exp(dot(kv[left], qt_s[h]) - lse[h]), 0.0)
            dst = (pt * (dot(kv[left], dot_in[h]) - delta_in[h])).astype(BF16)
            both = dot(dst, q_s[h]) + dot(pt.astype(BF16), do_in[h])
            totals[0] = both if i == 0 else totals[0] + both
            dq = dot(kt[:, left], dst)
            pt = jnp.where(keep_b, jnp.exp(dot(kv[right], qt_s[h, :, right]) - lse[h, :, right]), 0.0)
            dst = (pt * (dot(kv[right], dot_in[h, :, right]) - delta_in[h, :, right])).astype(BF16)
            both = dot(dst, q_s[h, right]) + dot(pt.astype(BF16), do_in[h, right])
            totals[1] = both if i == 0 else totals[1] + both
            dqt[h] += dq
            dqt[h, :, right] += dot(kt[:, right], dst)
        own_kv[g, left] = totals[0]
        own_kv[g, right] = totals[1]

    def kv_copy(g, k, dev):
        return remote(
            skv.at[g, k - 1], rkv.at[g, k - 1], s["ss"].at[16], s["dkv_r"].at[g], dev)

    gps = q_s

    def kv_wait(g):
        for count in range(1, NZ):

            @pl.when(z + count == NZ - 1)
            def _(count=count):
                part = rkv.at[g, 0:count]
                remote(part, part, s["ss"].at[16], s["dkv_r"].at[g], sib).wait_recv()
                total = own_kv[g]
                for k in range(count):
                    total = total + rkv[g, k].astype(F32)
                own_kv[g] = total

    def group_tiles(g):
        cos_t, sin_t = s["cos"][...], s["sin"][...]
        low = low_lanes(cos_t)
        kv = own_kv[g]

        def query(top, bottom):
            both = [dqt[h] if h is not None else jnp.zeros((64, ROWS), F32) for h in (top, bottom)]
            return jnp.transpose(jnp.concatenate(both, axis=0)) * (HEAD_DIM ** -0.5)

        def back(t):
            return t * cos_t - swap_halves(t) * sin_t

        if g == 0:
            return {
                0: back(query(0, 1)),
                1: back(jnp.where(low, query(2, None), turn(kv))),
                2: jnp.where(low, turn(kv), 0.0),
            }
        if g == 1:
            return {
                2: jnp.where(low, 0.0, back(query(None, 3))),
                3: back(query(4, 5)),
                4: jnp.where(low, back(kv), kv),
            }
        return {
            5: back(query(6, 7)),
            6: back(jnp.where(low, query(8, None), turn(kv))),
            7: jnp.where(low, turn(kv), 0.0),
        }

    def tiles_of(g):
        @pl.when(always)
        def _():
            for t, tile in group_tiles(g).items():
                if t == 2 and g == 0:
                    gps[2] = tile.astype(BF16)
                    continue
                if t == 2:
                    tile = tile + gps[2].astype(F32)
                low_tile = tile.astype(BF16)
                gps[t] = low_tile
                gq[t] = dot(n1t[...], low_tile).astype(BF16).reshape(NZ, 144, 128)

        red_q.core_start((READY[g]))

    dqt[...] = jnp.zeros_like(dqt)
    early = red_q.tile <= 4
    late = red_q.tile > 4
    own_one = jnp.where(z == NZ - 1, 9, 3)
    own_two = jnp.where(z == NZ - 1, 10, 6)

    def slot(t, carry):
        g = lax.div(t, 3)
        k = 3 - lax.rem(t, 3)

        @pl.when(jnp.logical_and(t < 9, z >= k))
        def _():
            for half, total in enumerate(attend(g, z - k)):
                skv[g, k - 1, 256 * half : 256 * half + 256] = total.astype(BF16)
            kv_copy(g, k, device(x, y, c, z - k)).start()

        @pl.when(jnp.logical_or(t == 2, jnp.logical_or(t == own_one, t == own_two)))
        def _():
            attend_own(jnp.where(t == 2, 0, jnp.where(t == own_one, 1, 2)))

        @pl.when(t == 0)
        def _():
            red_o.core_all(red_o.core_add)

        @pl.when(t == 2)
        def _():
            red_gu.first_sum()
            red_gu.z_start()
            red_o.first_start()

        @pl.when(t == 4)
        def _():
            kv_wait(0)
            tiles_of(0)

        @pl.when(t == 5)
        def _():
            red_q.core_add(READY[0])
            red_q.first_start(READY[0])
            red_gu.z_sum()
            red_gu.exchange_start()

        @pl.when(t == 9)
        def _():
            kv_wait(1)
            tiles_of(1)
            red_dn.first_sum()
            red_o.first_sum()
            red_q.core_add(READY[1])
            red_q.first_start(READY[1])
            red_gu.gather_start()

        return carry

    lax.fori_loop(0, 11, slot, 0)
    kv_wait(2)
    red_dn.z_start()
    red_o.z_start()
    tiles_of(2)
    low = low_lanes(s["cos"][...])

    def halves(t):
        tile = gps[t].astype(F32)
        return tile, turn(tile)

    (t0, _), (t1, u1), (t2, u2), (t3, u3) = [halves(t) for t in range(4)]
    (t4, u4), (t5, _), (t6, u6), (t7, _) = [halves(t) for t in range(4, 8)]
    ordered = [
        t0,
        jnp.where(low, t1, t2),
        t3,
        t5,
        jnp.where(low, t6, t1),
        jnp.where(low, t4, t6),
        jnp.where(low, t2, t4),
        t7,
    ]
    vecs.rc[0, 10:18, :] = jnp.concatenate(
        [jnp.sum(t, axis=0, keepdims=True) for t in ordered], axis=0)
    gn1 = dot(jnp.concatenate([t.astype(BF16) for t in ordered], axis=1), wq_v[...], 1, 1)
    inputs = jnp.transpose(tok_t[...].astype(F32))
    r = lax.rsqrt(jnp.mean(inputs * inputs, axis=-1, keepdims=True) + EPS)
    u = inputs * r
    f = gn1 * gain_one
    row = jnp.sum(gn1 * u, axis=0, keepdims=True)
    row = jnp.concatenate([row, jnp.zeros((1, 64), F32)], axis=1)
    for t in range(5):
        vecs.rc[0, t : t + 1, :] = row[:, 128 * t : 128 * t + 128]
        vecs.rc[0, 5 + t : 6 + t, :] = gain_row[:, 128 * t : 128 * t + 128]
    vecs.rc[0, 18:24, :] = jnp.zeros((6, 128), F32)
    vecs.start()
    red_q.core_add(READY[2])
    red_q.first_start(READY[2])
    vecs.next(0)

    @pl.when(early)
    def _():
        red_q.first_sum()
        red_q.z_start()

    grad_in[...] = jnp.transpose(gh[...] + r * (f - u * jnp.mean(f * u, axis=-1, keepdims=True)))

    def update(k, grad):
        new = adam_step(
            new_states[0][k][...], new_states[1][k][...], new_states[2][k][...], grad, RATE_MATRIX, DECAY_MATRIX)
        for i in range(3):
            new_states[i][k][...] = new[i]

    red_gu.gather_forward()
    @pl.when(late)
    def _():
        red_q.first_sum()
        red_q.z_start()

    vecs.next(1)
    red_dn.z_sum()
    red_dn.exchange_start()
    red_o.z_sum()
    red_o.exchange_start()

    @pl.when(early)
    def _():
        red_q.z_sum()
        red_q.exchange_start()

    @pl.when(late)
    def _():
        red_q.z_sum()
        red_q.exchange_start()

    red_dn.gather_start()
    red_o.gather_start()

    for load in state_loads:
        load.wait()
    red_gu.gather_wait()
    update(2, fin["gu"][...].astype(F32))
    @pl.when(early)
    def _():
        red_q.gather_start()

    vecs.next(2)

    @pl.when(late)
    def _():
        red_q.gather_start()

    red_dn.gather_forward()
    red_o.gather_forward()
    red_dn.gather_wait()
    update(3, jnp.transpose(fin["dn"][...].astype(F32)))
    red_o.gather_wait()
    update(1, fin["o"][:, 0:576].astype(F32))
    total = vecs.next(3)
    total = jnp.concatenate([total[t : t + 1, :] for t in range(18)], axis=1)
    pad = jnp.zeros((1, VW - 640), F32)
    flat = jnp.concatenate([total[:, 0:640], pad], axis=1)
    mid = jnp.concatenate([total[:, 640:1280], pad], axis=1)
    flat = flat + pltpu.roll(jnp.broadcast_to(mid, (8, VW)), 576, 1)[0:1, :]
    flat = flat + jnp.concatenate(
        [jnp.zeros((1, 1152), F32), total[:, 1280:2304], jnp.zeros((1, 128), F32)], axis=1)
    shift = lax.rem(VW - z * 528, VW)
    grad = pltpu.roll(jnp.broadcast_to(flat, (8, VW)), shift, 1)[0:1, 0:528]
    for load in vector_loads[1:]:
        load.wait()
    new = adam_step(*[v[...].reshape(1, 528) for v in new_vectors], grad, RATE_VECTOR, 0.0)
    for i in range(3):
        new_vectors[i][...] = new[i].reshape(528)
    red_q.gather_wait()
    tq = [fin["q"][:, 128 * t : 128 * t + 128].astype(F32) for t in range(8)]
    lowq = low_lanes(tq[0])
    ordered = [
        tq[0],
        jnp.where(lowq, tq[1], tq[2]),
        tq[3],
        tq[5],
        jnp.where(lowq, tq[6], tq[1]),
        jnp.where(lowq, tq[4], tq[6]),
        jnp.where(lowq, tq[2], tq[4]),
        tq[7],
    ]
    update(0, jnp.concatenate(ordered, axis=1)[:, 0:960])
    for red in (red_gu, red_dn, red_o):
        red.finish()
    red_q.finish()
    vecs.finish()
    for whole in sent:
        whole.wait_send()
    for count in range(1, NZ):

        @pl.when(z == count)
        def _(count=count):
            part = (skv.at[0], skv.at[0:2], skv)[count - 1]
            remote(part, part, s["ss"].at[16], s["dkv_r"].at[0], sib).wait_send()

    for d in range(1, NZ):

        @pl.when(z + d < NZ)
        def _(d=d):
            kv_sends[d - 1].wait_send()

    @pl.when(has_o)
    def _():
        o_over_z[1].wait_send()
        o_sent.wait_send()

    for core in range(2):

        @pl.when(c == core)
        def _(core=core):
            o_over_c[core][1].wait_send()

    @pl.when(c == 0)
    def _():
        for batch in (q_over_z, q_over_x, q_over_c):
            batch[1].wait_send()


MATRICES = ((144, 960), (144, D), (144, 2 * FF), (D, 384))


def train(tok_t, cot_t, cos_t, sin_t, vstates, states):
    sd = jax.ShapeDtypeStruct
    v = pl.BlockSpec(memory_space=VM)
    a = pl.BlockSpec(memory_space=ANY)
    dma = pltpu.SemaphoreType.DMA
    scratch = dict(
        wq=VM((D, QW), BF16), vec=VM((NZ, 1, VW), F32), cos=VM((ROWS, 128), F32), sin=VM((ROWS, 128), F32),
        b_out=VM((144, OW), BF16),
        q=VM((HEADS, ROWS, 128), BF16), qt=VM((HEADS, 128, ROWS), BF16), n1t=VM((D, ROWS), BF16),
        kv=VM((NZ, KV_HEADS, ROWS, 128), BF16),
        m=VM((HEADS, 1, ROWS), F32), l=VM((HEADS, 1, ROWS), F32), ot=VM((HEADS, 64, ROWS), F32),
        lse=VM((HEADS, 1, ROWS), F32), att=VM((ROWS, 640), BF16), wo=VM((D, OW), BF16),
        loc=dma((8,)), v_sem=dma((3,)), tok=VM((D, ROWS), BF16), ss=dma((17,)), rs=dma((16,)), os=dma((3,)), kv_s=dma((3,)), kv_r=dma((3,)),
        cot=VM((ROWS, D), BF16), gh=VM((ROWS, D), F32), n2=VM((ROWS, D), BF16), n2t=VM((D, ROWS), BF16),
        wgu=VM((2, D, 768), BF16), wds=VM((2, 384, D), BF16), w_sem=dma((2, 2)),
        do=VM((HEADS, ROWS, 128), BF16), dot=VM((HEADS, 128, ROWS), BF16), delta=VM((HEADS, 1, ROWS), F32),
        gain_row=VM((1, 640), F32),
        ggu=VM((2, 4, NZ, 144, 384), BF16), gdn=VM((2, NZ, 4, 48, D), BF16), go=VM((2, 4, NZ, 144, 128), BF16),
        gq=VM((8, NZ, 144, 128), BF16),
        fin=dict(gu=VM((144, 2 * FF), BF16), dn=VM((384, D), BF16), o=VM((144, QW), BF16), q=VM((144, QW), BF16)),
        own_kv=VM((KV_HEADS, ROWS, 128), F32),
        skv=VM((KV_HEADS, 3, ROWS, 128), BF16), rkv=VM((KV_HEADS, 3, ROWS, 128), BF16),
        dkv_r=dma((3,)), st_sem=dma((3, 4)),
        red_gu=Reduction.scratch((4, 4), 144, 384), red_dn=Reduction.scratch((4, 4), 48, D),
        red_o=Reduction.scratch((4, 4), 144, 128), red_q=TileReduction.scratch(),
        vecs=VectorSum.scratch(),
    )
    fast = lambda shape: VM(shape, F32)
    return pl.pallas_call(
        step_kernel,
        out_shape=(
            fast((D, ROWS)),
            fast((D, ROWS)),
            [[fast(shape) for shape in MATRICES] for _ in range(3)],
            [fast((528,)) for _ in range(3)],
            pltpu.HBM((D, OW), BF16),
            pltpu.HBM((D, 2 * FF), BF16),
            pltpu.HBM((FF, D), BF16),
        ),
        in_specs=[a, a, a, a, [a] * 3, [[a] * 4] * 3],
        out_specs=(v, v, [[v] * 4] * 3, [v] * 3, a, a, a),
        scratch_shapes=[scratch],
        compiler_params=pltpu.CompilerParams(
            collective_id=0, has_side_effects=True, vmem_limit_bytes=51 << 20),
        name="train_step",
    )(tok_t, cot_t, cos_t, sin_t, vstates, states)


def adam_step(weight, first_state, second_state, gradient, learn_rate, decay_rate):
    first_new = BETA_ONE * first_state + (1.0 - BETA_ONE) * gradient
    second_new = BETA_TWO * second_state + (1.0 - BETA_TWO) * gradient * gradient
    corr_one = 1.0 - BETA_ONE**STEP
    corr_two = 1.0 - BETA_TWO**STEP
    update = first_new / corr_one / (jnp.sqrt(second_new / corr_two) + ADAM_EPS)
    weight_new = weight - learn_rate * (update + decay_rate * weight)
    return (weight_new, first_new, second_new)


def store_kernel(sources, *rest):
    targets, sems = rest[:-1], rest[-1]
    copies = [
        pltpu.make_async_copy(a, b, sems.at[k])
        for k, (a, b) in enumerate(zip(jax.tree.leaves(sources), jax.tree.leaves(targets)))]
    for copy in copies:
        copy.start()
    for copy in copies:
        copy.wait()


def store(arrays):
    shapes = jax.tree.map(lambda t: jax.ShapeDtypeStruct(t.shape, t.dtype), arrays)
    count = len(jax.tree.leaves(arrays))
    v = pl.BlockSpec(memory_space=VM)
    a = pl.BlockSpec(memory_space=ANY)
    return pl.pallas_call(
        store_kernel,
        out_shape=shapes,
        in_specs=[jax.tree.map(lambda t: v, arrays)],
        out_specs=jax.tree.map(lambda t: a, arrays),
        scratch_shapes=[pltpu.SemaphoreType.DMA((count,))],
        compiler_params=pltpu.CompilerParams(vmem_limit_bytes=8 << 20),
        name="store",
    )(arrays)


def per_device(
    tokens, cotangent, w_qkv, w_out, w_gate_up, w_down, vectors,
    first_qkv, first_out, first_gate_up, first_down, first_vectors,
    second_qkv, second_out, second_gate_up, second_down, second_vectors,
):
    cos_np, sin_np = rope_tables()
    cos_t, sin_t = jnp.asarray(cos_np), jnp.asarray(sin_np)
    states = [
        [w_qkv, w_out, w_gate_up, w_down.T],
        [first_qkv, first_out, first_gate_up, first_down.T],
        [second_qkv, second_out, second_gate_up, second_down.T],
    ]
    vstates = [vectors, first_vectors, second_vectors]
    outs = train(
        tokens.T, cotangent.T, cos_t, sin_t, vstates, states)
    block_t, grad_t, matrices, vecs = store(tuple(outs[0:4]))
    out = [block_t.T, grad_t.T]
    for i in range(3):
        out += list(matrices[i][0:3]) + [matrices[i][3].T, vecs[i]]
    return tuple(out)


def solution(mesh):
    tokens = P(("dp", "ctx"), None)
    state = (P("ctx", None),) * 4 + (P("ctx"),)
    return jax.shard_map(
        per_device, mesh=mesh, in_specs=(tokens, tokens) + state * 3, out_specs=(tokens, tokens) + state * 3,
        check_vma=False,
    )
```

```python
import functools

import jax
import jax.numpy as jnp
import numpy as np
from jax import lax
from jax.experimental import pallas as pl
from jax.experimental.pallas import tpu as pltpu
from jax.sharding import PartitionSpec as P

D = 576
HEADS = 9
KV_HEADS = 3
GROUP = 3
HEAD_DIM = 64
FF = 1536
STEP = 10
LEN = 2048
ROWS = 512
QW = 1024
OW = 640
VW = 2304
NX = 4
NY = 4
NZ = 4

EPS = 1e-05
ROPE_BASE = 100000.0
MASK_FILL = -1e30
BETA_ONE = 0.9
BETA_TWO = 0.999
ADAM_EPS = 1e-08
RATE_MATRIX = 0.05
RATE_VECTOR = 0.5
DECAY_MATRIX = 0.1

F32 = jnp.float32
BF16 = jnp.bfloat16
MESH = pl.DeviceIdType.MESH
VM = pltpu.VMEM
ANY = pl.ANY


def rope_tables():
    half = HEAD_DIM // 2
    exponent = np.arange(half, dtype=np.float32) * np.float32(2.0 / HEAD_DIM)
    inverse = (np.float64(ROPE_BASE) ** (-exponent.astype(np.float64))).astype(np.float32)
    angles = np.arange(LEN, dtype=np.float32)[:, None] * inverse[None, :]
    cosine = np.cos(angles.astype(np.float64)).astype(np.float32)
    sine = np.sin(angles.astype(np.float64)).astype(np.float32)
    cos_all = np.concatenate([cosine] * 4, axis=1)
    sin_all = np.concatenate([-sine, sine, -sine, sine], axis=1)
    return cos_all, sin_all


def dot(a, b, ca=1, cb=0):
    return lax.dot_general(a, b, (((ca,), (cb,)), ((), ())), preferred_element_type=F32)


def place():
    dp = lax.axis_index("dp")
    z = lax.axis_index("ctx")
    x = lax.div(dp, NY * 2)
    y = lax.rem(lax.div(dp, 2), NY)
    c = lax.rem(dp, 2)
    return x, y, c, z


def device(x, y, c, z):
    return (x * (NY * 2) + y * 2 + c, z)


def wrap(i, n):
    return lax.rem(i, n)


def remote(src, dst, ssem, rsem, dev):
    return pltpu.make_async_remote_copy(
        src_ref=src, dst_ref=dst, send_sem=ssem, recv_sem=rsem, device_id=dev, device_id_type=MESH
    )


def greet(peers):
    barrier = pltpu.get_barrier_semaphore()
    for peer in peers:
        pl.semaphore_signal(barrier, inc=1, device_id=peer, device_id_type=MESH)
    pl.semaphore_wait(barrier, len(peers))


def swap_halves(v):
    width = v.shape[1]
    lane = lax.broadcasted_iota(jnp.int32, v.shape, 1)
    down = pltpu.roll(v, width - 32, 1)
    up = pltpu.roll(v, 32, 1)
    return jnp.where(lax.rem(lane, 64) < 32, down, up)


def low_lanes(v):
    lane = lax.broadcasted_iota(jnp.int32, v.shape, 1)
    return lane < 64


class Reduction:
    @staticmethod
    def scratch(lead, r, w):
        dma = pltpu.SemaphoreType.DMA
        return [
            VM(lead + (r, w), BF16), VM((3, 4, r, w), BF16), VM((4, r, w), BF16),
            VM((3, r, w), BF16), VM((4, r, w), BF16), dma((6,)), dma((10,)),
        ]

    def __init__(self, own, fin, fin_at, bufs, swap, z_first):
        self.own, self.fin, self.fin_at, self.z_first = own, fin, fin_at, z_first
        self.rc, self.r1, self.s1, self.r2, self.r3, self.ss, self.rs = bufs
        x, y, c, z = place()
        self.c, self.z = c, z
        flip = c != swap
        self.a, self.b = jnp.where(flip, y, x), jnp.where(flip, x, y)
        self.at = lambda a, b, cc, zz: device(jnp.where(flip, b, a), jnp.where(flip, a, b), cc, zz)
        self.other = self.at(self.a, self.b, 1 - c, z)

    def copy(self, src, dst, k, dev, into=None):
        return remote(src, dst, self.ss.at[k], self.rs.at[k if into is None else into], dev)

    def whole(self, ref, k):
        return self.copy(ref, ref, k, self.other)

    def mine(self, a, z):
        return (self.c, z, a) if self.z_first else (self.c, a, z)

    def all_z(self, a):
        return self.own.at[self.c, :, a] if self.z_first else self.own.at[self.c, a]

    def core_copy(self, k):
        return self.copy(self.own.at[1 - self.c, k], self.rc.at[k], 0, self.other, 6 + k)

    def core_add(self, k):
        self.core_copy(k).wait_recv()

        def add(j, carry):
            self.own[self.c, k, j] = self.own[self.c, k, j] + self.rc[k, j]
            return carry

        lax.fori_loop(0, 4, add, 0)

    def core_all(self, act):
        def one(k, carry):
            act(k)
            return carry

        lax.fori_loop(0, 4, one, 0)

    def first_copy(self, d):
        to = wrap(self.a + d, 4)
        return self.copy(self.all_z(to), self.r1.at[d - 1], 1, self.at(to, self.b, self.c, self.z))

    def first_start(self):
        for d in range(1, 4):
            self.first_copy(d).start()

    def first_piece(self, piece):
        d = wrap(piece + 4 - self.a, 4)

        @pl.when(d > 0)
        def _():
            self.first_copy(jnp.maximum(d, 1)).start()

    def first_sum(self):
        self.whole(self.r1, 1).wait_recv()

        def add(j, carry):
            total = self.own[self.mine(self.a, j)].astype(F32) + self.r1[0, j].astype(F32)
            total = total + self.r1[1, j].astype(F32) + self.r1[2, j].astype(F32)
            self.s1[j] = total.astype(BF16)
            return carry

        lax.fori_loop(0, 4, add, 0)

    def z_start(self):
        for d in range(1, 4):
            to = wrap(self.z + d, 4)
            self.copy(self.s1.at[to], self.r2.at[d - 1], 2, self.at(self.a, self.b, self.c, to)).start()

    def z_sum(self):
        self.whole(self.r2, 2).wait_recv()
        total = self.s1[self.z].astype(F32) + self.r2[0].astype(F32)
        total = total + self.r2[1].astype(F32) + self.r2[2].astype(F32)
        self.r3[self.b] = total.astype(BF16)

    def exchange_start(self):
        for d in range(1, 4):
            to = wrap(self.b + d, 4)
            ref = self.r3.at[self.b]
            self.copy(ref, ref, 3, self.at(self.a, to, self.c, self.z)).start()

    def gather_start(self):
        self.whole(self.r3.at[0:3], 3).wait_recv()
        total = self.r3[0].astype(F32) + self.r3[1].astype(F32)
        total = total + self.r3[2].astype(F32) + self.r3[3].astype(F32)
        where = self.fin_at(self.c, self.a, 1)
        self.fin[where] = total.astype(BF16)
        ref = self.fin.at[where]
        for d in range(1, 4):
            self.copy(ref, ref, 4, self.at(wrap(self.a + d, 4), self.b, self.c, self.z)).start()

    def gather_forward(self):
        self.whole(self.fin.at[self.fin_at(0, 0, 3)], 4).wait_recv()
        ref = self.fin.at[self.fin_at(self.c, 0, 4)]
        self.copy(ref, ref, 5, self.other).start()

    def gather_wait(self):
        self.whole(self.fin.at[self.fin_at(0, 0, 4)], 5).wait_recv()

    def finish(self):
        for ref, k in (
            (self.rc, 0), (self.r1, 1), (self.r2, 2), (self.r3.at[0:3], 3),
            (self.fin.at[self.fin_at(0, 0, 3)], 4), (self.fin.at[self.fin_at(0, 0, 4)], 5),
        ):
            self.whole(ref, k).wait_send()


class VectorSum:
    SCRATCH = 4

    @staticmethod
    def scratch():
        dma = pltpu.SemaphoreType.DMA
        return [VM((2, 24, 128), F32), VM((3, 4, 24, 128), F32), dma((4,)), dma((4,))]

    def __init__(self, bufs):
        self.rc, self.r, self.ss, self.rs = bufs
        x, y, c, z = place()
        self.sibling = device(x, y, 1 - c, z)

    def copy(self, src, dst, k, dev):
        return remote(src, dst, self.ss.at[k], self.rs.at[k], dev)

    def stage(self, k):
        ref = self.rc.at[1] if k == 0 else self.r.at[k - 1, 0:3]
        return self.copy(ref, ref, k, self.sibling)

    def start(self):
        self.copy(self.rc.at[0], self.rc.at[1], 0, self.sibling).start()

    def next(self, k):
        x, y, c, z = place()
        self.stage(k).wait_recv()
        if k == 0:
            total = self.rc[0] + self.rc[1]
        else:
            total = self.r[k - 1, 0] + self.r[k - 1, 1] + self.r[k - 1, 2] + self.r[k - 1, 3]
        if k == 3:
            return total
        me = (y, z, x)[k]
        self.r[k, me] = total
        for d in range(1, 4):
            to = wrap(me + d, 4)
            dev = (device(x, to, c, z), device(x, y, c, to), device(to, y, c, z))[k]
            self.copy(self.r.at[k, me], self.r.at[k, me], k + 1, dev).start()
        return None

    def finish(self):
        for k in range(4):
            self.stage(k).wait_send()


READY = ((0, 1), (2, 3, 4), (5, 6, 7))
TILE_A = (0, 1, 2, 3, 3, 0, 1, 2)


class TileReduction:
    @staticmethod
    def scratch():
        dma = pltpu.SemaphoreType.DMA
        return [
            VM((4, NZ, 144, 128), BF16), VM((3, NZ, 144, 128), BF16), VM((NZ, 144, 128), BF16),
            VM((3, 144, 128), BF16), VM((4, 144, 128), BF16), dma((5,)), dma((8,)),
        ]

    def __init__(self, own, fin, bufs):
        self.own, self.fin = own, fin
        self.rc, self.r1, self.s1, self.r2, self.r3, self.ss, self.rs = bufs
        self.x, self.y, self.c, self.z = place()
        self.flip = self.c == 1
        self.a, self.b = jnp.where(self.flip, self.y, self.x), jnp.where(self.flip, self.x, self.y)
        last = jnp.where(self.a == 3, 4, 5 + self.a)
        self.tile = jnp.where(self.c == lax.rem(self.a + 1, 2), self.a, last)

    def at(self, a, b, z, core=None):
        core = self.c if core is None else core
        return device(jnp.where(self.flip, b, a), jnp.where(self.flip, a, b), core, z)

    def whole(self, ref, k):
        return remote(
            ref, ref, self.ss.at[k], self.rs.at[3 + k], device(self.x, self.y, 1 - self.c, self.z))

    def core_copy(self, t):
        return remote(
            self.own.at[t], self.rc.at[t // 2], self.ss.at[0], self.rs.at[t // 2],
            device(self.x, self.y, 1 - self.c, self.z))

    def core_start(self, tiles):
        for t in tiles:

            @pl.when(self.c == t % 2)
            def _(t=t):
                self.core_copy(t).start()

    def core_add(self, tiles):
        for t in tiles:

            @pl.when(self.c != t % 2)
            def _(t=t):
                self.core_copy(t).wait_recv()
                for j in range(NZ):
                    self.own[t, j] = self.own[t, j] + self.rc[t // 2, j]

    def first_start(self, tiles):
        for t in tiles:
            to = TILE_A[t]

            @pl.when(jnp.logical_and(self.c != t % 2, self.a != to))
            def _(t=t, to=to):
                k = jnp.maximum(wrap(to + NX - self.a, NX) - 1, 0)
                remote(
                    self.own.at[t], self.r1.at[k], self.ss.at[1], self.rs.at[4],
                    self.at(to, self.b, self.z)).start()

    def first_sum(self):
        self.whole(self.r1, 1).wait_recv()
        for j in range(NZ):
            total = self.own[self.tile, j].astype(F32) + self.r1[0, j].astype(F32)
            total = total + self.r1[1, j].astype(F32) + self.r1[2, j].astype(F32)
            self.s1[j] = total.astype(BF16)

    def z_start(self):
        for d in range(1, NZ):
            to = wrap(self.z + d, NZ)
            remote(
                self.s1.at[to], self.r2.at[d - 1], self.ss.at[2], self.rs.at[5],
                device(self.x, self.y, self.c, to)).start()

    def z_sum(self):
        self.whole(self.r2, 2).wait_recv()
        total = self.s1[self.z].astype(F32) + self.r2[0].astype(F32)
        total = total + self.r2[1].astype(F32) + self.r2[2].astype(F32)
        self.r3[self.b] = total.astype(BF16)

    def exchange_start(self):
        ref = self.r3.at[self.b]
        for d in range(1, NY):
            remote(ref, ref, self.ss.at[3], self.rs.at[6],
                   self.at(self.a, wrap(self.b + d, NY), self.z)).start()

    def gather_start(self):
        self.whole(self.r3.at[0:3], 3).wait_recv()
        total = self.r3[0].astype(F32) + self.r3[1].astype(F32)
        total = total + self.r3[2].astype(F32) + self.r3[3].astype(F32)
        where = (slice(None), pl.ds(pl.multiple_of(self.tile * 128, 128), 128))
        self.fin[where] = total.astype(BF16)
        ref = self.fin.at[where]
        for e in range(2):
            for d in range(NX):
                if e or d:
                    remote(ref, ref, self.ss.at[4], self.rs.at[7],
                           self.at(wrap(self.a + d, 4), self.b, self.z, wrap(self.c + e, 2))).start()

    def gather_wait(self):
        self.whole(self.fin.at[:, 0:896], 4).wait_recv()

    def finish(self):
        for ref, k in (
            (self.rc, 0), (self.r1, 1), (self.r2, 2), (self.r3.at[0:3], 3), (self.fin.at[:, 0:896], 4),
        ):
            self.whole(ref, k).wait_send()


def step_kernel(
    tok_hbm, cot_hbm, cos_hbm, sin_hbm, vstates, states,
    block_out, grad_in, new_states, new_vectors, wgu_all, wdn_all, s,
):
    x, y, c, z = place()
    sib = device(x, y, 1 - c, z)
    zdev = [device(x, y, c, wrap(z + d, NZ)) for d in range(1, NZ)]
    xdev = [device(wrap(x + d, NX), y, c, z) for d in range(1, NX)]
    ydev = [device(x, wrap(y + d, NY), c, z) for d in range(1, NY)]
    peers = [sib] + xdev + ydev + zdev
    for d in range(1, 4):
        peers.append(device(wrap(x + d, NX), y, 1 - c, z))
        peers.append(device(x, wrap(y + d, NY), 1 - c, z))
    barrier = pltpu.get_barrier_semaphore()
    for peer in peers:
        pl.semaphore_signal(barrier, inc=1, device_id=peer, device_id_type=MESH)
    wq_v, vec_v, q_s, qt_s, kvs = s["wq"], s["vec"], s["q"], s["qt"], s["kv"]
    wo_all, b_gu, b_dn, n1t = s["wo"], s["ggu"].at[0, 0:2], s["gdn"].at[0, 0:2], s["n1t"]
    m_s, l_s, ot_s, lse, att = s["m"], s["l"], s["ot"], s["lse"], s["att"]
    loc_sem = s["loc"]
    row0 = pl.multiple_of(z * ROWS, ROWS)
    loads = [
        pltpu.make_async_copy(cos_hbm.at[pl.ds(row0, ROWS)], s["cos"], loc_sem.at[0]),
        pltpu.make_async_copy(sin_hbm.at[pl.ds(row0, ROWS)], s["sin"], loc_sem.at[1]),
        pltpu.make_async_copy(cot_hbm, s["n2t"], loc_sem.at[2]),
    ]
    masters = new_states[0]
    master_loads = [
        pltpu.make_async_copy(states[0][k], masters[k], s["st_sem"].at[0, k]) for k in range(4)]
    tok_t = s["tok"]
    tok_load = pltpu.make_async_copy(tok_hbm, tok_t, loc_sem.at[7])
    vector_loads = [
        pltpu.make_async_copy(vstates[i], new_vectors[i], s["v_sem"].at[i]) for i in range(3)]
    for load in vector_loads[0:1] + master_loads[0:1] + [tok_load] + master_loads[1:] + vector_loads[1:] + loads:
        load.start()
    vec_v[0] = jnp.zeros((1, VW), F32)
    vector_loads[0].wait()
    vec_v[0, :, 0:528] = new_vectors[0][...].reshape(1, 528)
    rolled = pltpu.roll(jnp.broadcast_to(vec_v[0], (8, VW)), z * 528, 1)
    vec_v[0] = rolled[0:1, :]
    qrows = pl.ds(pl.multiple_of(z * 144, 144), 144)
    master_loads[0].wait()
    wq_v[qrows, 0:896] = masters[0][:, 0:896].astype(BF16)
    wq_v[qrows, 896:1024] = jnp.concatenate(
        [masters[0][:, 896:960].astype(BF16), jnp.zeros((144, 64), BF16)], axis=1
    )
    pl.semaphore_wait(barrier, len(peers))

    sent = []

    def group(copies, name, shape):
        whole = remote(shape, shape, s["ss"].at[name], s["rs"].at[name], sib)
        return copies, whole

    def pair_of(name):
        return s["ss"].at[name], s["rs"].at[name]

    def begin(batch):
        for copy in batch[0]:
            copy.start()
        sent.append(batch[1])

    kcols = pl.ds(pl.multiple_of(512 + c * 256, 256), 256)
    xcols = pl.ds(pl.multiple_of(x * 128, 128), 128)
    ref_k, ref_q = wq_v.at[qrows, kcols], wq_v.at[qrows, xcols]
    k_over_z = group([remote(ref_k, ref_k, *pair_of(0), dev) for dev in zdev], 0, wq_v.at[0:432, 0:256])
    v_over_z = group(
        [remote(vec_v.at[0], vec_v.at[d], *pair_of(1), zdev[d - 1]) for d in range(1, NZ)], 1, vec_v.at[1:4])
    q_over_z = group([remote(ref_q, ref_q, *pair_of(2), dev) for dev in zdev], 2, wq_v.at[0:432, 0:128])
    begin(k_over_z)
    begin(v_over_z)

    @pl.when(c == 0)
    def _():
        for copy in q_over_z[0]:
            copy.start()

    def block_rows(e, n):
        return pl.ds(pl.multiple_of(wrap(z + NZ - e, NZ) * n, n), n)

    tok_load.wait()
    inputs = jnp.transpose(tok_t[...].astype(F32))
    s["gh"][...] = inputs
    unit = inputs * lax.rsqrt(jnp.mean(inputs * inputs, axis=-1, keepdims=True) + EPS)

    master_loads[1].wait()
    wo_all[qrows, 0:512] = masters[1][:, 0:512].astype(BF16)
    wo_all[qrows, 512:640] = jnp.concatenate(
        [masters[1][:, 512:576].astype(BF16), jnp.zeros((144, 64), BF16)], axis=1)
    own = []
    master_loads[2].wait()
    master_loads[3].wait()
    down = jnp.transpose(masters[3][...]).astype(BF16)
    zrows = pl.ds(pl.multiple_of(z * 384, 384), 384)
    for p in range(8):
        b_gu[p // 4, p % 4] = masters[2][:, 384 * p : 384 * p + 384].astype(BF16)
        b_dn[p // 4, p % 4] = down[48 * p : 48 * p + 48, :]
        own.append(
            pltpu.make_async_copy(
                b_gu.at[p // 4, p % 4], wgu_all.at[qrows, 384 * p : 384 * p + 384], loc_sem.at[5]))
        own.append(
            pltpu.make_async_copy(
                b_dn.at[p // 4, p % 4], wdn_all.at[pl.ds(pl.multiple_of(z * 384 + 48 * p, 48), 48), :],
                loc_sem.at[6]))
    own_done = [
        pltpu.make_async_copy(wgu_all.at[qrows, :], wgu_all.at[qrows, :], loc_sem.at[5]),
        pltpu.make_async_copy(wdn_all.at[zrows, :], wdn_all.at[zrows, :], loc_sem.at[6]),
    ]
    for copy in own:
        copy.start()

    w = wrap(x + y, 4)
    pgu = pl.multiple_of((c * 4 + w) * 384, 128)
    pdn = (c * 4 + y) * 48
    po = jnp.minimum(c * 4 + y, 4)
    has_o = c * 4 + y < 5
    oc = pl.multiple_of(po * 128, 128)

    def down_rows(zz):
        return wdn_all.at[pl.ds(pl.multiple_of(zz * 384 + pdn, 48), 48), :]

    o_over_z = group(
        [remote(wo_all.at[qrows, pl.ds(oc, 128)], wo_all.at[qrows, pl.ds(oc, 128)], *pair_of(3), dev) for dev in zdev],
        3, wo_all.at[0:432, 0:128])
    gu_over_z = group(
        [remote(b_gu.at[c, w], wgu_all.at[qrows, pl.ds(pgu, 384)], *pair_of(4), dev) for dev in zdev],
        4, wgu_all.at[0:432, 0:384])
    dn_over_z = group(
        [remote(b_dn.at[c, y], down_rows(z), *pair_of(5), dev) for dev in zdev], 5, wdn_all.at[0:144, :])

    def weights_over_z():
        @pl.when(has_o)
        def _():
            for copy in o_over_z[0]:
                copy.start()

        for copy in dn_over_z[0] + gu_over_z[0]:
            copy.start()

    weights_over_z()
    k_over_z[1].wait_recv()
    v_over_z[1].wait_recv()
    others = range(1, NZ)
    k_over_c = group(
        [remote(wq_v.at[block_rows(e, 144), kcols], wq_v.at[block_rows(e, 144), kcols], *pair_of(6), sib)
         for e in others], 6, wq_v.at[0:432, 0:256])
    begin(k_over_c)

    q_over_x = group(
        [remote(wq_v.at[block_rows(e, 144), xcols], wq_v.at[block_rows(e, 144), xcols], *pair_of(7), dev)
         for e in others for dev in xdev], 7, wq_v.at[0:432, 0:384])
    q_over_c = group(
        [remote(wq_v.at[block_rows(e, 144), 0:512], wq_v.at[block_rows(e, 144), 0:512], *pair_of(8), sib)
         for e in others], 8, wq_v.at[0:432, 0:512])

    @pl.when(c == 0)
    def _():
        q_over_z[1].wait_recv()
        for copy in q_over_x[0]:
            copy.start()

    raw = vec_v[0] + vec_v[1] + vec_v[2] + vec_v[3]
    raw = raw.astype(BF16).astype(F32)
    wide = jnp.broadcast_to(raw, (8, VW))
    gain_one = raw[:, 0:576]
    gain_two = pltpu.roll(wide, VW - 576, 1)[0:1, 0:576]
    bias = raw[:, 1152:2176]
    normed = unit * gain_one
    n1 = normed.astype(BF16)
    n1t[...] = jnp.transpose(normed).astype(BF16)
    for load in loads:
        load.wait()
    cosine, sine = s["cos"][...], s["sin"][...]

    k_over_c[1].wait_recv()

    def tile_of(v, t):
        return v[:, 128 * t : 128 * t + 128]

    def rotated(v):
        return v * cosine + swap_halves(v) * sine

    def turn(v):
        return pltpu.roll(v, 64, 1)

    proj = dot(n1, wq_v[:, 512:1024]) + bias[:, 512:1024]
    rot4, rot5 = rotated(tile_of(proj, 0)), rotated(tile_of(proj, 1))
    val6, val7 = tile_of(proj, 2), tile_of(proj, 3)
    low = low_lanes(rot4)
    kvs[z, 0] = jnp.where(low, turn(rot4), turn(val6)).astype(BF16)
    kvs[z, 1] = jnp.where(low, rot5, val6).astype(BF16)
    kvs[z, 2] = jnp.where(low, turn(rot5), turn(val7)).astype(BF16)
    kv_sends = []
    for d in range(1, NZ):
        kv_sends.append(
            remote(kvs.at[z], kvs.at[z], s["kv_s"].at[d - 1], s["kv_r"].at[d - 1],
                   device(x, y, c, wrap(z + d, NZ))))

        @pl.when(z + d < NZ)
        def _(d=d):
            kv_sends[d - 1].start()

    def put_query(h, part):
        qh = jnp.where(low, part, 0.0) * (HEAD_DIM ** -0.5)
        q_s[h] = qh.astype(BF16)
        qt_s[h] = jnp.transpose(qh).astype(BF16)

    put_query(8, rot4)
    s["cot"][...] = jnp.transpose(s["n2t"][...].astype(F32)).astype(BF16)

    @pl.when(c == 0)
    def _():
        q_over_x[1].wait_recv()
        for copy in q_over_c[0]:
            copy.start()

    @pl.when(c == 1)
    def _():
        q_over_c[1].wait_recv()

    proj = dot(n1, wq_v[:, 0:512]) + bias[:, 0:512]
    for t in range(4):
        rot = rotated(tile_of(proj, t))
        put_query(2 * t, rot)
        put_query(2 * t + 1, turn(rot))

    def step(j):
        kvt = [jnp.transpose(kvs[j, g].astype(F32)).astype(BF16)[64:128, :] for g in range(KV_HEADS)]
        heads = range(HEADS)
        sts = [dot(kvs[j, h // GROUP], qt_s[h]) for h in heads]
        olds = [m_s[h] for h in heads]
        peaks = [jnp.maximum(jnp.max(v, axis=0, keepdims=True), o) for v, o in zip(sts, olds)]
        alphas = [jnp.exp(o - p) for o, p in zip(olds, peaks)]
        ps = [jnp.exp(v - p) for v, p in zip(sts, peaks)]
        totals = [jnp.sum(p, axis=0, keepdims=True) + l_s[h] * a for h, p, a in zip(heads, ps, alphas)]
        outs = [dot(kvt[h // GROUP], p.astype(BF16)) + ot_s[h] * a for h, p, a in zip(heads, ps, alphas)]
        for h in heads:
            m_s[h] = peaks[h]
            l_s[h] = totals[h]
            ot_s[h] = outs[h]

    def visible(width):
        shape = (256, width)
        return lax.broadcasted_iota(jnp.int32, shape, 0) <= lax.broadcasted_iota(jnp.int32, shape, 1)

    right = slice(256, 512)
    always = z >= 0

    @pl.when(always)
    def _():
        keep_a, keep_b = visible(512), visible(256)
        kvt = [jnp.transpose(kvs[z, g].astype(F32)).astype(BF16)[64:128, :] for g in range(KV_HEADS)]
        heads = range(HEADS)
        st_a = [jnp.where(keep_a, dot(kvs[z, h // GROUP, 0:256], qt_s[h]), MASK_FILL) for h in heads]
        st_b = [jnp.where(keep_b, dot(kvs[z, h // GROUP, right], qt_s[h, :, right]), MASK_FILL) for h in heads]
        none = jnp.full((1, 256), MASK_FILL, F32)
        zero = jnp.zeros((1, 256), F32)
        zeros = jnp.zeros((64, 256), F32)
        peaks = [
            jnp.maximum(
                jnp.max(a, axis=0, keepdims=True),
                jnp.concatenate([none, jnp.max(b, axis=0, keepdims=True)], axis=1))
            for a, b in zip(st_a, st_b)]
        p_a = [jnp.exp(a - p) for a, p in zip(st_a, peaks)]
        p_b = [jnp.exp(b - p[:, right]) for b, p in zip(st_b, peaks)]
        totals = [
            jnp.sum(a, axis=0, keepdims=True) + jnp.concatenate([zero, jnp.sum(b, axis=0, keepdims=True)], axis=1)
            for a, b in zip(p_a, p_b)]
        outs = [
            dot(kvt[h // GROUP][:, 0:256], p_a[h].astype(BF16))
            + jnp.concatenate([zeros, dot(kvt[h // GROUP][:, right], p_b[h].astype(BF16))], axis=1)
            for h in heads]
        for h in heads:
            m_s[h] = peaks[h]
            l_s[h] = totals[h]
            ot_s[h] = outs[h]

    gu_over_z[1].wait_recv()
    dn_over_z[1].wait_recv()

    @pl.when(has_o)
    def _():
        o_over_z[1].wait_recv()

    def gu_piece(e, ww):
        return wgu_all.at[block_rows(e, 144), pl.ds(pl.multiple_of((c * 4 + ww) * 384, 128), 384)]

    def o_piece(e):
        return wo_all.at[block_rows(e, 144), pl.ds(oc, 128)]

    def dn_half(e):
        return wdn_all.at[
            pl.ds(pl.multiple_of(wrap(z + NZ - e, NZ) * 384 + c * 192, 192), 192), :]

    def dn_piece(e):
        return down_rows(wrap(z + NZ - e, NZ))

    gu_over_x = group(
        [remote(gu_piece(e, w), gu_piece(e, w), *pair_of(9), dev) for e in others for dev in xdev],
        9, wgu_all.at[0:432, 0:1152])
    dn_over_y = group(
        [remote(dn_piece(e), dn_piece(e), *pair_of(10), dev) for e in others for dev in ydev],
        10, wdn_all.at[0:432, :])
    o_over_y = [
        [remote(o_piece(e), o_piece(e), s["ss"].at[11], s["os"].at[d - 1], ydev[d - 1]) for e in others]
        for d in range(1, NY)]
    o_sent = remote(wo_all.at[0:432, 0:384], wo_all.at[0:432, 0:384], s["ss"].at[11], s["os"].at[0], sib)
    own_over_c = group(
        [remote(gu_piece(e, w), gu_piece(e, w), *pair_of(12), sib) for e in others], 12, wgu_all.at[0:432, 0:384])
    gu_over_c = group(
        [remote(gu_piece(e, wrap(w + d, NX)), gu_piece(e, wrap(w + d, NX)), *pair_of(13), sib)
         for e in others for d in range(1, NX)], 13, wgu_all.at[0:432, 0:1152])
    dn_over_c = group(
        [remote(dn_half(e), dn_half(e), *pair_of(14), sib) for e in others], 14, wdn_all.at[0:576, :])
    o_over_c = []
    for core, cols in enumerate((slice(0, 512), slice(512, 640))):
        o_over_c.append(
            group(
                [remote(wo_all.at[block_rows(e, 144), cols], wo_all.at[block_rows(e, 144), cols], *pair_of(15), sib)
                 for e in others], 15, wo_all.at[0:432, cols]))

    @pl.when(has_o)
    def _():
        for copies in o_over_y:
            for copy in copies:
                copy.start()

    begin(dn_over_y)
    begin(gu_over_x)
    begin(own_over_c)

    def earlier(d, carry):
        @pl.when(d == NZ - 1)
        def _():
            for dd in range(1, NY):
                from_y = wrap(y + NY - dd, NY)

                @pl.when(c * 4 + from_y < 5)
                def _(dd=dd):
                    remote(wo_all.at[0:432, 0:128], wo_all.at[0:432, 0:128], s["ss"].at[11], s["os"].at[dd - 1],
                           sib).wait_recv()

            for core in range(2):

                @pl.when(c == core)
                def _(core=core):
                    for copy in o_over_c[core][0]:
                        copy.start()

            dn_over_y[1].wait_recv()
            begin(dn_over_c)

        @pl.when(z >= d)
        def _():
            remote(kvs.at[z], kvs.at[z], s["kv_s"].at[d - 1], s["kv_r"].at[d - 1], sib).wait_recv()
            step(z - d)

        return carry

    lax.fori_loop(1, NZ, earlier, 0)

    for h in range(HEADS):
        ot_s[h] = ot_s[h] * (1.0 / l_s[h])
        lse[h] = m_s[h] + jnp.log(l_s[h])
    for t in range(5):
        top = ot_s[2 * t]
        bottom = ot_s[2 * t + 1] if 2 * t + 1 < HEADS else jnp.zeros((64, ROWS), F32)
        att[:, 128 * t : 128 * t + 128] = jnp.transpose(jnp.concatenate([top, bottom], axis=0)).astype(BF16)

    for core in range(2):

        @pl.when(c == core)
        def _(core=core):
            o_over_c[1 - core][1].wait_recv()

    for copy in own_done:
        copy.wait()
    wo = wo_all
    wgu, wds, w_sem = s["wgu"], s["wds"], s["w_sem"]

    def weights(i, slot):
        col = pl.multiple_of(wrap(w + i, 4) * 384, 384)
        return [
            pltpu.make_async_copy(
                wgu_all.at[:, pl.ds(col, 384)], wgu.at[slot, :, 0:384], w_sem.at[0, slot]),
            pltpu.make_async_copy(
                wgu_all.at[:, pl.ds(pl.multiple_of(col + FF, 384), 384)], wgu.at[slot, :, 384:768],
                w_sem.at[0, slot]),
            pltpu.make_async_copy(wdn_all.at[pl.ds(col, 384), :], wds.at[slot], w_sem.at[1, slot]),
        ]

    def weights_wait(slot):
        pltpu.make_async_copy(wgu_all.at[:, 0:768], wgu.at[slot], w_sem.at[0, slot]).wait()
        pltpu.make_async_copy(wdn_all.at[0:384, :], wds.at[slot], w_sem.at[1, slot]).wait()

    gu_over_z[1].wait_send()
    dn_over_z[1].wait_send()
    dn_over_c[1].wait_recv()
    own_over_c[1].wait_recv()
    for load in weights(0, 0):
        load.start()
    gu_over_x[1].wait_recv()
    begin(gu_over_c)

    ggu, gdn, go, gq, fin = s["ggu"], s["gdn"], s["go"], s["gq"], s["fin"]
    def columns(width):
        def at(cc, a, count):
            return (slice(None), pl.ds(pl.multiple_of((cc * 4 + a) * width, 128), count * width))

        return at

    def down_at(cc, a, count):
        return (pl.ds(pl.multiple_of((cc * 4 + a) * 48, 48), count * 48), slice(None))

    red_gu = Reduction(ggu, fin["gu"], columns(384), s["red_gu"], 0, False)
    red_dn = Reduction(gdn, fin["dn"], down_at, s["red_dn"], 1, True)
    red_o = Reduction(go, fin["o"], columns(128), s["red_o"], 0, False)
    red_q = TileReduction(gq, fin["q"], s["red_q"])
    vecs = VectorSum(s["vecs"])
    cot, gh, n2, n2t, gn2t = s["cot"], s["gh"], s["n2"], s["n2t"], grad_in
    do_in, dot_in, delta_in, gain_row = s["do"], s["dot"], s["delta"], s["gain_row"]
    dqt, own_kv, skv, rkv = ot_s, s["own_kv"], s["skv"], s["rkv"]

    gn2t[...] = jnp.zeros_like(gn2t)
    hid = gh[...] + dot(att[:, 0:576], wo[:, 0:576])
    inv_two = lax.rsqrt(jnp.mean(hid * hid, axis=-1, keepdims=True) + EPS)
    normed = hid * inv_two * gain_two
    n2[...] = normed.astype(BF16)
    n2t[...] = jnp.transpose(normed).astype(BF16)
    gh[...] = hid
    block_out[...] = jnp.transpose(hid)

    def chunk(i, carry):
        slot = lax.rem(i, 2)
        here = wrap(w + i, 4)
        @pl.when(i > 0)
        def _():
            red_gu.core_add(wrap(w + i + 3, 4))
            red_gu.first_piece(wrap(w + i + 3, 4))

        weights_wait(slot)

        @pl.when(jnp.logical_and(i > 0, i < 3))
        def _():
            for load in weights(i + 1, 1 - slot):
                load.start()

        both = dot(n2[...], wgu[slot])
        gate, up = both[:, 0:384], both[:, 384:768]
        sg = jax.nn.sigmoid(gate)
        silu = gate * sg
        act = (silu * up).astype(BF16)
        ga = dot(cot[...], wds[slot], 1, 1)
        gg = (ga * up * sg * (1.0 + gate * (1.0 - sg))).astype(BF16)
        gu = (ga * silu).astype(BF16)
        grads = jnp.concatenate([gg, gu], axis=1)
        both = dot(n2t[...], grads).astype(BF16)
        ggu[0, here] = both[:, 0:384].reshape(NZ, 144, 384)
        ggu[1, here] = both[:, 384:768].reshape(NZ, 144, 384)
        red_gu.core_copy(here).start()
        down = dot(act, cot[...], 0, 0).astype(BF16)
        for p in range(8):
            gdn[p // 4, here, p % 4] = down[48 * p : 48 * p + 48, :]
        red_dn.core_copy(here).start()

        @pl.when(i == 0)
        def _():
            gu_over_c[1].wait_recv()
            for load in weights(1, 1):
                load.start()

        block_out[...] += lax.dot_general(wds[slot], act, (((0,), (1,)), ((), ())), preferred_element_type=F32)
        gn2t[...] += dot(wgu[slot], grads, 1, 1)

        return carry

    lax.fori_loop(0, 4, chunk, 0)

    red_gu.core_add(wrap(w + 3, 4))
    red_gu.first_piece(wrap(w + 3, 4))
    state_loads = []
    for i in range(1, 3):
        for k in range(4):
            copy = pltpu.make_async_copy(states[i][k], new_states[i][k], s["st_sem"].at[i, k])
            copy.start()
            state_loads.append(copy)

    @pl.when(always)
    def _():
        hid = gh[...]
        inv_two = lax.rsqrt(jnp.mean(hid * hid, axis=-1, keepdims=True) + EPS)
        u = hid * inv_two
        e = jnp.transpose(gn2t[...])
        f = e * gain_two
        gain_row[:, 0:576] = jnp.sum(e * u, axis=0, keepdims=True)
        gain_row[:, 576:640] = jnp.zeros((1, 64), F32)
        grad_hidden = cot[...].astype(F32) + inv_two * (f - u * jnp.mean(f * u, axis=-1, keepdims=True))
        gh[...] = grad_hidden
        ghl = grad_hidden.astype(BF16)
        grad_out = dot(att[:, 0:576], ghl, 0, 0).astype(BF16)
        for p in range(8):
            if p < 4:
                part = grad_out[:, 128 * p : 128 * p + 128]
            elif p == 4:
                part = jnp.concatenate([grad_out[:, 512:576], jnp.zeros((D, 64), BF16)], axis=1)
            else:
                part = jnp.zeros((D, 128), BF16)
            go[p // 4, p % 4] = part.reshape(NZ, 144, 128)
        red_o.core_all(lambda k: red_o.core_copy(k).start())
        gm = dot(ghl, wo[:, 0:576], 1, 1).astype(BF16).astype(F32)
        gm = jnp.concatenate([gm, jnp.zeros((ROWS, 64), F32)], axis=1)
        for h in range(HEADS):
            part = gm[:, 128 * (h // 2) : 128 * (h // 2) + 128]
            part = part if h % 2 == 1 else turn(part)
            part = jnp.where(low_lanes(part), 0.0, part)
            do_in[h] = part.astype(BF16)
            part = jnp.transpose(part)
            dot_in[h] = part.astype(BF16)
            delta_in[h] = jnp.sum(part[64:128, :] * ot_s[h], axis=0, keepdims=True)

    red_dn.core_all(red_dn.core_add)
    red_dn.first_start()

    def attend(g, j):
        kv = kvs[j, g]
        kt = jnp.transpose(kv.astype(F32)).astype(BF16)[0:64, :]
        totals = [None, None]
        for i in range(GROUP):
            h = g * GROUP + i
            dq = None
            for half in range(2):
                rows = slice(256 * half, 256 * half + 256)
                pt = jnp.exp(dot(kv[rows], qt_s[h]) - lse[h])
                dst = (pt * (dot(kv[rows], dot_in[h]) - delta_in[h])).astype(BF16)
                both = dot(dst, q_s[h]) + dot(pt.astype(BF16), do_in[h])
                totals[half] = both if i == 0 else totals[half] + both
                part = dot(kt[:, rows], dst)
                dq = part if half == 0 else dq + part
            dqt[h] += dq
        return totals

    def attend_own(g):
        keep_a, keep_b = visible(512), visible(256)
        kv = kvs[z, g]
        kt = jnp.transpose(kv.astype(F32)).astype(BF16)[0:64, :]
        left = slice(0, 256)
        totals = [None, None]
        for i in range(GROUP):
            h = g * GROUP + i
            pt = jnp.where(keep_a, jnp.exp(dot(kv[left], qt_s[h]) - lse[h]), 0.0)
            dst = (pt * (dot(kv[left], dot_in[h]) - delta_in[h])).astype(BF16)
            both = dot(dst, q_s[h]) + dot(pt.astype(BF16), do_in[h])
            totals[0] = both if i == 0 else totals[0] + both
            dq = dot(kt[:, left], dst)
            pt = jnp.where(keep_b, jnp.exp(dot(kv[right], qt_s[h, :, right]) - lse[h, :, right]), 0.0)
            dst = (pt * (dot(kv[right], dot_in[h, :, right]) - delta_in[h, :, right])).astype(BF16)
            both = dot(dst, q_s[h, right]) + dot(pt.astype(BF16), do_in[h, right])
            totals[1] = both if i == 0 else totals[1] + both
            dqt[h] += dq
            dqt[h, :, right] += dot(kt[:, right], dst)
        own_kv[g, left] = totals[0]
        own_kv[g, right] = totals[1]

    def kv_copy(g, k, dev):
        return remote(
            skv.at[g, k - 1], rkv.at[g, k - 1], s["ss"].at[16], s["dkv_r"].at[g], dev)

    gps = q_s

    def kv_wait(g):
        for count in range(1, NZ):

            @pl.when(z + count == NZ - 1)
            def _(count=count):
                part = rkv.at[g, 0:count]
                remote(part, part, s["ss"].at[16], s["dkv_r"].at[g], sib).wait_recv()
                total = own_kv[g]
                for k in range(count):
                    total = total + rkv[g, k].astype(F32)
                own_kv[g] = total

    def group_tiles(g):
        cos_t, sin_t = s["cos"][...], s["sin"][...]
        low = low_lanes(cos_t)
        kv = own_kv[g]

        def query(top, bottom):
            both = [dqt[h] if h is not None else jnp.zeros((64, ROWS), F32) for h in (top, bottom)]
            return jnp.transpose(jnp.concatenate(both, axis=0)) * (HEAD_DIM ** -0.5)

        def back(t):
            return t * cos_t - swap_halves(t) * sin_t

        if g == 0:
            return {
                0: back(query(0, 1)),
                1: back(jnp.where(low, query(2, None), turn(kv))),
                2: jnp.where(low, turn(kv), 0.0),
            }
        if g == 1:
            return {
                2: jnp.where(low, 0.0, back(query(None, 3))),
                3: back(query(4, 5)),
                4: jnp.where(low, back(kv), kv),
            }
        return {
            5: back(query(6, 7)),
            6: back(jnp.where(low, query(8, None), turn(kv))),
            7: jnp.where(low, turn(kv), 0.0),
        }

    def tiles_of(g):
        @pl.when(always)
        def _():
            for t, tile in group_tiles(g).items():
                if t == 2 and g == 0:
                    gps[2] = tile.astype(BF16)
                    continue
                if t == 2:
                    tile = tile + gps[2].astype(F32)
                low_tile = tile.astype(BF16)
                gps[t] = low_tile
                gq[t] = dot(n1t[...], low_tile).astype(BF16).reshape(NZ, 144, 128)

        red_q.core_start((READY[g]))

    dqt[...] = jnp.zeros_like(dqt)
    early = red_q.tile <= 4
    late = red_q.tile > 4
    own_one = jnp.where(z == NZ - 1, 9, 3)
    own_two = jnp.where(z == NZ - 1, 10, 6)

    def slot(t, carry):
        g = lax.div(t, 3)
        k = 3 - lax.rem(t, 3)

        @pl.when(jnp.logical_and(t < 9, z >= k))
        def _():
            for half, total in enumerate(attend(g, z - k)):
                skv[g, k - 1, 256 * half : 256 * half + 256] = total.astype(BF16)
            kv_copy(g, k, device(x, y, c, z - k)).start()

        @pl.when(jnp.logical_or(t == 2, jnp.logical_or(t == own_one, t == own_two)))
        def _():
            attend_own(jnp.where(t == 2, 0, jnp.where(t == own_one, 1, 2)))

        @pl.when(t == 0)
        def _():
            red_o.core_all(red_o.core_add)

        @pl.when(t == 2)
        def _():
            red_gu.first_sum()
            red_gu.z_start()
            red_o.first_start()

        @pl.when(t == 4)
        def _():
            kv_wait(0)
            tiles_of(0)

        @pl.when(t == 5)
        def _():
            red_q.core_add(READY[0])
            red_q.first_start(READY[0])
            red_gu.z_sum()
            red_gu.exchange_start()

        @pl.when(t == 9)
        def _():
            kv_wait(1)
            tiles_of(1)
            red_dn.first_sum()
            red_o.first_sum()
            red_q.core_add(READY[1])
            red_q.first_start(READY[1])
            red_gu.gather_start()

        return carry

    lax.fori_loop(0, 11, slot, 0)
    kv_wait(2)
    red_dn.z_start()
    red_o.z_start()
    tiles_of(2)
    red_q.core_add(READY[2])
    red_q.first_start(READY[2])

    low = low_lanes(s["cos"][...])

    def halves(t):
        tile = gps[t].astype(F32)
        return tile, turn(tile)

    (t0, _), (t1, u1), (t2, u2), (t3, u3) = [halves(t) for t in range(4)]
    (t4, u4), (t5, _), (t6, u6), (t7, _) = [halves(t) for t in range(4, 8)]
    ordered = [
        t0,
        jnp.where(low, t1, t2),
        t3,
        t5,
        jnp.where(low, t6, t1),
        jnp.where(low, t4, t6),
        jnp.where(low, t2, t4),
        t7,
    ]
    vecs.rc[0, 10:18, :] = jnp.concatenate(
        [jnp.sum(t, axis=0, keepdims=True) for t in ordered], axis=0)
    gn1 = dot(jnp.concatenate([t.astype(BF16) for t in ordered], axis=1), wq_v[...], 1, 1)
    inputs = jnp.transpose(tok_t[...].astype(F32))
    r = lax.rsqrt(jnp.mean(inputs * inputs, axis=-1, keepdims=True) + EPS)
    u = inputs * r
    f = gn1 * gain_one
    row = jnp.sum(gn1 * u, axis=0, keepdims=True)
    row = jnp.concatenate([row, jnp.zeros((1, 64), F32)], axis=1)
    for t in range(5):
        vecs.rc[0, t : t + 1, :] = row[:, 128 * t : 128 * t + 128]
        vecs.rc[0, 5 + t : 6 + t, :] = gain_row[:, 128 * t : 128 * t + 128]
    vecs.rc[0, 18:24, :] = jnp.zeros((6, 128), F32)
    vecs.start()
    vecs.next(0)
    @pl.when(early)
    def _():
        red_q.first_sum()
        red_q.z_start()

    grad_in[...] = jnp.transpose(gh[...] + r * (f - u * jnp.mean(f * u, axis=-1, keepdims=True)))

    def update(k, grad):
        new = adam_step(
            new_states[0][k][...], new_states[1][k][...], new_states[2][k][...], grad, RATE_MATRIX, DECAY_MATRIX)
        for i in range(3):
            new_states[i][k][...] = new[i]

    red_gu.gather_forward()
    @pl.when(late)
    def _():
        red_q.first_sum()
        red_q.z_start()

    vecs.next(1)
    red_dn.z_sum()
    red_dn.exchange_start()
    red_o.z_sum()
    red_o.exchange_start()

    @pl.when(early)
    def _():
        red_q.z_sum()
        red_q.exchange_start()

    @pl.when(late)
    def _():
        red_q.z_sum()
        red_q.exchange_start()

    red_dn.gather_start()
    red_o.gather_start()

    for load in state_loads:
        load.wait()
    red_gu.gather_wait()
    update(2, fin["gu"][...].astype(F32))
    @pl.when(early)
    def _():
        red_q.gather_start()

    vecs.next(2)

    @pl.when(late)
    def _():
        red_q.gather_start()

    red_dn.gather_forward()
    red_o.gather_forward()
    red_dn.gather_wait()
    update(3, jnp.transpose(fin["dn"][...].astype(F32)))
    red_o.gather_wait()
    update(1, fin["o"][:, 0:576].astype(F32))
    total = vecs.next(3)
    total = jnp.concatenate([total[t : t + 1, :] for t in range(18)], axis=1)
    pad = jnp.zeros((1, VW - 640), F32)
    flat = jnp.concatenate([total[:, 0:640], pad], axis=1)
    mid = jnp.concatenate([total[:, 640:1280], pad], axis=1)
    flat = flat + pltpu.roll(jnp.broadcast_to(mid, (8, VW)), 576, 1)[0:1, :]
    flat = flat + jnp.concatenate(
        [jnp.zeros((1, 1152), F32), total[:, 1280:2304], jnp.zeros((1, 128), F32)], axis=1)
    shift = lax.rem(VW - z * 528, VW)
    grad = pltpu.roll(jnp.broadcast_to(flat, (8, VW)), shift, 1)[0:1, 0:528]
    for load in vector_loads[1:]:
        load.wait()
    new = adam_step(*[v[...].reshape(1, 528) for v in new_vectors], grad, RATE_VECTOR, 0.0)
    for i in range(3):
        new_vectors[i][...] = new[i].reshape(528)
    red_q.gather_wait()
    tq = [fin["q"][:, 128 * t : 128 * t + 128].astype(F32) for t in range(8)]
    lowq = low_lanes(tq[0])
    ordered = [
        tq[0],
        jnp.where(lowq, tq[1], tq[2]),
        tq[3],
        tq[5],
        jnp.where(lowq, tq[6], tq[1]),
        jnp.where(lowq, tq[4], tq[6]),
        jnp.where(lowq, tq[2], tq[4]),
        tq[7],
    ]
    update(0, jnp.concatenate(ordered, axis=1)[:, 0:960])
    for red in (red_gu, red_dn, red_o):
        red.finish()
    red_q.finish()
    vecs.finish()
    for whole in sent:
        whole.wait_send()
    for count in range(1, NZ):

        @pl.when(z == count)
        def _(count=count):
            part = (skv.at[0], skv.at[0:2], skv)[count - 1]
            remote(part, part, s["ss"].at[16], s["dkv_r"].at[0], sib).wait_send()

    for d in range(1, NZ):

        @pl.when(z + d < NZ)
        def _(d=d):
            kv_sends[d - 1].wait_send()

    @pl.when(has_o)
    def _():
        o_over_z[1].wait_send()
        o_sent.wait_send()

    for core in range(2):

        @pl.when(c == core)
        def _(core=core):
            o_over_c[core][1].wait_send()

    @pl.when(c == 0)
    def _():
        for batch in (q_over_z, q_over_x, q_over_c):
            batch[1].wait_send()


MATRICES = ((144, 960), (144, D), (144, 2 * FF), (D, 384))


def train(tok_t, cot_t, cos_t, sin_t, vstates, states):
    sd = jax.ShapeDtypeStruct
    v = pl.BlockSpec(memory_space=VM)
    a = pl.BlockSpec(memory_space=ANY)
    dma = pltpu.SemaphoreType.DMA
    scratch = dict(
        wq=VM((D, QW), BF16), vec=VM((NZ, 1, VW), F32), cos=VM((ROWS, 128), F32), sin=VM((ROWS, 128), F32),

        q=VM((HEADS, ROWS, 128), BF16), qt=VM((HEADS, 128, ROWS), BF16), n1t=VM((D, ROWS), BF16),
        kv=VM((NZ, KV_HEADS, ROWS, 128), BF16),
        m=VM((HEADS, 1, ROWS), F32), l=VM((HEADS, 1, ROWS), F32), ot=VM((HEADS, 64, ROWS), F32),
        lse=VM((HEADS, 1, ROWS), F32), att=VM((ROWS, 640), BF16), wo=VM((D, OW), BF16),
        loc=dma((8,)), v_sem=dma((3,)), tok=VM((D, ROWS), BF16), ss=dma((17,)), rs=dma((16,)), os=dma((3,)), kv_s=dma((3,)), kv_r=dma((3,)),
        cot=VM((ROWS, D), BF16), gh=VM((ROWS, D), F32), n2=VM((ROWS, D), BF16), n2t=VM((D, ROWS), BF16),
        wgu=VM((2, D, 768), BF16), wds=VM((2, 384, D), BF16), w_sem=dma((2, 2)),
        do=VM((HEADS, ROWS, 128), BF16), dot=VM((HEADS, 128, ROWS), BF16), delta=VM((HEADS, 1, ROWS), F32),
        gain_row=VM((1, 640), F32),
        ggu=VM((2, 4, NZ, 144, 384), BF16), gdn=VM((2, NZ, 4, 48, D), BF16), go=VM((2, 4, NZ, 144, 128), BF16),
        gq=VM((8, NZ, 144, 128), BF16),
        fin=dict(gu=VM((144, 2 * FF), BF16), dn=VM((384, D), BF16), o=VM((144, QW), BF16), q=VM((144, QW), BF16)),
        own_kv=VM((KV_HEADS, ROWS, 128), F32),
        skv=VM((KV_HEADS, 3, ROWS, 128), BF16), rkv=VM((KV_HEADS, 3, ROWS, 128), BF16),
        dkv_r=dma((3,)), st_sem=dma((3, 4)),
        red_gu=Reduction.scratch((4, 4), 144, 384), red_dn=Reduction.scratch((4, 4), 48, D),
        red_o=Reduction.scratch((4, 4), 144, 128), red_q=TileReduction.scratch(),
        vecs=VectorSum.scratch(),
    )
    fast = lambda shape: VM(shape, F32)
    return pl.pallas_call(
        step_kernel,
        out_shape=(
            fast((D, ROWS)),
            fast((D, ROWS)),
            [[fast(shape) for shape in MATRICES] for _ in range(3)],
            [fast((528,)) for _ in range(3)],
            pltpu.HBM((D, 2 * FF), BF16),
            pltpu.HBM((FF, D), BF16),
        ),
        in_specs=[a, a, a, a, [a] * 3, [[a] * 4] * 3],
        out_specs=(v, v, [[v] * 4] * 3, [v] * 3, a, a),
        scratch_shapes=[scratch],
        compiler_params=pltpu.CompilerParams(
            collective_id=0, has_side_effects=True, vmem_limit_bytes=51 << 20),
        name="train_step",
    )(tok_t, cot_t, cos_t, sin_t, vstates, states)


def adam_step(weight, first_state, second_state, gradient, learn_rate, decay_rate):
    first_new = BETA_ONE * first_state + (1.0 - BETA_ONE) * gradient
    second_new = BETA_TWO * second_state + (1.0 - BETA_TWO) * gradient * gradient
    corr_one = 1.0 - BETA_ONE**STEP
    corr_two = 1.0 - BETA_TWO**STEP
    update = first_new / corr_one / (jnp.sqrt(second_new / corr_two) + ADAM_EPS)
    weight_new = weight - learn_rate * (update + decay_rate * weight)
    return (weight_new, first_new, second_new)


def store_kernel(sources, *rest):
    targets, sems = rest[:-1], rest[-1]
    copies = [
        pltpu.make_async_copy(a, b, sems.at[k])
        for k, (a, b) in enumerate(zip(jax.tree.leaves(sources), jax.tree.leaves(targets)))]
    for copy in copies:
        copy.start()
    for copy in copies:
        copy.wait()


def store(arrays):
    shapes = jax.tree.map(lambda t: jax.ShapeDtypeStruct(t.shape, t.dtype), arrays)
    count = len(jax.tree.leaves(arrays))
    v = pl.BlockSpec(memory_space=VM)
    a = pl.BlockSpec(memory_space=ANY)
    return pl.pallas_call(
        store_kernel,
        out_shape=shapes,
        in_specs=[jax.tree.map(lambda t: v, arrays)],
        out_specs=jax.tree.map(lambda t: a, arrays),
        scratch_shapes=[pltpu.SemaphoreType.DMA((count,))],
        compiler_params=pltpu.CompilerParams(vmem_limit_bytes=8 << 20),
        name="store",
    )(arrays)


def per_device(
    tokens, cotangent, w_qkv, w_out, w_gate_up, w_down, vectors,
    first_qkv, first_out, first_gate_up, first_down, first_vectors,
    second_qkv, second_out, second_gate_up, second_down, second_vectors,
):
    cos_np, sin_np = rope_tables()
    cos_t, sin_t = jnp.asarray(cos_np), jnp.asarray(sin_np)
    states = [
        [w_qkv, w_out, w_gate_up, w_down.T],
        [first_qkv, first_out, first_gate_up, first_down.T],
        [second_qkv, second_out, second_gate_up, second_down.T],
    ]
    vstates = [vectors, first_vectors, second_vectors]
    outs = train(
        tokens.T, cotangent.T, cos_t, sin_t, vstates, states)
    block_t, grad_t, matrices, vecs = store(tuple(outs[0:4]))
    out = [block_t.T, grad_t.T]
    for i in range(3):
        out += list(matrices[i][0:3]) + [matrices[i][3].T, vecs[i]]
    return tuple(out)


def solution(mesh):
    tokens = P(("dp", "ctx"), None)
    state = (P("ctx", None),) * 4 + (P("ctx"),)
    return jax.shard_map(
        per_device, mesh=mesh, in_specs=(tokens, tokens) + state * 3, out_specs=(tokens, tokens) + state * 3,
        check_vma=False,
    )
```

```python
import functools

import jax
import jax.numpy as jnp
import numpy as np
from jax import lax
from jax.experimental import pallas as pl
from jax.experimental.pallas import tpu as pltpu
from jax.sharding import PartitionSpec as P

D = 576
HEADS = 9
KV_HEADS = 3
GROUP = 3
HEAD_DIM = 64
FF = 1536
STEP = 10
LEN = 2048
ROWS = 512
QW = 1024
OW = 640
VW = 2304
NX = 4
NY = 4
NZ = 4

EPS = 1e-05
ROPE_BASE = 100000.0
MASK_FILL = -1e30
BETA_ONE = 0.9
BETA_TWO = 0.999
ADAM_EPS = 1e-08
RATE_MATRIX = 0.05
RATE_VECTOR = 0.5
DECAY_MATRIX = 0.1

F32 = jnp.float32
BF16 = jnp.bfloat16
MESH = pl.DeviceIdType.MESH
VM = pltpu.VMEM
ANY = pl.ANY


def rope_tables():
    half = HEAD_DIM // 2
    exponent = np.arange(half, dtype=np.float32) * np.float32(2.0 / HEAD_DIM)
    inverse = (np.float64(ROPE_BASE) ** (-exponent.astype(np.float64))).astype(np.float32)
    angles = np.arange(LEN, dtype=np.float32)[:, None] * inverse[None, :]
    cosine = np.cos(angles.astype(np.float64)).astype(np.float32)
    sine = np.sin(angles.astype(np.float64)).astype(np.float32)
    cos_all = np.concatenate([cosine] * 4, axis=1)
    sin_all = np.concatenate([-sine, sine, -sine, sine], axis=1)
    return cos_all, sin_all


def dot(a, b, ca=1, cb=0):
    return lax.dot_general(a, b, (((ca,), (cb,)), ((), ())), preferred_element_type=F32)


def place():
    dp = lax.axis_index("dp")
    z = lax.axis_index("ctx")
    x = lax.div(dp, NY * 2)
    y = lax.rem(lax.div(dp, 2), NY)
    c = lax.rem(dp, 2)
    return x, y, c, z


def device(x, y, c, z):
    return (x * (NY * 2) + y * 2 + c, z)


def wrap(i, n):
    return lax.rem(i, n)


def remote(src, dst, ssem, rsem, dev):
    return pltpu.make_async_remote_copy(
        src_ref=src, dst_ref=dst, send_sem=ssem, recv_sem=rsem, device_id=dev, device_id_type=MESH
    )


def greet(peers):
    barrier = pltpu.get_barrier_semaphore()
    for peer in peers:
        pl.semaphore_signal(barrier, inc=1, device_id=peer, device_id_type=MESH)
    pl.semaphore_wait(barrier, len(peers))


def swap_halves(v):
    width = v.shape[1]
    lane = lax.broadcasted_iota(jnp.int32, v.shape, 1)
    down = pltpu.roll(v, width - 32, 1)
    up = pltpu.roll(v, 32, 1)
    return jnp.where(lax.rem(lane, 64) < 32, down, up)


def low_lanes(v):
    lane = lax.broadcasted_iota(jnp.int32, v.shape, 1)
    return lane < 64


class Reduction:
    @staticmethod
    def scratch(lead, r, w):
        dma = pltpu.SemaphoreType.DMA
        return [
            VM(lead + (r, w), BF16), VM((3, 4, r, w), BF16), VM((4, r, w), BF16),
            VM((3, r, w), BF16), VM((4, r, w), BF16), dma((6,)), dma((10,)),
        ]

    def __init__(self, own, fin, fin_at, bufs, swap, z_first):
        self.own, self.fin, self.fin_at, self.z_first = own, fin, fin_at, z_first
        self.rc, self.r1, self.s1, self.r2, self.r3, self.ss, self.rs = bufs
        x, y, c, z = place()
        self.c, self.z = c, z
        flip = c != swap
        self.a, self.b = jnp.where(flip, y, x), jnp.where(flip, x, y)
        self.at = lambda a, b, cc, zz: device(jnp.where(flip, b, a), jnp.where(flip, a, b), cc, zz)
        self.other = self.at(self.a, self.b, 1 - c, z)

    def copy(self, src, dst, k, dev, into=None):
        return remote(src, dst, self.ss.at[k], self.rs.at[k if into is None else into], dev)

    def whole(self, ref, k):
        return self.copy(ref, ref, k, self.other)

    def mine(self, a, z):
        return (self.c, z, a) if self.z_first else (self.c, a, z)

    def all_z(self, a):
        return self.own.at[self.c, :, a] if self.z_first else self.own.at[self.c, a]

    def core_copy(self, k):
        return self.copy(self.own.at[1 - self.c, k], self.rc.at[k], 0, self.other, 6 + k)

    def core_add(self, k):
        self.core_copy(k).wait_recv()

        def add(j, carry):
            self.own[self.c, k, j] = self.own[self.c, k, j] + self.rc[k, j]
            return carry

        lax.fori_loop(0, 4, add, 0)

    def core_all(self, act):
        def one(k, carry):
            act(k)
            return carry

        lax.fori_loop(0, 4, one, 0)

    def first_copy(self, d):
        to = wrap(self.a + d, 4)
        return self.copy(self.all_z(to), self.r1.at[d - 1], 1, self.at(to, self.b, self.c, self.z))

    def first_start(self):
        for d in range(1, 4):
            self.first_copy(d).start()

    def first_piece(self, piece):
        d = wrap(piece + 4 - self.a, 4)

        @pl.when(d > 0)
        def _():
            self.first_copy(jnp.maximum(d, 1)).start()

    def first_sum(self):
        self.whole(self.r1, 1).wait_recv()

        def add(j, carry):
            total = self.own[self.mine(self.a, j)].astype(F32) + self.r1[0, j].astype(F32)
            total = total + self.r1[1, j].astype(F32) + self.r1[2, j].astype(F32)
            self.s1[j] = total.astype(BF16)
            return carry

        lax.fori_loop(0, 4, add, 0)

    def z_start(self):
        for d in range(1, 4):
            to = wrap(self.z + d, 4)
            self.copy(self.s1.at[to], self.r2.at[d - 1], 2, self.at(self.a, self.b, self.c, to)).start()

    def z_sum(self):
        self.whole(self.r2, 2).wait_recv()
        total = self.s1[self.z].astype(F32) + self.r2[0].astype(F32)
        total = total + self.r2[1].astype(F32) + self.r2[2].astype(F32)
        self.r3[self.b] = total.astype(BF16)

    def exchange_start(self):
        for d in range(1, 4):
            to = wrap(self.b + d, 4)
            ref = self.r3.at[self.b]
            self.copy(ref, ref, 3, self.at(self.a, to, self.c, self.z)).start()

    def gather_start(self):
        self.whole(self.r3.at[0:3], 3).wait_recv()
        total = self.r3[0].astype(F32) + self.r3[1].astype(F32)
        total = total + self.r3[2].astype(F32) + self.r3[3].astype(F32)
        where = self.fin_at(self.c, self.a, 1)
        self.fin[where] = total.astype(BF16)
        ref = self.fin.at[where]
        for d in range(1, 4):
            self.copy(ref, ref, 4, self.at(wrap(self.a + d, 4), self.b, self.c, self.z)).start()

    def gather_forward(self):
        self.whole(self.fin.at[self.fin_at(0, 0, 3)], 4).wait_recv()
        ref = self.fin.at[self.fin_at(self.c, 0, 4)]
        self.copy(ref, ref, 5, self.other).start()

    def gather_wait(self):
        self.whole(self.fin.at[self.fin_at(0, 0, 4)], 5).wait_recv()

    def finish(self):
        for ref, k in (
            (self.rc, 0), (self.r1, 1), (self.r2, 2), (self.r3.at[0:3], 3),
            (self.fin.at[self.fin_at(0, 0, 3)], 4), (self.fin.at[self.fin_at(0, 0, 4)], 5),
        ):
            self.whole(ref, k).wait_send()


class VectorSum:
    SCRATCH = 4

    @staticmethod
    def scratch():
        dma = pltpu.SemaphoreType.DMA
        return [VM((2, 24, 128), F32), VM((3, 4, 24, 128), F32), dma((4,)), dma((4,))]

    def __init__(self, bufs):
        self.rc, self.r, self.ss, self.rs = bufs
        x, y, c, z = place()
        self.sibling = device(x, y, 1 - c, z)

    def copy(self, src, dst, k, dev):
        return remote(src, dst, self.ss.at[k], self.rs.at[k], dev)

    def stage(self, k):
        ref = self.rc.at[1] if k == 0 else self.r.at[k - 1, 0:3]
        return self.copy(ref, ref, k, self.sibling)

    def start(self):
        self.copy(self.rc.at[0], self.rc.at[1], 0, self.sibling).start()

    def next(self, k):
        x, y, c, z = place()
        self.stage(k).wait_recv()
        if k == 0:
            total = self.rc[0] + self.rc[1]
        else:
            total = self.r[k - 1, 0] + self.r[k - 1, 1] + self.r[k - 1, 2] + self.r[k - 1, 3]
        if k == 3:
            return total
        me = (y, z, x)[k]
        self.r[k, me] = total
        for d in range(1, 4):
            to = wrap(me + d, 4)
            dev = (device(x, to, c, z), device(x, y, c, to), device(to, y, c, z))[k]
            self.copy(self.r.at[k, me], self.r.at[k, me], k + 1, dev).start()
        return None

    def finish(self):
        for k in range(4):
            self.stage(k).wait_send()


READY = ((0, 1), (2, 3, 4), (5, 6, 7))
TILE_A = (0, 1, 2, 3, 3, 0, 1, 2)


class TileReduction:
    @staticmethod
    def scratch():
        dma = pltpu.SemaphoreType.DMA
        return [
            VM((4, NZ, 144, 128), BF16), VM((3, NZ, 144, 128), BF16), VM((NZ, 144, 128), BF16),
            VM((3, 144, 128), BF16), VM((4, 144, 128), BF16), dma((5,)), dma((8,)),
        ]

    def __init__(self, own, fin, bufs):
        self.own, self.fin = own, fin
        self.rc, self.r1, self.s1, self.r2, self.r3, self.ss, self.rs = bufs
        self.x, self.y, self.c, self.z = place()
        self.flip = self.c == 1
        self.a, self.b = jnp.where(self.flip, self.y, self.x), jnp.where(self.flip, self.x, self.y)
        last = jnp.where(self.a == 3, 4, 5 + self.a)
        self.tile = jnp.where(self.c == lax.rem(self.a + 1, 2), self.a, last)

    def at(self, a, b, z, core=None):
        core = self.c if core is None else core
        return device(jnp.where(self.flip, b, a), jnp.where(self.flip, a, b), core, z)

    def whole(self, ref, k):
        return remote(
            ref, ref, self.ss.at[k], self.rs.at[3 + k], device(self.x, self.y, 1 - self.c, self.z))

    def core_copy(self, t):
        return remote(
            self.own.at[t], self.rc.at[t // 2], self.ss.at[0], self.rs.at[t // 2],
            device(self.x, self.y, 1 - self.c, self.z))

    def core_start(self, tiles):
        for t in tiles:

            @pl.when(self.c == t % 2)
            def _(t=t):
                self.core_copy(t).start()

    def core_add(self, tiles):
        for t in tiles:

            @pl.when(self.c != t % 2)
            def _(t=t):
                self.core_copy(t).wait_recv()
                for j in range(NZ):
                    self.own[t, j] = self.own[t, j] + self.rc[t // 2, j]

    def first_start(self, tiles):
        for t in tiles:
            to = TILE_A[t]

            @pl.when(jnp.logical_and(self.c != t % 2, self.a != to))
            def _(t=t, to=to):
                k = jnp.maximum(wrap(to + NX - self.a, NX) - 1, 0)
                remote(
                    self.own.at[t], self.r1.at[k], self.ss.at[1], self.rs.at[4],
                    self.at(to, self.b, self.z)).start()

    def first_sum(self):
        self.whole(self.r1, 1).wait_recv()
        for j in range(NZ):
            total = self.own[self.tile, j].astype(F32) + self.r1[0, j].astype(F32)
            total = total + self.r1[1, j].astype(F32) + self.r1[2, j].astype(F32)
            self.s1[j] = total.astype(BF16)

    def z_start(self):
        for d in range(1, NZ):
            to = wrap(self.z + d, NZ)
            remote(
                self.s1.at[to], self.r2.at[d - 1], self.ss.at[2], self.rs.at[5],
                device(self.x, self.y, self.c, to)).start()

    def z_sum(self):
        self.whole(self.r2, 2).wait_recv()
        total = self.s1[self.z].astype(F32) + self.r2[0].astype(F32)
        total = total + self.r2[1].astype(F32) + self.r2[2].astype(F32)
        self.r3[self.b] = total.astype(BF16)

    def exchange_start(self):
        ref = self.r3.at[self.b]
        for d in range(1, NY):
            remote(ref, ref, self.ss.at[3], self.rs.at[6],
                   self.at(self.a, wrap(self.b + d, NY), self.z)).start()

    def gather_start(self):
        self.whole(self.r3.at[0:3], 3).wait_recv()
        total = self.r3[0].astype(F32) + self.r3[1].astype(F32)
        total = total + self.r3[2].astype(F32) + self.r3[3].astype(F32)
        where = (slice(None), pl.ds(pl.multiple_of(self.tile * 128, 128), 128))
        self.fin[where] = total.astype(BF16)
        ref = self.fin.at[where]
        for e in range(2):
            for d in range(NX):
                if e or d:
                    remote(ref, ref, self.ss.at[4], self.rs.at[7],
                           self.at(wrap(self.a + d, 4), self.b, self.z, wrap(self.c + e, 2))).start()

    def gather_wait(self):
        self.whole(self.fin.at[:, 0:896], 4).wait_recv()

    def finish(self):
        for ref, k in (
            (self.rc, 0), (self.r1, 1), (self.r2, 2), (self.r3.at[0:3], 3), (self.fin.at[:, 0:896], 4),
        ):
            self.whole(ref, k).wait_send()


def step_kernel(
    tok_hbm, cot_hbm, cos_hbm, sin_hbm, vstates, states,
    block_out, grad_in, new_states, new_vectors, wgu_all, wdn_all, s,
):
    x, y, c, z = place()
    sib = device(x, y, 1 - c, z)
    zdev = [device(x, y, c, wrap(z + d, NZ)) for d in range(1, NZ)]
    xdev = [device(wrap(x + d, NX), y, c, z) for d in range(1, NX)]
    ydev = [device(x, wrap(y + d, NY), c, z) for d in range(1, NY)]
    peers = [sib] + xdev + ydev + zdev
    for d in range(1, 4):
        peers.append(device(wrap(x + d, NX), y, 1 - c, z))
        peers.append(device(x, wrap(y + d, NY), 1 - c, z))
    barrier = pltpu.get_barrier_semaphore()
    for peer in peers:
        pl.semaphore_signal(barrier, inc=1, device_id=peer, device_id_type=MESH)
    wq_v, vec_v, q_s, qt_s, kvs = s["wq"], s["vec"], s["q"], s["qt"], s["kv"]
    wo_all, b_gu, b_dn, n1t = s["wo"], s["ggu"].at[0, 0:2], s["gdn"].at[0, 0:2], s["n1t"]
    m_s, l_s, ot_s, lse, att = s["m"], s["l"], s["ot"], s["lse"], s["att"]
    loc_sem = s["loc"]
    row0 = pl.multiple_of(z * ROWS, ROWS)
    loads = [
        pltpu.make_async_copy(cos_hbm.at[pl.ds(row0, ROWS)], s["cos"], loc_sem.at[0]),
        pltpu.make_async_copy(sin_hbm.at[pl.ds(row0, ROWS)], s["sin"], loc_sem.at[1]),
        pltpu.make_async_copy(cot_hbm, s["n2t"], loc_sem.at[2]),
    ]
    masters = new_states[0]
    master_loads = [
        pltpu.make_async_copy(states[0][k], masters[k], s["st_sem"].at[0, k]) for k in range(4)]
    tok_t = s["tok"]
    tok_load = pltpu.make_async_copy(tok_hbm, tok_t, loc_sem.at[7])
    vector_loads = [
        pltpu.make_async_copy(vstates[i], new_vectors[i], s["v_sem"].at[i]) for i in range(3)]
    for load in vector_loads[0:1] + master_loads[0:1] + [tok_load] + master_loads[1:] + vector_loads[1:] + loads:
        load.start()
    vec_v[0] = jnp.zeros((1, VW), F32)
    vector_loads[0].wait()
    vec_v[0, :, 0:528] = new_vectors[0][...].reshape(1, 528)
    rolled = pltpu.roll(jnp.broadcast_to(vec_v[0], (8, VW)), z * 528, 1)
    vec_v[0] = rolled[0:1, :]
    qrows = pl.ds(pl.multiple_of(z * 144, 144), 144)
    master_loads[0].wait()
    wq_v[qrows, 0:896] = masters[0][:, 0:896].astype(BF16)
    wq_v[qrows, 896:1024] = jnp.concatenate(
        [masters[0][:, 896:960].astype(BF16), jnp.zeros((144, 64), BF16)], axis=1
    )
    pl.semaphore_wait(barrier, len(peers))

    sent = []

    def group(copies, name, shape):
        whole = remote(shape, shape, s["ss"].at[name], s["rs"].at[name], sib)
        return copies, whole

    def pair_of(name):
        return s["ss"].at[name], s["rs"].at[name]

    def begin(batch):
        for copy in batch[0]:
            copy.start()
        sent.append(batch[1])

    kcols = pl.ds(pl.multiple_of(512 + c * 256, 256), 256)
    xcols = pl.ds(pl.multiple_of(x * 128, 128), 128)
    ref_k, ref_q = wq_v.at[qrows, kcols], wq_v.at[qrows, xcols]
    k_over_z = group([remote(ref_k, ref_k, *pair_of(0), dev) for dev in zdev], 0, wq_v.at[0:432, 0:256])
    v_over_z = group(
        [remote(vec_v.at[0], vec_v.at[d], *pair_of(1), zdev[d - 1]) for d in range(1, NZ)], 1, vec_v.at[1:4])
    q_over_z = group([remote(ref_q, ref_q, *pair_of(2), dev) for dev in zdev], 2, wq_v.at[0:432, 0:128])
    begin(k_over_z)
    begin(v_over_z)

    @pl.when(c == 0)
    def _():
        for copy in q_over_z[0]:
            copy.start()

    def block_rows(e, n):
        return pl.ds(pl.multiple_of(wrap(z + NZ - e, NZ) * n, n), n)

    tok_load.wait()
    inputs = jnp.transpose(tok_t[...].astype(F32))
    s["gh"][...] = inputs
    unit = inputs * lax.rsqrt(jnp.mean(inputs * inputs, axis=-1, keepdims=True) + EPS)

    master_loads[1].wait()
    wo_all[qrows, 0:512] = masters[1][:, 0:512].astype(BF16)
    wo_all[qrows, 512:640] = jnp.concatenate(
        [masters[1][:, 512:576].astype(BF16), jnp.zeros((144, 64), BF16)], axis=1)
    own = []
    master_loads[2].wait()
    master_loads[3].wait()
    down = jnp.transpose(masters[3][...]).astype(BF16)
    zrows = pl.ds(pl.multiple_of(z * 384, 384), 384)
    for p in range(8):
        b_gu[p // 4, p % 4] = masters[2][:, 384 * p : 384 * p + 384].astype(BF16)
        b_dn[p // 4, p % 4] = down[48 * p : 48 * p + 48, :]
        own.append(
            pltpu.make_async_copy(
                b_gu.at[p // 4, p % 4], wgu_all.at[qrows, 384 * p : 384 * p + 384], loc_sem.at[5]))
        own.append(
            pltpu.make_async_copy(
                b_dn.at[p // 4, p % 4], wdn_all.at[pl.ds(pl.multiple_of(z * 384 + 48 * p, 48), 48), :],
                loc_sem.at[6]))
    own_done = [
        pltpu.make_async_copy(wgu_all.at[qrows, :], wgu_all.at[qrows, :], loc_sem.at[5]),
        pltpu.make_async_copy(wdn_all.at[zrows, :], wdn_all.at[zrows, :], loc_sem.at[6]),
    ]
    for copy in own:
        copy.start()

    w = wrap(x + y, 4)
    pgu = pl.multiple_of((c * 4 + w) * 384, 128)
    pdn = (c * 4 + y) * 48
    po = jnp.minimum(c * 4 + y, 4)
    has_o = c * 4 + y < 5
    oc = pl.multiple_of(po * 128, 128)

    def down_rows(zz):
        return wdn_all.at[pl.ds(pl.multiple_of(zz * 384 + pdn, 48), 48), :]

    o_over_z = group(
        [remote(wo_all.at[qrows, pl.ds(oc, 128)], wo_all.at[qrows, pl.ds(oc, 128)], *pair_of(3), dev) for dev in zdev],
        3, wo_all.at[0:432, 0:128])
    gu_over_z = group(
        [remote(b_gu.at[c, w], wgu_all.at[qrows, pl.ds(pgu, 384)], *pair_of(4), dev) for dev in zdev],
        4, wgu_all.at[0:432, 0:384])
    dn_over_z = group(
        [remote(b_dn.at[c, y], down_rows(z), *pair_of(5), dev) for dev in zdev], 5, wdn_all.at[0:144, :])

    def weights_over_z():
        @pl.when(has_o)
        def _():
            for copy in o_over_z[0]:
                copy.start()

        for copy in dn_over_z[0] + gu_over_z[0]:
            copy.start()

    weights_over_z()
    k_over_z[1].wait_recv()
    v_over_z[1].wait_recv()
    others = range(1, NZ)
    k_over_c = group(
        [remote(wq_v.at[block_rows(e, 144), kcols], wq_v.at[block_rows(e, 144), kcols], *pair_of(6), sib)
         for e in others], 6, wq_v.at[0:432, 0:256])
    begin(k_over_c)

    q_over_x = group(
        [remote(wq_v.at[block_rows(e, 144), xcols], wq_v.at[block_rows(e, 144), xcols], *pair_of(7), dev)
         for e in others for dev in xdev], 7, wq_v.at[0:432, 0:384])
    q_over_c = group(
        [remote(wq_v.at[block_rows(e, 144), 0:512], wq_v.at[block_rows(e, 144), 0:512], *pair_of(8), sib)
         for e in others], 8, wq_v.at[0:432, 0:512])

    @pl.when(c == 0)
    def _():
        q_over_z[1].wait_recv()
        for copy in q_over_x[0]:
            copy.start()

    raw = vec_v[0] + vec_v[1] + vec_v[2] + vec_v[3]
    raw = raw.astype(BF16).astype(F32)
    wide = jnp.broadcast_to(raw, (8, VW))
    gain_one = raw[:, 0:576]
    gain_two = pltpu.roll(wide, VW - 576, 1)[0:1, 0:576]
    bias = raw[:, 1152:2176]
    normed = unit * gain_one
    n1 = normed.astype(BF16)
    n1t[...] = jnp.transpose(normed).astype(BF16)
    for load in loads:
        load.wait()
    cosine, sine = s["cos"][...], s["sin"][...]

    k_over_c[1].wait_recv()

    def tile_of(v, t):
        return v[:, 128 * t : 128 * t + 128]

    def rotated(v):
        return v * cosine + swap_halves(v) * sine

    def turn(v):
        return pltpu.roll(v, 64, 1)

    proj = dot(n1, wq_v[:, 512:1024]) + bias[:, 512:1024]
    rot4, rot5 = rotated(tile_of(proj, 0)), rotated(tile_of(proj, 1))
    val6, val7 = tile_of(proj, 2), tile_of(proj, 3)
    low = low_lanes(rot4)
    kvs[z, 0] = jnp.where(low, turn(rot4), turn(val6)).astype(BF16)
    kvs[z, 1] = jnp.where(low, rot5, val6).astype(BF16)
    kvs[z, 2] = jnp.where(low, turn(rot5), turn(val7)).astype(BF16)
    kv_sends = []
    for d in range(1, NZ):
        kv_sends.append(
            remote(kvs.at[z], kvs.at[z], s["kv_s"].at[d - 1], s["kv_r"].at[d - 1],
                   device(x, y, c, wrap(z + d, NZ))))

        @pl.when(z + d < NZ)
        def _(d=d):
            kv_sends[d - 1].start()

    def put_query(h, part):
        qh = jnp.where(low, part, 0.0) * (HEAD_DIM ** -0.5)
        q_s[h] = qh.astype(BF16)
        qt_s[h] = jnp.transpose(qh).astype(BF16)

    put_query(8, rot4)
    s["cot"][...] = jnp.transpose(s["n2t"][...].astype(F32)).astype(BF16)

    @pl.when(c == 0)
    def _():
        q_over_x[1].wait_recv()
        for copy in q_over_c[0]:
            copy.start()

    @pl.when(c == 1)
    def _():
        q_over_c[1].wait_recv()

    proj = dot(n1, wq_v[:, 0:512]) + bias[:, 0:512]
    for t in range(4):
        rot = rotated(tile_of(proj, t))
        put_query(2 * t, rot)
        put_query(2 * t + 1, turn(rot))

    def step(j):
        kvt = [jnp.transpose(kvs[j, g].astype(F32)).astype(BF16)[64:128, :] for g in range(KV_HEADS)]
        heads = range(HEADS)
        sts = [dot(kvs[j, h // GROUP], qt_s[h]) for h in heads]
        olds = [m_s[h] for h in heads]
        peaks = [jnp.maximum(jnp.max(v, axis=0, keepdims=True), o) for v, o in zip(sts, olds)]
        alphas = [jnp.exp(o - p) for o, p in zip(olds, peaks)]
        ps = [jnp.exp(v - p) for v, p in zip(sts, peaks)]
        totals = [jnp.sum(p, axis=0, keepdims=True) + l_s[h] * a for h, p, a in zip(heads, ps, alphas)]
        outs = [dot(kvt[h // GROUP], p.astype(BF16)) + ot_s[h] * a for h, p, a in zip(heads, ps, alphas)]
        for h in heads:
            m_s[h] = peaks[h]
            l_s[h] = totals[h]
            ot_s[h] = outs[h]

    def visible(width):
        shape = (256, width)
        return lax.broadcasted_iota(jnp.int32, shape, 0) <= lax.broadcasted_iota(jnp.int32, shape, 1)

    right = slice(256, 512)
    always = z >= 0

    gu_over_z[1].wait_recv()
    dn_over_z[1].wait_recv()

    @pl.when(has_o)
    def _():
        o_over_z[1].wait_recv()

    def gu_piece(e, ww):
        return wgu_all.at[block_rows(e, 144), pl.ds(pl.multiple_of((c * 4 + ww) * 384, 128), 384)]

    def o_piece(e):
        return wo_all.at[block_rows(e, 144), pl.ds(oc, 128)]

    def dn_half(e):
        return wdn_all.at[
            pl.ds(pl.multiple_of(wrap(z + NZ - e, NZ) * 384 + c * 192, 192), 192), :]

    def dn_piece(e):
        return down_rows(wrap(z + NZ - e, NZ))

    gu_over_x = group(
        [remote(gu_piece(e, w), gu_piece(e, w), *pair_of(9), dev) for e in others for dev in xdev],
        9, wgu_all.at[0:432, 0:1152])
    dn_over_y = group(
        [remote(dn_piece(e), dn_piece(e), *pair_of(10), dev) for e in others for dev in ydev],
        10, wdn_all.at[0:432, :])
    o_over_y = [
        [remote(o_piece(e), o_piece(e), s["ss"].at[11], s["os"].at[d - 1], ydev[d - 1]) for e in others]
        for d in range(1, NY)]
    o_sent = remote(wo_all.at[0:432, 0:384], wo_all.at[0:432, 0:384], s["ss"].at[11], s["os"].at[0], sib)
    own_over_c = group(
        [remote(gu_piece(e, w), gu_piece(e, w), *pair_of(12), sib) for e in others], 12, wgu_all.at[0:432, 0:384])
    gu_over_c = group(
        [remote(gu_piece(e, wrap(w + d, NX)), gu_piece(e, wrap(w + d, NX)), *pair_of(13), sib)
         for e in others for d in range(1, NX)], 13, wgu_all.at[0:432, 0:1152])
    dn_over_c = group(
        [remote(dn_half(e), dn_half(e), *pair_of(14), sib) for e in others], 14, wdn_all.at[0:576, :])
    o_over_c = []
    for core, cols in enumerate((slice(0, 512), slice(512, 640))):
        o_over_c.append(
            group(
                [remote(wo_all.at[block_rows(e, 144), cols], wo_all.at[block_rows(e, 144), cols], *pair_of(15), sib)
                 for e in others], 15, wo_all.at[0:432, cols]))

    @pl.when(has_o)
    def _():
        for copies in o_over_y:
            for copy in copies:
                copy.start()

    begin(dn_over_y)
    begin(gu_over_x)
    begin(own_over_c)

    @pl.when(always)
    def _():
        keep_a, keep_b = visible(512), visible(256)
        kvt = [jnp.transpose(kvs[z, g].astype(F32)).astype(BF16)[64:128, :] for g in range(KV_HEADS)]
        heads = range(HEADS)
        st_a = [jnp.where(keep_a, dot(kvs[z, h // GROUP, 0:256], qt_s[h]), MASK_FILL) for h in heads]
        st_b = [jnp.where(keep_b, dot(kvs[z, h // GROUP, right], qt_s[h, :, right]), MASK_FILL) for h in heads]
        none = jnp.full((1, 256), MASK_FILL, F32)
        zero = jnp.zeros((1, 256), F32)
        zeros = jnp.zeros((64, 256), F32)
        peaks = [
            jnp.maximum(
                jnp.max(a, axis=0, keepdims=True),
                jnp.concatenate([none, jnp.max(b, axis=0, keepdims=True)], axis=1))
            for a, b in zip(st_a, st_b)]
        p_a = [jnp.exp(a - p) for a, p in zip(st_a, peaks)]
        p_b = [jnp.exp(b - p[:, right]) for b, p in zip(st_b, peaks)]
        totals = [
            jnp.sum(a, axis=0, keepdims=True) + jnp.concatenate([zero, jnp.sum(b, axis=0, keepdims=True)], axis=1)
            for a, b in zip(p_a, p_b)]
        outs = [
            dot(kvt[h // GROUP][:, 0:256], p_a[h].astype(BF16))
            + jnp.concatenate([zeros, dot(kvt[h // GROUP][:, right], p_b[h].astype(BF16))], axis=1)
            for h in heads]
        for h in heads:
            m_s[h] = peaks[h]
            l_s[h] = totals[h]
            ot_s[h] = outs[h]

    def earlier(d, carry):
        @pl.when(d == NZ - 1)
        def _():
            for dd in range(1, NY):
                from_y = wrap(y + NY - dd, NY)

                @pl.when(c * 4 + from_y < 5)
                def _(dd=dd):
                    remote(wo_all.at[0:432, 0:128], wo_all.at[0:432, 0:128], s["ss"].at[11], s["os"].at[dd - 1],
                           sib).wait_recv()

            for core in range(2):

                @pl.when(c == core)
                def _(core=core):
                    for copy in o_over_c[core][0]:
                        copy.start()

            dn_over_y[1].wait_recv()
            begin(dn_over_c)

        @pl.when(z >= d)
        def _():
            remote(kvs.at[z], kvs.at[z], s["kv_s"].at[d - 1], s["kv_r"].at[d - 1], sib).wait_recv()
            step(z - d)

        return carry

    lax.fori_loop(1, NZ, earlier, 0)

    for h in range(HEADS):
        ot_s[h] = ot_s[h] * (1.0 / l_s[h])
        lse[h] = m_s[h] + jnp.log(l_s[h])
    for t in range(5):
        top = ot_s[2 * t]
        bottom = ot_s[2 * t + 1] if 2 * t + 1 < HEADS else jnp.zeros((64, ROWS), F32)
        att[:, 128 * t : 128 * t + 128] = jnp.transpose(jnp.concatenate([top, bottom], axis=0)).astype(BF16)

    for core in range(2):

        @pl.when(c == core)
        def _(core=core):
            o_over_c[1 - core][1].wait_recv()

    for copy in own_done:
        copy.wait()
    wo = wo_all
    wgu, wds, w_sem = s["wgu"], s["wds"], s["w_sem"]

    def weights(i, slot):
        col = pl.multiple_of(wrap(w + i, 4) * 384, 384)
        return [
            pltpu.make_async_copy(
                wgu_all.at[:, pl.ds(col, 384)], wgu.at[slot, :, 0:384], w_sem.at[0, slot]),
            pltpu.make_async_copy(
                wgu_all.at[:, pl.ds(pl.multiple_of(col + FF, 384), 384)], wgu.at[slot, :, 384:768],
                w_sem.at[0, slot]),
            pltpu.make_async_copy(wdn_all.at[pl.ds(col, 384), :], wds.at[slot], w_sem.at[1, slot]),
        ]

    def weights_wait(slot):
        pltpu.make_async_copy(wgu_all.at[:, 0:768], wgu.at[slot], w_sem.at[0, slot]).wait()
        pltpu.make_async_copy(wdn_all.at[0:384, :], wds.at[slot], w_sem.at[1, slot]).wait()

    gu_over_z[1].wait_send()
    dn_over_z[1].wait_send()
    dn_over_c[1].wait_recv()
    own_over_c[1].wait_recv()
    for load in weights(0, 0):
        load.start()
    gu_over_x[1].wait_recv()
    begin(gu_over_c)

    ggu, gdn, go, gq, fin = s["ggu"], s["gdn"], s["go"], s["gq"], s["fin"]
    def columns(width):
        def at(cc, a, count):
            return (slice(None), pl.ds(pl.multiple_of((cc * 4 + a) * width, 128), count * width))

        return at

    def down_at(cc, a, count):
        return (pl.ds(pl.multiple_of((cc * 4 + a) * 48, 48), count * 48), slice(None))

    red_gu = Reduction(ggu, fin["gu"], columns(384), s["red_gu"], 0, False)
    red_dn = Reduction(gdn, fin["dn"], down_at, s["red_dn"], 1, True)
    red_o = Reduction(go, fin["o"], columns(128), s["red_o"], 0, False)
    red_q = TileReduction(gq, fin["q"], s["red_q"])
    vecs = VectorSum(s["vecs"])
    cot, gh, n2, n2t, gn2t = s["cot"], s["gh"], s["n2"], s["n2t"], grad_in
    do_in, dot_in, delta_in, gain_row = s["do"], s["dot"], s["delta"], s["gain_row"]
    dqt, own_kv, skv, rkv = ot_s, s["own_kv"], s["skv"], s["rkv"]

    gn2t[...] = jnp.zeros_like(gn2t)
    hid = gh[...] + dot(att[:, 0:576], wo[:, 0:576])
    inv_two = lax.rsqrt(jnp.mean(hid * hid, axis=-1, keepdims=True) + EPS)
    normed = hid * inv_two * gain_two
    n2[...] = normed.astype(BF16)
    n2t[...] = jnp.transpose(normed).astype(BF16)
    gh[...] = hid
    block_out[...] = jnp.transpose(hid)

    def chunk(i, carry):
        slot = lax.rem(i, 2)
        here = wrap(w + i, 4)
        @pl.when(i > 0)
        def _():
            red_gu.core_add(wrap(w + i + 3, 4))
            red_gu.first_piece(wrap(w + i + 3, 4))

        weights_wait(slot)

        @pl.when(jnp.logical_and(i > 0, i < 3))
        def _():
            for load in weights(i + 1, 1 - slot):
                load.start()

        both = dot(n2[...], wgu[slot])
        gate, up = both[:, 0:384], both[:, 384:768]
        sg = jax.nn.sigmoid(gate)
        silu = gate * sg
        act = (silu * up).astype(BF16)
        ga = dot(cot[...], wds[slot], 1, 1)
        gg = (ga * up * sg * (1.0 + gate * (1.0 - sg))).astype(BF16)
        gu = (ga * silu).astype(BF16)
        grads = jnp.concatenate([gg, gu], axis=1)
        both = dot(n2t[...], grads).astype(BF16)
        ggu[0, here] = both[:, 0:384].reshape(NZ, 144, 384)
        ggu[1, here] = both[:, 384:768].reshape(NZ, 144, 384)
        red_gu.core_copy(here).start()
        down = dot(act, cot[...], 0, 0).astype(BF16)
        for p in range(8):
            gdn[p // 4, here, p % 4] = down[48 * p : 48 * p + 48, :]
        red_dn.core_copy(here).start()

        @pl.when(i == 0)
        def _():
            gu_over_c[1].wait_recv()
            for load in weights(1, 1):
                load.start()

        block_out[...] += lax.dot_general(wds[slot], act, (((0,), (1,)), ((), ())), preferred_element_type=F32)
        gn2t[...] += dot(wgu[slot], grads, 1, 1)

        return carry

    lax.fori_loop(0, 4, chunk, 0)

    red_gu.core_add(wrap(w + 3, 4))
    red_gu.first_piece(wrap(w + 3, 4))
    state_loads = []
    for i in range(1, 3):
        for k in range(4):
            copy = pltpu.make_async_copy(states[i][k], new_states[i][k], s["st_sem"].at[i, k])
            copy.start()
            state_loads.append(copy)

    @pl.when(always)
    def _():
        hid = gh[...]
        inv_two = lax.rsqrt(jnp.mean(hid * hid, axis=-1, keepdims=True) + EPS)
        u = hid * inv_two
        e = jnp.transpose(gn2t[...])
        f = e * gain_two
        gain_row[:, 0:576] = jnp.sum(e * u, axis=0, keepdims=True)
        gain_row[:, 576:640] = jnp.zeros((1, 64), F32)
        grad_hidden = cot[...].astype(F32) + inv_two * (f - u * jnp.mean(f * u, axis=-1, keepdims=True))
        gh[...] = grad_hidden
        ghl = grad_hidden.astype(BF16)
        grad_out = dot(att[:, 0:576], ghl, 0, 0).astype(BF16)
        for p in range(8):
            if p < 4:
                part = grad_out[:, 128 * p : 128 * p + 128]
            elif p == 4:
                part = jnp.concatenate([grad_out[:, 512:576], jnp.zeros((D, 64), BF16)], axis=1)
            else:
                part = jnp.zeros((D, 128), BF16)
            go[p // 4, p % 4] = part.reshape(NZ, 144, 128)
        red_o.core_all(lambda k: red_o.core_copy(k).start())
        gm = dot(ghl, wo[:, 0:576], 1, 1).astype(BF16).astype(F32)
        gm = jnp.concatenate([gm, jnp.zeros((ROWS, 64), F32)], axis=1)
        for h in range(HEADS):
            part = gm[:, 128 * (h // 2) : 128 * (h // 2) + 128]
            part = part if h % 2 == 1 else turn(part)
            part = jnp.where(low_lanes(part), 0.0, part)
            do_in[h] = part.astype(BF16)
            part = jnp.transpose(part)
            dot_in[h] = part.astype(BF16)
            delta_in[h] = jnp.sum(part[64:128, :] * ot_s[h], axis=0, keepdims=True)

    red_dn.core_all(red_dn.core_add)
    red_dn.first_start()

    def attend(g, j):
        kv = kvs[j, g]
        kt = jnp.transpose(kv.astype(F32)).astype(BF16)[0:64, :]
        totals = [None, None]
        for i in range(GROUP):
            h = g * GROUP + i
            dq = None
            for half in range(2):
                rows = slice(256 * half, 256 * half + 256)
                pt = jnp.exp(dot(kv[rows], qt_s[h]) - lse[h])
                dst = (pt * (dot(kv[rows], dot_in[h]) - delta_in[h])).astype(BF16)
                both = dot(dst, q_s[h]) + dot(pt.astype(BF16), do_in[h])
                totals[half] = both if i == 0 else totals[half] + both
                part = dot(kt[:, rows], dst)
                dq = part if half == 0 else dq + part
            dqt[h] += dq
        return totals

    def attend_own(g):
        keep_a, keep_b = visible(512), visible(256)
        kv = kvs[z, g]
        kt = jnp.transpose(kv.astype(F32)).astype(BF16)[0:64, :]
        left = slice(0, 256)
        totals = [None, None]
        for i in range(GROUP):
            h = g * GROUP + i
            pt = jnp.where(keep_a, jnp.exp(dot(kv[left], qt_s[h]) - lse[h]), 0.0)
            dst = (pt * (dot(kv[left], dot_in[h]) - delta_in[h])).astype(BF16)
            both = dot(dst, q_s[h]) + dot(pt.astype(BF16), do_in[h])
            totals[0] = both if i == 0 else totals[0] + both
            dq = dot(kt[:, left], dst)
            pt = jnp.where(keep_b, jnp.exp(dot(kv[right], qt_s[h, :, right]) - lse[h, :, right]), 0.0)
            dst = (pt * (dot(kv[right], dot_in[h, :, right]) - delta_in[h, :, right])).astype(BF16)
            both = dot(dst, q_s[h, right]) + dot(pt.astype(BF16), do_in[h, right])
            totals[1] = both if i == 0 else totals[1] + both
            dqt[h] += dq
            dqt[h, :, right] += dot(kt[:, right], dst)
        own_kv[g, left] = totals[0]
        own_kv[g, right] = totals[1]

    def kv_copy(g, k, dev):
        return remote(
            skv.at[g, k - 1], rkv.at[g, k - 1], s["ss"].at[16], s["dkv_r"].at[g], dev)

    gps = q_s

    def kv_wait(g):
        for count in range(1, NZ):

            @pl.when(z + count == NZ - 1)
            def _(count=count):
                part = rkv.at[g, 0:count]
                remote(part, part, s["ss"].at[16], s["dkv_r"].at[g], sib).wait_recv()
                total = own_kv[g]
                for k in range(count):
                    total = total + rkv[g, k].astype(F32)
                own_kv[g] = total

    def group_tiles(g):
        cos_t, sin_t = s["cos"][...], s["sin"][...]
        low = low_lanes(cos_t)
        kv = own_kv[g]

        def query(top, bottom):
            both = [dqt[h] if h is not None else jnp.zeros((64, ROWS), F32) for h in (top, bottom)]
            return jnp.transpose(jnp.concatenate(both, axis=0)) * (HEAD_DIM ** -0.5)

        def back(t):
            return t * cos_t - swap_halves(t) * sin_t

        if g == 0:
            return {
                0: back(query(0, 1)),
                1: back(jnp.where(low, query(2, None), turn(kv))),
                2: jnp.where(low, turn(kv), 0.0),
            }
        if g == 1:
            return {
                2: jnp.where(low, 0.0, back(query(None, 3))),
                3: back(query(4, 5)),
                4: jnp.where(low, back(kv), kv),
            }
        return {
            5: back(query(6, 7)),
            6: back(jnp.where(low, query(8, None), turn(kv))),
            7: jnp.where(low, turn(kv), 0.0),
        }

    def tiles_of(g):
        @pl.when(always)
        def _():
            for t, tile in group_tiles(g).items():
                if t == 2 and g == 0:
                    gps[2] = tile.astype(BF16)
                    continue
                if t == 2:
                    tile = tile + gps[2].astype(F32)
                low_tile = tile.astype(BF16)
                gps[t] = low_tile
                gq[t] = dot(n1t[...], low_tile).astype(BF16).reshape(NZ, 144, 128)

        red_q.core_start((READY[g]))

    dqt[...] = jnp.zeros_like(dqt)
    early = red_q.tile <= 4
    late = red_q.tile > 4
    own_one = jnp.where(z == NZ - 1, 9, 3)
    own_two = jnp.where(z == NZ - 1, 10, 6)

    def slot(t, carry):
        g = lax.div(t, 3)
        k = 3 - lax.rem(t, 3)

        @pl.when(jnp.logical_and(t < 9, z >= k))
        def _():
            for half, total in enumerate(attend(g, z - k)):
                skv[g, k - 1, 256 * half : 256 * half + 256] = total.astype(BF16)
            kv_copy(g, k, device(x, y, c, z - k)).start()

        @pl.when(jnp.logical_or(t == 2, jnp.logical_or(t == own_one, t == own_two)))
        def _():
            attend_own(jnp.where(t == 2, 0, jnp.where(t == own_one, 1, 2)))

        @pl.when(t == 0)
        def _():
            red_o.core_all(red_o.core_add)

        @pl.when(t == 2)
        def _():
            red_gu.first_sum()
            red_gu.z_start()
            red_o.first_start()

        @pl.when(t == 4)
        def _():
            kv_wait(0)
            tiles_of(0)

        @pl.when(t == 5)
        def _():
            red_q.core_add(READY[0])
            red_q.first_start(READY[0])
            red_gu.z_sum()
            red_gu.exchange_start()

        @pl.when(t == 9)
        def _():
            kv_wait(1)
            tiles_of(1)
            red_dn.first_sum()
            red_o.first_sum()
            red_q.core_add(READY[1])
            red_q.first_start(READY[1])
            red_gu.gather_start()

        return carry

    lax.fori_loop(0, 11, slot, 0)
    kv_wait(2)
    red_dn.z_start()
    red_o.z_start()
    tiles_of(2)
    red_q.core_add(READY[2])
    red_q.first_start(READY[2])

    low = low_lanes(s["cos"][...])

    def halves(t):
        tile = gps[t].astype(F32)
        return tile, turn(tile)

    (t0, _), (t1, u1), (t2, u2), (t3, u3) = [halves(t) for t in range(4)]
    (t4, u4), (t5, _), (t6, u6), (t7, _) = [halves(t) for t in range(4, 8)]
    ordered = [
        t0,
        jnp.where(low, t1, t2),
        t3,
        t5,
        jnp.where(low, t6, t1),
        jnp.where(low, t4, t6),
        jnp.where(low, t2, t4),
        t7,
    ]
    vecs.rc[0, 10:18, :] = jnp.concatenate(
        [jnp.sum(t, axis=0, keepdims=True) for t in ordered], axis=0)
    gn1 = dot(jnp.concatenate([t.astype(BF16) for t in ordered], axis=1), wq_v[...], 1, 1)
    inputs = jnp.transpose(tok_t[...].astype(F32))
    r = lax.rsqrt(jnp.mean(inputs * inputs, axis=-1, keepdims=True) + EPS)
    u = inputs * r
    f = gn1 * gain_one
    row = jnp.sum(gn1 * u, axis=0, keepdims=True)
    row = jnp.concatenate([row, jnp.zeros((1, 64), F32)], axis=1)
    for t in range(5):
        vecs.rc[0, t : t + 1, :] = row[:, 128 * t : 128 * t + 128]
        vecs.rc[0, 5 + t : 6 + t, :] = gain_row[:, 128 * t : 128 * t + 128]
    vecs.rc[0, 18:24, :] = jnp.zeros((6, 128), F32)
    vecs.start()
    @pl.when(early)
    def _():
        red_q.first_sum()
        red_q.z_start()

    grad_in[...] = jnp.transpose(gh[...] + r * (f - u * jnp.mean(f * u, axis=-1, keepdims=True)))

    def update(k, grad):
        new = adam_step(
            new_states[0][k][...], new_states[1][k][...], new_states[2][k][...], grad, RATE_MATRIX, DECAY_MATRIX)
        for i in range(3):
            new_states[i][k][...] = new[i]

    vecs.next(0)
    red_gu.gather_forward()
    red_dn.z_sum()
    red_dn.exchange_start()
    red_o.z_sum()
    red_o.exchange_start()

    @pl.when(late)
    def _():
        red_q.first_sum()
        red_q.z_start()

    vecs.next(1)
    @pl.when(early)
    def _():
        red_q.z_sum()
        red_q.exchange_start()

    @pl.when(late)
    def _():
        red_q.z_sum()
        red_q.exchange_start()

    red_dn.gather_start()
    red_o.gather_start()

    for load in state_loads:
        load.wait()
    red_gu.gather_wait()
    update(2, fin["gu"][...].astype(F32))
    @pl.when(early)
    def _():
        red_q.gather_start()

    vecs.next(2)

    @pl.when(late)
    def _():
        red_q.gather_start()

    red_dn.gather_forward()
    red_o.gather_forward()
    red_dn.gather_wait()
    update(3, jnp.transpose(fin["dn"][...].astype(F32)))
    red_o.gather_wait()
    update(1, fin["o"][:, 0:576].astype(F32))
    total = vecs.next(3)
    total = jnp.concatenate([total[t : t + 1, :] for t in range(18)], axis=1)
    pad = jnp.zeros((1, VW - 640), F32)
    flat = jnp.concatenate([total[:, 0:640], pad], axis=1)
    mid = jnp.concatenate([total[:, 640:1280], pad], axis=1)
    flat = flat + pltpu.roll(jnp.broadcast_to(mid, (8, VW)), 576, 1)[0:1, :]
    flat = flat + jnp.concatenate(
        [jnp.zeros((1, 1152), F32), total[:, 1280:2304], jnp.zeros((1, 128), F32)], axis=1)
    shift = lax.rem(VW - z * 528, VW)
    grad = pltpu.roll(jnp.broadcast_to(flat, (8, VW)), shift, 1)[0:1, 0:528]
    for load in vector_loads[1:]:
        load.wait()
    new = adam_step(*[v[...].reshape(1, 528) for v in new_vectors], grad, RATE_VECTOR, 0.0)
    for i in range(3):
        new_vectors[i][...] = new[i].reshape(528)
    red_q.gather_wait()
    tq = [fin["q"][:, 128 * t : 128 * t + 128].astype(F32) for t in range(8)]
    lowq = low_lanes(tq[0])
    ordered = [
        tq[0],
        jnp.where(lowq, tq[1], tq[2]),
        tq[3],
        tq[5],
        jnp.where(lowq, tq[6], tq[1]),
        jnp.where(lowq, tq[4], tq[6]),
        jnp.where(lowq, tq[2], tq[4]),
        tq[7],
    ]
    update(0, jnp.concatenate(ordered, axis=1)[:, 0:960])
    for red in (red_gu, red_dn, red_o):
        red.finish()
    red_q.finish()
    vecs.finish()
    for whole in sent:
        whole.wait_send()
    for count in range(1, NZ):

        @pl.when(z == count)
        def _(count=count):
            part = (skv.at[0], skv.at[0:2], skv)[count - 1]
            remote(part, part, s["ss"].at[16], s["dkv_r"].at[0], sib).wait_send()

    for d in range(1, NZ):

        @pl.when(z + d < NZ)
        def _(d=d):
            kv_sends[d - 1].wait_send()

    @pl.when(has_o)
    def _():
        o_over_z[1].wait_send()
        o_sent.wait_send()

    for core in range(2):

        @pl.when(c == core)
        def _(core=core):
            o_over_c[core][1].wait_send()

    @pl.when(c == 0)
    def _():
        for batch in (q_over_z, q_over_x, q_over_c):
            batch[1].wait_send()


MATRICES = ((144, 960), (144, D), (144, 2 * FF), (D, 384))


def train(tok_t, cot_t, cos_t, sin_t, vstates, states):
    sd = jax.ShapeDtypeStruct
    v = pl.BlockSpec(memory_space=VM)
    a = pl.BlockSpec(memory_space=ANY)
    dma = pltpu.SemaphoreType.DMA
    scratch = dict(
        wq=VM((D, QW), BF16), vec=VM((NZ, 1, VW), F32), cos=VM((ROWS, 128), F32), sin=VM((ROWS, 128), F32),

        q=VM((HEADS, ROWS, 128), BF16), qt=VM((HEADS, 128, ROWS), BF16), n1t=VM((D, ROWS), BF16),
        kv=VM((NZ, KV_HEADS, ROWS, 128), BF16),
        m=VM((HEADS, 1, ROWS), F32), l=VM((HEADS, 1, ROWS), F32), ot=VM((HEADS, 64, ROWS), F32),
        lse=VM((HEADS, 1, ROWS), F32), att=VM((ROWS, 640), BF16), wo=VM((D, OW), BF16),
        loc=dma((8,)), v_sem=dma((3,)), tok=VM((D, ROWS), BF16), ss=dma((17,)), rs=dma((16,)), os=dma((3,)), kv_s=dma((3,)), kv_r=dma((3,)),
        cot=VM((ROWS, D), BF16), gh=VM((ROWS, D), F32), n2=VM((ROWS, D), BF16), n2t=VM((D, ROWS), BF16),
        wgu=VM((2, D, 768), BF16), wds=VM((2, 384, D), BF16), w_sem=dma((2, 2)),
        do=VM((HEADS, ROWS, 128), BF16), dot=VM((HEADS, 128, ROWS), BF16), delta=VM((HEADS, 1, ROWS), F32),
        gain_row=VM((1, 640), F32),
        ggu=VM((2, 4, NZ, 144, 384), BF16), gdn=VM((2, NZ, 4, 48, D), BF16), go=VM((2, 4, NZ, 144, 128), BF16),
        gq=VM((8, NZ, 144, 128), BF16),
        fin=dict(gu=VM((144, 2 * FF), BF16), dn=VM((384, D), BF16), o=VM((144, QW), BF16), q=VM((144, QW), BF16)),
        own_kv=VM((KV_HEADS, ROWS, 128), F32),
        skv=VM((KV_HEADS, 3, ROWS, 128), BF16), rkv=VM((KV_HEADS, 3, ROWS, 128), BF16),
        dkv_r=dma((3,)), st_sem=dma((3, 4)),
        red_gu=Reduction.scratch((4, 4), 144, 384), red_dn=Reduction.scratch((4, 4), 48, D),
        red_o=Reduction.scratch((4, 4), 144, 128), red_q=TileReduction.scratch(),
        vecs=VectorSum.scratch(),
    )
    fast = lambda shape: VM(shape, F32)
    return pl.pallas_call(
        step_kernel,
        out_shape=(
            fast((D, ROWS)),
            fast((D, ROWS)),
            [[fast(shape) for shape in MATRICES] for _ in range(3)],
            [fast((528,)) for _ in range(3)],
            pltpu.HBM((D, 2 * FF), BF16),
            pltpu.HBM((FF, D), BF16),
        ),
        in_specs=[a, a, a, a, [a] * 3, [[a] * 4] * 3],
        out_specs=(v, v, [[v] * 4] * 3, [v] * 3, a, a),
        scratch_shapes=[scratch],
        compiler_params=pltpu.CompilerParams(
            collective_id=0, has_side_effects=True, vmem_limit_bytes=51 << 20),
        name="train_step",
    )(tok_t, cot_t, cos_t, sin_t, vstates, states)


def adam_step(weight, first_state, second_state, gradient, learn_rate, decay_rate):
    first_new = BETA_ONE * first_state + (1.0 - BETA_ONE) * gradient
    second_new = BETA_TWO * second_state + (1.0 - BETA_TWO) * gradient * gradient
    corr_one = 1.0 - BETA_ONE**STEP
    corr_two = 1.0 - BETA_TWO**STEP
    update = first_new / corr_one / (jnp.sqrt(second_new / corr_two) + ADAM_EPS)
    weight_new = weight - learn_rate * (update + decay_rate * weight)
    return (weight_new, first_new, second_new)


def store_kernel(sources, *rest):
    targets, sems = rest[:-1], rest[-1]
    copies = [
        pltpu.make_async_copy(a, b, sems.at[k])
        for k, (a, b) in enumerate(zip(jax.tree.leaves(sources), jax.tree.leaves(targets)))]
    for copy in copies:
        copy.start()
    for copy in copies:
        copy.wait()


def store(arrays):
    shapes = jax.tree.map(lambda t: jax.ShapeDtypeStruct(t.shape, t.dtype), arrays)
    count = len(jax.tree.leaves(arrays))
    v = pl.BlockSpec(memory_space=VM)
    a = pl.BlockSpec(memory_space=ANY)
    return pl.pallas_call(
        store_kernel,
        out_shape=shapes,
        in_specs=[jax.tree.map(lambda t: v, arrays)],
        out_specs=jax.tree.map(lambda t: a, arrays),
        scratch_shapes=[pltpu.SemaphoreType.DMA((count,))],
        compiler_params=pltpu.CompilerParams(vmem_limit_bytes=8 << 20),
        name="store",
    )(arrays)


def per_device(
    tokens, cotangent, w_qkv, w_out, w_gate_up, w_down, vectors,
    first_qkv, first_out, first_gate_up, first_down, first_vectors,
    second_qkv, second_out, second_gate_up, second_down, second_vectors,
):
    cos_np, sin_np = rope_tables()
    cos_t, sin_t = jnp.asarray(cos_np), jnp.asarray(sin_np)
    states = [
        [w_qkv, w_out, w_gate_up, w_down.T],
        [first_qkv, first_out, first_gate_up, first_down.T],
        [second_qkv, second_out, second_gate_up, second_down.T],
    ]
    vstates = [vectors, first_vectors, second_vectors]
    outs = train(
        tokens.T, cotangent.T, cos_t, sin_t, vstates, states)
    block_t, grad_t, matrices, vecs = store(tuple(outs[0:4]))
    out = [block_t.T, grad_t.T]
    for i in range(3):
        out += list(matrices[i][0:3]) + [matrices[i][3].T, vecs[i]]
    return tuple(out)


def solution(mesh):
    tokens = P(("dp", "ctx"), None)
    state = (P("ctx", None),) * 4 + (P("ctx"),)
    return jax.shard_map(
        per_device, mesh=mesh, in_specs=(tokens, tokens) + state * 3, out_specs=(tokens, tokens) + state * 3,
        check_vma=False,
    )
```

```python
import functools

import jax
import jax.numpy as jnp
import numpy as np
from jax import lax
from jax.experimental import pallas as pl
from jax.experimental.pallas import tpu as pltpu
from jax.sharding import PartitionSpec as P

D = 576
HEADS = 9
KV_HEADS = 3
GROUP = 3
HEAD_DIM = 64
FF = 1536
STEP = 10
LEN = 2048
ROWS = 512
QW = 1024
OW = 640
VW = 2304
NX = 4
NY = 4
NZ = 4

EPS = 1e-05
ROPE_BASE = 100000.0
MASK_FILL = -1e30
BETA_ONE = 0.9
BETA_TWO = 0.999
ADAM_EPS = 1e-08
RATE_MATRIX = 0.05
RATE_VECTOR = 0.5
DECAY_MATRIX = 0.1

F32 = jnp.float32
BF16 = jnp.bfloat16
MESH = pl.DeviceIdType.MESH
VM = pltpu.VMEM
ANY = pl.ANY


def rope_tables():
    half = HEAD_DIM // 2
    exponent = np.arange(half, dtype=np.float32) * np.float32(2.0 / HEAD_DIM)
    inverse = (np.float64(ROPE_BASE) ** (-exponent.astype(np.float64))).astype(np.float32)
    angles = np.arange(LEN, dtype=np.float32)[:, None] * inverse[None, :]
    cosine = np.cos(angles.astype(np.float64)).astype(np.float32)
    sine = np.sin(angles.astype(np.float64)).astype(np.float32)
    cos_all = np.concatenate([cosine] * 4, axis=1)
    sin_all = np.concatenate([-sine, sine, -sine, sine], axis=1)
    return cos_all, sin_all


def dot(a, b, ca=1, cb=0):
    return lax.dot_general(a, b, (((ca,), (cb,)), ((), ())), preferred_element_type=F32)


def place():
    dp = lax.axis_index("dp")
    z = lax.axis_index("ctx")
    x = lax.div(dp, NY * 2)
    y = lax.rem(lax.div(dp, 2), NY)
    c = lax.rem(dp, 2)
    return x, y, c, z


def device(x, y, c, z):
    return (x * (NY * 2) + y * 2 + c, z)


def wrap(i, n):
    return lax.rem(i, n)


def remote(src, dst, ssem, rsem, dev):
    return pltpu.make_async_remote_copy(
        src_ref=src, dst_ref=dst, send_sem=ssem, recv_sem=rsem, device_id=dev, device_id_type=MESH
    )


def greet(peers):
    barrier = pltpu.get_barrier_semaphore()
    for peer in peers:
        pl.semaphore_signal(barrier, inc=1, device_id=peer, device_id_type=MESH)
    pl.semaphore_wait(barrier, len(peers))


def swap_halves(v):
    width = v.shape[1]
    lane = lax.broadcasted_iota(jnp.int32, v.shape, 1)
    down = pltpu.roll(v, width - 32, 1)
    up = pltpu.roll(v, 32, 1)
    return jnp.where(lax.rem(lane, 64) < 32, down, up)


def low_lanes(v):
    lane = lax.broadcasted_iota(jnp.int32, v.shape, 1)
    return lane < 64


class Reduction:
    @staticmethod
    def scratch(lead, r, w):
        dma = pltpu.SemaphoreType.DMA
        return [
            VM(lead + (r, w), BF16), VM((3, 4, r, w), BF16), VM((4, r, w), BF16),
            VM((3, r, w), BF16), VM((4, r, w), BF16), dma((6,)), dma((10,)),
        ]

    def __init__(self, own, fin, fin_at, bufs, swap, z_first):
        self.own, self.fin, self.fin_at, self.z_first = own, fin, fin_at, z_first
        self.rc, self.r1, self.s1, self.r2, self.r3, self.ss, self.rs = bufs
        x, y, c, z = place()
        self.c, self.z = c, z
        flip = c != swap
        self.a, self.b = jnp.where(flip, y, x), jnp.where(flip, x, y)
        self.at = lambda a, b, cc, zz: device(jnp.where(flip, b, a), jnp.where(flip, a, b), cc, zz)
        self.other = self.at(self.a, self.b, 1 - c, z)

    def copy(self, src, dst, k, dev, into=None):
        return remote(src, dst, self.ss.at[k], self.rs.at[k if into is None else into], dev)

    def whole(self, ref, k):
        return self.copy(ref, ref, k, self.other)

    def mine(self, a, z):
        return (self.c, z, a) if self.z_first else (self.c, a, z)

    def all_z(self, a):
        return self.own.at[self.c, :, a] if self.z_first else self.own.at[self.c, a]

    def core_copy(self, k):
        return self.copy(self.own.at[1 - self.c, k], self.rc.at[k], 0, self.other, 6 + k)

    def core_add(self, k):
        self.core_copy(k).wait_recv()

        def add(j, carry):
            self.own[self.c, k, j] = self.own[self.c, k, j] + self.rc[k, j]
            return carry

        lax.fori_loop(0, 4, add, 0)

    def core_all(self, act):
        def one(k, carry):
            act(k)
            return carry

        lax.fori_loop(0, 4, one, 0)

    def first_copy(self, d):
        to = wrap(self.a + d, 4)
        return self.copy(self.all_z(to), self.r1.at[d - 1], 1, self.at(to, self.b, self.c, self.z))

    def first_start(self):
        for d in range(1, 4):
            self.first_copy(d).start()

    def first_piece(self, piece):
        d = wrap(piece + 4 - self.a, 4)

        @pl.when(d > 0)
        def _():
            self.first_copy(jnp.maximum(d, 1)).start()

    def first_sum(self):
        self.whole(self.r1, 1).wait_recv()

        def add(j, carry):
            total = self.own[self.mine(self.a, j)].astype(F32) + self.r1[0, j].astype(F32)
            total = total + self.r1[1, j].astype(F32) + self.r1[2, j].astype(F32)
            self.s1[j] = total.astype(BF16)
            return carry

        lax.fori_loop(0, 4, add, 0)

    def z_start(self):
        for d in range(1, 4):
            to = wrap(self.z + d, 4)
            self.copy(self.s1.at[to], self.r2.at[d - 1], 2, self.at(self.a, self.b, self.c, to)).start()

    def z_sum(self):
        self.whole(self.r2, 2).wait_recv()
        total = self.s1[self.z].astype(F32) + self.r2[0].astype(F32)
        total = total + self.r2[1].astype(F32) + self.r2[2].astype(F32)
        self.r3[self.b] = total.astype(BF16)

    def exchange_start(self):
        for d in range(1, 4):
            to = wrap(self.b + d, 4)
            ref = self.r3.at[self.b]
            self.copy(ref, ref, 3, self.at(self.a, to, self.c, self.z)).start()

    def gather_start(self):
        self.whole(self.r3.at[0:3], 3).wait_recv()
        total = self.r3[0].astype(F32) + self.r3[1].astype(F32)
        total = total + self.r3[2].astype(F32) + self.r3[3].astype(F32)
        where = self.fin_at(self.c, self.a, 1)
        self.fin[where] = total.astype(BF16)
        ref = self.fin.at[where]
        for d in range(1, 4):
            self.copy(ref, ref, 4, self.at(wrap(self.a + d, 4), self.b, self.c, self.z)).start()

    def gather_forward(self):
        self.whole(self.fin.at[self.fin_at(0, 0, 3)], 4).wait_recv()
        ref = self.fin.at[self.fin_at(self.c, 0, 4)]
        self.copy(ref, ref, 5, self.other).start()

    def gather_wait(self):
        self.whole(self.fin.at[self.fin_at(0, 0, 4)], 5).wait_recv()

    def finish(self):
        for ref, k in (
            (self.rc, 0), (self.r1, 1), (self.r2, 2), (self.r3.at[0:3], 3),
            (self.fin.at[self.fin_at(0, 0, 3)], 4), (self.fin.at[self.fin_at(0, 0, 4)], 5),
        ):
            self.whole(ref, k).wait_send()


class VectorSum:
    SCRATCH = 4

    @staticmethod
    def scratch():
        dma = pltpu.SemaphoreType.DMA
        return [VM((2, 24, 128), F32), VM((3, 4, 24, 128), F32), dma((4,)), dma((4,))]

    def __init__(self, bufs):
        self.rc, self.r, self.ss, self.rs = bufs
        x, y, c, z = place()
        self.sibling = device(x, y, 1 - c, z)

    def copy(self, src, dst, k, dev):
        return remote(src, dst, self.ss.at[k], self.rs.at[k], dev)

    def stage(self, k):
        ref = self.rc.at[1] if k == 0 else self.r.at[k - 1, 0:3]
        return self.copy(ref, ref, k, self.sibling)

    def start(self):
        self.copy(self.rc.at[0], self.rc.at[1], 0, self.sibling).start()

    def next(self, k):
        x, y, c, z = place()
        self.stage(k).wait_recv()
        if k == 0:
            total = self.rc[0] + self.rc[1]
        else:
            total = self.r[k - 1, 0] + self.r[k - 1, 1] + self.r[k - 1, 2] + self.r[k - 1, 3]
        if k == 3:
            return total
        me = (y, z, x)[k]
        self.r[k, me] = total
        for d in range(1, 4):
            to = wrap(me + d, 4)
            dev = (device(x, to, c, z), device(x, y, c, to), device(to, y, c, z))[k]
            self.copy(self.r.at[k, me], self.r.at[k, me], k + 1, dev).start()
        return None

    def finish(self):
        for k in range(4):
            self.stage(k).wait_send()


READY = ((0, 1), (2, 3, 4), (5, 6, 7))
TILE_A = (0, 1, 2, 3, 3, 0, 1, 2)


class TileReduction:
    @staticmethod
    def scratch():
        dma = pltpu.SemaphoreType.DMA
        return [
            VM((4, NZ, 144, 128), BF16), VM((3, NZ, 144, 128), BF16), VM((NZ, 144, 128), BF16),
            VM((3, 144, 128), BF16), VM((4, 144, 128), BF16), dma((5,)), dma((8,)),
        ]

    def __init__(self, own, fin, bufs):
        self.own, self.fin = own, fin
        self.rc, self.r1, self.s1, self.r2, self.r3, self.ss, self.rs = bufs
        self.x, self.y, self.c, self.z = place()
        self.flip = self.c == 1
        self.a, self.b = jnp.where(self.flip, self.y, self.x), jnp.where(self.flip, self.x, self.y)
        last = jnp.where(self.a == 3, 4, 5 + self.a)
        self.tile = jnp.where(self.c == lax.rem(self.a + 1, 2), self.a, last)

    def at(self, a, b, z, core=None):
        core = self.c if core is None else core
        return device(jnp.where(self.flip, b, a), jnp.where(self.flip, a, b), core, z)

    def whole(self, ref, k):
        return remote(
            ref, ref, self.ss.at[k], self.rs.at[3 + k], device(self.x, self.y, 1 - self.c, self.z))

    def core_copy(self, t):
        return remote(
            self.own.at[t], self.rc.at[t // 2], self.ss.at[0], self.rs.at[t // 2],
            device(self.x, self.y, 1 - self.c, self.z))

    def core_start(self, tiles):
        for t in tiles:

            @pl.when(self.c == t % 2)
            def _(t=t):
                self.core_copy(t).start()

    def core_add(self, tiles):
        for t in tiles:

            @pl.when(self.c != t % 2)
            def _(t=t):
                self.core_copy(t).wait_recv()
                for j in range(NZ):
                    self.own[t, j] = self.own[t, j] + self.rc[t // 2, j]

    def first_start(self, tiles):
        for t in tiles:
            to = TILE_A[t]

            @pl.when(jnp.logical_and(self.c != t % 2, self.a != to))
            def _(t=t, to=to):
                k = jnp.maximum(wrap(to + NX - self.a, NX) - 1, 0)
                remote(
                    self.own.at[t], self.r1.at[k], self.ss.at[1], self.rs.at[4],
                    self.at(to, self.b, self.z)).start()

    def first_sum(self):
        self.whole(self.r1, 1).wait_recv()
        for j in range(NZ):
            total = self.own[self.tile, j].astype(F32) + self.r1[0, j].astype(F32)
            total = total + self.r1[1, j].astype(F32) + self.r1[2, j].astype(F32)
            self.s1[j] = total.astype(BF16)

    def z_start(self):
        for d in range(1, NZ):
            to = wrap(self.z + d, NZ)
            remote(
                self.s1.at[to], self.r2.at[d - 1], self.ss.at[2], self.rs.at[5],
                device(self.x, self.y, self.c, to)).start()

    def z_sum(self):
        self.whole(self.r2, 2).wait_recv()
        total = self.s1[self.z].astype(F32) + self.r2[0].astype(F32)
        total = total + self.r2[1].astype(F32) + self.r2[2].astype(F32)
        self.r3[self.b] = total.astype(BF16)

    def exchange_start(self):
        ref = self.r3.at[self.b]
        for d in range(1, NY):
            remote(ref, ref, self.ss.at[3], self.rs.at[6],
                   self.at(self.a, wrap(self.b + d, NY), self.z)).start()

    def gather_start(self):
        self.whole(self.r3.at[0:3], 3).wait_recv()
        total = self.r3[0].astype(F32) + self.r3[1].astype(F32)
        total = total + self.r3[2].astype(F32) + self.r3[3].astype(F32)
        where = (slice(None), pl.ds(pl.multiple_of(self.tile * 128, 128), 128))
        self.fin[where] = total.astype(BF16)
        ref = self.fin.at[where]
        for e in range(2):
            for d in range(NX):
                if e or d:
                    remote(ref, ref, self.ss.at[4], self.rs.at[7],
                           self.at(wrap(self.a + d, 4), self.b, self.z, wrap(self.c + e, 2))).start()

    def gather_wait(self):
        self.whole(self.fin.at[:, 0:896], 4).wait_recv()

    def finish(self):
        for ref, k in (
            (self.rc, 0), (self.r1, 1), (self.r2, 2), (self.r3.at[0:3], 3), (self.fin.at[:, 0:896], 4),
        ):
            self.whole(ref, k).wait_send()


def step_kernel(
    tok_hbm, cot_hbm, cos_hbm, sin_hbm, vstates, states,
    block_out, grad_in, new_states, new_vectors, wgu_all, wdn_all, s,
):
    x, y, c, z = place()
    sib = device(x, y, 1 - c, z)
    zdev = [device(x, y, c, wrap(z + d, NZ)) for d in range(1, NZ)]
    xdev = [device(wrap(x + d, NX), y, c, z) for d in range(1, NX)]
    ydev = [device(x, wrap(y + d, NY), c, z) for d in range(1, NY)]
    peers = [sib] + xdev + ydev + zdev
    for d in range(1, 4):
        peers.append(device(wrap(x + d, NX), y, 1 - c, z))
        peers.append(device(x, wrap(y + d, NY), 1 - c, z))
    barrier = pltpu.get_barrier_semaphore()
    for peer in peers:
        pl.semaphore_signal(barrier, inc=1, device_id=peer, device_id_type=MESH)
    wq_v, vec_v, q_s, qt_s, kvs = s["wq"], s["vec"], s["q"], s["qt"], s["kv"]
    wo_all, b_gu, b_dn, n1t = s["wo"], s["ggu"].at[0, 0:2], s["gdn"].at[0, 0:2], s["n1t"]
    m_s, l_s, ot_s, lse, att = s["m"], s["l"], s["ot"], s["lse"], s["att"]
    loc_sem = s["loc"]
    row0 = pl.multiple_of(z * ROWS, ROWS)
    loads = [
        pltpu.make_async_copy(cos_hbm.at[pl.ds(row0, ROWS)], s["cos"], loc_sem.at[0]),
        pltpu.make_async_copy(sin_hbm.at[pl.ds(row0, ROWS)], s["sin"], loc_sem.at[1]),
        pltpu.make_async_copy(cot_hbm, s["n2t"], loc_sem.at[2]),
    ]
    masters = new_states[0]
    master_loads = [
        pltpu.make_async_copy(states[0][k], masters[k], s["st_sem"].at[0, k]) for k in range(4)]
    tok_t = s["tok"]
    tok_load = pltpu.make_async_copy(tok_hbm, tok_t, loc_sem.at[7])
    vector_loads = [
        pltpu.make_async_copy(vstates[i], new_vectors[i], s["v_sem"].at[i]) for i in range(3)]
    for load in vector_loads[0:1] + master_loads[0:1] + [tok_load] + master_loads[1:] + vector_loads[1:] + loads:
        load.start()
    vec_v[0] = jnp.zeros((1, VW), F32)
    vector_loads[0].wait()
    vec_v[0, :, 0:528] = new_vectors[0][...].reshape(1, 528)
    rolled = pltpu.roll(jnp.broadcast_to(vec_v[0], (8, VW)), z * 528, 1)
    vec_v[0] = rolled[0:1, :]
    qrows = pl.ds(pl.multiple_of(z * 144, 144), 144)
    master_loads[0].wait()
    wq_v[qrows, 0:896] = masters[0][:, 0:896].astype(BF16)
    wq_v[qrows, 896:1024] = jnp.concatenate(
        [masters[0][:, 896:960].astype(BF16), jnp.zeros((144, 64), BF16)], axis=1
    )
    pl.semaphore_wait(barrier, len(peers))

    sent = []

    def group(copies, name, shape):
        whole = remote(shape, shape, s["ss"].at[name], s["rs"].at[name], sib)
        return copies, whole

    def pair_of(name):
        return s["ss"].at[name], s["rs"].at[name]

    def begin(batch):
        for copy in batch[0]:
            copy.start()
        sent.append(batch[1])

    kcols = pl.ds(pl.multiple_of(512 + c * 256, 256), 256)
    xcols = pl.ds(pl.multiple_of(x * 128, 128), 128)
    ref_k, ref_q = wq_v.at[qrows, kcols], wq_v.at[qrows, xcols]
    k_over_z = group([remote(ref_k, ref_k, *pair_of(0), dev) for dev in zdev], 0, wq_v.at[0:432, 0:256])
    v_over_z = group(
        [remote(vec_v.at[0], vec_v.at[d], *pair_of(1), zdev[d - 1]) for d in range(1, NZ)], 1, vec_v.at[1:4])
    q_over_z = group([remote(ref_q, ref_q, *pair_of(2), dev) for dev in zdev], 2, wq_v.at[0:432, 0:128])
    begin(k_over_z)
    begin(v_over_z)

    @pl.when(c == 0)
    def _():
        for copy in q_over_z[0]:
            copy.start()

    def block_rows(e, n):
        return pl.ds(pl.multiple_of(wrap(z + NZ - e, NZ) * n, n), n)

    tok_load.wait()
    inputs = jnp.transpose(tok_t[...].astype(F32))
    s["gh"][...] = inputs
    unit = inputs * lax.rsqrt(jnp.mean(inputs * inputs, axis=-1, keepdims=True) + EPS)

    master_loads[1].wait()
    wo_all[qrows, 0:512] = masters[1][:, 0:512].astype(BF16)
    wo_all[qrows, 512:640] = jnp.concatenate(
        [masters[1][:, 512:576].astype(BF16), jnp.zeros((144, 64), BF16)], axis=1)
    own = []
    master_loads[2].wait()
    master_loads[3].wait()
    down = jnp.transpose(masters[3][...]).astype(BF16)
    zrows = pl.ds(pl.multiple_of(z * 384, 384), 384)
    for p in range(8):
        b_gu[p // 4, p % 4] = masters[2][:, 384 * p : 384 * p + 384].astype(BF16)
        b_dn[p // 4, p % 4] = down[48 * p : 48 * p + 48, :]
        own.append(
            pltpu.make_async_copy(
                b_gu.at[p // 4, p % 4], wgu_all.at[qrows, 384 * p : 384 * p + 384], loc_sem.at[5]))
        own.append(
            pltpu.make_async_copy(
                b_dn.at[p // 4, p % 4], wdn_all.at[pl.ds(pl.multiple_of(z * 384 + 48 * p, 48), 48), :],
                loc_sem.at[6]))
    own_done = [
        pltpu.make_async_copy(wgu_all.at[qrows, :], wgu_all.at[qrows, :], loc_sem.at[5]),
        pltpu.make_async_copy(wdn_all.at[zrows, :], wdn_all.at[zrows, :], loc_sem.at[6]),
    ]
    for copy in own:
        copy.start()

    w = wrap(x + y, 4)
    pgu = pl.multiple_of((c * 4 + w) * 384, 128)
    pdn = (c * 4 + y) * 48
    po = jnp.minimum(c * 4 + y, 4)
    has_o = c * 4 + y < 5
    oc = pl.multiple_of(po * 128, 128)

    def down_rows(zz):
        return wdn_all.at[pl.ds(pl.multiple_of(zz * 384 + pdn, 48), 48), :]

    o_over_z = group(
        [remote(wo_all.at[qrows, pl.ds(oc, 128)], wo_all.at[qrows, pl.ds(oc, 128)], *pair_of(3), dev) for dev in zdev],
        3, wo_all.at[0:432, 0:128])
    gu_over_z = group(
        [remote(b_gu.at[c, w], wgu_all.at[qrows, pl.ds(pgu, 384)], *pair_of(4), dev) for dev in zdev],
        4, wgu_all.at[0:432, 0:384])
    dn_over_z = group(
        [remote(b_dn.at[c, y], down_rows(z), *pair_of(5), dev) for dev in zdev], 5, wdn_all.at[0:144, :])

    def weights_over_z():
        @pl.when(has_o)
        def _():
            for copy in o_over_z[0]:
                copy.start()

        for copy in dn_over_z[0] + gu_over_z[0]:
            copy.start()

    weights_over_z()
    k_over_z[1].wait_recv()
    v_over_z[1].wait_recv()
    others = range(1, NZ)
    k_over_c = group(
        [remote(wq_v.at[block_rows(e, 144), kcols], wq_v.at[block_rows(e, 144), kcols], *pair_of(6), sib)
         for e in others], 6, wq_v.at[0:432, 0:256])
    begin(k_over_c)

    q_over_x = group(
        [remote(wq_v.at[block_rows(e, 144), xcols], wq_v.at[block_rows(e, 144), xcols], *pair_of(7), dev)
         for e in others for dev in xdev], 7, wq_v.at[0:432, 0:384])
    q_over_c = group(
        [remote(wq_v.at[block_rows(e, 144), 0:512], wq_v.at[block_rows(e, 144), 0:512], *pair_of(8), sib)
         for e in others], 8, wq_v.at[0:432, 0:512])

    @pl.when(c == 0)
    def _():
        q_over_z[1].wait_recv()
        for copy in q_over_x[0]:
            copy.start()

    raw = vec_v[0] + vec_v[1] + vec_v[2] + vec_v[3]
    raw = raw.astype(BF16).astype(F32)
    wide = jnp.broadcast_to(raw, (8, VW))
    gain_one = raw[:, 0:576]
    gain_two = pltpu.roll(wide, VW - 576, 1)[0:1, 0:576]
    bias = raw[:, 1152:2176]
    normed = unit * gain_one
    n1 = normed.astype(BF16)
    n1t[...] = jnp.transpose(normed).astype(BF16)
    for load in loads:
        load.wait()
    cosine, sine = s["cos"][...], s["sin"][...]

    k_over_c[1].wait_recv()

    def tile_of(v, t):
        return v[:, 128 * t : 128 * t + 128]

    def rotated(v):
        return v * cosine + swap_halves(v) * sine

    def turn(v):
        return pltpu.roll(v, 64, 1)

    proj = dot(n1, wq_v[:, 512:1024]) + bias[:, 512:1024]
    rot4, rot5 = rotated(tile_of(proj, 0)), rotated(tile_of(proj, 1))
    val6, val7 = tile_of(proj, 2), tile_of(proj, 3)
    low = low_lanes(rot4)
    kvs[z, 0] = jnp.where(low, turn(rot4), turn(val6)).astype(BF16)
    kvs[z, 1] = jnp.where(low, rot5, val6).astype(BF16)
    kvs[z, 2] = jnp.where(low, turn(rot5), turn(val7)).astype(BF16)
    kv_sends = []
    for d in range(1, NZ):
        kv_sends.append(
            remote(kvs.at[z], kvs.at[z], s["kv_s"].at[d - 1], s["kv_r"].at[d - 1],
                   device(x, y, c, wrap(z + d, NZ))))

        @pl.when(z + d < NZ)
        def _(d=d):
            kv_sends[d - 1].start()

    def put_query(h, part):
        qh = jnp.where(low, part, 0.0) * (HEAD_DIM ** -0.5)
        q_s[h] = qh.astype(BF16)
        qt_s[h] = jnp.transpose(qh).astype(BF16)

    put_query(8, rot4)
    s["cot"][...] = jnp.transpose(s["n2t"][...].astype(F32)).astype(BF16)

    @pl.when(c == 0)
    def _():
        q_over_x[1].wait_recv()
        for copy in q_over_c[0]:
            copy.start()

    @pl.when(c == 1)
    def _():
        q_over_c[1].wait_recv()

    proj = dot(n1, wq_v[:, 0:512]) + bias[:, 0:512]
    for t in range(4):
        rot = rotated(tile_of(proj, t))
        put_query(2 * t, rot)
        put_query(2 * t + 1, turn(rot))

    def step(j):
        kvt = [jnp.transpose(kvs[j, g].astype(F32)).astype(BF16)[64:128, :] for g in range(KV_HEADS)]
        heads = range(HEADS)
        sts = [dot(kvs[j, h // GROUP], qt_s[h]) for h in heads]
        olds = [m_s[h] for h in heads]
        peaks = [jnp.maximum(jnp.max(v, axis=0, keepdims=True), o) for v, o in zip(sts, olds)]
        alphas = [jnp.exp(o - p) for o, p in zip(olds, peaks)]
        ps = [jnp.exp(v - p) for v, p in zip(sts, peaks)]
        totals = [jnp.sum(p, axis=0, keepdims=True) + l_s[h] * a for h, p, a in zip(heads, ps, alphas)]
        outs = [dot(kvt[h // GROUP], p.astype(BF16)) + ot_s[h] * a for h, p, a in zip(heads, ps, alphas)]
        for h in heads:
            m_s[h] = peaks[h]
            l_s[h] = totals[h]
            ot_s[h] = outs[h]

    def visible(width):
        shape = (256, width)
        return lax.broadcasted_iota(jnp.int32, shape, 0) <= lax.broadcasted_iota(jnp.int32, shape, 1)

    right = slice(256, 512)
    always = z >= 0

    gu_over_z[1].wait_recv()
    dn_over_z[1].wait_recv()

    @pl.when(has_o)
    def _():
        o_over_z[1].wait_recv()

    def gu_piece(e, ww):
        return wgu_all.at[block_rows(e, 144), pl.ds(pl.multiple_of((c * 4 + ww) * 384, 128), 384)]

    def o_piece(e):
        return wo_all.at[block_rows(e, 144), pl.ds(oc, 128)]

    def dn_half(e):
        return wdn_all.at[
            pl.ds(pl.multiple_of(wrap(z + NZ - e, NZ) * 384 + c * 192, 192), 192), :]

    def dn_piece(e):
        return down_rows(wrap(z + NZ - e, NZ))

    gu_over_x = group(
        [remote(gu_piece(e, w), gu_piece(e, w), *pair_of(9), dev) for e in others for dev in xdev],
        9, wgu_all.at[0:432, 0:1152])
    dn_over_y = group(
        [remote(dn_piece(e), dn_piece(e), *pair_of(10), dev) for e in others for dev in ydev],
        10, wdn_all.at[0:432, :])
    o_over_y = [
        [remote(o_piece(e), o_piece(e), s["ss"].at[11], s["os"].at[d - 1], ydev[d - 1]) for e in others]
        for d in range(1, NY)]
    o_sent = remote(wo_all.at[0:432, 0:384], wo_all.at[0:432, 0:384], s["ss"].at[11], s["os"].at[0], sib)
    own_over_c = group(
        [remote(gu_piece(e, w), gu_piece(e, w), *pair_of(12), sib) for e in others], 12, wgu_all.at[0:432, 0:384])
    gu_over_c = group(
        [remote(gu_piece(e, wrap(w + d, NX)), gu_piece(e, wrap(w + d, NX)), *pair_of(13), sib)
         for e in others for d in range(1, NX)], 13, wgu_all.at[0:432, 0:1152])
    dn_over_c = group(
        [remote(dn_half(e), dn_half(e), *pair_of(14), sib) for e in others], 14, wdn_all.at[0:576, :])
    o_over_c = []
    for core, cols in enumerate((slice(0, 512), slice(512, 640))):
        o_over_c.append(
            group(
                [remote(wo_all.at[block_rows(e, 144), cols], wo_all.at[block_rows(e, 144), cols], *pair_of(15), sib)
                 for e in others], 15, wo_all.at[0:432, cols]))

    @pl.when(has_o)
    def _():
        for copies in o_over_y:
            for copy in copies:
                copy.start()

    begin(dn_over_y)
    begin(gu_over_x)
    begin(own_over_c)

    @pl.when(always)
    def _():
        keep_a, keep_b = visible(512), visible(256)
        kvt = [jnp.transpose(kvs[z, g].astype(F32)).astype(BF16)[64:128, :] for g in range(KV_HEADS)]
        heads = range(HEADS)
        st_a = [jnp.where(keep_a, dot(kvs[z, h // GROUP, 0:256], qt_s[h]), MASK_FILL) for h in heads]
        st_b = [jnp.where(keep_b, dot(kvs[z, h // GROUP, right], qt_s[h, :, right]), MASK_FILL) for h in heads]
        none = jnp.full((1, 256), MASK_FILL, F32)
        zero = jnp.zeros((1, 256), F32)
        zeros = jnp.zeros((64, 256), F32)
        peaks = [
            jnp.maximum(
                jnp.max(a, axis=0, keepdims=True),
                jnp.concatenate([none, jnp.max(b, axis=0, keepdims=True)], axis=1))
            for a, b in zip(st_a, st_b)]
        p_a = [jnp.exp(a - p) for a, p in zip(st_a, peaks)]
        p_b = [jnp.exp(b - p[:, right]) for b, p in zip(st_b, peaks)]
        totals = [
            jnp.sum(a, axis=0, keepdims=True) + jnp.concatenate([zero, jnp.sum(b, axis=0, keepdims=True)], axis=1)
            for a, b in zip(p_a, p_b)]
        outs = [
            dot(kvt[h // GROUP][:, 0:256], p_a[h].astype(BF16))
            + jnp.concatenate([zeros, dot(kvt[h // GROUP][:, right], p_b[h].astype(BF16))], axis=1)
            for h in heads]
        for h in heads:
            m_s[h] = peaks[h]
            l_s[h] = totals[h]
            ot_s[h] = outs[h]

    def earlier(d, carry):
        @pl.when(d == jnp.where(z == NZ - 2, NZ - 2, NZ - 1))
        def _():
            for dd in range(1, NY):
                from_y = wrap(y + NY - dd, NY)

                @pl.when(c * 4 + from_y < 5)
                def _(dd=dd):
                    remote(wo_all.at[0:432, 0:128], wo_all.at[0:432, 0:128], s["ss"].at[11], s["os"].at[dd - 1],
                           sib).wait_recv()

            for core in range(2):

                @pl.when(c == core)
                def _(core=core):
                    for copy in o_over_c[core][0]:
                        copy.start()

            dn_over_y[1].wait_recv()
            begin(dn_over_c)

        @pl.when(z >= d)
        def _():
            remote(kvs.at[z], kvs.at[z], s["kv_s"].at[d - 1], s["kv_r"].at[d - 1], sib).wait_recv()
            step(z - d)

        return carry

    lax.fori_loop(1, NZ, earlier, 0)

    for h in range(HEADS):
        ot_s[h] = ot_s[h] * (1.0 / l_s[h])
        lse[h] = m_s[h] + jnp.log(l_s[h])
    for t in range(5):
        top = ot_s[2 * t]
        bottom = ot_s[2 * t + 1] if 2 * t + 1 < HEADS else jnp.zeros((64, ROWS), F32)
        att[:, 128 * t : 128 * t + 128] = jnp.transpose(jnp.concatenate([top, bottom], axis=0)).astype(BF16)

    for core in range(2):

        @pl.when(c == core)
        def _(core=core):
            o_over_c[1 - core][1].wait_recv()

    for copy in own_done:
        copy.wait()
    wo = wo_all
    wgu, wds, w_sem = s["wgu"], s["wds"], s["w_sem"]

    def weights(i, slot):
        col = pl.multiple_of(wrap(w + i, 4) * 384, 384)
        return [
            pltpu.make_async_copy(
                wgu_all.at[:, pl.ds(col, 384)], wgu.at[slot, :, 0:384], w_sem.at[0, slot]),
            pltpu.make_async_copy(
                wgu_all.at[:, pl.ds(pl.multiple_of(col + FF, 384), 384)], wgu.at[slot, :, 384:768],
                w_sem.at[0, slot]),
            pltpu.make_async_copy(wdn_all.at[pl.ds(col, 384), :], wds.at[slot], w_sem.at[1, slot]),
        ]

    def weights_wait(slot):
        pltpu.make_async_copy(wgu_all.at[:, 0:768], wgu.at[slot], w_sem.at[0, slot]).wait()
        pltpu.make_async_copy(wdn_all.at[0:384, :], wds.at[slot], w_sem.at[1, slot]).wait()

    gu_over_z[1].wait_send()
    dn_over_z[1].wait_send()
    dn_over_c[1].wait_recv()
    own_over_c[1].wait_recv()
    for load in weights(0, 0):
        load.start()
    gu_over_x[1].wait_recv()
    begin(gu_over_c)

    ggu, gdn, go, gq, fin = s["ggu"], s["gdn"], s["go"], s["gq"], s["fin"]
    def columns(width):
        def at(cc, a, count):
            return (slice(None), pl.ds(pl.multiple_of((cc * 4 + a) * width, 128), count * width))

        return at

    def down_at(cc, a, count):
        return (pl.ds(pl.multiple_of((cc * 4 + a) * 48, 48), count * 48), slice(None))

    red_gu = Reduction(ggu, fin["gu"], columns(384), s["red_gu"], 0, False)
    red_dn = Reduction(gdn, fin["dn"], down_at, s["red_dn"], 1, True)
    red_o = Reduction(go, fin["o"], columns(128), s["red_o"], 0, False)
    red_q = TileReduction(gq, fin["q"], s["red_q"])
    vecs = VectorSum(s["vecs"])
    cot, gh, n2, n2t, gn2t = s["cot"], s["gh"], s["n2"], s["n2t"], grad_in
    do_in, dot_in, delta_in, gain_row = s["do"], s["dot"], s["delta"], s["gain_row"]
    dqt, own_kv, skv, rkv = ot_s, s["own_kv"], s["skv"], s["rkv"]

    gn2t[...] = jnp.zeros_like(gn2t)
    hid = gh[...] + dot(att[:, 0:576], wo[:, 0:576])
    inv_two = lax.rsqrt(jnp.mean(hid * hid, axis=-1, keepdims=True) + EPS)
    normed = hid * inv_two * gain_two
    n2[...] = normed.astype(BF16)
    n2t[...] = jnp.transpose(normed).astype(BF16)
    gh[...] = hid
    block_out[...] = jnp.transpose(hid)

    def chunk(i, carry):
        slot = lax.rem(i, 2)
        here = wrap(w + i, 4)
        @pl.when(i > 0)
        def _():
            red_gu.core_add(wrap(w + i + 3, 4))
            red_gu.first_piece(wrap(w + i + 3, 4))

        weights_wait(slot)

        @pl.when(jnp.logical_and(i > 0, i < 3))
        def _():
            for load in weights(i + 1, 1 - slot):
                load.start()

        both = dot(n2[...], wgu[slot])
        gate, up = both[:, 0:384], both[:, 384:768]
        sg = jax.nn.sigmoid(gate)
        silu = gate * sg
        act = (silu * up).astype(BF16)
        ga = dot(cot[...], wds[slot], 1, 1)
        gg = (ga * up * sg * (1.0 + gate * (1.0 - sg))).astype(BF16)
        gu = (ga * silu).astype(BF16)
        grads = jnp.concatenate([gg, gu], axis=1)
        both = dot(n2t[...], grads).astype(BF16)
        ggu[0, here] = both[:, 0:384].reshape(NZ, 144, 384)
        ggu[1, here] = both[:, 384:768].reshape(NZ, 144, 384)
        red_gu.core_copy(here).start()
        down = dot(act, cot[...], 0, 0).astype(BF16)
        for p in range(8):
            gdn[p // 4, here, p % 4] = down[48 * p : 48 * p + 48, :]
        red_dn.core_copy(here).start()

        @pl.when(i == 0)
        def _():
            gu_over_c[1].wait_recv()
            for load in weights(1, 1):
                load.start()

        block_out[...] += lax.dot_general(wds[slot], act, (((0,), (1,)), ((), ())), preferred_element_type=F32)
        gn2t[...] += dot(wgu[slot], grads, 1, 1)

        return carry

    lax.fori_loop(0, 4, chunk, 0)

    red_gu.core_add(wrap(w + 3, 4))
    red_gu.first_piece(wrap(w + 3, 4))
    state_loads = []
    for i in range(1, 3):
        for k in range(4):
            copy = pltpu.make_async_copy(states[i][k], new_states[i][k], s["st_sem"].at[i, k])
            copy.start()
            state_loads.append(copy)

    @pl.when(always)
    def _():
        hid = gh[...]
        inv_two = lax.rsqrt(jnp.mean(hid * hid, axis=-1, keepdims=True) + EPS)
        u = hid * inv_two
        e = jnp.transpose(gn2t[...])
        f = e * gain_two
        gain_row[:, 0:576] = jnp.sum(e * u, axis=0, keepdims=True)
        gain_row[:, 576:640] = jnp.zeros((1, 64), F32)
        grad_hidden = cot[...].astype(F32) + inv_two * (f - u * jnp.mean(f * u, axis=-1, keepdims=True))
        gh[...] = grad_hidden
        ghl = grad_hidden.astype(BF16)
        grad_out = dot(att[:, 0:576], ghl, 0, 0).astype(BF16)
        for p in range(8):
            if p < 4:
                part = grad_out[:, 128 * p : 128 * p + 128]
            elif p == 4:
                part = jnp.concatenate([grad_out[:, 512:576], jnp.zeros((D, 64), BF16)], axis=1)
            else:
                part = jnp.zeros((D, 128), BF16)
            go[p // 4, p % 4] = part.reshape(NZ, 144, 128)
        red_o.core_all(lambda k: red_o.core_copy(k).start())
        gm = dot(ghl, wo[:, 0:576], 1, 1).astype(BF16).astype(F32)
        gm = jnp.concatenate([gm, jnp.zeros((ROWS, 64), F32)], axis=1)
        for h in range(HEADS):
            part = gm[:, 128 * (h // 2) : 128 * (h // 2) + 128]
            part = part if h % 2 == 1 else turn(part)
            part = jnp.where(low_lanes(part), 0.0, part)
            do_in[h] = part.astype(BF16)
            part = jnp.transpose(part)
            dot_in[h] = part.astype(BF16)
            delta_in[h] = jnp.sum(part[64:128, :] * ot_s[h], axis=0, keepdims=True)

    red_dn.core_all(red_dn.core_add)
    red_dn.first_start()

    def attend(g, j):
        kv = kvs[j, g]
        kt = jnp.transpose(kv.astype(F32)).astype(BF16)[0:64, :]
        totals = [None, None]
        for i in range(GROUP):
            h = g * GROUP + i
            dq = None
            for half in range(2):
                rows = slice(256 * half, 256 * half + 256)
                pt = jnp.exp(dot(kv[rows], qt_s[h]) - lse[h])
                dst = (pt * (dot(kv[rows], dot_in[h]) - delta_in[h])).astype(BF16)
                both = dot(dst, q_s[h]) + dot(pt.astype(BF16), do_in[h])
                totals[half] = both if i == 0 else totals[half] + both
                part = dot(kt[:, rows], dst)
                dq = part if half == 0 else dq + part
            dqt[h] += dq
        return totals

    def attend_own(g):
        keep_a, keep_b = visible(512), visible(256)
        kv = kvs[z, g]
        kt = jnp.transpose(kv.astype(F32)).astype(BF16)[0:64, :]
        left = slice(0, 256)
        totals = [None, None]
        for i in range(GROUP):
            h = g * GROUP + i
            pt = jnp.where(keep_a, jnp.exp(dot(kv[left], qt_s[h]) - lse[h]), 0.0)
            dst = (pt * (dot(kv[left], dot_in[h]) - delta_in[h])).astype(BF16)
            both = dot(dst, q_s[h]) + dot(pt.astype(BF16), do_in[h])
            totals[0] = both if i == 0 else totals[0] + both
            dq = dot(kt[:, left], dst)
            pt = jnp.where(keep_b, jnp.exp(dot(kv[right], qt_s[h, :, right]) - lse[h, :, right]), 0.0)
            dst = (pt * (dot(kv[right], dot_in[h, :, right]) - delta_in[h, :, right])).astype(BF16)
            both = dot(dst, q_s[h, right]) + dot(pt.astype(BF16), do_in[h, right])
            totals[1] = both if i == 0 else totals[1] + both
            dqt[h] += dq
            dqt[h, :, right] += dot(kt[:, right], dst)
        own_kv[g, left] = totals[0]
        own_kv[g, right] = totals[1]

    def kv_copy(g, k, dev):
        return remote(
            skv.at[g, k - 1], rkv.at[g, k - 1], s["ss"].at[16], s["dkv_r"].at[g], dev)

    gps = q_s

    def kv_wait(g):
        for count in range(1, NZ):

            @pl.when(z + count == NZ - 1)
            def _(count=count):
                part = rkv.at[g, 0:count]
                remote(part, part, s["ss"].at[16], s["dkv_r"].at[g], sib).wait_recv()
                total = own_kv[g]
                for k in range(count):
                    total = total + rkv[g, k].astype(F32)
                own_kv[g] = total

    def group_tiles(g):
        cos_t, sin_t = s["cos"][...], s["sin"][...]
        low = low_lanes(cos_t)
        kv = own_kv[g]

        def query(top, bottom):
            both = [dqt[h] if h is not None else jnp.zeros((64, ROWS), F32) for h in (top, bottom)]
            return jnp.transpose(jnp.concatenate(both, axis=0)) * (HEAD_DIM ** -0.5)

        def back(t):
            return t * cos_t - swap_halves(t) * sin_t

        if g == 0:
            return {
                0: back(query(0, 1)),
                1: back(jnp.where(low, query(2, None), turn(kv))),
                2: jnp.where(low, turn(kv), 0.0),
            }
        if g == 1:
            return {
                2: jnp.where(low, 0.0, back(query(None, 3))),
                3: back(query(4, 5)),
                4: jnp.where(low, back(kv), kv),
            }
        return {
            5: back(query(6, 7)),
            6: back(jnp.where(low, query(8, None), turn(kv))),
            7: jnp.where(low, turn(kv), 0.0),
        }

    def tiles_of(g):
        @pl.when(always)
        def _():
            for t, tile in group_tiles(g).items():
                if t == 2 and g == 0:
                    gps[2] = tile.astype(BF16)
                    continue
                if t == 2:
                    tile = tile + gps[2].astype(F32)
                low_tile = tile.astype(BF16)
                gps[t] = low_tile
                gq[t] = dot(n1t[...], low_tile).astype(BF16).reshape(NZ, 144, 128)

        red_q.core_start((READY[g]))

    dqt[...] = jnp.zeros_like(dqt)
    early = red_q.tile <= 4
    late = red_q.tile > 4
    own_one = jnp.where(z == NZ - 1, 9, 3)
    own_two = jnp.where(z == NZ - 1, 10, 6)

    def slot(t, carry):
        g = lax.div(t, 3)
        k = 3 - lax.rem(t, 3)

        @pl.when(jnp.logical_and(t < 9, z >= k))
        def _():
            for half, total in enumerate(attend(g, z - k)):
                skv[g, k - 1, 256 * half : 256 * half + 256] = total.astype(BF16)
            kv_copy(g, k, device(x, y, c, z - k)).start()

        @pl.when(jnp.logical_or(t == 2, jnp.logical_or(t == own_one, t == own_two)))
        def _():
            attend_own(jnp.where(t == 2, 0, jnp.where(t == own_one, 1, 2)))

        @pl.when(t == 0)
        def _():
            red_o.core_all(red_o.core_add)

        @pl.when(t == 2)
        def _():
            red_gu.first_sum()
            red_gu.z_start()
            red_o.first_start()

        @pl.when(t == 4)
        def _():
            kv_wait(0)
            tiles_of(0)

        @pl.when(t == 5)
        def _():
            red_q.core_add(READY[0])
            red_q.first_start(READY[0])
            red_gu.z_sum()
            red_gu.exchange_start()

        @pl.when(t == 9)
        def _():
            kv_wait(1)
            tiles_of(1)
            red_dn.first_sum()
            red_o.first_sum()
            red_q.core_add(READY[1])
            red_q.first_start(READY[1])
            red_gu.gather_start()

        return carry

    lax.fori_loop(0, 11, slot, 0)
    kv_wait(2)
    red_dn.z_start()
    red_o.z_start()
    tiles_of(2)
    red_q.core_add(READY[2])
    red_q.first_start(READY[2])

    low = low_lanes(s["cos"][...])

    def halves(t):
        tile = gps[t].astype(F32)
        return tile, turn(tile)

    (t0, _), (t1, u1), (t2, u2), (t3, u3) = [halves(t) for t in range(4)]
    (t4, u4), (t5, _), (t6, u6), (t7, _) = [halves(t) for t in range(4, 8)]
    ordered = [
        t0,
        jnp.where(low, t1, t2),
        t3,
        t5,
        jnp.where(low, t6, t1),
        jnp.where(low, t4, t6),
        jnp.where(low, t2, t4),
        t7,
    ]
    vecs.rc[0, 10:18, :] = jnp.concatenate(
        [jnp.sum(t, axis=0, keepdims=True) for t in ordered], axis=0)
    gn1 = dot(jnp.concatenate([t.astype(BF16) for t in ordered], axis=1), wq_v[...], 1, 1)
    inputs = jnp.transpose(tok_t[...].astype(F32))
    r = lax.rsqrt(jnp.mean(inputs * inputs, axis=-1, keepdims=True) + EPS)
    u = inputs * r
    f = gn1 * gain_one
    row = jnp.sum(gn1 * u, axis=0, keepdims=True)
    row = jnp.concatenate([row, jnp.zeros((1, 64), F32)], axis=1)
    for t in range(5):
        vecs.rc[0, t : t + 1, :] = row[:, 128 * t : 128 * t + 128]
        vecs.rc[0, 5 + t : 6 + t, :] = gain_row[:, 128 * t : 128 * t + 128]
    vecs.rc[0, 18:24, :] = jnp.zeros((6, 128), F32)
    vecs.start()
    @pl.when(early)
    def _():
        red_q.first_sum()
        red_q.z_start()

    grad_in[...] = jnp.transpose(gh[...] + r * (f - u * jnp.mean(f * u, axis=-1, keepdims=True)))

    def update(k, grad):
        new = adam_step(
            new_states[0][k][...], new_states[1][k][...], new_states[2][k][...], grad, RATE_MATRIX, DECAY_MATRIX)
        for i in range(3):
            new_states[i][k][...] = new[i]

    vecs.next(0)
    red_gu.gather_forward()
    red_dn.z_sum()
    red_dn.exchange_start()
    red_o.z_sum()
    red_o.exchange_start()

    @pl.when(late)
    def _():
        red_q.first_sum()
        red_q.z_start()

    vecs.next(1)
    @pl.when(early)
    def _():
        red_q.z_sum()
        red_q.exchange_start()

    @pl.when(late)
    def _():
        red_q.z_sum()
        red_q.exchange_start()

    red_dn.gather_start()
    red_o.gather_start()

    for load in state_loads:
        load.wait()
    red_gu.gather_wait()
    update(2, fin["gu"][...].astype(F32))
    @pl.when(early)
    def _():
        red_q.gather_start()

    vecs.next(2)

    @pl.when(late)
    def _():
        red_q.gather_start()

    red_dn.gather_forward()
    red_o.gather_forward()
    red_dn.gather_wait()
    update(3, jnp.transpose(fin["dn"][...].astype(F32)))
    red_o.gather_wait()
    update(1, fin["o"][:, 0:576].astype(F32))
    total = vecs.next(3)
    total = jnp.concatenate([total[t : t + 1, :] for t in range(18)], axis=1)
    pad = jnp.zeros((1, VW - 640), F32)
    flat = jnp.concatenate([total[:, 0:640], pad], axis=1)
    mid = jnp.concatenate([total[:, 640:1280], pad], axis=1)
    flat = flat + pltpu.roll(jnp.broadcast_to(mid, (8, VW)), 576, 1)[0:1, :]
    flat = flat + jnp.concatenate(
        [jnp.zeros((1, 1152), F32), total[:, 1280:2304], jnp.zeros((1, 128), F32)], axis=1)
    shift = lax.rem(VW - z * 528, VW)
    grad = pltpu.roll(jnp.broadcast_to(flat, (8, VW)), shift, 1)[0:1, 0:528]
    for load in vector_loads[1:]:
        load.wait()
    new = adam_step(*[v[...].reshape(1, 528) for v in new_vectors], grad, RATE_VECTOR, 0.0)
    for i in range(3):
        new_vectors[i][...] = new[i].reshape(528)
    red_q.gather_wait()
    tq = [fin["q"][:, 128 * t : 128 * t + 128].astype(F32) for t in range(8)]
    lowq = low_lanes(tq[0])
    ordered = [
        tq[0],
        jnp.where(lowq, tq[1], tq[2]),
        tq[3],
        tq[5],
        jnp.where(lowq, tq[6], tq[1]),
        jnp.where(lowq, tq[4], tq[6]),
        jnp.where(lowq, tq[2], tq[4]),
        tq[7],
    ]
    update(0, jnp.concatenate(ordered, axis=1)[:, 0:960])
    for red in (red_gu, red_dn, red_o):
        red.finish()
    red_q.finish()
    vecs.finish()
    for whole in sent:
        whole.wait_send()
    for count in range(1, NZ):

        @pl.when(z == count)
        def _(count=count):
            part = (skv.at[0], skv.at[0:2], skv)[count - 1]
            remote(part, part, s["ss"].at[16], s["dkv_r"].at[0], sib).wait_send()

    for d in range(1, NZ):

        @pl.when(z + d < NZ)
        def _(d=d):
            kv_sends[d - 1].wait_send()

    @pl.when(has_o)
    def _():
        o_over_z[1].wait_send()
        o_sent.wait_send()

    for core in range(2):

        @pl.when(c == core)
        def _(core=core):
            o_over_c[core][1].wait_send()

    @pl.when(c == 0)
    def _():
        for batch in (q_over_z, q_over_x, q_over_c):
            batch[1].wait_send()


MATRICES = ((144, 960), (144, D), (144, 2 * FF), (D, 384))


def train(tok_t, cot_t, cos_t, sin_t, vstates, states):
    sd = jax.ShapeDtypeStruct
    v = pl.BlockSpec(memory_space=VM)
    a = pl.BlockSpec(memory_space=ANY)
    dma = pltpu.SemaphoreType.DMA
    scratch = dict(
        wq=VM((D, QW), BF16), vec=VM((NZ, 1, VW), F32), cos=VM((ROWS, 128), F32), sin=VM((ROWS, 128), F32),

        q=VM((HEADS, ROWS, 128), BF16), qt=VM((HEADS, 128, ROWS), BF16), n1t=VM((D, ROWS), BF16),
        kv=VM((NZ, KV_HEADS, ROWS, 128), BF16),
        m=VM((HEADS, 1, ROWS), F32), l=VM((HEADS, 1, ROWS), F32), ot=VM((HEADS, 64, ROWS), F32),
        lse=VM((HEADS, 1, ROWS), F32), att=VM((ROWS, 640), BF16), wo=VM((D, OW), BF16),
        loc=dma((8,)), v_sem=dma((3,)), tok=VM((D, ROWS), BF16), ss=dma((17,)), rs=dma((16,)), os=dma((3,)), kv_s=dma((3,)), kv_r=dma((3,)),
        cot=VM((ROWS, D), BF16), gh=VM((ROWS, D), F32), n2=VM((ROWS, D), BF16), n2t=VM((D, ROWS), BF16),
        wgu=VM((2, D, 768), BF16), wds=VM((2, 384, D), BF16), w_sem=dma((2, 2)),
        do=VM((HEADS, ROWS, 128), BF16), dot=VM((HEADS, 128, ROWS), BF16), delta=VM((HEADS, 1, ROWS), F32),
        gain_row=VM((1, 640), F32),
        ggu=VM((2, 4, NZ, 144, 384), BF16), gdn=VM((2, NZ, 4, 48, D), BF16), go=VM((2, 4, NZ, 144, 128), BF16),
        gq=VM((8, NZ, 144, 128), BF16),
        fin=dict(gu=VM((144, 2 * FF), BF16), dn=VM((384, D), BF16), o=VM((144, QW), BF16), q=VM((144, QW), BF16)),
        own_kv=VM((KV_HEADS, ROWS, 128), F32),
        skv=VM((KV_HEADS, 3, ROWS, 128), BF16), rkv=VM((KV_HEADS, 3, ROWS, 128), BF16),
        dkv_r=dma((3,)), st_sem=dma((3, 4)),
        red_gu=Reduction.scratch((4, 4), 144, 384), red_dn=Reduction.scratch((4, 4), 48, D),
        red_o=Reduction.scratch((4, 4), 144, 128), red_q=TileReduction.scratch(),
        vecs=VectorSum.scratch(),
    )
    fast = lambda shape: VM(shape, F32)
    return pl.pallas_call(
        step_kernel,
        out_shape=(
            fast((D, ROWS)),
            fast((D, ROWS)),
            [[fast(shape) for shape in MATRICES] for _ in range(3)],
            [fast((528,)) for _ in range(3)],
            pltpu.HBM((D, 2 * FF), BF16),
            pltpu.HBM((FF, D), BF16),
        ),
        in_specs=[a, a, a, a, [a] * 3, [[a] * 4] * 3],
        out_specs=(v, v, [[v] * 4] * 3, [v] * 3, a, a),
        scratch_shapes=[scratch],
        compiler_params=pltpu.CompilerParams(
            collective_id=0, has_side_effects=True, vmem_limit_bytes=51 << 20),
        name="train_step",
    )(tok_t, cot_t, cos_t, sin_t, vstates, states)


def adam_step(weight, first_state, second_state, gradient, learn_rate, decay_rate):
    first_new = BETA_ONE * first_state + (1.0 - BETA_ONE) * gradient
    second_new = BETA_TWO * second_state + (1.0 - BETA_TWO) * gradient * gradient
    corr_one = 1.0 - BETA_ONE**STEP
    corr_two = 1.0 - BETA_TWO**STEP
    update = first_new / corr_one / (jnp.sqrt(second_new / corr_two) + ADAM_EPS)
    weight_new = weight - learn_rate * (update + decay_rate * weight)
    return (weight_new, first_new, second_new)


def store_kernel(sources, *rest):
    targets, sems = rest[:-1], rest[-1]
    copies = [
        pltpu.make_async_copy(a, b, sems.at[k])
        for k, (a, b) in enumerate(zip(jax.tree.leaves(sources), jax.tree.leaves(targets)))]
    for copy in copies:
        copy.start()
    for copy in copies:
        copy.wait()


def store(arrays):
    shapes = jax.tree.map(lambda t: jax.ShapeDtypeStruct(t.shape, t.dtype), arrays)
    count = len(jax.tree.leaves(arrays))
    v = pl.BlockSpec(memory_space=VM)
    a = pl.BlockSpec(memory_space=ANY)
    return pl.pallas_call(
        store_kernel,
        out_shape=shapes,
        in_specs=[jax.tree.map(lambda t: v, arrays)],
        out_specs=jax.tree.map(lambda t: a, arrays),
        scratch_shapes=[pltpu.SemaphoreType.DMA((count,))],
        compiler_params=pltpu.CompilerParams(vmem_limit_bytes=8 << 20),
        name="store",
    )(arrays)


def per_device(
    tokens, cotangent, w_qkv, w_out, w_gate_up, w_down, vectors,
    first_qkv, first_out, first_gate_up, first_down, first_vectors,
    second_qkv, second_out, second_gate_up, second_down, second_vectors,
):
    cos_np, sin_np = rope_tables()
    cos_t, sin_t = jnp.asarray(cos_np), jnp.asarray(sin_np)
    states = [
        [w_qkv, w_out, w_gate_up, w_down.T],
        [first_qkv, first_out, first_gate_up, first_down.T],
        [second_qkv, second_out, second_gate_up, second_down.T],
    ]
    vstates = [vectors, first_vectors, second_vectors]
    outs = train(
        tokens.T, cotangent.T, cos_t, sin_t, vstates, states)
    block_t, grad_t, matrices, vecs = store(tuple(outs[0:4]))
    out = [block_t.T, grad_t.T]
    for i in range(3):
        out += list(matrices[i][0:3]) + [matrices[i][3].T, vecs[i]]
    return tuple(out)


def solution(mesh):
    tokens = P(("dp", "ctx"), None)
    state = (P("ctx", None),) * 4 + (P("ctx"),)
    return jax.shard_map(
        per_device, mesh=mesh, in_specs=(tokens, tokens) + state * 3, out_specs=(tokens, tokens) + state * 3,
        check_vma=False,
    )
```
